512 devices in a mesh: section: 4 (over y), task: 32 (over z, core), row: 4 (over x).
Axes of the slice: x: 4, y: 4, z: 16, core: 2. Of those that a mesh axis runs over, the one named last changes fastest.
Arguments:
- hidden: bfloat16 [4096, 5120], P(('section', 'row'), 'task'), may hold values from -6 to 6
- piece_weight: bfloat16 [5120, 4096], P('task'), may hold values from -0.078125 to 0.078125
- task_embed: bfloat16 [8192, 512], P('task'), may hold values from -0.25 to 0.25
- task_bias: float32 [8192, 8], P('task'), may hold values from -4 to 4
- event_bin: int32 [4096, 8192], P(('section', 'row'), 'task'), may hold values from 0 to 7
- censored: int32 [4096, 8192], P(('section', 'row'), 'task'), may hold values 0 or 1
- patient_id: int32 [4096], P(('section', 'row')), may hold values from 0 to 255
- patient_rows: int32 [256], replicated, may hold values from 1 to 9
Outputs:
- hidden_grad: bfloat16 [4096, 5120], P(('section', 'row'), 'task')
- task_grad: float32 [8192, 512], P('task')
- loss: float32 [], replicated
The draws below stay inside these ranges and needn't reach their ends.
All inputs are finite; a program needn't handle non-finite values. No bound on the sum of `censored` on one device may be relied on, other than what follows from the above.
Results may differ from the reference program's by a relative error of at most 0.025.
Values may be sent and summed in bfloat16 or wider, within the bound.
A program may use at most 64 MiB of HBM per device.

```python
import math
import jax
import jax.numpy as jnp
import numpy as np
from jax import lax

D = 5120
PIECES = 8
PW = 512
TASK_DEV = 256
TASKS = 8192
ROWS = 4096
PATIENTS = 256
N_TASK = 32


def draw_hidden(key, part):
    key = jax.random.fold_in(key, 11)
    place = jnp.arange(ROWS, dtype=jnp.float32)[:, None] / ROWS
    base = jax.random.normal(key, (ROWS, D), jnp.float32)
    ramp = 0.5 + place
    return jnp.clip(base * ramp, -6.0, 6.0).astype(jnp.bfloat16)


def draw_task_bias(key, part):
    key = jax.random.fold_in(key, 23)
    place = jnp.arange(TASKS, dtype=jnp.float32)[:, None] / TASKS
    base = 0.5 * jax.random.normal(key, (TASKS, PIECES), jnp.float32)
    ramp = -2.0 + 3.0 * place
    return jnp.clip(base + ramp, -4.0, 4.0).astype(jnp.float32)


def plant(values, stream_key, least, largest):
    index_at = [jax.random.randint(jax.random.fold_in(stream_key, axis), (), 0, length) for axis, length in enumerate(values.shape)]
    main_axis = values.shape.index(max(values.shape))
    neighbour = index_at[:main_axis] + [(index_at[main_axis] + 1) % values.shape[main_axis]] + index_at[main_axis + 1:]
    return values.at[tuple(index_at)].set(least).at[tuple(neighbour)].set(largest)


def levels(rng, extent, pieces, low, largest):
    gain, own = 1.0, jax.random.fold_in(rng, 6)
    for position, blocks in pieces:
        steps = jnp.exp(jax.random.uniform(jax.random.fold_in(own, position), (blocks,), jnp.float32, low / len(pieces), largest / len(pieces)))
        gain = gain * jnp.repeat(steps, extent[position] // blocks).reshape([-1 if axis == position else 1 for axis in range(len(extent))])
    return gain


def rank_table(amount, lean):
    portions = [(1 << 20) // math.isqrt(rank ** lean) + 1 for rank in range(1, amount + 1)]
    spread = 1 + sum(portions) // (1 << 30)
    return np.cumsum(np.array([max(1, weight // spread) for weight in portions]))


def ranked_ids(own_key, extent, number_of, skew):
    table = rank_table(number_of, skew)
    pick = jax.random.randint(jax.random.fold_in(own_key, 1), extent, 0, int(table[number_of - 1]))
    standing = jnp.searchsorted(jnp.asarray(table, jnp.int32), pick, side="right")
    return jax.random.permutation(jax.random.fold_in(own_key, 2), number_of)[standing].astype(jnp.int32)


def gaussian(rng, extent, width, reach, cuts=(), held_as=jnp.bfloat16):
    array = width * jax.random.normal(rng, extent, jnp.float32)
    if cuts:
        array = array * levels(rng, extent, cuts, -0.22, 0.18)
    return jnp.clip(array, -reach, reach).astype(held_as)


def setup_inputs(seed: int = 0) -> dict:
    key_of = jax.random.split(jax.random.key(seed), 9)
    hidden = draw_hidden(jax.random.fold_in(key_of[8], 71), 0)
    piece_weight = gaussian(key_of[1], (D, PIECES * PW), D ** -0.5, 0.078125, ((0, 32),))
    task_embed = gaussian(key_of[2], (TASKS, PW), PW ** -0.5, 0.25, ((0, 32),))
    task_bias = draw_task_bias(jax.random.fold_in(key_of[8], 71), 0)
    event_bin = plant(jax.random.randint(key_of[4], (ROWS, TASKS), 0, PIECES), jax.random.fold_in(key_of[4], 1), 0, PIECES - 1).astype(jnp.int32)
    censored = plant((jax.random.randint(key_of[5], (ROWS, TASKS), 0, 4) < 3).astype(jnp.int32), jax.random.fold_in(key_of[5], 1), 0, 1)
    patient_id = plant(ranked_ids(key_of[6], (ROWS,), PATIENTS, 2), jax.random.fold_in(key_of[6], 3), 0, PATIENTS - 1).astype(jnp.int32)
    patient_rows = plant(jax.random.randint(key_of[7], (PATIENTS,), 1, 10), jax.random.fold_in(key_of[7], 1), 1, 9).astype(jnp.int32)
    return dict(hidden=hidden, piece_weight=piece_weight, task_embed=task_embed, task_bias=task_bias, event_bin=event_bin, censored=censored, patient_id=patient_id, patient_rows=patient_rows)


def block_terms(zvals, weight_row, embed, bias, bins, flags):
    logits = jnp.einsum('rpk,tk->rpt', zvals.astype(jnp.float32), embed.astype(jnp.float32)) + bias.T[None]
    piece = jnp.arange(PIECES, dtype=jnp.int32)[None, :, None]
    edge = bins[:, None, :]
    exposure = jnp.where(piece < edge, 1.0, jnp.where(piece == edge, 0.5, 0.0)).astype(jnp.float32)
    event = jnp.where(piece == edge, (1 - flags)[:, None, :], 0).astype(jnp.float32)
    hazard = exposure * jnp.exp(logits)
    scale = weight_row[:, None, None]
    nll = jnp.sum(scale * (hazard - event * logits))
    grads = (scale * (hazard - event)).astype(jnp.bfloat16)
    return nll, grads


def reference(hidden, piece_weight, task_embed, task_bias, event_bin, censored, patient_id, patient_rows):
    weight_row = 1.0 / patient_rows[patient_id].astype(jnp.float32)
    zflat = jnp.dot(hidden, piece_weight, preferred_element_type=jnp.float32).astype(jnp.bfloat16)
    zvals = zflat.reshape(ROWS, PIECES, PW)
    embeds = task_embed.reshape(N_TASK, TASK_DEV, PW)
    biases = task_bias.reshape(N_TASK, TASK_DEV, PIECES)
    bins = event_bin.reshape(ROWS, N_TASK, TASK_DEV).transpose(1, 0, 2)
    flags = censored.reshape(ROWS, N_TASK, TASK_DEV).transpose(1, 0, 2)

    def step(carry, block):
        grad_sum, total = carry
        embed, bias, bin_block, flag_block = block
        nll, grads = block_terms(zvals, weight_row, embed, bias, bin_block, flag_block)
        part = jnp.einsum('rpt,tk->rpk', grads.astype(jnp.float32), embed.astype(jnp.float32))
        part = lax.optimization_barrier(part.astype(jnp.bfloat16)).astype(jnp.float32)
        task_part = jnp.einsum('rpt,rpk->tk', grads.astype(jnp.float32), zvals.astype(jnp.float32))
        return (grad_sum + part, total + nll), task_part

    start = (jnp.zeros((ROWS, PIECES, PW), jnp.float32), jnp.zeros((), jnp.float32))
    (grad_sum, total), task_parts = lax.scan(step, start, (embeds, biases, bins, flags))
    piece_grad = grad_sum.astype(jnp.bfloat16).reshape(ROWS, PIECES * PW)
    hidden_grad = jnp.dot(piece_grad, piece_weight.T, preferred_element_type=jnp.float32).astype(jnp.bfloat16)
    task_grad = task_parts.reshape(TASKS, PW) / PATIENTS
    loss = total / (PATIENTS * TASKS)
    return hidden_grad, task_grad, loss
```

```python
import functools

import jax
import jax.numpy as jnp
from jax import lax
from jax.experimental import pallas as pl
from jax.experimental.pallas import tpu as pltpu
from jax.sharding import PartitionSpec as P

MESH = pl.DeviceIdType.MESH
F32 = jnp.float32
BF16 = jnp.bfloat16
LANES = 128
STREAMS = 4
NT = (((1,), (1,)), ((), ()))
TN = (((0,), (0,)), ((), ()))


def when(cond, fn):
    if isinstance(cond, bool):
        if cond:
            fn()
    else:
        pl.when(cond)(fn)


def kernel(
    loss_scale,
    grad_scale,
    hid_hbm,
    pw_hbm,
    te_hbm,
    bias_hbm,
    bins_hbm,
    cens_hbm,
    pid_ref,
    prow_ref,
    hg_out,
    tg_out,
    loss_out,
    hid,
    pw,
    te,
    bias,
    bias_t,
    bins,
    cens,
    wrow,
    part,
    rs_buf,
    zbuf,
    pgf,
    gbuf,
    loss_acc,
    loss_x,
    loss_y,
    loss_pair,
    tg_acc,
    tg_send,
    tg_recv,
    tx_send,
    tx_recv,
    ty_send,
    ty_recv,
    tg_fin,
    acc_own,
    acc_sib,
    hg_send,
    hg_recv,
    send_sem,
    recv_sem,
    local_sem,
    pair_send,
    pair_recv,
    px_send,
    px_recv,
    py_send,
    py_recv,
):
    rows = hid.shape[1]
    depth = hid.shape[2]
    half_cols = pw.shape[2]
    tasks = te.shape[1]
    nz = part.shape[0]
    far = nz // 2
    pieces = half_cols // te.shape[2]
    per_piece = nz // pieces
    rb = rows // STREAMS
    nx = lax.axis_size("row")
    ny = lax.axis_size("section")
    task = lax.axis_index("task")
    x = lax.axis_index("row")
    y = lax.axis_index("section")
    z = task // 2
    core = task % 2
    sib = z * 2 + 1 - core

    def wrap(v):
        return (v + 2 * nz) % nz

    def z_dev(off):
        return wrap(z + off) * 2 + core

    def copy_to(src, dst, ss, rs, **where):
        return pltpu.make_async_remote_copy(
            src_ref=src,
            dst_ref=dst,
            send_sem=ss,
            recv_sem=rs,
            device_id=where,
            device_id_type=MESH,
        )

    mine = pl.ds(pl.multiple_of(core * half_cols, half_cols), half_cols)
    other = pl.ds(pl.multiple_of((1 - core) * half_cols, half_cols), half_cols)
    loads = [
        (hid_hbm, hid.at[0]),
        (pw_hbm.at[:, mine], pw.at[0]),
        (te_hbm, te.at[0]),
        (bias_hbm, bias.at[0]),
        (bins_hbm, bins.at[0]),
        (cens_hbm, cens.at[0]),
    ]
    loads = [pltpu.make_async_copy(a, b, local_sem.at[i]) for i, (a, b) in enumerate(loads)]
    for load in loads:
        load.start()

    barrier = pltpu.get_barrier_semaphore()
    peers = [dict(task=sib), dict(task=z_dev(1)), dict(task=z_dev(-1))]
    peers += [dict(row=(x + j) % nx) for j in range(1, nx)]
    peers += [dict(section=(y + j) % ny) for j in range(1, ny)]
    for peer in peers:
        pl.semaphore_signal(barrier, inc=1, device_id=peer, device_id_type=MESH)
    pl.semaphore_wait(barrier, len(peers))

    pair = [
        (pw_hbm.at[:, other], pw.at[1]),
        (hid_hbm, hid.at[1]),
        (te_hbm, te.at[1]),
        (bias_hbm, bias.at[1]),
        (bins_hbm, bins.at[1]),
        (cens_hbm, cens.at[1]),
    ]
    pair = [
        copy_to(a, b, pair_send.at[i], pair_recv.at[i], task=sib) for i, (a, b) in enumerate(pair)
    ]
    for copy in pair:
        copy.start()

    for ph in range(2):
        for st in range(STREAMS):
            span = pl.ds(st * rb, rb)
            d = 0 if st < STREAMS // 2 else 1
            rs_buf[ph, d, 0, span, :] = jnp.zeros((rb, LANES), BF16)
            rs_buf[ph, 1 - d, 1, span, :] = jnp.zeros((rb, LANES), BF16)

    loads[0].wait()
    loads[1].wait()

    def block(i):
        return pl.ds(pl.multiple_of(i * 256, 256), 256)

    @pl.loop(0, nz // 2)
    def _(i):
        value = jnp.dot(hid[0], pw[0, :, block(i)], preferred_element_type=F32)
        part[2 * i] = value[:, :LANES]
        part[2 * i + 1] = value[:, LANES:]

    pair[0].wait_recv()
    pair[1].wait_recv()

    @pl.loop(0, nz // 2)
    def _(i):
        value = jnp.dot(hid[1], pw[1, :, block(i)], preferred_element_type=F32)
        part[2 * i] += value[:, :LANES]
        part[2 * i + 1] += value[:, LANES:]

    def long_way(st):
        return 0 if st < STREAMS // 2 else 1

    def rs_copy(ph, d, st, s, span, sgn):
        return copy_to(
            rs_buf.at[ph, d, s, span, :],
            rs_buf.at[ph, d, s + 1, span, :],
            send_sem.at[2 * ph, d, st, s],
            recv_sem.at[2 * ph, d, st, s],
            task=z_dev(sgn),
        )

    def rs_one(ph, d, st, s, sgn, first):
        span = pl.ds(pl.multiple_of(st * rb, rb), rb)

        def arrive():
            rs_copy(ph, d, st, s - 1, span, sgn).wait_recv()

        def step():
            when(s > first, arrive)
            c = wrap(z + sgn * (far - s))
            total = rs_buf[ph, d, s, span, :].astype(F32) + part[c, span, :]
            rs_buf[ph, d, s, span, :] = total.astype(BF16)
            rs_copy(ph, d, st, s, span, sgn).start()

        when(s >= first, step)

    def rs_step(ph, s):
        for st in range(STREAMS):
            for d in (long_way(st), 1 - long_way(st)):
                rs_one(ph, d, st, s, 1 - 2 * d, 0 if d == long_way(st) else 1)

    def rs_sent(ph, s):
        for st in range(STREAMS):
            span = pl.ds(st * rb, rb)
            for d in range(2):
                def sent(d=d, st=st, span=span):
                    rs_copy(ph, d, st, s, span, 1 - 2 * d).wait_send()

                if d == long_way(st):
                    sent()
                else:
                    when(s >= 1, sent)

    def rs_total(ph, st):
        span = pl.ds(st * rb, rb)
        for d in range(2):
            rs_copy(ph, d, st, far - 1, span, 1 - 2 * d).wait_recv()
        total = part[z, span, :] + rs_buf[ph, 0, far, span, :].astype(F32)
        return total + rs_buf[ph, 1, far, span, :].astype(F32)

    def ag_span(ph, st):
        extra = 16 if ph == 1 and st == STREAMS - 1 else 0
        return pl.ds(st * rb, rb + extra)

    def ag_copy(ph, d, st, s):
        buf = zbuf if ph == 0 else pgf
        sgn = 1 - 2 * d
        ref = buf.at[wrap(z - sgn * s), ag_span(ph, st), :]
        return copy_to(
            ref, ref, send_sem.at[2 * ph + 1, d, st, s], recv_sem.at[2 * ph + 1, d, st, s],
            task=z_dev(sgn),
        )

    def ag_arrived(ph, d, st, s):
        buf = zbuf if ph == 0 else pgf
        sgn = 1 - 2 * d
        ref = buf.at[wrap(z - sgn * (s + 1)), ag_span(ph, st), :]
        copy_to(
            ref, ref, send_sem.at[2 * ph + 1, d, st, s], recv_sem.at[2 * ph + 1, d, st, s],
            task=z_dev(sgn),
        ).wait_recv()

    def ag_step(ph, s):
        for st in range(STREAMS):
            for d in (long_way(st), 1 - long_way(st)):
                when(s > 0, functools.partial(ag_arrived, ph, d, st, s - 1))
                send = functools.partial(lambda d, st: ag_copy(ph, d, st, s).start(), d, st)
                if d == long_way(st):
                    send()
                else:
                    when(s < far - 1, send)

    def ag_sent(ph, s):
        for st in range(STREAMS):
            for d in range(2):
                sent = functools.partial(lambda d, st: ag_copy(ph, d, st, s).wait_send(), d, st)
                if d == long_way(st):
                    sent()
                else:
                    when(s < far - 1, sent)

    def ag_last(ph):
        for st in range(STREAMS):
            ag_arrived(ph, long_way(st), st, far - 1)

    @pl.loop(0, far)
    def _(s):
        rs_step(0, s)

    for st in range(STREAMS):
        zbuf[z, pl.ds(st * rb, rb), :] = rs_total(0, st).astype(BF16)
        for d in range(2):
            ag_copy(0, d, st, 0).start()

    ids = jnp.broadcast_to(pid_ref[...].astype(F32), (prow_ref.shape[1], rows)).T
    lane = lax.broadcasted_iota(jnp.int32, ids.shape, 1).astype(F32)
    record = jnp.where(ids == lane, prow_ref[...].astype(F32), 0.0)
    weight = 1.0 / jnp.sum(record, axis=1, keepdims=True)
    wrow[...] = jnp.broadcast_to(weight, wrow.shape)
    for i in (2, 3, 4, 5):
        loads[i].wait()
        pair[i].wait_recv()
    for h in range(2):
        bias_t[h] = bias[h].T
    loss_acc[...] = jnp.zeros_like(loss_acc)
    tg_acc[...] = jnp.zeros_like(tg_acc)
    rs_sent(0, 0)

    @pl.loop(1, far)
    def _(s):
        ag_step(0, s)
        rs_sent(0, s)

    ag_last(0)

    def head(st):
        span = pl.ds(pl.multiple_of(st * rb, rb), rb)
        zs = jnp.concatenate(
            [
                jnp.concatenate(
                    [zbuf[p * per_piece + k, span, :] for k in range(per_piece)], axis=1
                )
                for p in range(pieces)
            ],
            axis=0,
        )
        total = None
        for h in range(2):
            dots = lax.dot_general(zs, te[h], NT, preferred_element_type=F32)
            edge = bins[h, span, :]
            alive = (1 - cens[h, span, :]).astype(F32)
            weight = wrow[span, :]
            grads = []
            nll = None
            for p in range(pieces):
                piece = core * pieces + p
                logits = dots[p * rb : (p + 1) * rb] + bias_t[h, pl.ds(piece, 1), :]
                hazard = jnp.exp(logits)
                at = edge == piece
                hazard = jnp.where(edge > piece, hazard, jnp.where(at, 0.5 * hazard, 0.0))
                event = jnp.where(at, alive, 0.0)
                term = hazard - event * logits
                nll = term if nll is None else nll + term
                grad = (weight * (hazard - event)).astype(BF16)
                gbuf[h, p, span, :] = grad
                grads.append(grad)
            nll = (weight * nll).reshape(rb // 8, 8, tasks).sum(axis=0)
            loss_acc[...] += nll
            grads = jnp.concatenate(grads, axis=0)
            dots = jnp.dot(grads, te[h], preferred_element_type=F32)
            total = dots if total is None else total + dots
        for p in range(pieces):
            for k in range(per_piece):
                part[p * per_piece + k, span, :] = total[
                    p * rb : (p + 1) * rb, k * LANES : (k + 1) * LANES
                ]
        d = st // (STREAMS // 2)
        rs_one(1, d, st, 0, 1 - 2 * d, 0)

    @pl.loop(0, STREAMS)
    def _(st):
        head(st)

    def x_copy(j, src, dst, k):
        return copy_to(
            src, dst, px_send.at[k, j - 1], px_recv.at[k, j - 1], row=(x + j) % nx
        )

    def y_copy(j, src, dst, k):
        return copy_to(
            src, dst, py_send.at[k, j - 1], py_recv.at[k, j - 1], section=(y + j) % ny
        )

    def loss_x_copy(j):
        return x_copy(j, loss_x.at[x], loss_x.at[x], 0)

    def loss_y_copy(j):
        return y_copy(j, loss_y.at[y], loss_y.at[y], 0)

    bx = tasks // nx
    by = bx // ny

    def tgx_copy(j):
        peer = (x + j) % nx
        src = tx_send.at[pl.ds(pl.multiple_of(peer * bx, bx), bx), :]
        return x_copy(j, src, tx_recv.at[j - 1], 1)

    def tgy_copy(j):
        peer = (y + j) % ny
        src = ty_send.at[pl.ds(pl.multiple_of(peer * by, by), by), :]
        return y_copy(j, src, ty_recv.at[j - 1], 1)

    def agy_copy(j):
        ref = tg_fin.at[pl.ds(pl.multiple_of(x * bx + y * by, by), by), :]
        return y_copy(j, ref, ref, 2)

    def agx_copy(j):
        ref = tg_fin.at[pl.ds(pl.multiple_of(x * bx, bx), bx), :]
        return x_copy(j, ref, ref, 2)

    tg_copy = copy_to(tg_send, tg_recv, pair_send.at[6], pair_recv.at[6], task=sib)

    loss_x[x] = loss_acc[:, :LANES] + loss_acc[:, LANES:]
    for j in range(1, nx):
        loss_x_copy(j).start()
    ag_sent(0, 0)

    @pl.loop(1, far)
    def _(s):
        rs_step(1, s)
        ag_sent(0, s)

        @pl.when(s <= pieces)
        def _():
            p = s - 1
            zp = jnp.concatenate([zbuf[p * per_piece + k] for k in range(per_piece)], axis=1)
            for h in range(2):
                tg_acc[h] += lax.dot_general(gbuf[h, p], zp, TN, preferred_element_type=F32)

        @pl.when(s == 3)
        def _():
            for j in range(1, nx):
                loss_x_copy(j).wait()
            loss_y[y] = sum(loss_x[i] for i in range(1, nx)) + loss_x[0]
            for j in range(1, ny):
                loss_y_copy(j).start()

        @pl.when(s == pieces + 1)
        def _():
            tg_send[...] = tg_acc[1].astype(BF16)
            tg_copy.start()

        @pl.when(s == pieces + 2)
        def _():
            tg_copy.wait()
            tg_acc[0] += tg_recv[...].astype(F32)
            tx_send[...] = tg_acc[0].astype(BF16)
            for j in range(1, nx):
                tgx_copy(j).start()

    for j in range(1, ny):
        loss_y_copy(j).wait()
    own = sum(loss_y[i] for i in range(1, ny)) + loss_y[0]
    own = jnp.sum(jnp.sum(own, axis=0, keepdims=True), axis=1, keepdims=True)
    own = jnp.broadcast_to(own, (16, LANES))
    place = lax.broadcasted_iota(jnp.int32, own.shape, 1)
    place += LANES * lax.broadcasted_iota(jnp.int32, own.shape, 0)
    high = own.astype(BF16).astype(F32)
    rest = own - high
    middle = rest.astype(BF16).astype(F32)
    low = rest - middle
    terms = jnp.where(
        place == 0, high, jnp.where(place == 1, middle, jnp.where(place == 2, low, 0.0))
    )
    pgf[z, pl.ds(rows, 16), :] = terms.astype(BF16)

    for st in range(STREAMS):
        pgf[z, pl.ds(st * rb, rb), :] = rs_total(1, st).astype(BF16)
        for d in range(2):
            ag_copy(1, d, st, 0).start()
    rs_sent(1, 0)

    def cols(c):
        return pl.ds(pl.multiple_of(c * LANES, LANES), LANES)

    def add_chunk(c):
        value = pgf[c, pl.ds(0, rows), :]
        for h, acc in ((0, acc_own), (1, acc_sib)):
            acc[...] += lax.dot_general(
                value, pw[h, :, cols(c)], NT, preferred_element_type=F32
            )

    acc_own[...] = jnp.zeros_like(acc_own)
    acc_sib[...] = jnp.zeros_like(acc_sib)
    add_chunk(z)

    @pl.loop(1, far)
    def _(s):
        ag_step(1, s)
        rs_sent(1, s)
        ag_sent(1, s - 1)
        c0, c1 = wrap(z - s), wrap(z + s)
        value = jnp.concatenate([pgf[c0, pl.ds(0, rows), :], pgf[c1, pl.ds(0, rows), :]], axis=1)
        for h, acc in ((0, acc_own), (1, acc_sib)):
            w = jnp.concatenate([pw[h, :, cols(c0)], pw[h, :, cols(c1)]], axis=1)
            acc[...] += lax.dot_general(value, w, NT, preferred_element_type=F32)

        @pl.when(s == 1)
        def _():
            total = tg_acc[0, pl.ds(pl.multiple_of(x * bx, bx), bx), :]
            for j in range(1, nx):
                tgx_copy(j).wait()
                total += tx_recv[j - 1].astype(F32)
            tg_acc[0, pl.ds(0, bx), :] = total
            ty_send[...] = total.astype(BF16)
            for j in range(1, ny):
                tgy_copy(j).start()

        @pl.when(s == 3)
        def _():
            total = tg_acc[0, pl.ds(pl.multiple_of(y * by, by), by), :]
            for j in range(1, ny):
                tgy_copy(j).wait()
                total += ty_recv[j - 1].astype(F32)
            place = pl.ds(pl.multiple_of(x * bx + y * by, by), by)
            tg_fin[place, :] = (total * grad_scale).astype(BF16)
            for j in range(1, ny):
                agy_copy(j).start()

        @pl.when(s == 5)
        def _():
            for j in range(1, ny):
                agy_copy(j).wait_send()
                from_y = (y + ny - j) % ny
                ref = tg_fin.at[pl.ds(pl.multiple_of(x * bx + from_y * by, by), by), :]
                y_copy(j, ref, ref, 2).wait_recv()
            for j in range(1, nx):
                agx_copy(j).start()

    for j in range(1, nx):
        agx_copy(j).wait_send()
        from_x = (x + nx - j) % nx
        ref = tg_fin.at[pl.ds(pl.multiple_of(from_x * bx, bx), bx), :]
        x_copy(j, ref, ref, 2).wait_recv()
    tg_out[...] = tg_fin[...].astype(F32)

    ag_last(1)
    add_chunk(wrap(z + far))
    hg_send[...] = acc_sib[...].astype(BF16)
    hg_copy = copy_to(hg_send, hg_recv, pair_send.at[7], pair_recv.at[7], task=sib)
    hg_copy.start()
    total = pgf[0, pl.ds(rows, 16), :].astype(F32)
    for c in range(1, nz):
        total += pgf[c, pl.ds(rows, 16), :].astype(F32)
    loss_pair[core] = total
    ref = loss_pair.at[core]
    loss_copy = copy_to(ref, ref, pair_send.at[8], pair_recv.at[8], task=sib)
    loss_copy.start()
    ag_sent(1, far - 1)
    for copy in pair:
        copy.wait_send()
    loss_copy.wait()
    total = loss_pair[0] + loss_pair[1]
    loss_out[0, 0] = jnp.sum(total) * loss_scale
    hg_copy.wait()
    hg_out[...] = (acc_own[...] + hg_recv[...].astype(F32)).astype(BF16)


def shards(
    hidden, piece_weight, task_embed, task_bias, event_bin, censored, patient_id, patient_rows
):
    patients = patient_rows.shape[0]
    rows, depth = hidden.shape
    tasks, width = task_embed.shape
    pieces = task_bias.shape[1]
    n_task = lax.axis_size("task")
    nx, ny = lax.axis_size("row"), lax.axis_size("section")
    nz = n_task // 2
    half = pieces * width // 2
    bx = tasks // nx
    by = bx // ny
    slots = nz // 2 + 1
    vmem = pl.BlockSpec(memory_space=pltpu.VMEM)
    anywhere = pl.BlockSpec(memory_space=pl.ANY)
    dma = pltpu.SemaphoreType.DMA
    hg, tg, loss = pl.pallas_call(
        functools.partial(kernel, 1.0 / (patients * tasks * n_task), 1.0 / patients),
        out_shape=(
            jax.ShapeDtypeStruct((rows, depth), BF16),
            jax.ShapeDtypeStruct((tasks, width), F32),
            jax.ShapeDtypeStruct((1, 1), F32),
        ),
        in_specs=[anywhere] * 6 + [vmem] * 2,
        out_specs=(vmem, vmem, pl.BlockSpec(memory_space=pltpu.SMEM)),
        scratch_shapes=[
            pltpu.VMEM((2, rows, depth), BF16),
            pltpu.VMEM((2, depth, half), BF16),
            pltpu.VMEM((2, tasks, width), BF16),
            pltpu.VMEM((2, tasks, pieces), F32),
            pltpu.VMEM((2, pieces, tasks), F32),
            pltpu.VMEM((2, rows, tasks), jnp.int32),
            pltpu.VMEM((2, rows, tasks), jnp.int32),
            pltpu.VMEM((rows, tasks), F32),
            pltpu.VMEM((nz, rows, LANES), F32),
            pltpu.VMEM((2, 2, slots, rows, LANES), BF16),
            pltpu.VMEM((nz, rows, LANES), BF16),
            pltpu.VMEM((nz, rows + 16, LANES), BF16),
            pltpu.VMEM((2, pieces // 2, rows, tasks), BF16),
            pltpu.VMEM((8, tasks), F32),
            pltpu.VMEM((nx, 8, LANES), F32),
            pltpu.VMEM((ny, 8, LANES), F32),
            pltpu.VMEM((2, 16, LANES), F32),
            pltpu.VMEM((2, tasks, width), F32),
            pltpu.VMEM((tasks, width), BF16),
            pltpu.VMEM((tasks, width), BF16),
            pltpu.VMEM((tasks, width), BF16),
            pltpu.VMEM((nx - 1, bx, width), BF16),
            pltpu.VMEM((bx, width), BF16),
            pltpu.VMEM((ny - 1, by, width), BF16),
            pltpu.VMEM((tasks, width), BF16),
            pltpu.VMEM((rows, depth), F32),
            pltpu.VMEM((rows, depth), F32),
            pltpu.VMEM((rows, depth), BF16),
            pltpu.VMEM((rows, depth), BF16),
            dma((4, 2, STREAMS, nz // 2)),
            dma((4, 2, STREAMS, nz // 2)),
            dma((6,)),
            dma((9,)),
            dma((9,)),
            dma((3, nx - 1)),
            dma((3, nx - 1)),
            dma((3, ny - 1)),
            dma((3, ny - 1)),
        ],
        compiler_params=pltpu.CompilerParams(
            collective_id=0, has_side_effects=True, vmem_limit_bytes=40 * 1024 * 1024
        ),
        cost_estimate=pl.CostEstimate(
            flops=2400000000, bytes_accessed=4000000, transcendentals=600000
        ),
    )(
        hidden,
        piece_weight,
        task_embed,
        task_bias,
        event_bin,
        censored,
        patient_id.reshape(1, rows),
        patient_rows.reshape(1, patients),
    )
    return hg, tg, loss.reshape(())


def solution(mesh):
    return jax.shard_map(
        shards,
        mesh=mesh,
        in_specs=(
            P(("section", "row"), "task"),
            P("task", None),
            P("task", None),
            P("task", None),
            P(("section", "row"), "task"),
            P(("section", "row"), "task"),
            P(("section", "row")),
            P(),
        ),
        out_specs=(P(("section", "row"), "task"), P("task", None), P()),
        check_vma=False,
    )
```

```python
import functools

import jax
import jax.numpy as jnp
from jax import lax
from jax.experimental import pallas as pl
from jax.experimental.pallas import tpu as pltpu
from jax.sharding import PartitionSpec as P

MESH = pl.DeviceIdType.MESH
F32 = jnp.float32
BF16 = jnp.bfloat16
LANES = 128
STREAMS = 2
NT = (((1,), (1,)), ((), ()))
TN = (((0,), (0,)), ((), ()))


def when(cond, fn):
    if isinstance(cond, bool):
        if cond:
            fn()
    else:
        pl.when(cond)(fn)


def kernel(
    loss_scale,
    grad_scale,
    hid_hbm,
    pw_hbm,
    te_hbm,
    bias_hbm,
    bins_hbm,
    cens_hbm,
    pid_ref,
    prow_ref,
    hg_out,
    tg_out,
    loss_out,
    hid,
    hid_rows,
    pw,
    te,
    bias,
    bins,
    cens,
    wrow,
    part,
    rs_buf,
    zbuf,
    pgf,
    gbuf,
    loss_acc,
    loss_x,
    loss_y,
    loss_pair,
    tg_acc,
    tg_send,
    tg_recv,
    tx_send,
    tx_recv,
    ty_send,
    ty_recv,
    tg_fin,
    acc_own,
    acc_sib,
    hg_send,
    hg_recv,
    send_sem,
    recv_sem,
    local_sem,
    pair_send,
    pair_recv,
    px_send,
    px_recv,
    py_send,
    py_recv,
):
    rows = hid.shape[2]
    half_cols = pw.shape[2]
    tasks = te.shape[1]
    nz = part.shape[0]
    far = nz // 2
    pieces = half_cols // te.shape[2]
    per_piece = nz // pieces
    rb = rows // STREAMS
    nx = lax.axis_size("row")
    ny = lax.axis_size("section")
    task = lax.axis_index("task")
    x = lax.axis_index("row")
    y = lax.axis_index("section")
    z = task // 2
    core = task % 2
    sib = z * 2 + 1 - core

    def wrap(v):
        return (v + 2 * nz) % nz

    def z_dev(off):
        return wrap(z + off) * 2 + core

    def copy_to(src, dst, ss, rs, **where):
        return pltpu.make_async_remote_copy(
            src_ref=src,
            dst_ref=dst,
            send_sem=ss,
            recv_sem=rs,
            device_id=where,
            device_id_type=MESH,
        )

    mine = pl.ds(pl.multiple_of(core * half_cols, half_cols), half_cols)
    other = pl.ds(pl.multiple_of((1 - core) * half_cols, half_cols), half_cols)
    loads = [
        (hid_hbm, hid.at[0]),
        (pw_hbm.at[:, mine], pw.at[0]),
        (te_hbm, te.at[0]),
        (bias_hbm, bias.at[0]),
        (bins_hbm, bins.at[0]),
        (cens_hbm, cens.at[0]),
    ]
    loads = [pltpu.make_async_copy(a, b, local_sem.at[i]) for i, (a, b) in enumerate(loads)]
    for load in loads:
        load.start()

    barrier = pltpu.get_barrier_semaphore()
    peers = [dict(task=sib), dict(task=z_dev(1)), dict(task=z_dev(-1))]
    peers += [dict(row=(x + j) % nx) for j in range(1, nx)]
    peers += [dict(section=(y + j) % ny) for j in range(1, ny)]
    for peer in peers:
        pl.semaphore_signal(barrier, inc=1, device_id=peer, device_id_type=MESH)
    pl.semaphore_wait(barrier, len(peers))

    pair = [
        (pw_hbm.at[:, other], pw.at[1]),
        (hid_hbm, hid.at[1]),
        (te_hbm, te.at[1]),
        (bias_hbm, bias.at[1]),
        (bins_hbm, bins.at[1]),
        (cens_hbm, cens.at[1]),
    ]
    pair = [
        copy_to(a, b, pair_send.at[i], pair_recv.at[i], task=sib) for i, (a, b) in enumerate(pair)
    ]
    for copy in pair:
        copy.start()

    for ph in range(2):
        for st in range(STREAMS):
            span = pl.ds(st * rb, rb)
            d = 0 if st < STREAMS // 2 else 1
            rs_buf[ph, d, 0, span, :] = jnp.zeros((rb, LANES), BF16)
            rs_buf[ph, 1 - d, 1, span, :] = jnp.zeros((rb, LANES), BF16)

    loads[0].wait()
    loads[1].wait()

    def block(i):
        return pl.ds(pl.multiple_of(i * 256, 256), 256)

    hid_rows[...] = hid[0].T

    @pl.loop(0, nz // 2)
    def _(i):
        value = jnp.dot(hid_rows[...], pw[0, :, block(i)], preferred_element_type=F32)
        part[2 * i] = value[:, :LANES]
        part[2 * i + 1] = value[:, LANES:]

    pair[0].wait_recv()
    pair[1].wait_recv()

    hid_rows[...] = hid[1].T

    @pl.loop(0, nz // 2)
    def _(i):
        value = jnp.dot(hid_rows[...], pw[1, :, block(i)], preferred_element_type=F32)
        part[2 * i] += value[:, :LANES]
        part[2 * i + 1] += value[:, LANES:]

    def long_way(st):
        return 0 if st < STREAMS // 2 else 1

    def rs_copy(ph, d, st, s, span, sgn):
        return copy_to(
            rs_buf.at[ph, d, s, span, :],
            rs_buf.at[ph, d, s + 1, span, :],
            send_sem.at[2 * ph, d, st, s],
            recv_sem.at[2 * ph, d, st, s],
            task=z_dev(sgn),
        )

    def rs_one(ph, d, st, s, sgn, first):
        span = pl.ds(pl.multiple_of(st * rb, rb), rb)

        def arrive():
            rs_copy(ph, d, st, s - 1, span, sgn).wait_recv()

        def step():
            when(s > first, arrive)
            c = wrap(z + sgn * (far - s))
            total = rs_buf[ph, d, s, span, :].astype(F32) + part[c, span, :]
            rs_buf[ph, d, s, span, :] = total.astype(BF16)
            rs_copy(ph, d, st, s, span, sgn).start()

        when(s >= first, step)

    def rs_step(ph, s):
        for st in range(STREAMS):
            for d in (long_way(st), 1 - long_way(st)):
                rs_one(ph, d, st, s, 1 - 2 * d, 0 if d == long_way(st) else 1)

    def rs_sent(ph, s):
        for st in range(STREAMS):
            span = pl.ds(st * rb, rb)
            for d in range(2):
                def sent(d=d, st=st, span=span):
                    rs_copy(ph, d, st, s, span, 1 - 2 * d).wait_send()

                if d == long_way(st):
                    sent()
                else:
                    when(s >= 1, sent)

    def rs_total(ph, st):
        span = pl.ds(st * rb, rb)
        for d in range(2):
            rs_copy(ph, d, st, far - 1, span, 1 - 2 * d).wait_recv()
        total = part[z, span, :] + rs_buf[ph, 0, far, span, :].astype(F32)
        return total + rs_buf[ph, 1, far, span, :].astype(F32)

    def ag_span(ph, st):
        extra = 16 if ph == 1 and st == STREAMS - 1 else 0
        return pl.ds(st * rb, rb + extra)

    def ag_copy(ph, d, st, s):
        buf = zbuf if ph == 0 else pgf
        sgn = 1 - 2 * d
        ref = buf.at[wrap(z - sgn * s), ag_span(ph, st), :]
        return copy_to(
            ref, ref, send_sem.at[2 * ph + 1, d, st, s], recv_sem.at[2 * ph + 1, d, st, s],
            task=z_dev(sgn),
        )

    def ag_arrived(ph, d, st, s):
        buf = zbuf if ph == 0 else pgf
        sgn = 1 - 2 * d
        ref = buf.at[wrap(z - sgn * (s + 1)), ag_span(ph, st), :]
        copy_to(
            ref, ref, send_sem.at[2 * ph + 1, d, st, s], recv_sem.at[2 * ph + 1, d, st, s],
            task=z_dev(sgn),
        ).wait_recv()

    def ag_step(ph, s):
        for st in range(STREAMS):
            for d in (long_way(st), 1 - long_way(st)):
                when(s > 0, functools.partial(ag_arrived, ph, d, st, s - 1))
                send = functools.partial(lambda d, st: ag_copy(ph, d, st, s).start(), d, st)
                if d == long_way(st):
                    send()
                else:
                    when(s < far - 1, send)

    def ag_sent(ph, s):
        for st in range(STREAMS):
            for d in range(2):
                sent = functools.partial(lambda d, st: ag_copy(ph, d, st, s).wait_send(), d, st)
                if d == long_way(st):
                    sent()
                else:
                    when(s < far - 1, sent)

    def ag_last(ph):
        for st in range(STREAMS):
            ag_arrived(ph, long_way(st), st, far - 1)

    @pl.loop(0, far)
    def _(s):
        rs_step(0, s)

    for st in range(STREAMS):
        zbuf[z, pl.ds(st * rb, rb), :] = rs_total(0, st).astype(BF16)
        for d in range(2):
            ag_copy(0, d, st, 0).start()

    ids = jnp.broadcast_to(pid_ref[...].astype(F32), (prow_ref.shape[1], rows)).T
    lane = lax.broadcasted_iota(jnp.int32, ids.shape, 1).astype(F32)
    record = jnp.where(ids == lane, prow_ref[...].astype(F32), 0.0)
    weight = 1.0 / jnp.sum(record, axis=1, keepdims=True)
    wrow[...] = jnp.broadcast_to(weight, wrow.shape)
    for i in (2, 3, 4, 5):
        loads[i].wait()
        pair[i].wait_recv()
    loss_acc[...] = jnp.zeros_like(loss_acc)
    tg_acc[...] = jnp.zeros_like(tg_acc)
    rs_sent(0, 0)

    @pl.loop(1, far)
    def _(s):
        ag_step(0, s)
        rs_sent(0, s)

    ag_last(0)

    def head(st):
        span = pl.ds(pl.multiple_of(st * rb, rb), rb)
        zs = jnp.concatenate(
            [
                jnp.concatenate(
                    [zbuf[p * per_piece + k, span, :] for k in range(per_piece)], axis=1
                )
                for p in range(pieces)
            ],
            axis=0,
        )
        total = None
        for h in range(2):
            dots = lax.dot_general(zs, te[h], NT, preferred_element_type=F32)
            edge = bins[h, span, :]
            alive = (1 - cens[h, span, :]).astype(F32)
            weight = wrow[span, :]
            grads = []
            nll = None
            for p in range(pieces):
                piece = core * pieces + p
                logits = dots[p * rb : (p + 1) * rb] + bias[h, pl.ds(piece, 1), :]
                hazard = jnp.exp(logits)
                at = edge == piece
                hazard = jnp.where(edge > piece, hazard, jnp.where(at, 0.5 * hazard, 0.0))
                event = jnp.where(at, alive, 0.0)
                term = hazard - event * logits
                nll = term if nll is None else nll + term
                grad = (weight * (hazard - event)).astype(BF16)
                gbuf[h, p, span, :] = grad
                grads.append(grad)
            nll = (weight * nll).reshape(rb // 8, 8, tasks).sum(axis=0)
            loss_acc[...] += nll
            grads = jnp.concatenate(grads, axis=0)
            dots = jnp.dot(grads, te[h], preferred_element_type=F32)
            total = dots if total is None else total + dots
        for p in range(pieces):
            for k in range(per_piece):
                part[p * per_piece + k, span, :] = total[
                    p * rb : (p + 1) * rb, k * LANES : (k + 1) * LANES
                ]
        d = st // (STREAMS // 2)
        rs_one(1, d, st, 0, 1 - 2 * d, 0)

    @pl.loop(0, STREAMS)
    def _(st):
        head(st)

    def x_copy(j, src, dst, k):
        return copy_to(
            src, dst, px_send.at[k, j - 1], px_recv.at[k, j - 1], row=(x + j) % nx
        )

    def y_copy(j, src, dst, k):
        return copy_to(
            src, dst, py_send.at[k, j - 1], py_recv.at[k, j - 1], section=(y + j) % ny
        )

    def loss_x_copy(j):
        return x_copy(j, loss_x.at[x], loss_x.at[x], 0)

    def loss_y_copy(j):
        return y_copy(j, loss_y.at[y], loss_y.at[y], 0)

    bx = tasks // nx
    by = bx // ny

    def tgx_copy(j):
        peer = (x + j) % nx
        src = tx_send.at[pl.ds(pl.multiple_of(peer * bx, bx), bx), :]
        return x_copy(j, src, tx_recv.at[j - 1], 1)

    def tgy_copy(j):
        peer = (y + j) % ny
        src = ty_send.at[pl.ds(pl.multiple_of(peer * by, by), by), :]
        return y_copy(j, src, ty_recv.at[j - 1], 1)

    def agy_copy(j):
        ref = tg_fin.at[pl.ds(pl.multiple_of(x * bx + y * by, by), by), :]
        return y_copy(j, ref, ref, 2)

    def agx_copy(j):
        ref = tg_fin.at[pl.ds(pl.multiple_of(x * bx, bx), bx), :]
        return x_copy(j, ref, ref, 2)

    tg_copy = copy_to(tg_send, tg_recv, pair_send.at[6], pair_recv.at[6], task=sib)

    loss_x[x] = loss_acc[:, :LANES] + loss_acc[:, LANES:]
    for j in range(1, nx):
        loss_x_copy(j).start()
    ag_sent(0, 0)

    @pl.loop(1, far)
    def _(s):
        rs_step(1, s)
        ag_sent(0, s)

        @pl.when(s <= pieces)
        def _():
            p = s - 1
            zp = jnp.concatenate([zbuf[p * per_piece + k] for k in range(per_piece)], axis=1)
            for h in range(2):
                tg_acc[h] += lax.dot_general(gbuf[h, p], zp, TN, preferred_element_type=F32)

        @pl.when(s == 3)
        def _():
            for j in range(1, nx):
                loss_x_copy(j).wait()
            loss_y[y] = sum(loss_x[i] for i in range(1, nx)) + loss_x[0]
            for j in range(1, ny):
                loss_y_copy(j).start()

        @pl.when(s == pieces + 1)
        def _():
            tg_send[...] = tg_acc[1].astype(BF16)
            tg_copy.start()

        @pl.when(s == pieces + 2)
        def _():
            tg_copy.wait()
            tg_acc[0] += tg_recv[...].astype(F32)
            tx_send[...] = tg_acc[0].astype(BF16)
            for j in range(1, nx):
                tgx_copy(j).start()

    for j in range(1, ny):
        loss_y_copy(j).wait()
    own = sum(loss_y[i] for i in range(1, ny)) + loss_y[0]
    own = jnp.sum(jnp.sum(own, axis=0, keepdims=True), axis=1, keepdims=True)
    own = jnp.broadcast_to(own, (16, LANES))
    place = lax.broadcasted_iota(jnp.int32, own.shape, 1)
    place += LANES * lax.broadcasted_iota(jnp.int32, own.shape, 0)
    high = own.astype(BF16).astype(F32)
    rest = own - high
    middle = rest.astype(BF16).astype(F32)
    low = rest - middle
    terms = jnp.where(
        place == 0, high, jnp.where(place == 1, middle, jnp.where(place == 2, low, 0.0))
    )
    pgf[z, pl.ds(rows, 16), :] = terms.astype(BF16)

    for st in range(STREAMS):
        pgf[z, pl.ds(st * rb, rb), :] = rs_total(1, st).astype(BF16)
        for d in range(2):
            ag_copy(1, d, st, 0).start()
    rs_sent(1, 0)

    def cols(c):
        return pl.ds(pl.multiple_of(c * LANES, LANES), LANES)

    def add_chunk(c):
        value = pgf[c, pl.ds(0, rows), :]
        for h, acc in ((0, acc_own), (1, acc_sib)):
            acc[...] += lax.dot_general(
                pw[h, :, cols(c)], value, NT, preferred_element_type=F32
            )

    acc_own[...] = jnp.zeros_like(acc_own)
    acc_sib[...] = jnp.zeros_like(acc_sib)
    add_chunk(z)

    @pl.loop(1, far)
    def _(s):
        ag_step(1, s)
        rs_sent(1, s)
        ag_sent(1, s - 1)
        c0, c1 = wrap(z - s), wrap(z + s)
        value = jnp.concatenate([pgf[c0, pl.ds(0, rows), :], pgf[c1, pl.ds(0, rows), :]], axis=1)
        for h, acc in ((0, acc_own), (1, acc_sib)):
            w = jnp.concatenate([pw[h, :, cols(c0)], pw[h, :, cols(c1)]], axis=1)
            acc[...] += lax.dot_general(w, value, NT, preferred_element_type=F32)

        @pl.when(s == 1)
        def _():
            total = tg_acc[0, pl.ds(pl.multiple_of(x * bx, bx), bx), :]
            for j in range(1, nx):
                tgx_copy(j).wait()
                total += tx_recv[j - 1].astype(F32)
            tg_acc[0, pl.ds(0, bx), :] = total
            ty_send[...] = total.astype(BF16)
            for j in range(1, ny):
                tgy_copy(j).start()

        @pl.when(s == 3)
        def _():
            total = tg_acc[0, pl.ds(pl.multiple_of(y * by, by), by), :]
            for j in range(1, ny):
                tgy_copy(j).wait()
                total += ty_recv[j - 1].astype(F32)
            place = pl.ds(pl.multiple_of(x * bx + y * by, by), by)
            tg_fin[place, :] = (total * grad_scale).astype(BF16)
            for j in range(1, ny):
                agy_copy(j).start()

        @pl.when(s == 5)
        def _():
            for j in range(1, ny):
                agy_copy(j).wait_send()
                from_y = (y + ny - j) % ny
                ref = tg_fin.at[pl.ds(pl.multiple_of(x * bx + from_y * by, by), by), :]
                y_copy(j, ref, ref, 2).wait_recv()
            for j in range(1, nx):
                agx_copy(j).start()

    for j in range(1, nx):
        agx_copy(j).wait_send()
        from_x = (x + nx - j) % nx
        ref = tg_fin.at[pl.ds(pl.multiple_of(from_x * bx, bx), bx), :]
        x_copy(j, ref, ref, 2).wait_recv()
    tg_out[...] = tg_fin[...].astype(F32)

    ag_last(1)
    add_chunk(wrap(z + far))
    hg_send[...] = acc_sib[...].astype(BF16)
    hg_copy = copy_to(hg_send, hg_recv, pair_send.at[7], pair_recv.at[7], task=sib)
    hg_copy.start()
    total = pgf[0, pl.ds(rows, 16), :].astype(F32)
    for c in range(1, nz):
        total += pgf[c, pl.ds(rows, 16), :].astype(F32)
    loss_pair[core] = total
    ref = loss_pair.at[core]
    loss_copy = copy_to(ref, ref, pair_send.at[8], pair_recv.at[8], task=sib)
    loss_copy.start()
    ag_sent(1, far - 1)
    for copy in pair:
        copy.wait_send()
    loss_copy.wait()
    total = loss_pair[0] + loss_pair[1]
    loss_out[0, 0] = jnp.sum(total) * loss_scale
    hg_copy.wait()
    hg_out[...] = (acc_own[...] + hg_recv[...].astype(F32)).astype(BF16)


def shards(
    hidden, piece_weight, task_embed, task_bias, event_bin, censored, patient_id, patient_rows
):
    patients = patient_rows.shape[0]
    rows, depth = hidden.shape
    tasks, width = task_embed.shape
    pieces = task_bias.shape[1]
    n_task = lax.axis_size("task")
    nx, ny = lax.axis_size("row"), lax.axis_size("section")
    nz = n_task // 2
    half = pieces * width // 2
    bx = tasks // nx
    by = bx // ny
    slots = nz // 2 + 1
    vmem = pl.BlockSpec(memory_space=pltpu.VMEM)
    in_hbm = pl.BlockSpec(memory_space=pltpu.HBM)
    dma = pltpu.SemaphoreType.DMA
    hg, tg, loss = pl.pallas_call(
        functools.partial(kernel, 1.0 / (patients * tasks * n_task), 1.0 / patients),
        out_shape=(
            jax.ShapeDtypeStruct((depth, rows), BF16),
            jax.ShapeDtypeStruct((tasks, width), F32),
            jax.ShapeDtypeStruct((1, 1), F32),
        ),
        in_specs=[in_hbm] * 6 + [vmem] * 2,
        out_specs=(vmem, vmem, pl.BlockSpec(memory_space=pltpu.SMEM)),
        scratch_shapes=[
            pltpu.VMEM((2, depth, rows), BF16),
            pltpu.VMEM((rows, depth), BF16),
            pltpu.VMEM((2, depth, half), BF16),
            pltpu.VMEM((2, tasks, width), BF16),
            pltpu.VMEM((2, pieces, tasks), F32),
            pltpu.VMEM((2, rows, tasks), jnp.int32),
            pltpu.VMEM((2, rows, tasks), jnp.int32),
            pltpu.VMEM((rows, tasks), F32),
            pltpu.VMEM((nz, rows, LANES), F32),
            pltpu.VMEM((2, 2, slots, rows, LANES), BF16),
            pltpu.VMEM((nz, rows, LANES), BF16),
            pltpu.VMEM((nz, rows + 16, LANES), BF16),
            pltpu.VMEM((2, pieces // 2, rows, tasks), BF16),
            pltpu.VMEM((8, tasks), F32),
            pltpu.VMEM((nx, 8, LANES), F32),
            pltpu.VMEM((ny, 8, LANES), F32),
            pltpu.VMEM((2, 16, LANES), F32),
            pltpu.VMEM((2, tasks, width), F32),
            pltpu.VMEM((tasks, width), BF16),
            pltpu.VMEM((tasks, width), BF16),
            pltpu.VMEM((tasks, width), BF16),
            pltpu.VMEM((nx - 1, bx, width), BF16),
            pltpu.VMEM((bx, width), BF16),
            pltpu.VMEM((ny - 1, by, width), BF16),
            pltpu.VMEM((tasks, width), BF16),
            pltpu.VMEM((depth, rows), F32),
            pltpu.VMEM((depth, rows), F32),
            pltpu.VMEM((depth, rows), BF16),
            pltpu.VMEM((depth, rows), BF16),
            dma((4, 2, STREAMS, nz // 2)),
            dma((4, 2, STREAMS, nz // 2)),
            dma((6,)),
            dma((9,)),
            dma((9,)),
            dma((3, nx - 1)),
            dma((3, nx - 1)),
            dma((3, ny - 1)),
            dma((3, ny - 1)),
        ],
        compiler_params=pltpu.CompilerParams(
            collective_id=0, has_side_effects=True, vmem_limit_bytes=63 * 1024 * 1024
        ),
        cost_estimate=pl.CostEstimate(
            flops=2400000000, bytes_accessed=4000000, transcendentals=600000
        ),
    )(
        hidden.T,
        piece_weight,
        task_embed,
        task_bias.T,
        event_bin,
        censored,
        patient_id.reshape(1, rows),
        patient_rows.reshape(1, patients),
    )
    return hg.T, tg, loss.reshape(())


def solution(mesh):
    return jax.shard_map(
        shards,
        mesh=mesh,
        in_specs=(
            P(("section", "row"), "task"),
            P("task", None),
            P("task", None),
            P("task", None),
            P(("section", "row"), "task"),
            P(("section", "row"), "task"),
            P(("section", "row")),
            P(),
        ),
        out_specs=(P(("section", "row"), "task"), P("task", None), P()),
        check_vma=False,
    )
```

```python
import functools

import jax
import jax.numpy as jnp
from jax import lax
from jax.experimental import pallas as pl
from jax.experimental.pallas import tpu as pltpu
from jax.sharding import PartitionSpec as P

MESH = pl.DeviceIdType.MESH
F32 = jnp.float32
BF16 = jnp.bfloat16
LANES = 128
STREAMS = 2
CHAIN = (2, 4, 6, 8)
NT = (((1,), (1,)), ((), ()))
TN = (((0,), (0,)), ((), ()))


def kernel(
    loss_scale,
    grad_scale,
    hid_hbm,
    pw_hbm,
    te_hbm,
    bias_hbm,
    bins_hbm,
    cens_hbm,
    pid_ref,
    prow_ref,
    hg_out,
    tg_out,
    loss_out,
    hid,
    hid_rows,
    pw,
    te,
    bias,
    bins,
    cens,
    wrow,
    part,
    rs_out,
    rs_in,
    zbuf,
    pgf,
    gbuf,
    loss_acc,
    loss_x,
    loss_y,
    loss_pair,
    tg_acc,
    tg_send,
    tg_recv,
    tx_send,
    tx_recv,
    ty_send,
    ty_recv,
    tg_fin,
    acc_own,
    acc_sib,
    hg_send,
    hg_recv,
    send_sem,
    recv_sem,
    local_sem,
    pair_send,
    pair_recv,
    px_send,
    px_recv,
    py_send,
    py_recv,
):
    rows = hid.shape[2]
    half_cols = pw.shape[2]
    tasks = te.shape[1]
    nz = part.shape[0]
    far = nz // 2
    pieces = half_cols // te.shape[2]
    per_piece = nz // pieces
    rb = rows // STREAMS
    nx = lax.axis_size("row")
    ny = lax.axis_size("section")
    task = lax.axis_index("task")
    x = lax.axis_index("row")
    y = lax.axis_index("section")
    z = task // 2
    core = task % 2
    sib = z * 2 + 1 - core

    def wrap(v):
        return (v + 2 * nz) % nz

    def z_dev(off):
        return wrap(z + off) * 2 + core

    def copy_to(src, dst, ss, rs, **where):
        return pltpu.make_async_remote_copy(
            src_ref=src,
            dst_ref=dst,
            send_sem=ss,
            recv_sem=rs,
            device_id=where,
            device_id_type=MESH,
        )

    mine = pl.ds(pl.multiple_of(core * half_cols, half_cols), half_cols)
    other = pl.ds(pl.multiple_of((1 - core) * half_cols, half_cols), half_cols)
    loads = [
        (hid_hbm, hid.at[0]),
        (pw_hbm.at[:, mine], pw.at[0]),
        (te_hbm, te.at[0]),
        (bias_hbm, bias.at[0]),
        (bins_hbm, bins.at[0]),
        (cens_hbm, cens.at[0]),
    ]
    loads = [pltpu.make_async_copy(a, b, local_sem.at[i]) for i, (a, b) in enumerate(loads)]
    for load in loads:
        load.start()

    barrier = pltpu.get_barrier_semaphore()
    strides = sorted({b - a for a, b in zip((0,) + CHAIN, CHAIN)} | {1})
    peers = [dict(task=sib)] + [dict(task=z_dev(s * n)) for n in strides for s in (1, -1)]
    peers += [dict(row=(x + j) % nx) for j in range(1, nx)]
    peers += [dict(section=(y + j) % ny) for j in range(1, ny)]
    for peer in peers:
        pl.semaphore_signal(barrier, inc=1, device_id=peer, device_id_type=MESH)
    pl.semaphore_wait(barrier, len(peers))

    pair = [
        (pw_hbm.at[:, other], pw.at[1]),
        (hid_hbm, hid.at[1]),
        (te_hbm, te.at[1]),
        (bias_hbm, bias.at[1]),
        (bins_hbm, bins.at[1]),
        (cens_hbm, cens.at[1]),
    ]
    pair = [
        copy_to(a, b, pair_send.at[i], pair_recv.at[i], task=sib) for i, (a, b) in enumerate(pair)
    ]
    for copy in pair:
        copy.start()

    loads[0].wait()
    loads[1].wait()

    def block(i):
        return pl.ds(pl.multiple_of(i * 256, 256), 256)

    hid_rows[...] = hid[0].T

    @pl.loop(0, nz // 2)
    def _(i):
        value = jnp.dot(hid_rows[...], pw[0, :, block(i)], preferred_element_type=F32)
        part[2 * i] = value[:, :LANES]
        part[2 * i + 1] = value[:, LANES:]

    pair[0].wait_recv()
    pair[1].wait_recv()

    hid_rows[...] = hid[1].T

    @pl.loop(0, nz // 2)
    def _(i):
        value = jnp.dot(hid_rows[...], pw[1, :, block(i)], preferred_element_type=F32)
        part[2 * i] += value[:, :LANES]
        part[2 * i + 1] += value[:, LANES:]

    def long_way(st):
        return 0 if st < STREAMS // 2 else 1

    def stops(d, st):
        return [c for c in CHAIN if c < far or d == long_way(st)]

    def before(off):
        return max([0] + [c for c in CHAIN if c < off])

    def behind(stop, d, st):
        last = far if d == long_way(st) else far - 1
        found = [off for off in range(1, last + 1) if before(off) == stop]
        return sorted(found, key=lambda off: off not in CHAIN)

    def sides(st):
        return (long_way(st), 1 - long_way(st))

    def rs_copy(ph, d, st, off):
        span = pl.ds(st * rb, rb)
        return copy_to(
            rs_out.at[ph, d, off - 1, span, :],
            rs_in.at[ph, d, off - 1, span, :],
            send_sem.at[2 * ph, d, st, off - 1],
            recv_sem.at[2 * ph, d, st, off - 1],
            task=z_dev((1 - 2 * d) * (off - before(off))),
        )

    def rs_send(ph, d, st, off):
        span = pl.ds(st * rb, rb)
        total = part[wrap(z + (1 - 2 * d) * off), span, :]
        if off in stops(d, st):
            for other in behind(off, d, st):
                rs_copy(ph, d, st, other).wait_recv()
                total += rs_in[ph, d, other - 1, span, :].astype(F32)
        rs_out[ph, d, off - 1, span, :] = total.astype(BF16)
        rs_copy(ph, d, st, off).start()

    def rs_total(ph, st):
        span = pl.ds(st * rb, rb)
        total = part[z, span, :]
        for d in sides(st):
            for other in behind(0, d, st):
                rs_copy(ph, d, st, other).wait_recv()
                total += rs_in[ph, d, other - 1, span, :].astype(F32)
        return total

    def rs_first(ph, st):
        for d in sides(st):
            rs_send(ph, d, st, far if d == long_way(st) else far - 1)

    def rs_stage(ph, k):
        stop = ([0] + list(CHAIN))[-1 - k]
        if k > 0:
            for st in range(STREAMS):
                for d in sides(st):
                    if stop != far - 1 or d == long_way(st):
                        rs_send(ph, d, st, stop)
        for off in range(stop - 1, before(stop), -1):
            for st in range(STREAMS):
                for d in sides(st):
                    if off != far - 1 or d == long_way(st):
                        rs_send(ph, d, st, off)

    def rs_sent(ph):
        for st in range(STREAMS):
            for d in range(2):
                for off in range(1, far + 1 if d == long_way(st) else far):
                    rs_copy(ph, d, st, off).wait_send()

    def ag_copy(ph, d, st, off):
        buf = zbuf if ph == 0 else pgf
        extra = 16 if ph == 1 and st == STREAMS - 1 else 0
        sgn = 1 - 2 * d
        ref = buf.at[wrap(z - sgn * before(off)), pl.ds(st * rb, rb + extra), :]
        return copy_to(
            ref,
            ref,
            send_sem.at[2 * ph + 1, d, st, off - 1],
            recv_sem.at[2 * ph + 1, d, st, off - 1],
            task=z_dev(sgn * (off - before(off))),
        )

    def ag_arrived(ph, off):
        buf = zbuf if ph == 0 else pgf
        for st in range(STREAMS):
            extra = 16 if ph == 1 and st == STREAMS - 1 else 0
            for d in sides(st):
                if off < far or d == long_way(st):
                    ref = buf.at[wrap(z - (1 - 2 * d) * off), pl.ds(st * rb, rb + extra), :]
                    copy_to(
                        ref,
                        ref,
                        send_sem.at[2 * ph + 1, d, st, off - 1],
                        recv_sem.at[2 * ph + 1, d, st, off - 1],
                        task=z_dev((1 - 2 * d) * (off - before(off))),
                    ).wait_recv()

    def ag_send(ph, st, stop):
        for d in sides(st):
            for off in behind(stop, d, st):
                ag_copy(ph, d, st, off).start()

    def ag_stage(ph, k):
        stop = CHAIN[k - 1]
        ag_arrived(ph, stop)
        for st in range(STREAMS):
            ag_send(ph, st, stop)

    def ag_sent(ph):
        for st in range(STREAMS):
            for d in range(2):
                for off in range(1, far + 1 if d == long_way(st) else far):
                    ag_copy(ph, d, st, off).wait_send()

    between = [off for off in range(1, far) if off not in CHAIN]

    for st in range(STREAMS):
        rs_first(0, st)
    for k in range(len(CHAIN)):
        rs_stage(0, k)

    for st in range(STREAMS):
        zbuf[z, pl.ds(st * rb, rb), :] = rs_total(0, st).astype(BF16)
        ag_send(0, st, 0)

    ids = jnp.broadcast_to(pid_ref[...].astype(F32), (prow_ref.shape[1], rows)).T
    lane = lax.broadcasted_iota(jnp.int32, ids.shape, 1).astype(F32)
    record = jnp.where(ids == lane, prow_ref[...].astype(F32), 0.0)
    weight = 1.0 / jnp.sum(record, axis=1, keepdims=True)
    wrow[...] = jnp.broadcast_to(weight, wrow.shape)
    for i in (2, 3, 4, 5):
        loads[i].wait()
        pair[i].wait_recv()
    loss_acc[...] = jnp.zeros_like(loss_acc)
    tg_acc[...] = jnp.zeros_like(tg_acc)
    rs_sent(0)
    for k in range(1, len(CHAIN) + 1):
        ag_stage(0, k)
    for off in between:
        ag_arrived(0, off)

    def head(st):
        span = pl.ds(pl.multiple_of(st * rb, rb), rb)
        zs = jnp.concatenate(
            [
                jnp.concatenate(
                    [zbuf[p * per_piece + k, span, :] for k in range(per_piece)], axis=1
                )
                for p in range(pieces)
            ],
            axis=0,
        )
        total = None
        for h in range(2):
            dots = lax.dot_general(zs, te[h], NT, preferred_element_type=F32)
            edge = bins[h, span, :]
            alive = (1 - cens[h, span, :]).astype(F32)
            weight = wrow[span, :]
            grads = []
            nll = None
            for p in range(pieces):
                piece = core * pieces + p
                logits = dots[p * rb : (p + 1) * rb] + bias[h, pl.ds(piece, 1), :]
                hazard = jnp.exp(logits)
                at = edge == piece
                hazard = jnp.where(edge > piece, hazard, jnp.where(at, 0.5 * hazard, 0.0))
                event = jnp.where(at, alive, 0.0)
                term = hazard - event * logits
                nll = term if nll is None else nll + term
                grad = (weight * (hazard - event)).astype(BF16)
                gbuf[h, p, span, :] = grad
                grads.append(grad)
            nll = (weight * nll).reshape(rb // 8, 8, tasks).sum(axis=0)
            loss_acc[...] += nll
            grads = jnp.concatenate(grads, axis=0)
            dots = jnp.dot(grads, te[h], preferred_element_type=F32)
            total = dots if total is None else total + dots
        for p in range(pieces):
            for k in range(per_piece):
                part[p * per_piece + k, span, :] = total[
                    p * rb : (p + 1) * rb, k * LANES : (k + 1) * LANES
                ]

    for st in range(STREAMS):
        head(st)
        rs_first(1, st)

    def x_copy(j, src, dst, k):
        return copy_to(
            src, dst, px_send.at[k, j - 1], px_recv.at[k, j - 1], row=(x + j) % nx
        )

    def y_copy(j, src, dst, k):
        return copy_to(
            src, dst, py_send.at[k, j - 1], py_recv.at[k, j - 1], section=(y + j) % ny
        )

    def loss_x_copy(j):
        return x_copy(j, loss_x.at[x], loss_x.at[x], 0)

    def loss_y_copy(j):
        return y_copy(j, loss_y.at[y], loss_y.at[y], 0)

    bx = tasks // nx
    by = bx // ny

    def tgx_copy(j):
        peer = (x + j) % nx
        src = tx_send.at[pl.ds(pl.multiple_of(peer * bx, bx), bx), :]
        return x_copy(j, src, tx_recv.at[j - 1], 1)

    def tgy_copy(j):
        peer = (y + j) % ny
        src = ty_send.at[pl.ds(pl.multiple_of(peer * by, by), by), :]
        return y_copy(j, src, ty_recv.at[j - 1], 1)

    def agy_copy(j):
        ref = tg_fin.at[pl.ds(pl.multiple_of(x * bx + y * by, by), by), :]
        return y_copy(j, ref, ref, 2)

    def agx_copy(j):
        ref = tg_fin.at[pl.ds(pl.multiple_of(x * bx, bx), bx), :]
        return x_copy(j, ref, ref, 2)

    tg_copy = copy_to(tg_send, tg_recv, pair_send.at[6], pair_recv.at[6], task=sib)

    loss_x[x] = loss_acc[:, :LANES] + loss_acc[:, LANES:]
    for j in range(1, nx):
        loss_x_copy(j).start()
    def tg_piece(p):
        zp = jnp.concatenate([zbuf[p * per_piece + k] for k in range(per_piece)], axis=1)
        for h in range(2):
            tg_acc[h] += lax.dot_general(gbuf[h, p], zp, TN, preferred_element_type=F32)

    for k in range(len(CHAIN)):
        rs_stage(1, k)
        if k == 0:
            ag_sent(0)
            for p in range(pieces // 2):
                tg_piece(p)
        if k == 1:
            for p in range(pieces // 2, pieces):
                tg_piece(p)
            tg_send[...] = tg_acc[1].astype(BF16)
            tg_copy.start()
            for j in range(1, nx):
                loss_x_copy(j).wait()
            loss_y[y] = sum(loss_x[i] for i in range(1, nx)) + loss_x[0]
            for j in range(1, ny):
                loss_y_copy(j).start()
        if k == 2:
            tg_copy.wait()
            tg_acc[0] += tg_recv[...].astype(F32)
            tx_send[...] = tg_acc[0].astype(BF16)
            for j in range(1, nx):
                tgx_copy(j).start()
        if k == 3:
            total = tg_acc[0, pl.ds(pl.multiple_of(x * bx, bx), bx), :]
            for j in range(1, nx):
                tgx_copy(j).wait()
                total += tx_recv[j - 1].astype(F32)
            tg_acc[0, pl.ds(0, bx), :] = total
            ty_send[...] = total.astype(BF16)
            for j in range(1, ny):
                tgy_copy(j).start()

    for j in range(1, ny):
        loss_y_copy(j).wait()
    own = sum(loss_y[i] for i in range(1, ny)) + loss_y[0]
    own = jnp.sum(jnp.sum(own, axis=0, keepdims=True), axis=1, keepdims=True)
    own = jnp.broadcast_to(own, (16, LANES))
    place = lax.broadcasted_iota(jnp.int32, own.shape, 1)
    place += LANES * lax.broadcasted_iota(jnp.int32, own.shape, 0)
    high = own.astype(BF16).astype(F32)
    rest = own - high
    middle = rest.astype(BF16).astype(F32)
    low = rest - middle
    terms = jnp.where(
        place == 0, high, jnp.where(place == 1, middle, jnp.where(place == 2, low, 0.0))
    )
    pgf[z, pl.ds(rows, 16), :] = terms.astype(BF16)

    for st in range(STREAMS):
        pgf[z, pl.ds(st * rb, rb), :] = rs_total(1, st).astype(BF16)
        ag_send(1, st, 0)
    rs_sent(1)

    def cols(c):
        return pl.ds(pl.multiple_of(c * LANES, LANES), LANES)

    def add_chunks(chunks):
        value = jnp.concatenate([pgf[c, pl.ds(0, rows), :] for c in chunks], axis=1)
        for h, acc in ((0, acc_own), (1, acc_sib)):
            w = jnp.concatenate([pw[h, :, cols(c)] for c in chunks], axis=1)
            acc[...] += lax.dot_general(w, value, NT, preferred_element_type=F32)

    def add_pair(off):
        add_chunks([wrap(z - off), wrap(z + off)])

    acc_own[...] = jnp.zeros_like(acc_own)
    acc_sib[...] = jnp.zeros_like(acc_sib)
    add_chunks([z])

    total = tg_acc[0, pl.ds(pl.multiple_of(y * by, by), by), :]
    for j in range(1, ny):
        tgy_copy(j).wait()
        total += ty_recv[j - 1].astype(F32)
    place = pl.ds(pl.multiple_of(x * bx + y * by, by), by)
    tg_fin[place, :] = (total * grad_scale).astype(BF16)
    for j in range(1, ny):
        agy_copy(j).start()

    for k in range(1, len(CHAIN) + 1):
        ag_stage(1, k)
        if k < len(CHAIN):
            add_pair(CHAIN[k - 1])
        for off in between:
            if before(off) == ([0] + list(CHAIN))[k - 1]:
                ag_arrived(1, off)
                add_pair(off)
        if k == 1:
            for j in range(1, ny):
                agy_copy(j).wait_send()
                from_y = (y + ny - j) % ny
                ref = tg_fin.at[pl.ds(pl.multiple_of(x * bx + from_y * by, by), by), :]
                y_copy(j, ref, ref, 2).wait_recv()
            for j in range(1, nx):
                agx_copy(j).start()
        if k == 2:
            for j in range(1, nx):
                agx_copy(j).wait_send()
                from_x = (x + nx - j) % nx
                ref = tg_fin.at[pl.ds(pl.multiple_of(from_x * bx, bx), bx), :]
                x_copy(j, ref, ref, 2).wait_recv()
            tg_out[...] = tg_fin[...].astype(F32)

    add_chunks([wrap(z + far)])
    hg_send[...] = acc_sib[...].astype(BF16)
    hg_copy = copy_to(hg_send, hg_recv, pair_send.at[7], pair_recv.at[7], task=sib)
    hg_copy.start()
    total = pgf[0, pl.ds(rows, 16), :].astype(F32)
    for c in range(1, nz):
        total += pgf[c, pl.ds(rows, 16), :].astype(F32)
    loss_pair[core] = total
    ref = loss_pair.at[core]
    loss_copy = copy_to(ref, ref, pair_send.at[8], pair_recv.at[8], task=sib)
    loss_copy.start()
    ag_sent(1)
    for copy in pair:
        copy.wait_send()
    loss_copy.wait()
    total = loss_pair[0] + loss_pair[1]
    loss_out[0, 0] = jnp.sum(total) * loss_scale
    hg_copy.wait()
    hg_out[...] = (acc_own[...] + hg_recv[...].astype(F32)).astype(BF16)


def shards(
    hidden, piece_weight, task_embed, task_bias, event_bin, censored, patient_id, patient_rows
):
    patients = patient_rows.shape[0]
    rows, depth = hidden.shape
    tasks, width = task_embed.shape
    pieces = task_bias.shape[1]
    n_task = lax.axis_size("task")
    nx, ny = lax.axis_size("row"), lax.axis_size("section")
    nz = n_task // 2
    half = pieces * width // 2
    bx = tasks // nx
    by = bx // ny
    vmem = pl.BlockSpec(memory_space=pltpu.VMEM)
    in_hbm = pl.BlockSpec(memory_space=pltpu.HBM)
    dma = pltpu.SemaphoreType.DMA
    hg, tg, loss = pl.pallas_call(
        functools.partial(kernel, 1.0 / (patients * tasks * n_task), 1.0 / patients),
        out_shape=(
            jax.ShapeDtypeStruct((depth, rows), BF16),
            jax.ShapeDtypeStruct((tasks, width), F32),
            jax.ShapeDtypeStruct((1, 1), F32),
        ),
        in_specs=[in_hbm] * 6 + [vmem] * 2,
        out_specs=(vmem, vmem, pl.BlockSpec(memory_space=pltpu.SMEM)),
        scratch_shapes=[
            pltpu.VMEM((2, depth, rows), BF16),
            pltpu.VMEM((rows, depth), BF16),
            pltpu.VMEM((2, depth, half), BF16),
            pltpu.VMEM((2, tasks, width), BF16),
            pltpu.VMEM((2, pieces, tasks), F32),
            pltpu.VMEM((2, rows, tasks), jnp.int32),
            pltpu.VMEM((2, rows, tasks), jnp.int32),
            pltpu.VMEM((rows, tasks), F32),
            pltpu.VMEM((nz, rows, LANES), F32),
            pltpu.VMEM((2, 2, nz // 2, rows, LANES), BF16),
            pltpu.VMEM((2, 2, nz // 2, rows, LANES), BF16),
            pltpu.VMEM((nz, rows, LANES), BF16),
            pltpu.VMEM((nz, rows + 16, LANES), BF16),
            pltpu.VMEM((2, pieces // 2, rows, tasks), BF16),
            pltpu.VMEM((8, tasks), F32),
            pltpu.VMEM((nx, 8, LANES), F32),
            pltpu.VMEM((ny, 8, LANES), F32),
            pltpu.VMEM((2, 16, LANES), F32),
            pltpu.VMEM((2, tasks, width), F32),
            pltpu.VMEM((tasks, width), BF16),
            pltpu.VMEM((tasks, width), BF16),
            pltpu.VMEM((tasks, width), BF16),
            pltpu.VMEM((nx - 1, bx, width), BF16),
            pltpu.VMEM((bx, width), BF16),
            pltpu.VMEM((ny - 1, by, width), BF16),
            pltpu.VMEM((tasks, width), BF16),
            pltpu.VMEM((depth, rows), F32),
            pltpu.VMEM((depth, rows), F32),
            pltpu.VMEM((depth, rows), BF16),
            pltpu.VMEM((depth, rows), BF16),
            dma((4, 2, STREAMS, nz // 2)),
            dma((4, 2, STREAMS, nz // 2)),
            dma((6,)),
            dma((9,)),
            dma((9,)),
            dma((3, nx - 1)),
            dma((3, nx - 1)),
            dma((3, ny - 1)),
            dma((3, ny - 1)),
        ],
        compiler_params=pltpu.CompilerParams(
            collective_id=0, has_side_effects=True, vmem_limit_bytes=63 * 1024 * 1024
        ),
        cost_estimate=pl.CostEstimate(
            flops=2400000000, bytes_accessed=4000000, transcendentals=600000
        ),
    )(
        hidden.T,
        piece_weight,
        task_embed,
        task_bias.T,
        event_bin,
        censored,
        patient_id.reshape(1, rows),
        patient_rows.reshape(1, patients),
    )
    return hg.T, tg, loss.reshape(())


def solution(mesh):
    return jax.shard_map(
        shards,
        mesh=mesh,
        in_specs=(
            P(("section", "row"), "task"),
            P("task", None),
            P("task", None),
            P("task", None),
            P(("section", "row"), "task"),
            P(("section", "row"), "task"),
            P(("section", "row")),
            P(),
        ),
        out_specs=(P(("section", "row"), "task"), P("task", None), P()),
        check_vma=False,
    )
```

```python
import functools

import jax
import jax.numpy as jnp
from jax import lax
from jax.experimental import pallas as pl
from jax.experimental.pallas import tpu as pltpu
from jax.sharding import PartitionSpec as P

MESH = pl.DeviceIdType.MESH
F32 = jnp.float32
BF16 = jnp.bfloat16
LANES = 128
STREAMS = 2
CHAIN = (2, 4, 6, 8)
LAG = 1
NT = (((1,), (1,)), ((), ()))
TN = (((0,), (0,)), ((), ()))


def kernel(
    loss_scale,
    grad_scale,
    hid_hbm,
    pw_hbm,
    te_hbm,
    bias_hbm,
    bins_hbm,
    cens_hbm,
    pid_hbm,
    prow_hbm,
    hg_out,
    tg_out,
    loss_out,
    pid_ref,
    prow_ref,
    hid,
    hid_rows,
    pw,
    te,
    bias,
    bins,
    cens,
    wrow,
    part,
    rs_out,
    rs_in,
    zbuf,
    pgf,
    gbuf,
    loss_acc,
    loss_x,
    loss_y,
    loss_pair,
    tg_acc,
    tg_send,
    tg_recv,
    tx_send,
    tx_recv,
    ty_send,
    ty_recv,
    tg_fin,
    acc_own,
    acc_sib,
    hg_send,
    hg_recv,
    send_sem,
    recv_sem,
    local_sem,
    pair_send,
    pair_recv,
    pw_send,
    pw_recv,
    px_send,
    px_recv,
    py_send,
    py_recv,
):
    rows = hid.shape[2]
    half_cols = pw.shape[2]
    tasks = te.shape[1]
    nz = part.shape[0]
    far = nz // 2
    pieces = half_cols // te.shape[2]
    per_piece = nz // pieces
    rb = rows // STREAMS
    nx = lax.axis_size("row")
    ny = lax.axis_size("section")
    task = lax.axis_index("task")
    x = lax.axis_index("row")
    y = lax.axis_index("section")
    z = task // 2
    core = task % 2
    sib = z * 2 + 1 - core

    def wrap(v):
        return (v + 2 * nz) % nz

    def z_dev(off):
        return wrap(z + off) * 2 + core

    def copy_to(src, dst, ss, rs, **where):
        return pltpu.make_async_remote_copy(
            src_ref=src,
            dst_ref=dst,
            send_sem=ss,
            recv_sem=rs,
            device_id=where,
            device_id_type=MESH,
        )

    mine = pl.ds(pl.multiple_of(core * half_cols, half_cols), half_cols)
    loads = [
        (hid_hbm, hid.at[0]),
        (pw_hbm.at[:, mine], pw.at[0]),
        (te_hbm, te.at[0]),
        (bias_hbm, bias.at[0]),
        (bins_hbm, bins.at[0]),
        (cens_hbm, cens.at[0]),
        (pid_hbm, pid_ref),
        (prow_hbm, prow_ref),
    ]
    loads = [pltpu.make_async_copy(a, b, local_sem.at[i]) for i, (a, b) in enumerate(loads)]
    for load in loads:
        load.start()

    barrier = pltpu.get_barrier_semaphore()
    strides = sorted({b - a for a, b in zip((0,) + CHAIN, CHAIN)} | {1})
    peers = [dict(task=sib)] + [dict(task=z_dev(s * n)) for n in strides for s in (1, -1)]
    peers += [dict(row=(x + j) % nx) for j in range(1, nx)]
    peers += [dict(section=(y + j) % ny) for j in range(1, ny)]
    for peer in peers:
        pl.semaphore_signal(barrier, inc=1, device_id=peer, device_id_type=MESH)
    pl.semaphore_wait(barrier, len(peers))

    pair = [
        (hid_hbm, hid.at[1]),
        (te_hbm, te.at[1]),
        (bias_hbm, bias.at[1]),
        (bins_hbm, bins.at[1]),
        (cens_hbm, cens.at[1]),
    ]
    pair = [
        copy_to(a, b, pair_send.at[i], pair_recv.at[i], task=sib) for i, (a, b) in enumerate(pair)
    ]

    part_cols = half_cols // far

    def pw_copy(n):
        q = (wrap(z + far) // 2 + n + far) % far
        there = pl.ds(
            pl.multiple_of((1 - core) * half_cols + q * part_cols, part_cols), part_cols
        )
        here = pl.ds(pl.multiple_of(q * part_cols, part_cols), part_cols)
        return copy_to(
            pw_hbm.at[:, there], pw.at[1, :, here], pw_send.at[q], pw_recv.at[q], task=sib
        )

    pw_order = [0] + [s * n for n in range(1, far // 2) for s in (1, -1)] + [far // 2]
    pair[0].start()
    for n in pw_order:
        pw_copy(n).start()
    for copy in pair[1:]:
        copy.start()

    def long_way(st):
        return 0 if st < STREAMS // 2 else 1

    def stops(d, st):
        return [c for c in CHAIN if c < far or d == long_way(st)]

    def before(off):
        return max([0] + [c for c in CHAIN if c < off])

    def behind(stop, d, st):
        last = far if d == long_way(st) else far - 1
        found = [off for off in range(1, last + 1) if before(off) == stop]
        return sorted(found, key=lambda off: off not in CHAIN)

    def sides(st):
        return (long_way(st), 1 - long_way(st))

    def rs_copy(ph, d, st, off):
        span = pl.ds(st * rb, rb)
        return copy_to(
            rs_out.at[ph, d, off - 1, span, :],
            rs_in.at[ph, d, off - 1, span, :],
            send_sem.at[2 * ph, d, st, off - 1],
            recv_sem.at[2 * ph, d, st, off - 1],
            task=z_dev((1 - 2 * d) * (off - before(off))),
        )

    def cols(c):
        return pl.ds(pl.multiple_of(c * LANES, LANES), LANES)

    def own_part(ph, off, span):
        c = wrap(z + off)
        if ph == 1:
            return part[c, span, :]
        total = jnp.dot(hid_rows[0, span, :], pw[0, :, cols(c)], preferred_element_type=F32)
        return total + jnp.dot(
            hid_rows[1, span, :], pw[1, :, cols(c)], preferred_element_type=F32
        )

    def rs_send(ph, d, st, off):
        span = pl.ds(st * rb, rb)
        total = own_part(ph, (1 - 2 * d) * off, span)
        if off in stops(d, st):
            for other in behind(off, d, st):
                rs_copy(ph, d, st, other).wait_recv()
                total += rs_in[ph, d, other - 1, span, :].astype(F32)
        rs_out[ph, d, off - 1, span, :] = total.astype(BF16)
        rs_copy(ph, d, st, off).start()

    def rs_total(ph, st):
        span = pl.ds(st * rb, rb)
        total = own_part(ph, 0, span)
        for d in sides(st):
            for other in behind(0, d, st):
                rs_copy(ph, d, st, other).wait_recv()
                total += rs_in[ph, d, other - 1, span, :].astype(F32)
        return total

    def rs_stage(ph, st, k):
        stop = ([0] + list(CHAIN))[-1 - k]
        for d in sides(st):
            if k == 0:
                rs_send(ph, d, st, far if d == long_way(st) else far - 1)
            elif stop != far - 1 or d == long_way(st):
                rs_send(ph, d, st, stop)
        for off in range(stop - 1, before(stop), -1):
            for d in sides(st):
                if off != far - 1 or d == long_way(st):
                    rs_send(ph, d, st, off)

    def rs_sent(ph):
        for st in range(STREAMS):
            for d in range(2):
                for off in range(1, far + 1 if d == long_way(st) else far):
                    rs_copy(ph, d, st, off).wait_send()

    def ag_copy(ph, d, st, off):
        buf = zbuf if ph == 0 else pgf
        extra = 16 if ph == 1 and st == STREAMS - 1 else 0
        sgn = 1 - 2 * d
        ref = buf.at[wrap(z - sgn * before(off)), pl.ds(st * rb, rb + extra), :]
        return copy_to(
            ref,
            ref,
            send_sem.at[2 * ph + 1, d, st, off - 1],
            recv_sem.at[2 * ph + 1, d, st, off - 1],
            task=z_dev(sgn * (off - before(off))),
        )

    def ag_arrived(ph, d, st, off):
        buf = zbuf if ph == 0 else pgf
        extra = 16 if ph == 1 and st == STREAMS - 1 else 0
        sgn = 1 - 2 * d
        if off < far or d == long_way(st):
            ref = buf.at[wrap(z - sgn * off), pl.ds(st * rb, rb + extra), :]
            copy_to(
                ref,
                ref,
                send_sem.at[2 * ph + 1, d, st, off - 1],
                recv_sem.at[2 * ph + 1, d, st, off - 1],
                task=z_dev(sgn * (off - before(off))),
            ).wait_recv()

    def ag_stage(ph, st, k):
        stop = ([0] + list(CHAIN))[k]
        for d in sides(st):
            if k > 0:
                ag_arrived(ph, d, st, stop)
            for off in behind(stop, d, st)[:1]:
                ag_copy(ph, d, st, off).start()
        for d in sides(st):
            for off in behind(stop, d, st)[1:]:
                ag_copy(ph, d, st, off).start()

    def ag_sent(ph):
        for st in range(STREAMS):
            for d in range(2):
                for off in range(1, far + 1 if d == long_way(st) else far):
                    ag_copy(ph, d, st, off).wait_send()

    between = [off for off in range(1, far) if off not in CHAIN]

    def prepare():
        loads[6].wait()
        loads[7].wait()
        ids = jnp.broadcast_to(pid_ref[...].astype(F32), (prow_ref.shape[1], rows)).T
        lane = lax.broadcasted_iota(jnp.int32, ids.shape, 1).astype(F32)
        record = jnp.where(ids == lane, prow_ref[...].astype(F32), 0.0)
        weight = 1.0 / jnp.sum(record, axis=1, keepdims=True)
        wrow[...] = jnp.broadcast_to(weight, wrow.shape)
        loss_acc[...] = jnp.zeros_like(loss_acc)
        tg_acc[...] = jnp.zeros_like(tg_acc)
        acc_own[...] = jnp.zeros_like(acc_own)
        acc_sib[...] = jnp.zeros_like(acc_sib)

    def head(st):
        span = pl.ds(pl.multiple_of(st * rb, rb), rb)
        zs = jnp.concatenate(
            [
                jnp.concatenate(
                    [zbuf[p * per_piece + k, span, :] for k in range(per_piece)], axis=1
                )
                for p in range(pieces)
            ],
            axis=0,
        )
        total = None
        for h in range(2):
            dots = lax.dot_general(zs, te[h], NT, preferred_element_type=F32)
            edge = bins[h, span, :]
            alive = (1 - cens[h, span, :]).astype(F32)
            weight = wrow[span, :]
            grads = []
            nll = None
            for p in range(pieces):
                piece = core * pieces + p
                logits = dots[p * rb : (p + 1) * rb] + bias[h, pl.ds(piece, 1), :]
                hazard = jnp.exp(logits)
                at = edge == piece
                hazard = jnp.where(edge > piece, hazard, jnp.where(at, 0.5 * hazard, 0.0))
                event = jnp.where(at, alive, 0.0)
                term = hazard - event * logits
                nll = term if nll is None else nll + term
                grad = (weight * (hazard - event)).astype(BF16)
                gbuf[h, p, span, :] = grad
                grads.append(grad)
            nll = (weight * nll).reshape(rb // 8, 8, tasks).sum(axis=0)
            loss_acc[...] += nll
            grads = jnp.concatenate(grads, axis=0)
            dots = jnp.dot(grads, te[h], preferred_element_type=F32)
            total = dots if total is None else total + dots
        for p in range(pieces):
            for k in range(per_piece):
                part[p * per_piece + k, span, :] = total[
                    p * rb : (p + 1) * rb, k * LANES : (k + 1) * LANES
                ]

    def x_copy(j, src, dst, k):
        return copy_to(
            src, dst, px_send.at[k, j - 1], px_recv.at[k, j - 1], row=(x + j) % nx
        )

    def y_copy(j, src, dst, k):
        return copy_to(
            src, dst, py_send.at[k, j - 1], py_recv.at[k, j - 1], section=(y + j) % ny
        )

    def loss_x_copy(j):
        return x_copy(j, loss_x.at[x], loss_x.at[x], 0)

    def loss_y_copy(j):
        return y_copy(j, loss_y.at[y], loss_y.at[y], 0)

    bx = tasks // nx
    by = bx // ny

    def tgx_copy(j):
        peer = (x + j) % nx
        src = tx_send.at[pl.ds(pl.multiple_of(peer * bx, bx), bx), :]
        return x_copy(j, src, tx_recv.at[j - 1], 1)

    def tgy_copy(j):
        peer = (y + j) % ny
        src = ty_send.at[pl.ds(pl.multiple_of(peer * by, by), by), :]
        return y_copy(j, src, ty_recv.at[j - 1], 1)

    def agy_copy(j):
        ref = tg_fin.at[pl.ds(pl.multiple_of(x * bx + y * by, by), by), :]
        return y_copy(j, ref, ref, 2)

    def agx_copy(j):
        ref = tg_fin.at[pl.ds(pl.multiple_of(x * bx, bx), bx), :]
        return x_copy(j, ref, ref, 2)

    tg_copy = copy_to(tg_send, tg_recv, pair_send.at[5], pair_recv.at[5], task=sib)

    def tg_piece(p):
        zp = jnp.concatenate([zbuf[p * per_piece + k] for k in range(per_piece)], axis=1)
        for h in range(2):
            tg_acc[h] += lax.dot_general(gbuf[h, p], zp, TN, preferred_element_type=F32)

    def loss_terms():
        own = sum(loss_y[i] for i in range(1, ny)) + loss_y[0]
        own = jnp.sum(jnp.sum(own, axis=0, keepdims=True), axis=1, keepdims=True)
        own = jnp.broadcast_to(own, (16, LANES))
        place = lax.broadcasted_iota(jnp.int32, own.shape, 1)
        place += LANES * lax.broadcasted_iota(jnp.int32, own.shape, 0)
        high = own.astype(BF16).astype(F32)
        rest = own - high
        middle = rest.astype(BF16).astype(F32)
        low = rest - middle
        terms = jnp.where(
            place == 0, high, jnp.where(place == 1, middle, jnp.where(place == 2, low, 0.0))
        )
        pgf[z, pl.ds(rows, 16), :] = terms.astype(BF16)

    def plane():
        loss_x[x] = loss_acc[:, :LANES] + loss_acc[:, LANES:]
        for j in range(1, nx):
            loss_x_copy(j).start()
        for p in range(pieces // 2):
            tg_piece(p)
        yield
        for p in range(pieces // 2, pieces):
            tg_piece(p)
        tg_send[...] = tg_acc[1].astype(BF16)
        tg_copy.start()
        for j in range(1, nx):
            loss_x_copy(j).wait()
        loss_y[y] = sum(loss_x[i] for i in range(1, nx)) + loss_x[0]
        for j in range(1, ny):
            loss_y_copy(j).start()
        yield
        tg_copy.wait()
        tg_acc[0] += tg_recv[...].astype(F32)
        tx_send[...] = tg_acc[0].astype(BF16)
        for j in range(1, nx):
            tgx_copy(j).start()
        for j in range(1, ny):
            loss_y_copy(j).wait()
        loss_terms()
        yield
        total = tg_acc[0, pl.ds(pl.multiple_of(x * bx, bx), bx), :]
        for j in range(1, nx):
            tgx_copy(j).wait()
            total += tx_recv[j - 1].astype(F32)
        tg_acc[0, pl.ds(0, bx), :] = total
        ty_send[...] = total.astype(BF16)
        for j in range(1, ny):
            tgy_copy(j).start()
        yield
        total = tg_acc[0, pl.ds(pl.multiple_of(y * by, by), by), :]
        for j in range(1, ny):
            tgy_copy(j).wait()
            total += ty_recv[j - 1].astype(F32)
        place = pl.ds(pl.multiple_of(x * bx + y * by, by), by)
        tg_fin[place, :] = (total * grad_scale).astype(BF16)
        for j in range(1, ny):
            agy_copy(j).start()
        yield
        for j in range(1, ny):
            agy_copy(j).wait_send()
            from_y = (y + ny - j) % ny
            ref = tg_fin.at[pl.ds(pl.multiple_of(x * bx + from_y * by, by), by), :]
            y_copy(j, ref, ref, 2).wait_recv()
        for j in range(1, nx):
            agx_copy(j).start()
        yield
        for j in range(1, nx):
            agx_copy(j).wait_send()
            from_x = (x + nx - j) % nx
            ref = tg_fin.at[pl.ds(pl.multiple_of(from_x * bx, bx), bx), :]
            x_copy(j, ref, ref, 2).wait_recv()
        tg_out[...] = tg_fin[...]

    def add_chunks(st, offs):
        span = pl.ds(st * rb, rb)
        chunks = [wrap(z + off) for off in offs]
        value = jnp.concatenate([pgf[c, span, :] for c in chunks], axis=1)
        for h, acc in ((0, acc_own), (1, acc_sib)):
            w = jnp.concatenate([pw[h, :, cols(c)] for c in chunks], axis=1)
            acc[:, span] += lax.dot_general(w, value, NT, preferred_element_type=F32)

    def hg_copy(st):
        return copy_to(
            hg_send.at[st], hg_recv.at[st], pair_send.at[6 + st], pair_recv.at[6 + st], task=sib
        )

    def stream(st):
        span = pl.ds(st * rb, rb)
        n = len(CHAIN)
        for k in range(n):
            if st == 0:
                for m in pw_order:
                    if abs(m) == k + 1 or (k == 0 and m == 0):
                        pw_copy(m).wait_recv()
            rs_stage(0, st, k)
            yield
        zbuf[z, span, :] = rs_total(0, st).astype(BF16)
        for k in range(n):
            ag_stage(0, st, k)
            yield
        ag_stage(0, st, n)
        for off in between:
            for d in sides(st):
                ag_arrived(0, d, st, off)
        if st == 0:
            for i in range(1, 5):
                loads[1 + i].wait()
                pair[i].wait_recv()
        head(st)
        for k in range(n):
            rs_stage(1, st, k)
            yield
        pgf[z, span, :] = rs_total(1, st).astype(BF16)
        for k in range(n + 1):
            ag_stage(1, st, k)
            if k == 0:
                add_chunks(st, [0])
            else:
                if k < n:
                    add_chunks(st, [-CHAIN[k - 1], CHAIN[k - 1]])
                for off in between:
                    if before(off) == ([0] + list(CHAIN))[k - 1]:
                        for d in sides(st):
                            ag_arrived(1, d, st, off)
                        add_chunks(st, [-off, off])
            if k < n:
                yield
        add_chunks(st, [far])
        hg_send[st] = acc_sib[:, span].astype(BF16)
        hg_copy(st).start()

    loads[0].wait()
    loads[1].wait()
    hid_rows[0] = hid[0].T
    pair[0].wait_recv()
    hid_rows[1] = hid[1].T
    heads_done = len(CHAIN) * 2 + 1
    running = {st: stream(st) for st in range(STREAMS)}
    beside = None
    slot = 0
    while running:
        for st in reversed(range(STREAMS)):
            if st in running and slot >= st * LAG:
                if next(running[st], True):
                    del running[st]
        if slot == 0:
            prepare()
        if slot == (STREAMS - 1) * LAG + heads_done - 1:
            beside = plane()
        if slot == heads_done:
            rs_sent(0)
        if beside is not None and next(beside, True):
            beside = None
        slot += 1
    if beside is not None:
        for _ in beside:
            pass

    total = pgf[0, pl.ds(rows, 16), :].astype(F32)
    for c in range(1, nz):
        total += pgf[c, pl.ds(rows, 16), :].astype(F32)
    loss_pair[core] = total
    ref = loss_pair.at[core]
    last = 6 + STREAMS
    loss_copy = copy_to(ref, ref, pair_send.at[last], pair_recv.at[last], task=sib)
    loss_copy.start()
    ag_sent(0)
    rs_sent(1)
    ag_sent(1)
    for copy in pair:
        copy.wait_send()
    for n in pw_order:
        pw_copy(n).wait_send()
    loss_copy.wait()
    total = loss_pair[0] + loss_pair[1]
    loss_out[0, 0] = jnp.sum(total) * loss_scale
    for st in range(STREAMS):
        span = pl.ds(st * rb, rb)
        hg_copy(st).wait()
        hg_out[:, span] = (acc_own[:, span] + hg_recv[st].astype(F32)).astype(BF16)


def shards(
    hidden, piece_weight, task_embed, task_bias, event_bin, censored, patient_id, patient_rows
):
    patients = patient_rows.shape[0]
    rows, depth = hidden.shape
    tasks, width = task_embed.shape
    pieces = task_bias.shape[1]
    n_task = lax.axis_size("task")
    nx, ny = lax.axis_size("row"), lax.axis_size("section")
    nz = n_task // 2
    half = pieces * width // 2
    bx = tasks // nx
    by = bx // ny
    vmem = pl.BlockSpec(memory_space=pltpu.VMEM)
    in_hbm = pl.BlockSpec(memory_space=pltpu.HBM)
    dma = pltpu.SemaphoreType.DMA
    hg, tg, loss = pl.pallas_call(
        functools.partial(kernel, 1.0 / (patients * tasks * n_task), 1.0 / patients),
        out_shape=(
            jax.ShapeDtypeStruct((depth, rows), BF16),
            jax.ShapeDtypeStruct((tasks, width), BF16),
            jax.ShapeDtypeStruct((1, 1), F32),
        ),
        in_specs=[in_hbm] * 8,
        out_specs=(vmem, vmem, pl.BlockSpec(memory_space=pltpu.SMEM)),
        scratch_shapes=[
            pltpu.VMEM((1, rows), jnp.int32),
            pltpu.VMEM((1, patients), jnp.int32),
            pltpu.VMEM((2, depth, rows), BF16),
            pltpu.VMEM((2, rows, depth), BF16),
            pltpu.VMEM((2, depth, half), BF16),
            pltpu.VMEM((2, tasks, width), BF16),
            pltpu.VMEM((2, pieces, tasks), F32),
            pltpu.VMEM((2, rows, tasks), jnp.int32),
            pltpu.VMEM((2, rows, tasks), jnp.int32),
            pltpu.VMEM((rows, tasks), F32),
            pltpu.VMEM((nz, rows, LANES), F32),
            pltpu.VMEM((2, 2, nz // 2, rows, LANES), BF16),
            pltpu.VMEM((2, 2, nz // 2, rows, LANES), BF16),
            pltpu.VMEM((nz, rows, LANES), BF16),
            pltpu.VMEM((nz, rows + 16, LANES), BF16),
            pltpu.VMEM((2, pieces // 2, rows, tasks), BF16),
            pltpu.VMEM((8, tasks), F32),
            pltpu.VMEM((nx, 8, LANES), F32),
            pltpu.VMEM((ny, 8, LANES), F32),
            pltpu.VMEM((2, 16, LANES), F32),
            pltpu.VMEM((2, tasks, width), F32),
            pltpu.VMEM((tasks, width), BF16),
            pltpu.VMEM((tasks, width), BF16),
            pltpu.VMEM((tasks, width), BF16),
            pltpu.VMEM((nx - 1, bx, width), BF16),
            pltpu.VMEM((bx, width), BF16),
            pltpu.VMEM((ny - 1, by, width), BF16),
            pltpu.VMEM((tasks, width), BF16),
            pltpu.VMEM((depth, rows), F32),
            pltpu.VMEM((depth, rows), F32),
            pltpu.VMEM((STREAMS, depth, rows // STREAMS), BF16),
            pltpu.VMEM((STREAMS, depth, rows // STREAMS), BF16),
            dma((4, 2, STREAMS, nz // 2)),
            dma((4, 2, STREAMS, nz // 2)),
            dma((8,)),
            dma((7 + STREAMS,)),
            dma((7 + STREAMS,)),
            dma((nz // 2,)),
            dma((nz // 2,)),
            dma((3, nx - 1)),
            dma((3, nx - 1)),
            dma((3, ny - 1)),
            dma((3, ny - 1)),
        ],
        compiler_params=pltpu.CompilerParams(
            collective_id=0, has_side_effects=True, vmem_limit_bytes=63 * 1024 * 1024
        ),
        cost_estimate=pl.CostEstimate(
            flops=2400000000, bytes_accessed=4000000, transcendentals=600000
        ),
    )(
        hidden.T,
        piece_weight,
        task_embed,
        task_bias.T,
        event_bin,
        censored,
        patient_id.reshape(1, rows),
        patient_rows.reshape(1, patients),
    )
    return hg.T, tg.astype(F32), loss.reshape(())


def solution(mesh):
    return jax.shard_map(
        shards,
        mesh=mesh,
        in_specs=(
            P(("section", "row"), "task"),
            P("task", None),
            P("task", None),
            P("task", None),
            P(("section", "row"), "task"),
            P(("section", "row"), "task"),
            P(("section", "row")),
            P(),
        ),
        out_specs=(P(("section", "row"), "task"), P("task", None), P()),
        check_vma=False,
    )
```

```python
import functools

import jax
import jax.numpy as jnp
from jax import lax
from jax.experimental import pallas as pl
from jax.experimental.pallas import tpu as pltpu
from jax.sharding import PartitionSpec as P

MESH = pl.DeviceIdType.MESH
F32 = jnp.float32
BF16 = jnp.bfloat16
LANES = 128
STREAMS = 2
CHAIN = (2, 4, 6, 8)
LAG = 1
NT = (((1,), (1,)), ((), ()))
TN = (((0,), (0,)), ((), ()))


def kernel(
    loss_scale,
    grad_scale,
    hid_hbm,
    pw_hbm,
    te_hbm,
    bias_hbm,
    bins_hbm,
    cens_hbm,
    pid_hbm,
    prow_hbm,
    hg_out,
    tg_out,
    loss_out,
    pid_ref,
    prow_ref,
    hid,
    hid_rows,
    pw,
    te,
    bias,
    bins,
    cens,
    wrow,
    part,
    rs_out,
    rs_in,
    zbuf,
    pgf,
    gbuf,
    loss_acc,
    loss_x,
    loss_y,
    loss_pair,
    tg_acc,
    tg_send,
    tg_recv,
    tx_send,
    tx_recv,
    ty_send,
    ty_recv,
    tg_fin,
    acc_own,
    acc_sib,
    hg_send,
    hg_recv,
    send_sem,
    recv_sem,
    local_sem,
    pair_send,
    pair_recv,
    pw_send,
    pw_recv,
    px_send,
    px_recv,
    py_send,
    py_recv,
):
    rows = hid.shape[2]
    half_cols = pw.shape[2]
    tasks = te.shape[1]
    nz = part.shape[0]
    far = nz // 2
    pieces = half_cols // te.shape[2]
    per_piece = nz // pieces
    rb = rows // STREAMS
    nx = lax.axis_size("row")
    ny = lax.axis_size("section")
    task = lax.axis_index("task")
    x = lax.axis_index("row")
    y = lax.axis_index("section")
    z = task // 2
    core = task % 2
    sib = z * 2 + 1 - core

    def wrap(v):
        return (v + 2 * nz) % nz

    def z_dev(off):
        return wrap(z + off) * 2 + core

    def copy_to(src, dst, ss, rs, **where):
        return pltpu.make_async_remote_copy(
            src_ref=src,
            dst_ref=dst,
            send_sem=ss,
            recv_sem=rs,
            device_id=where,
            device_id_type=MESH,
        )

    mine = pl.ds(pl.multiple_of(core * half_cols, half_cols), half_cols)
    loads = [
        (hid_hbm, hid.at[0]),
        (pw_hbm.at[:, mine], pw.at[0]),
        (te_hbm, te.at[0]),
        (bias_hbm, bias.at[0]),
        (bins_hbm, bins.at[0]),
        (cens_hbm, cens.at[0]),
        (pid_hbm, pid_ref),
        (prow_hbm, prow_ref),
    ]
    loads = [pltpu.make_async_copy(a, b, local_sem.at[i]) for i, (a, b) in enumerate(loads)]
    for load in loads:
        load.start()

    barrier = pltpu.get_barrier_semaphore()
    strides = sorted({b - a for a, b in zip((0,) + CHAIN, CHAIN)} | {1})
    peers = [dict(task=sib)] + [dict(task=z_dev(s * n)) for n in strides for s in (1, -1)]
    peers += [dict(row=(x + j) % nx) for j in range(1, nx)]
    peers += [dict(section=(y + j) % ny) for j in range(1, ny)]
    for peer in peers:
        pl.semaphore_signal(barrier, inc=1, device_id=peer, device_id_type=MESH)
    pl.semaphore_wait(barrier, len(peers))

    pair = [
        (hid_hbm, hid.at[1]),
        (te_hbm, te.at[1]),
        (bias_hbm, bias.at[1]),
        (bins_hbm, bins.at[1]),
        (cens_hbm, cens.at[1]),
    ]
    pair = [
        copy_to(a, b, pair_send.at[i], pair_recv.at[i], task=sib) for i, (a, b) in enumerate(pair)
    ]

    part_cols = half_cols // far

    def pw_copy(n):
        q = (wrap(z + far) // 2 + n + far) % far
        there = pl.ds(
            pl.multiple_of((1 - core) * half_cols + q * part_cols, part_cols), part_cols
        )
        here = pl.ds(pl.multiple_of(q * part_cols, part_cols), part_cols)
        return copy_to(
            pw_hbm.at[:, there], pw.at[1, :, here], pw_send.at[q], pw_recv.at[q], task=sib
        )

    pw_order = [0] + [s * n for n in range(1, far // 2) for s in (1, -1)] + [far // 2]
    pair[0].start()
    for n in pw_order:
        pw_copy(n).start()
    for copy in pair[1:]:
        copy.start()

    def long_way(st):
        return 0 if st < STREAMS // 2 else 1

    def stops(d, st):
        return [c for c in CHAIN if c < far or d == long_way(st)]

    def before(off):
        return max([0] + [c for c in CHAIN if c < off])

    def behind(stop, d, st):
        last = far if d == long_way(st) else far - 1
        found = [off for off in range(1, last + 1) if before(off) == stop]
        return sorted(found, key=lambda off: off not in CHAIN)

    def sides(st):
        return (long_way(st), 1 - long_way(st))

    def rs_copy(ph, d, st, off):
        span = pl.ds(st * rb, rb)
        return copy_to(
            rs_out.at[ph, d, off - 1, span, :],
            rs_in.at[ph, d, off - 1, span, :],
            send_sem.at[2 * ph, d, st, off - 1],
            recv_sem.at[2 * ph, d, st, off - 1],
            task=z_dev((1 - 2 * d) * (off - before(off))),
        )

    def cols(c):
        return pl.ds(pl.multiple_of(c * LANES, LANES), LANES)

    def fill(k):
        stop = ([0] + list(CHAIN))[-1 - k]
        for off in [stop] + list(range(before(stop) + 1, stop)):
            chunks = [wrap(z + off)] if off in (0, far) else [wrap(z - off), wrap(z + off)]
            total = None
            for h in range(2):
                w = jnp.concatenate([pw[h, :, cols(c)] for c in chunks], axis=1)
                dots = jnp.dot(hid_rows[h], w, preferred_element_type=F32)
                total = dots if total is None else total + dots
            for i, c in enumerate(chunks):
                part[c] = total[:, i * LANES : (i + 1) * LANES]

    def rs_send(ph, d, st, off):
        span = pl.ds(st * rb, rb)
        total = part[wrap(z + (1 - 2 * d) * off), span, :]
        if off in stops(d, st):
            for other in behind(off, d, st):
                rs_copy(ph, d, st, other).wait_recv()
                total += rs_in[ph, d, other - 1, span, :].astype(F32)
        rs_out[ph, d, off - 1, span, :] = total.astype(BF16)
        rs_copy(ph, d, st, off).start()

    def rs_total(ph, st):
        span = pl.ds(st * rb, rb)
        total = part[z, span, :]
        for d in sides(st):
            for other in behind(0, d, st):
                rs_copy(ph, d, st, other).wait_recv()
                total += rs_in[ph, d, other - 1, span, :].astype(F32)
        return total

    def rs_stage(ph, st, k):
        stop = ([0] + list(CHAIN))[-1 - k]
        for d in sides(st):
            if k == 0:
                rs_send(ph, d, st, far if d == long_way(st) else far - 1)
            elif stop != far - 1 or d == long_way(st):
                rs_send(ph, d, st, stop)
        for off in range(stop - 1, before(stop), -1):
            for d in sides(st):
                if off != far - 1 or d == long_way(st):
                    rs_send(ph, d, st, off)

    def rs_sent(ph, st):
        for d in range(2):
            for off in range(1, far + 1 if d == long_way(st) else far):
                rs_copy(ph, d, st, off).wait_send()

    def ag_copy(ph, d, st, off):
        buf = zbuf if ph == 0 else pgf
        extra = 16 if ph == 1 and st == STREAMS - 1 else 0
        sgn = 1 - 2 * d
        ref = buf.at[wrap(z - sgn * before(off)), pl.ds(st * rb, rb + extra), :]
        return copy_to(
            ref,
            ref,
            send_sem.at[2 * ph + 1, d, st, off - 1],
            recv_sem.at[2 * ph + 1, d, st, off - 1],
            task=z_dev(sgn * (off - before(off))),
        )

    def ag_arrived(ph, d, st, off):
        buf = zbuf if ph == 0 else pgf
        extra = 16 if ph == 1 and st == STREAMS - 1 else 0
        sgn = 1 - 2 * d
        if off < far or d == long_way(st):
            ref = buf.at[wrap(z - sgn * off), pl.ds(st * rb, rb + extra), :]
            copy_to(
                ref,
                ref,
                send_sem.at[2 * ph + 1, d, st, off - 1],
                recv_sem.at[2 * ph + 1, d, st, off - 1],
                task=z_dev(sgn * (off - before(off))),
            ).wait_recv()

    def ag_stage(ph, st, k):
        stop = ([0] + list(CHAIN))[k]
        for d in sides(st):
            if k > 0:
                ag_arrived(ph, d, st, stop)
            for off in behind(stop, d, st)[:1]:
                ag_copy(ph, d, st, off).start()
        for d in sides(st):
            for off in behind(stop, d, st)[1:]:
                ag_copy(ph, d, st, off).start()

    def ag_sent(ph, st, first, last):
        for d in range(2):
            for off in range(first, last + 1):
                if off < far or d == long_way(st):
                    ag_copy(ph, d, st, off).wait_send()

    between = [off for off in range(1, far) if off not in CHAIN]

    def prepare():
        loads[6].wait()
        loads[7].wait()
        ids = jnp.broadcast_to(pid_ref[...].astype(F32), (prow_ref.shape[1], rows)).T
        lane = lax.broadcasted_iota(jnp.int32, ids.shape, 1).astype(F32)
        record = jnp.where(ids == lane, prow_ref[...].astype(F32), 0.0)
        weight = 1.0 / jnp.sum(record, axis=1, keepdims=True)
        wrow[...] = jnp.broadcast_to(weight, wrow.shape)
        loss_acc[...] = jnp.zeros_like(loss_acc)
        tg_acc[...] = jnp.zeros_like(tg_acc)
        acc_own[...] = jnp.zeros_like(acc_own)
        acc_sib[...] = jnp.zeros_like(acc_sib)

    def head(st):
        span = pl.ds(pl.multiple_of(st * rb, rb), rb)
        zs = jnp.concatenate(
            [
                jnp.concatenate(
                    [zbuf[p * per_piece + k, span, :] for k in range(per_piece)], axis=1
                )
                for p in range(pieces)
            ],
            axis=0,
        )
        total = None
        for h in range(2):
            dots = lax.dot_general(zs, te[h], NT, preferred_element_type=F32)
            edge = bins[h, span, :]
            alive = (1 - cens[h, span, :]).astype(F32)
            weight = wrow[span, :]
            grads = []
            nll = None
            for p in range(pieces):
                piece = core * pieces + p
                logits = dots[p * rb : (p + 1) * rb] + bias[h, pl.ds(piece, 1), :]
                hazard = jnp.exp(logits)
                at = edge == piece
                hazard = jnp.where(edge > piece, hazard, jnp.where(at, 0.5 * hazard, 0.0))
                event = jnp.where(at, alive, 0.0)
                term = hazard - event * logits
                nll = term if nll is None else nll + term
                grad = (weight * (hazard - event)).astype(BF16)
                gbuf[h, p, span, :] = grad
                grads.append(grad)
            nll = (weight * nll).reshape(rb // 8, 8, tasks).sum(axis=0)
            loss_acc[...] += nll
            grads = jnp.concatenate(grads, axis=0)
            dots = jnp.dot(grads, te[h], preferred_element_type=F32)
            total = dots if total is None else total + dots
        for p in range(pieces):
            for k in range(per_piece):
                part[p * per_piece + k, span, :] = total[
                    p * rb : (p + 1) * rb, k * LANES : (k + 1) * LANES
                ]

    def x_copy(j, src, dst, k):
        return copy_to(
            src, dst, px_send.at[k, j - 1], px_recv.at[k, j - 1], row=(x + j) % nx
        )

    def y_copy(j, src, dst, k):
        return copy_to(
            src, dst, py_send.at[k, j - 1], py_recv.at[k, j - 1], section=(y + j) % ny
        )

    def loss_x_copy(j):
        return x_copy(j, loss_x.at[x], loss_x.at[x], 0)

    def loss_y_copy(j):
        return y_copy(j, loss_y.at[y], loss_y.at[y], 0)

    bx = tasks // nx
    by = bx // ny

    def tgx_copy(j):
        peer = (x + j) % nx
        src = tx_send.at[pl.ds(pl.multiple_of(peer * bx, bx), bx), :]
        return x_copy(j, src, tx_recv.at[j - 1], 1)

    def tgy_copy(j):
        peer = (y + j) % ny
        src = ty_send.at[pl.ds(pl.multiple_of(peer * by, by), by), :]
        return y_copy(j, src, ty_recv.at[j - 1], 1)

    def agy_copy(j):
        ref = tg_fin.at[pl.ds(pl.multiple_of(x * bx + y * by, by), by), :]
        return y_copy(j, ref, ref, 2)

    def agx_copy(j):
        ref = tg_fin.at[pl.ds(pl.multiple_of(x * bx, bx), bx), :]
        return x_copy(j, ref, ref, 2)

    tg_copy = copy_to(tg_send, tg_recv, pair_send.at[5], pair_recv.at[5], task=sib)

    def tg_piece(p):
        zp = jnp.concatenate([zbuf[p * per_piece + k] for k in range(per_piece)], axis=1)
        for h in range(2):
            tg_acc[h] += lax.dot_general(gbuf[h, p], zp, TN, preferred_element_type=F32)

    def loss_terms():
        own = sum(loss_y[i] for i in range(1, ny)) + loss_y[0]
        own = jnp.sum(jnp.sum(own, axis=0, keepdims=True), axis=1, keepdims=True)
        own = jnp.broadcast_to(own, (16, LANES))
        place = lax.broadcasted_iota(jnp.int32, own.shape, 1)
        place += LANES * lax.broadcasted_iota(jnp.int32, own.shape, 0)
        high = own.astype(BF16).astype(F32)
        rest = own - high
        middle = rest.astype(BF16).astype(F32)
        low = rest - middle
        terms = jnp.where(
            place == 0, high, jnp.where(place == 1, middle, jnp.where(place == 2, low, 0.0))
        )
        pgf[z, pl.ds(rows, 16), :] = terms.astype(BF16)

    def plane():
        loss_x[x] = loss_acc[:, :LANES] + loss_acc[:, LANES:]
        for j in range(1, nx):
            loss_x_copy(j).start()
        for p in range(pieces // 2):
            tg_piece(p)
        yield
        for p in range(pieces // 2, pieces):
            tg_piece(p)
        tg_send[...] = tg_acc[1].astype(BF16)
        tg_copy.start()
        for j in range(1, nx):
            loss_x_copy(j).wait()
        loss_y[y] = sum(loss_x[i] for i in range(1, nx)) + loss_x[0]
        for j in range(1, ny):
            loss_y_copy(j).start()
        yield
        tg_copy.wait()
        tg_acc[0] += tg_recv[...].astype(F32)
        tx_send[...] = tg_acc[0].astype(BF16)
        for j in range(1, nx):
            tgx_copy(j).start()
        for j in range(1, ny):
            loss_y_copy(j).wait()
        loss_terms()
        yield
        total = tg_acc[0, pl.ds(pl.multiple_of(x * bx, bx), bx), :]
        for j in range(1, nx):
            tgx_copy(j).wait()
            total += tx_recv[j - 1].astype(F32)
        tg_acc[0, pl.ds(0, bx), :] = total
        ty_send[...] = total.astype(BF16)
        for j in range(1, ny):
            tgy_copy(j).start()
        yield
        total = tg_acc[0, pl.ds(pl.multiple_of(y * by, by), by), :]
        for j in range(1, ny):
            tgy_copy(j).wait()
            total += ty_recv[j - 1].astype(F32)
        place = pl.ds(pl.multiple_of(x * bx + y * by, by), by)
        tg_fin[place, :] = (total * grad_scale).astype(BF16)
        for j in range(1, ny):
            agy_copy(j).start()
        yield
        for j in range(1, ny):
            agy_copy(j).wait_send()
            from_y = (y + ny - j) % ny
            ref = tg_fin.at[pl.ds(pl.multiple_of(x * bx + from_y * by, by), by), :]
            y_copy(j, ref, ref, 2).wait_recv()
        for j in range(1, nx):
            agx_copy(j).start()
        yield
        for j in range(1, nx):
            agx_copy(j).wait_send()
            from_x = (x + nx - j) % nx
            ref = tg_fin.at[pl.ds(pl.multiple_of(from_x * bx, bx), bx), :]
            x_copy(j, ref, ref, 2).wait_recv()
        tg_out[...] = tg_fin[...]

    def add_chunks(st, offs):
        span = pl.ds(st * rb, rb)
        chunks = [wrap(z + off) for off in offs]
        value = jnp.concatenate([pgf[c, span, :] for c in chunks], axis=1)
        for h, acc in ((0, acc_own), (1, acc_sib)):
            w = jnp.concatenate([pw[h, :, cols(c)] for c in chunks], axis=1)
            acc[:, span] += lax.dot_general(w, value, NT, preferred_element_type=F32)

    def hg_copy(st):
        return copy_to(
            hg_send.at[st], hg_recv.at[st], pair_send.at[6 + st], pair_recv.at[6 + st], task=sib
        )

    def stream(st):
        span = pl.ds(st * rb, rb)
        n = len(CHAIN)
        for k in range(n):
            rs_stage(0, st, k)
            yield
            if st == 0:
                for m in pw_order:
                    if abs(m) == k + 2:
                        pw_copy(m).wait_recv()
                fill(k + 1)
            yield
        zbuf[z, span, :] = rs_total(0, st).astype(BF16)
        for k in range(n):
            ag_stage(0, st, k)
            yield
            if k == 1:
                rs_sent(0, st)
            if st == 0 and k == 2:
                for copy in pair:
                    copy.wait_send()
                for m in pw_order:
                    pw_copy(m).wait_send()
            yield
        ag_stage(0, st, n)
        for off in between:
            for d in sides(st):
                ag_arrived(0, d, st, off)
        if st == 0:
            for i in range(1, 5):
                loads[1 + i].wait()
                pair[i].wait_recv()
        head(st)
        for k in range(n):
            rs_stage(1, st, k)
            yield
            if k == 1:
                ag_sent(0, st, 1, far)
            yield
        pgf[z, span, :] = rs_total(1, st).astype(BF16)
        for k in range(n + 1):
            ag_stage(1, st, k)
            yield
            if k == 0:
                add_chunks(st, [0])
            else:
                offs = [CHAIN[k - 1]]
                for off in between:
                    if before(off) == ([0] + list(CHAIN))[k - 1]:
                        for d in sides(st):
                            ag_arrived(1, d, st, off)
                        offs.append(off)
                add_chunks(st, [s * off for off in offs for s in (1, -1) if s * off > -far])
            if k == 1:
                rs_sent(1, st)
            if k == n - 1:
                ag_sent(1, st, 1, CHAIN[n - 2])
            if k == n:
                hg_send[st] = acc_sib[:, span].astype(BF16)
                hg_copy(st).start()
            yield

    loads[0].wait()
    loads[1].wait()
    hid_rows[0] = hid[0].T
    pair[0].wait_recv()
    hid_rows[1] = hid[1].T
    for m in pw_order:
        if abs(m) <= 1:
            pw_copy(m).wait_recv()
    fill(0)
    heads_done = len(CHAIN) * 2 + 1
    running = {st: stream(st) for st in range(STREAMS)}
    beside = None
    slot = 0
    while running:
        active = [st for st in reversed(range(STREAMS)) if st in running and slot >= st * LAG]
        for st in active:
            next(running[st])
        for st in active:
            next(running[st])
        if slot == 0:
            prepare()
        if slot == (STREAMS - 1) * LAG + heads_done - 1:
            beside = plane()
        if beside is not None and next(beside, True):
            beside = None
        for st in active:
            if slot - st * LAG == 4 * len(CHAIN):
                for _ in running.pop(st):
                    pass
        slot += 1
    if beside is not None:
        for _ in beside:
            pass

    total = pgf[0, pl.ds(rows, 16), :].astype(F32)
    for c in range(1, nz):
        total += pgf[c, pl.ds(rows, 16), :].astype(F32)
    loss_pair[core] = total
    ref = loss_pair.at[core]
    last = 6 + STREAMS
    loss_copy = copy_to(ref, ref, pair_send.at[last], pair_recv.at[last], task=sib)
    loss_copy.start()
    for st in range(STREAMS):
        ag_sent(1, st, CHAIN[-2] + 1, far)
    loss_copy.wait()
    total = loss_pair[0] + loss_pair[1]
    loss_out[0, 0] = jnp.sum(total) * loss_scale
    for st in range(STREAMS):
        span = pl.ds(st * rb, rb)
        hg_copy(st).wait()
        hg_out[:, span] = (acc_own[:, span] + hg_recv[st].astype(F32)).astype(BF16)


def shards(
    hidden, piece_weight, task_embed, task_bias, event_bin, censored, patient_id, patient_rows
):
    patients = patient_rows.shape[0]
    rows, depth = hidden.shape
    tasks, width = task_embed.shape
    pieces = task_bias.shape[1]
    n_task = lax.axis_size("task")
    nx, ny = lax.axis_size("row"), lax.axis_size("section")
    nz = n_task // 2
    half = pieces * width // 2
    bx = tasks // nx
    by = bx // ny
    vmem = pl.BlockSpec(memory_space=pltpu.VMEM)
    in_hbm = pl.BlockSpec(memory_space=pltpu.HBM)
    dma = pltpu.SemaphoreType.DMA
    hg, tg, loss = pl.pallas_call(
        functools.partial(kernel, 1.0 / (patients * tasks * n_task), 1.0 / patients),
        out_shape=(
            jax.ShapeDtypeStruct((depth, rows), BF16),
            jax.ShapeDtypeStruct((tasks, width), BF16),
            jax.ShapeDtypeStruct((1, 1), F32),
        ),
        in_specs=[in_hbm] * 8,
        out_specs=(vmem, vmem, pl.BlockSpec(memory_space=pltpu.SMEM)),
        scratch_shapes=[
            pltpu.VMEM((1, rows), jnp.int32),
            pltpu.VMEM((1, patients), jnp.int32),
            pltpu.VMEM((2, depth, rows), BF16),
            pltpu.VMEM((2, rows, depth), BF16),
            pltpu.VMEM((2, depth, half), BF16),
            pltpu.VMEM((2, tasks, width), BF16),
            pltpu.VMEM((2, pieces, tasks), F32),
            pltpu.VMEM((2, rows, tasks), jnp.int32),
            pltpu.VMEM((2, rows, tasks), jnp.int32),
            pltpu.VMEM((rows, tasks), F32),
            pltpu.VMEM((nz, rows, LANES), F32),
            pltpu.VMEM((2, 2, nz // 2, rows, LANES), BF16),
            pltpu.VMEM((2, 2, nz // 2, rows, LANES), BF16),
            pltpu.VMEM((nz, rows, LANES), BF16),
            pltpu.VMEM((nz, rows + 16, LANES), BF16),
            pltpu.VMEM((2, pieces // 2, rows, tasks), BF16),
            pltpu.VMEM((8, tasks), F32),
            pltpu.VMEM((nx, 8, LANES), F32),
            pltpu.VMEM((ny, 8, LANES), F32),
            pltpu.VMEM((2, 16, LANES), F32),
            pltpu.VMEM((2, tasks, width), F32),
            pltpu.VMEM((tasks, width), BF16),
            pltpu.VMEM((tasks, width), BF16),
            pltpu.VMEM((tasks, width), BF16),
            pltpu.VMEM((nx - 1, bx, width), BF16),
            pltpu.VMEM((bx, width), BF16),
            pltpu.VMEM((ny - 1, by, width), BF16),
            pltpu.VMEM((tasks, width), BF16),
            pltpu.VMEM((depth, rows), F32),
            pltpu.VMEM((depth, rows), F32),
            pltpu.VMEM((STREAMS, depth, rows // STREAMS), BF16),
            pltpu.VMEM((STREAMS, depth, rows // STREAMS), BF16),
            dma((4, 2, STREAMS, nz // 2)),
            dma((4, 2, STREAMS, nz // 2)),
            dma((8,)),
            dma((7 + STREAMS,)),
            dma((7 + STREAMS,)),
            dma((nz // 2,)),
            dma((nz // 2,)),
            dma((3, nx - 1)),
            dma((3, nx - 1)),
            dma((3, ny - 1)),
            dma((3, ny - 1)),
        ],
        compiler_params=pltpu.CompilerParams(
            collective_id=0, has_side_effects=True, vmem_limit_bytes=63 * 1024 * 1024
        ),
        cost_estimate=pl.CostEstimate(
            flops=2400000000, bytes_accessed=4000000, transcendentals=600000
        ),
    )(
        hidden.T,
        piece_weight,
        task_embed,
        task_bias.T,
        event_bin,
        censored,
        patient_id.reshape(1, rows),
        patient_rows.reshape(1, patients),
    )
    return hg.T, tg.astype(F32), loss.reshape(())


def solution(mesh):
    return jax.shard_map(
        shards,
        mesh=mesh,
        in_specs=(
            P(("section", "row"), "task"),
            P("task", None),
            P("task", None),
            P("task", None),
            P(("section", "row"), "task"),
            P(("section", "row"), "task"),
            P(("section", "row")),
            P(),
        ),
        out_specs=(P(("section", "row"), "task"), P("task", None), P()),
        check_vma=False,
    )
```

```python
import functools

import jax
import jax.numpy as jnp
from jax import lax
from jax.experimental import pallas as pl
from jax.experimental.pallas import tpu as pltpu
from jax.sharding import PartitionSpec as P

MESH = pl.DeviceIdType.MESH
F32 = jnp.float32
BF16 = jnp.bfloat16
LANES = 128
STREAMS = 2
CHAIN = (2, 4, 6, 7, 8)
LAG = 1
NT = (((1,), (1,)), ((), ()))
TN = (((0,), (0,)), ((), ()))


def kernel(
    loss_scale,
    grad_scale,
    hid_hbm,
    pw_hbm,
    te_hbm,
    bias_hbm,
    bins_hbm,
    cens_hbm,
    pid_hbm,
    prow_hbm,
    hg_out,
    tg_out,
    loss_out,
    pid_ref,
    prow_ref,
    hid,
    hid_rows,
    pw,
    te,
    bias,
    bins,
    cens,
    wrow,
    part,
    rs_out,
    rs_in,
    zbuf,
    pgf,
    gbuf,
    loss_acc,
    loss_x,
    loss_y,
    loss_pair,
    tg_acc,
    tg_send,
    tg_recv,
    tx_send,
    tx_recv,
    ty_send,
    ty_recv,
    tg_fin,
    acc_own,
    acc_sib,
    hg_send,
    hg_recv,
    send_sem,
    recv_sem,
    local_sem,
    pair_send,
    pair_recv,
    pw_send,
    pw_recv,
    px_send,
    px_recv,
    py_send,
    py_recv,
):
    rows = hid.shape[2]
    half_cols = pw.shape[2]
    tasks = te.shape[1]
    nz = part.shape[0]
    far = nz // 2
    pieces = half_cols // te.shape[2]
    per_piece = nz // pieces
    rb = rows // STREAMS
    nx = lax.axis_size("row")
    ny = lax.axis_size("section")
    task = lax.axis_index("task")
    x = lax.axis_index("row")
    y = lax.axis_index("section")
    z = task // 2
    core = task % 2
    sib = z * 2 + 1 - core

    def wrap(v):
        return (v + 2 * nz) % nz

    def z_dev(off):
        return wrap(z + off) * 2 + core

    def copy_to(src, dst, ss, rs, **where):
        return pltpu.make_async_remote_copy(
            src_ref=src,
            dst_ref=dst,
            send_sem=ss,
            recv_sem=rs,
            device_id=where,
            device_id_type=MESH,
        )

    mine = pl.ds(pl.multiple_of(core * half_cols, half_cols), half_cols)
    loads = [
        (hid_hbm, hid.at[0]),
        (pw_hbm.at[:, mine], pw.at[0]),
        (te_hbm, te.at[0]),
        (bias_hbm, bias.at[0]),
        (bins_hbm, bins.at[0]),
        (cens_hbm, cens.at[0]),
        (pid_hbm, pid_ref),
        (prow_hbm, prow_ref),
    ]
    loads = [pltpu.make_async_copy(a, b, local_sem.at[i]) for i, (a, b) in enumerate(loads)]
    for load in loads:
        load.start()

    barrier = pltpu.get_barrier_semaphore()
    strides = sorted({b - a for a, b in zip((0,) + CHAIN, CHAIN)} | {1})
    peers = [dict(task=sib)] + [dict(task=z_dev(s * n)) for n in strides for s in (1, -1)]
    peers += [dict(row=(x + j) % nx) for j in range(1, nx)]
    peers += [dict(section=(y + j) % ny) for j in range(1, ny)]
    for peer in peers:
        pl.semaphore_signal(barrier, inc=1, device_id=peer, device_id_type=MESH)
    pl.semaphore_wait(barrier, len(peers))

    pair = [
        (hid_hbm, hid.at[1]),
        (te_hbm, te.at[1]),
        (bias_hbm, bias.at[1]),
        (bins_hbm, bins.at[1]),
        (cens_hbm, cens.at[1]),
    ]
    pair = [
        copy_to(a, b, pair_send.at[i], pair_recv.at[i], task=sib) for i, (a, b) in enumerate(pair)
    ]

    part_cols = half_cols // far

    def pw_copy(n):
        q = (wrap(z + far) // 2 + n + far) % far
        there = pl.ds(
            pl.multiple_of((1 - core) * half_cols + q * part_cols, part_cols), part_cols
        )
        here = pl.ds(pl.multiple_of(q * part_cols, part_cols), part_cols)
        return copy_to(
            pw_hbm.at[:, there], pw.at[1, :, here], pw_send.at[q], pw_recv.at[q], task=sib
        )

    pw_order = [0] + [s * n for n in range(1, far // 2) for s in (1, -1)] + [far // 2]
    pair[0].start()
    for n in pw_order:
        pw_copy(n).start()
    for copy in pair[1:]:
        copy.start()

    def long_way(st):
        return 0 if st < STREAMS // 2 else 1

    def stops(d, st):
        return [c for c in CHAIN if c < far or d == long_way(st)]

    def before(off):
        return max([0] + [c for c in CHAIN if c < off])

    def behind(stop, d, st):
        last = far if d == long_way(st) else far - 1
        found = [off for off in range(1, last + 1) if before(off) == stop]
        return sorted(found, key=lambda off: off not in CHAIN)

    def sides(st):
        return (long_way(st), 1 - long_way(st))

    def rs_copy(ph, d, st, off):
        span = pl.ds(st * rb, rb)
        return copy_to(
            rs_out.at[ph, d, off - 1, span, :],
            rs_in.at[ph, d, off - 1, span, :],
            send_sem.at[2 * ph, d, st, off - 1],
            recv_sem.at[2 * ph, d, st, off - 1],
            task=z_dev((1 - 2 * d) * (off - before(off))),
        )

    def cols(c):
        return pl.ds(pl.multiple_of(c * LANES, LANES), LANES)

    def fill(k):
        stop = ([0] + list(CHAIN))[-1 - k]
        offs = [stop] + list(range(before(stop) + 1, stop))
        if k == 0:
            offs = [far, far - 1]
        for off in offs:
            chunks = [wrap(z + off)] if off in (0, far) else [wrap(z - off), wrap(z + off)]
            total = None
            for h in range(2):
                w = jnp.concatenate([pw[h, :, cols(c)] for c in chunks], axis=1)
                dots = jnp.dot(hid_rows[h], w, preferred_element_type=F32)
                total = dots if total is None else total + dots
            for i, c in enumerate(chunks):
                part[c] = total[:, i * LANES : (i + 1) * LANES]

    def rs_send(ph, d, st, off):
        span = pl.ds(st * rb, rb)
        total = part[wrap(z + (1 - 2 * d) * off), span, :]
        if off in stops(d, st):
            for other in behind(off, d, st):
                rs_copy(ph, d, st, other).wait_recv()
                total += rs_in[ph, d, other - 1, span, :].astype(F32)
        rs_out[ph, d, off - 1, span, :] = total.astype(BF16)
        rs_copy(ph, d, st, off).start()

    def rs_total(ph, st):
        span = pl.ds(st * rb, rb)
        total = part[z, span, :]
        for d in sides(st):
            for other in behind(0, d, st):
                rs_copy(ph, d, st, other).wait_recv()
                total += rs_in[ph, d, other - 1, span, :].astype(F32)
        return total

    def rs_stage(ph, st, k):
        stop = ([0] + list(CHAIN))[-1 - k]
        for d in sides(st):
            if k == 0:
                rs_send(ph, d, st, far if d == long_way(st) else far - 1)
            elif stop != far - 1 or d == long_way(st):
                rs_send(ph, d, st, stop)
        for off in range(stop - 1, before(stop), -1):
            for d in sides(st):
                if off != far - 1 or d == long_way(st):
                    rs_send(ph, d, st, off)

    def rs_sent(ph, st):
        for d in range(2):
            for off in range(1, far + 1 if d == long_way(st) else far):
                rs_copy(ph, d, st, off).wait_send()

    def ag_copy(ph, d, st, off):
        buf = zbuf if ph == 0 else pgf
        extra = 16 if ph == 1 and st == STREAMS - 1 else 0
        sgn = 1 - 2 * d
        ref = buf.at[wrap(z - sgn * before(off)), pl.ds(st * rb, rb + extra), :]
        return copy_to(
            ref,
            ref,
            send_sem.at[2 * ph + 1, d, st, off - 1],
            recv_sem.at[2 * ph + 1, d, st, off - 1],
            task=z_dev(sgn * (off - before(off))),
        )

    def ag_arrived(ph, d, st, off):
        buf = zbuf if ph == 0 else pgf
        extra = 16 if ph == 1 and st == STREAMS - 1 else 0
        sgn = 1 - 2 * d
        if off < far or d == long_way(st):
            ref = buf.at[wrap(z - sgn * off), pl.ds(st * rb, rb + extra), :]
            copy_to(
                ref,
                ref,
                send_sem.at[2 * ph + 1, d, st, off - 1],
                recv_sem.at[2 * ph + 1, d, st, off - 1],
                task=z_dev(sgn * (off - before(off))),
            ).wait_recv()

    def ag_stage(ph, st, k):
        stop = ([0] + list(CHAIN))[k]
        for d in sides(st):
            if k > 0:
                ag_arrived(ph, d, st, stop)
            for off in behind(stop, d, st)[:1]:
                ag_copy(ph, d, st, off).start()
        for d in sides(st):
            for off in behind(stop, d, st)[1:]:
                ag_copy(ph, d, st, off).start()

    def ag_sent(ph, st, first, last):
        for d in range(2):
            for off in range(first, last + 1):
                if off < far or d == long_way(st):
                    ag_copy(ph, d, st, off).wait_send()

    between = [off for off in range(1, far) if off not in CHAIN]

    def prepare():
        loads[6].wait()
        loads[7].wait()
        ids = jnp.broadcast_to(pid_ref[...].astype(F32), (prow_ref.shape[1], rows)).T
        lane = lax.broadcasted_iota(jnp.int32, ids.shape, 1).astype(F32)
        record = jnp.where(ids == lane, prow_ref[...].astype(F32), 0.0)
        weight = 1.0 / jnp.sum(record, axis=1, keepdims=True)
        wrow[...] = jnp.broadcast_to(weight, wrow.shape)
        loss_acc[...] = jnp.zeros_like(loss_acc)
        tg_acc[...] = jnp.zeros_like(tg_acc)
        acc_own[...] = jnp.zeros_like(acc_own)
        acc_sib[...] = jnp.zeros_like(acc_sib)

    def head(st):
        span = pl.ds(pl.multiple_of(st * rb, rb), rb)
        zs = jnp.concatenate(
            [
                jnp.concatenate(
                    [zbuf[p * per_piece + k, span, :] for k in range(per_piece)], axis=1
                )
                for p in range(pieces)
            ],
            axis=0,
        )
        total = None
        for h in range(2):
            dots = lax.dot_general(zs, te[h], NT, preferred_element_type=F32)
            edge = bins[h, span, :]
            alive = (1 - cens[h, span, :]).astype(F32)
            weight = wrow[span, :]
            grads = []
            nll = None
            for p in range(pieces):
                piece = core * pieces + p
                logits = dots[p * rb : (p + 1) * rb] + bias[h, pl.ds(piece, 1), :]
                hazard = jnp.exp(logits)
                at = edge == piece
                hazard = jnp.where(edge > piece, hazard, jnp.where(at, 0.5 * hazard, 0.0))
                event = jnp.where(at, alive, 0.0)
                term = hazard - event * logits
                nll = term if nll is None else nll + term
                grad = (weight * (hazard - event)).astype(BF16)
                gbuf[h, p, span, :] = grad
                grads.append(grad)
            nll = (weight * nll).reshape(rb // 8, 8, tasks).sum(axis=0)
            loss_acc[...] += nll
            grads = jnp.concatenate(grads, axis=0)
            dots = jnp.dot(grads, te[h], preferred_element_type=F32)
            total = dots if total is None else total + dots
        for p in range(pieces):
            for k in range(per_piece):
                part[p * per_piece + k, span, :] = total[
                    p * rb : (p + 1) * rb, k * LANES : (k + 1) * LANES
                ]

    def x_copy(j, src, dst, k):
        return copy_to(
            src, dst, px_send.at[k, j - 1], px_recv.at[k, j - 1], row=(x + j) % nx
        )

    def y_copy(j, src, dst, k):
        return copy_to(
            src, dst, py_send.at[k, j - 1], py_recv.at[k, j - 1], section=(y + j) % ny
        )

    def loss_x_copy(j):
        return x_copy(j, loss_x.at[x], loss_x.at[x], 0)

    def loss_y_copy(j):
        return y_copy(j, loss_y.at[y], loss_y.at[y], 0)

    bx = tasks // nx
    by = bx // ny

    def tgx_copy(j):
        peer = (x + j) % nx
        src = tx_send.at[pl.ds(pl.multiple_of(peer * bx, bx), bx), :]
        return x_copy(j, src, tx_recv.at[j - 1], 1)

    def tgy_copy(j):
        peer = (y + j) % ny
        src = ty_send.at[pl.ds(pl.multiple_of(peer * by, by), by), :]
        return y_copy(j, src, ty_recv.at[j - 1], 1)

    def agy_copy(j):
        ref = tg_fin.at[pl.ds(pl.multiple_of(x * bx + y * by, by), by), :]
        return y_copy(j, ref, ref, 2)

    def agx_copy(j):
        ref = tg_fin.at[pl.ds(pl.multiple_of(x * bx, bx), bx), :]
        return x_copy(j, ref, ref, 2)

    tg_copy = copy_to(tg_send, tg_recv, pair_send.at[5], pair_recv.at[5], task=sib)

    def tg_piece(p):
        zp = jnp.concatenate([zbuf[p * per_piece + k] for k in range(per_piece)], axis=1)
        for h in range(2):
            tg_acc[h] += lax.dot_general(gbuf[h, p], zp, TN, preferred_element_type=F32)

    def loss_terms():
        own = sum(loss_y[i] for i in range(1, ny)) + loss_y[0]
        own = jnp.sum(jnp.sum(own, axis=0, keepdims=True), axis=1, keepdims=True)
        own = jnp.broadcast_to(own, (16, LANES))
        place = lax.broadcasted_iota(jnp.int32, own.shape, 1)
        place += LANES * lax.broadcasted_iota(jnp.int32, own.shape, 0)
        high = own.astype(BF16).astype(F32)
        rest = own - high
        middle = rest.astype(BF16).astype(F32)
        low = rest - middle
        terms = jnp.where(
            place == 0, high, jnp.where(place == 1, middle, jnp.where(place == 2, low, 0.0))
        )
        pgf[z, pl.ds(rows, 16), :] = terms.astype(BF16)

    def plane():
        loss_x[x] = loss_acc[:, :LANES] + loss_acc[:, LANES:]
        for j in range(1, nx):
            loss_x_copy(j).start()
        for p in range(pieces // 2):
            tg_piece(p)
        yield
        for p in range(pieces // 2, pieces):
            tg_piece(p)
        tg_send[...] = tg_acc[1].astype(BF16)
        tg_copy.start()
        for j in range(1, nx):
            loss_x_copy(j).wait()
        loss_y[y] = sum(loss_x[i] for i in range(1, nx)) + loss_x[0]
        for j in range(1, ny):
            loss_y_copy(j).start()
        yield
        tg_copy.wait()
        tg_acc[0] += tg_recv[...].astype(F32)
        tx_send[...] = tg_acc[0].astype(BF16)
        for j in range(1, nx):
            tgx_copy(j).start()
        for j in range(1, ny):
            loss_y_copy(j).wait()
        loss_terms()
        yield
        total = tg_acc[0, pl.ds(pl.multiple_of(x * bx, bx), bx), :]
        for j in range(1, nx):
            tgx_copy(j).wait()
            total += tx_recv[j - 1].astype(F32)
        tg_acc[0, pl.ds(0, bx), :] = total
        ty_send[...] = total.astype(BF16)
        for j in range(1, ny):
            tgy_copy(j).start()
        yield
        total = tg_acc[0, pl.ds(pl.multiple_of(y * by, by), by), :]
        for j in range(1, ny):
            tgy_copy(j).wait()
            total += ty_recv[j - 1].astype(F32)
        place = pl.ds(pl.multiple_of(x * bx + y * by, by), by)
        tg_fin[place, :] = (total * grad_scale).astype(BF16)
        for j in range(1, ny):
            agy_copy(j).start()
        yield
        for j in range(1, ny):
            agy_copy(j).wait_send()
            from_y = (y + ny - j) % ny
            ref = tg_fin.at[pl.ds(pl.multiple_of(x * bx + from_y * by, by), by), :]
            y_copy(j, ref, ref, 2).wait_recv()
        for j in range(1, nx):
            agx_copy(j).start()
        yield
        for j in range(1, nx):
            agx_copy(j).wait_send()
            from_x = (x + nx - j) % nx
            ref = tg_fin.at[pl.ds(pl.multiple_of(from_x * bx, bx), bx), :]
            x_copy(j, ref, ref, 2).wait_recv()
        tg_out[...] = tg_fin[...]

    def add_chunks(st, offs):
        span = pl.ds(st * rb, rb)
        chunks = [wrap(z + off) for off in offs]
        value = jnp.concatenate([pgf[c, span, :] for c in chunks], axis=1)
        for h, acc in ((0, acc_own), (1, acc_sib)):
            w = jnp.concatenate([pw[h, :, cols(c)] for c in chunks], axis=1)
            acc[:, span] += lax.dot_general(w, value, NT, preferred_element_type=F32)

    def hg_copy(st):
        return copy_to(
            hg_send.at[st], hg_recv.at[st], pair_send.at[6 + st], pair_recv.at[6 + st], task=sib
        )

    def stream(st):
        span = pl.ds(st * rb, rb)
        n = len(CHAIN)
        for k in range(n):
            rs_stage(0, st, k)
            yield
            if st == 0:
                for m in pw_order:
                    if abs(m) == k + 2:
                        pw_copy(m).wait_recv()
                fill(k + 1)
            yield
        zbuf[z, span, :] = rs_total(0, st).astype(BF16)
        for k in range(n):
            ag_stage(0, st, k)
            yield
            if k == 1:
                rs_sent(0, st)
            if st == 0 and k == 2:
                for copy in pair:
                    copy.wait_send()
                for m in pw_order:
                    pw_copy(m).wait_send()
            yield
        ag_stage(0, st, n)
        for off in between:
            for d in sides(st):
                ag_arrived(0, d, st, off)
        if st == 0:
            for i in range(1, 5):
                loads[1 + i].wait()
                pair[i].wait_recv()
        head(st)
        for k in range(n):
            rs_stage(1, st, k)
            yield
            if k == 1:
                ag_sent(0, st, 1, far)
            yield
        pgf[z, span, :] = rs_total(1, st).astype(BF16)
        for k in range(n + 1):
            ag_stage(1, st, k)
            yield
            if k == 0:
                add_chunks(st, [0])
            else:
                offs = [CHAIN[k - 1]]
                for off in between:
                    if before(off) == ([0] + list(CHAIN))[k - 1]:
                        for d in sides(st):
                            ag_arrived(1, d, st, off)
                        offs.append(off)
                add_chunks(st, [s * off for off in offs for s in (1, -1) if s * off > -far])
            if k == 1:
                rs_sent(1, st)
            if k == n - 1:
                ag_sent(1, st, 1, CHAIN[n - 2])
            if k == n:
                hg_send[st] = acc_sib[:, span].astype(BF16)
                hg_copy(st).start()
            yield

    loads[0].wait()
    loads[1].wait()
    hid_rows[0] = hid[0].T
    pair[0].wait_recv()
    hid_rows[1] = hid[1].T
    for m in pw_order:
        if abs(m) <= 1:
            pw_copy(m).wait_recv()
    fill(0)
    heads_done = len(CHAIN) * 2 + 1
    running = {st: stream(st) for st in range(STREAMS)}
    beside = None
    slot = 0
    while running:
        active = [st for st in reversed(range(STREAMS)) if st in running and slot >= st * LAG]
        for st in active:
            next(running[st])
        for st in active:
            next(running[st])
        if slot == 0:
            prepare()
        if slot == (STREAMS - 1) * LAG + heads_done - 1:
            beside = plane()
        if beside is not None and next(beside, True):
            beside = None
        for st in active:
            if slot - st * LAG == 4 * len(CHAIN):
                for _ in running.pop(st):
                    pass
        slot += 1
    if beside is not None:
        for _ in beside:
            pass

    total = pgf[0, pl.ds(rows, 16), :].astype(F32)
    for c in range(1, nz):
        total += pgf[c, pl.ds(rows, 16), :].astype(F32)
    loss_pair[core] = total
    ref = loss_pair.at[core]
    last = 6 + STREAMS
    loss_copy = copy_to(ref, ref, pair_send.at[last], pair_recv.at[last], task=sib)
    loss_copy.start()
    for st in range(STREAMS):
        ag_sent(1, st, CHAIN[-2] + 1, far)
    loss_copy.wait()
    total = loss_pair[0] + loss_pair[1]
    loss_out[0, 0] = jnp.sum(total) * loss_scale
    for st in range(STREAMS):
        span = pl.ds(st * rb, rb)
        hg_copy(st).wait()
        hg_out[:, span] = (acc_own[:, span] + hg_recv[st].astype(F32)).astype(BF16)


def shards(
    hidden, piece_weight, task_embed, task_bias, event_bin, censored, patient_id, patient_rows
):
    patients = patient_rows.shape[0]
    rows, depth = hidden.shape
    tasks, width = task_embed.shape
    pieces = task_bias.shape[1]
    n_task = lax.axis_size("task")
    nx, ny = lax.axis_size("row"), lax.axis_size("section")
    nz = n_task // 2
    half = pieces * width // 2
    bx = tasks // nx
    by = bx // ny
    vmem = pl.BlockSpec(memory_space=pltpu.VMEM)
    in_hbm = pl.BlockSpec(memory_space=pltpu.HBM)
    dma = pltpu.SemaphoreType.DMA
    hg, tg, loss = pl.pallas_call(
        functools.partial(kernel, 1.0 / (patients * tasks * n_task), 1.0 / patients),
        out_shape=(
            jax.ShapeDtypeStruct((depth, rows), BF16),
            jax.ShapeDtypeStruct((tasks, width), BF16),
            jax.ShapeDtypeStruct((1, 1), F32),
        ),
        in_specs=[in_hbm] * 8,
        out_specs=(vmem, vmem, pl.BlockSpec(memory_space=pltpu.SMEM)),
        scratch_shapes=[
            pltpu.VMEM((1, rows), jnp.int32),
            pltpu.VMEM((1, patients), jnp.int32),
            pltpu.VMEM((2, depth, rows), BF16),
            pltpu.VMEM((2, rows, depth), BF16),
            pltpu.VMEM((2, depth, half), BF16),
            pltpu.VMEM((2, tasks, width), BF16),
            pltpu.VMEM((2, pieces, tasks), F32),
            pltpu.VMEM((2, rows, tasks), jnp.int32),
            pltpu.VMEM((2, rows, tasks), jnp.int32),
            pltpu.VMEM((rows, tasks), F32),
            pltpu.VMEM((nz, rows, LANES), F32),
            pltpu.VMEM((2, 2, nz // 2, rows, LANES), BF16),
            pltpu.VMEM((2, 2, nz // 2, rows, LANES), BF16),
            pltpu.VMEM((nz, rows, LANES), BF16),
            pltpu.VMEM((nz, rows + 16, LANES), BF16),
            pltpu.VMEM((2, pieces // 2, rows, tasks), BF16),
            pltpu.VMEM((8, tasks), F32),
            pltpu.VMEM((nx, 8, LANES), F32),
            pltpu.VMEM((ny, 8, LANES), F32),
            pltpu.VMEM((2, 16, LANES), F32),
            pltpu.VMEM((2, tasks, width), F32),
            pltpu.VMEM((tasks, width), BF16),
            pltpu.VMEM((tasks, width), BF16),
            pltpu.VMEM((tasks, width), BF16),
            pltpu.VMEM((nx - 1, bx, width), BF16),
            pltpu.VMEM((bx, width), BF16),
            pltpu.VMEM((ny - 1, by, width), BF16),
            pltpu.VMEM((tasks, width), BF16),
            pltpu.VMEM((depth, rows), F32),
            pltpu.VMEM((depth, rows), F32),
            pltpu.VMEM((STREAMS, depth, rows // STREAMS), BF16),
            pltpu.VMEM((STREAMS, depth, rows // STREAMS), BF16),
            dma((4, 2, STREAMS, nz // 2)),
            dma((4, 2, STREAMS, nz // 2)),
            dma((8,)),
            dma((7 + STREAMS,)),
            dma((7 + STREAMS,)),
            dma((nz // 2,)),
            dma((nz // 2,)),
            dma((3, nx - 1)),
            dma((3, nx - 1)),
            dma((3, ny - 1)),
            dma((3, ny - 1)),
        ],
        compiler_params=pltpu.CompilerParams(
            collective_id=0, has_side_effects=True, vmem_limit_bytes=63 * 1024 * 1024
        ),
        cost_estimate=pl.CostEstimate(
            flops=2400000000, bytes_accessed=4000000, transcendentals=600000
        ),
    )(
        hidden.T,
        piece_weight,
        task_embed,
        task_bias.T,
        event_bin,
        censored,
        patient_id.reshape(1, rows),
        patient_rows.reshape(1, patients),
    )
    return hg.T, tg.astype(F32), loss.reshape(())


def solution(mesh):
    return jax.shard_map(
        shards,
        mesh=mesh,
        in_specs=(
            P(("section", "row"), "task"),
            P("task", None),
            P("task", None),
            P("task", None),
            P(("section", "row"), "task"),
            P(("section", "row"), "task"),
            P(("section", "row")),
            P(),
        ),
        out_specs=(P(("section", "row"), "task"), P("task", None), P()),
        check_vma=False,
    )
```

```python
import functools

import jax
import jax.numpy as jnp
from jax import lax
from jax.experimental import pallas as pl
from jax.experimental.pallas import tpu as pltpu
from jax.sharding import PartitionSpec as P

MESH = pl.DeviceIdType.MESH
F32 = jnp.float32
BF16 = jnp.bfloat16
LANES = 128
STREAMS = 2
CHAIN = (2, 4, 6, 8)
LAG = 1
QUAD = 4
NT = (((1,), (1,)), ((), ()))
TN = (((0,), (0,)), ((), ()))


def kernel(
    loss_scale,
    grad_scale,
    hid_hbm,
    pw_hbm,
    te_hbm,
    bias_hbm,
    bins_hbm,
    cens_hbm,
    pid_hbm,
    prow_hbm,
    hg_out,
    tg_out,
    loss_out,
    pid_ref,
    prow_ref,
    hid,
    hid_rows,
    pw,
    te,
    bias,
    bins,
    cens,
    code_out,
    codes,
    wrow,
    part,
    rs_out,
    rs_in,
    zbuf,
    part2,
    q_out,
    q_in,
    pgf,
    gbuf,
    loss_acc,
    loss_x,
    loss_y,
    loss_v,
    loss_u,
    loss_pair,
    tg_acc,
    tg_send,
    tg_recv,
    ta_send,
    tb_send,
    ta_recv,
    tb_recv,
    ua_send,
    ub_send,
    ua_recv,
    ub_recv,
    tv_send,
    tv_recv,
    fin_a,
    fin_b,
    acc_own,
    acc_sib,
    hg_send,
    hg_recv,
    rs_ss,
    rs_rs,
    a1_ss,
    a1_rs,
    q_ss,
    q_rs,
    a2_ss,
    a2_rs,
    local_sem,
    pair_ss,
    pair_rs,
    pw_ss,
    pw_rs,
    code_ss,
    code_rs,
    tez_ss,
    tez_rs,
    bz_ss,
    bz_rs,
    tey_ss,
    tey_rs,
    tex_ss,
    tex_rs,
    lx_ss,
    lx_rs,
    ly_ss,
    ly_rs,
    lv_ss,
    lv_rs,
    lu_ss,
    lu_rs,
    xa_ss,
    xa_rs,
    xb_ss,
    xb_rs,
    ya_ss,
    ya_rs,
    yb_ss,
    yb_rs,
    tv_ss,
    tv_rs,
    gxa_ss,
    gxa_rs,
    gxb_ss,
    gxb_rs,
    gya_ss,
    gya_rs,
    gyb_ss,
    gyb_rs,
):
    rows = hid.shape[2]
    half_cols = pw.shape[2]
    tasks = te.shape[1]
    width = te.shape[2]
    nz = part.shape[0]
    far = nz // 2
    pieces = half_cols // width
    rq = rows // QUAD
    rb = rq // STREAMS
    nx = lax.axis_size("row")
    ny = lax.axis_size("section")
    task = lax.axis_index("task")
    x = lax.axis_index("row")
    y = lax.axis_index("section")
    z = task // 2
    core = task % 2
    sib = z * 2 + 1 - core
    u = z // QUAD
    v = z % QUAD
    n_u = nz // QUAD

    def wrap(c):
        return (c + 2 * nz) % nz

    def z_dev(off):
        return wrap(z + off) * 2 + core

    def v_dev(j):
        return (u * QUAD + (v + j) % QUAD) * 2 + core

    def copy_to(src, dst, ss, rs, **where):
        return pltpu.make_async_remote_copy(
            src_ref=src,
            dst_ref=dst,
            send_sem=ss,
            recv_sem=rs,
            device_id=where,
            device_id_type=MESH,
        )

    def ds(start, size):
        return pl.ds(pl.multiple_of(start, size), size)

    mine = ds(core * half_cols, half_cols)
    loads = [
        (hid_hbm, hid.at[0]),
        (pw_hbm.at[:, mine], pw.at[0]),
        (te_hbm, te.at[0]),
        (bias_hbm, bias.at[0]),
        (bins_hbm, bins),
        (cens_hbm, cens),
        (pid_hbm, pid_ref),
        (prow_hbm, prow_ref),
    ]
    loads = [pltpu.make_async_copy(a, b, local_sem.at[i]) for i, (a, b) in enumerate(loads)]
    for load in loads:
        load.start()

    barrier = pltpu.get_barrier_semaphore()
    peers = [dict(task=sib), dict(task=z_dev(far))]
    peers += [dict(task=z_dev(s * n)) for n in (1, 2, QUAD) for s in (1, -1)]
    peers += [dict(task=v_dev(j)) for j in range(1, QUAD)]
    peers += [dict(row=(x + j) % nx) for j in range(1, nx)]
    peers += [dict(section=(y + j) % ny) for j in range(1, ny)]
    for peer in peers:
        pl.semaphore_signal(barrier, inc=1, device_id=peer, device_id_type=MESH)
    pl.semaphore_wait(barrier, len(peers))

    hid_copy = copy_to(hid_hbm, hid.at[1], pair_ss.at[0], pair_rs.at[0], task=sib)
    te_copy = copy_to(te_hbm, te.at[QUAD], pair_ss.at[1], pair_rs.at[1], task=sib)

    def pw_copy(n):
        q = (wrap(z + far) // QUAD + n + n_u) % n_u
        there = ds((1 - core) * half_cols + q * width, width)
        return copy_to(
            pw_hbm.at[:, there], pw.at[1, :, ds(q * width, width)], pw_ss.at[q], pw_rs.at[q],
            task=sib,
        )

    pw_order = [0, 1, -1, 2]
    hid_copy.start()
    for n in pw_order:
        pw_copy(n).start()
    te_copy.start()

    def long_way(st):
        return 0 if st < STREAMS // 2 else 1

    def sides(st):
        return (long_way(st), 1 - long_way(st))

    def stops(d, st):
        return [c for c in CHAIN if c < far or d == long_way(st)]

    def before(off):
        return max([0] + [c for c in CHAIN if c < off])

    def behind(stop, d, st):
        last = far if d == long_way(st) else far - 1
        found = [off for off in range(1, last + 1) if before(off) == stop]
        return sorted(found, key=lambda off: off not in CHAIN)

    def rows_of(st):
        return pl.ds(st * rb, rb)

    def rs_copy(d, st, off):
        return copy_to(
            rs_out.at[d, off - 1, rows_of(st), :],
            rs_in.at[d, off - 1, rows_of(st), :],
            rs_ss.at[d, st, off - 1],
            rs_rs.at[d, st, off - 1],
            task=z_dev((1 - 2 * d) * (off - before(off))),
        )

    def fill(k):
        stop = ([0] + list(CHAIN))[-1 - k]
        offs = [stop] + list(range(before(stop) + 1, stop))
        if k == 0:
            offs = [far, far - 1]
        for off in offs:
            for c in [wrap(z + off)] if off in (0, far) else [wrap(z - off), wrap(z + off)]:
                total = None
                for h in range(2):
                    dots = jnp.dot(
                        hid_rows[h, ds(c % QUAD * rq, rq), :],
                        pw[h, :, ds(c // QUAD * width, width)],
                        preferred_element_type=F32,
                    )
                    total = dots if total is None else total + dots
                part[c] = total

    def rs_send(d, st, off):
        total = part[wrap(z + (1 - 2 * d) * off), rows_of(st), :]
        if off in stops(d, st):
            for other in behind(off, d, st):
                rs_copy(d, st, other).wait_recv()
                total += rs_in[d, other - 1, rows_of(st), :].astype(F32)
        rs_out[d, off - 1, rows_of(st), :] = total.astype(BF16)
        rs_copy(d, st, off).start()

    def rs_total(st):
        total = part[z, rows_of(st), :]
        for d in sides(st):
            for other in behind(0, d, st):
                rs_copy(d, st, other).wait_recv()
                total += rs_in[d, other - 1, rows_of(st), :].astype(F32)
        return total

    def rs_stage(st, k):
        stop = ([0] + list(CHAIN))[-1 - k]
        for d in sides(st):
            if k == 0:
                rs_send(d, st, far if d == long_way(st) else far - 1)
            elif stop != far - 1 or d == long_way(st):
                rs_send(d, st, stop)
        for off in range(stop - 1, before(stop), -1):
            for d in sides(st):
                if off != far - 1 or d == long_way(st):
                    rs_send(d, st, off)

    def rs_sent(st):
        for d in range(2):
            for off in range(1, far + 1 if d == long_way(st) else far):
                rs_copy(d, st, off).wait_send()

    def a1_copy(d, st, step, arriving=False):
        sgn = 1 - 2 * d
        piece = (u - sgn * (step + (1 if arriving else 0)) + 2 * n_u) % n_u
        ref = zbuf.at[piece, rows_of(st), :]
        return copy_to(
            ref, ref, a1_ss.at[d, st, step], a1_rs.at[d, st, step], task=z_dev(sgn * QUAD)
        )

    def a1_sent(st):
        for d, step in ((0, 0), (1, 0), (long_way(st), 1)):
            a1_copy(d, st, step).wait_send()

    def q_copy(d, st, step):
        sgn = 1 - 2 * d
        return copy_to(
            q_out.at[d, step, rows_of(st), :],
            q_in.at[d, step, rows_of(st), :],
            q_ss.at[d, st, step],
            q_rs.at[d, st, step],
            task=z_dev(sgn * QUAD),
        )

    def q_send(d, st, step, ahead):
        sgn = 1 - 2 * d
        total = part2[(u + sgn * ahead + 2 * n_u) % n_u, rows_of(st), :]
        if step == 1 and d == long_way(st):
            q_copy(d, st, 0).wait_recv()
            total += q_in[d, 0, rows_of(st), :].astype(F32)
        q_out[d, step, rows_of(st), :] = total.astype(BF16)
        q_copy(d, st, step).start()

    def q_total(st):
        total = part2[u, rows_of(st), :]
        for d in range(2):
            q_copy(d, st, 1).wait_recv()
            total += q_in[d, 1, rows_of(st), :].astype(F32)
        return total

    def q_sent(st):
        for d, step in ((long_way(st), 0), (0, 1), (1, 1)):
            q_copy(d, st, step).wait_send()

    def a2_copy(d, st, off, arriving=False):
        sgn = 1 - 2 * d
        ref = pgf.at[wrap(z - sgn * (off if arriving else before(off))), rows_of(st), :]
        return copy_to(
            ref,
            ref,
            a2_ss.at[d, st, off - 1],
            a2_rs.at[d, st, off - 1],
            task=z_dev(sgn * (off - before(off))),
        )

    def a2_arrived(d, st, off):
        if off < far or d == long_way(st):
            a2_copy(d, st, off, True).wait_recv()

    def a2_stage(st, k):
        stop = ([0] + list(CHAIN))[k]
        for d in sides(st):
            if k > 0:
                a2_arrived(d, st, stop)
            for off in behind(stop, d, st)[:1]:
                a2_copy(d, st, off).start()
        for d in sides(st):
            for off in behind(stop, d, st)[1:]:
                a2_copy(d, st, off).start()

    def a2_sent(st, first, last):
        for d in range(2):
            for off in range(first, last + 1):
                if off < far or d == long_way(st):
                    a2_copy(d, st, off).wait_send()

    between = [off for off in range(1, far) if off not in CHAIN]

    def prepare():
        loads[6].wait()
        loads[7].wait()
        ids = jnp.broadcast_to(pid_ref[...].astype(F32), (prow_ref.shape[1], rows)).T
        lane = lax.broadcasted_iota(jnp.int32, ids.shape, 1).astype(F32)
        record = jnp.where(ids == lane, prow_ref[...].astype(F32), 0.0)
        weight = 1.0 / jnp.sum(record, axis=1, keepdims=True)
        wrow[...] = jnp.broadcast_to(weight, wrow.shape)
        loss_acc[...] = jnp.zeros_like(loss_acc)
        acc_own[...] = jnp.zeros_like(acc_own)
        acc_sib[...] = jnp.zeros_like(acc_sib)

    def code_copy(j):
        src = code_out.at[:, ds((v + j) % QUAD * rq, rq), :]
        return copy_to(
            src, codes.at[QUAD - j], code_ss.at[j - 1], code_rs.at[QUAD - j - 1], task=v_dev(j)
        )

    def code_arrived(j):
        ref = codes.at[j]
        copy_to(ref, ref, code_ss.at[j - 1], code_rs.at[j - 1], task=v_dev(j)).wait_recv()

    share = tasks // (nx * ny)

    def tez_copy(j):
        where = ds((x * ny + y) * share, share)
        return copy_to(
            te.at[0, where, :],
            te.at[QUAD - j, where, :],
            tez_ss.at[j - 1],
            tez_rs.at[QUAD - j - 1],
            task=v_dev(j),
        )

    def tez_arrived(j):
        ref = te.at[j, ds((x * ny + y) * share, share), :]
        copy_to(ref, ref, tez_ss.at[j - 1], tez_rs.at[j - 1], task=v_dev(j)).wait_recv()

    def bz_copy(j):
        return copy_to(
            bias.at[0], bias.at[QUAD - j], bz_ss.at[j - 1], bz_rs.at[QUAD - j - 1], task=v_dev(j)
        )

    def bz_arrived(j):
        ref = bias.at[j]
        copy_to(ref, ref, bz_ss.at[j - 1], bz_rs.at[j - 1], task=v_dev(j)).wait_recv()

    others = pl.ds(1, QUAD - 1)

    def tey_copy(j, arriving=False):
        at = (y + ny - j) % ny if arriving else y
        ref = te.at[others, ds((x * ny + at) * share, share), :]
        return copy_to(ref, ref, tey_ss.at[j - 1], tey_rs.at[j - 1], section=(y + j) % ny)

    def tex_copy(j, arriving=False):
        at = (x + nx - j) % nx if arriving else x
        ref = te.at[others, ds(at * ny * share, ny * share), :]
        return copy_to(ref, ref, tex_ss.at[j - 1], tex_rs.at[j - 1], row=(x + j) % nx)

    te_sib = copy_to(
        te.at[others], te.at[pl.ds(QUAD + 1, QUAD - 1)], pair_ss.at[2], pair_rs.at[2], task=sib
    )
    first = pl.ds(0, QUAD)
    second = pl.ds(QUAD, QUAD)
    codes_sib = copy_to(codes.at[first], codes.at[second], pair_ss.at[3], pair_rs.at[3], task=sib)
    bias_sib = copy_to(bias.at[first], bias.at[second], pair_ss.at[4], pair_rs.at[4], task=sib)

    def gather():
        for i in (2, 3, 4, 5):
            loads[i].wait()
        code_out[0] = bins[...].astype(F32).astype(BF16)
        code_out[1] = cens[...].astype(F32).astype(BF16)
        codes[0] = code_out[:, ds(v * rq, rq), :]
        for j in range(1, QUAD):
            tez_copy(j).start()
        code_copy(2).start()
        yield
        for j in range(1, QUAD):
            tez_arrived(j)
        for j in range(1, ny):
            tey_copy(j).start()
        code_copy(1).start()
        yield
        for j in range(1, ny):
            tey_copy(j).wait_send()
            tey_copy(j, True).wait_recv()
        for j in range(1, nx):
            tex_copy(j).start()
        code_copy(3).start()
        for j in range(1, QUAD):
            bz_copy(j).start()
        yield
        for j in range(1, QUAD):
            tez_copy(j).wait_send()
        yield
        for j in range(1, QUAD):
            code_arrived(j)
            bz_arrived(j)
        codes_sib.start()
        bias_sib.start()
        for j in range(1, nx):
            tex_copy(j).wait_send()
            tex_copy(j, True).wait_recv()
        te_sib.start()
        for j in range(1, QUAD):
            code_copy(j).wait_send()
            bz_copy(j).wait_send()
        hid_copy.wait_send()
        te_copy.wait_send()
        for m in pw_order:
            pw_copy(m).wait_send()

    def gathered():
        te_copy.wait_recv()
        codes_sib.wait()
        bias_sib.wait()
        te_sib.wait()

    def head(st):
        span = rows_of(st)
        zs = jnp.concatenate([zbuf[p, span, :] for p in range(pieces)], axis=0)
        weight = wrow[ds(v * rq + st * rb, rb), :]
        total = None
        nll = None
        for b in range(2 * QUAD):
            dots = lax.dot_general(zs, te[b], NT, preferred_element_type=F32)
            edge = codes[b, 0, span, :].astype(F32)
            alive = 1.0 - codes[b, 1, span, :].astype(F32)
            grads = []
            for p in range(pieces):
                piece = core * pieces + p
                at_piece = piece.astype(F32)
                logits = dots[p * rb : (p + 1) * rb] + bias[b, pl.ds(piece, 1), :]
                hazard = jnp.exp(logits)
                at = edge == at_piece
                hazard = jnp.where(edge > at_piece, hazard, jnp.where(at, 0.5 * hazard, 0.0))
                event = jnp.where(at, alive, 0.0)
                term = hazard - event * logits
                nll = term if nll is None else nll + term
                grads.append((weight * (hazard - event)).astype(BF16))
            grads = jnp.concatenate(grads, axis=0)
            gbuf[b, st] = grads
            dots = jnp.dot(grads, te[b], preferred_element_type=F32)
            total = dots if total is None else total + dots
        loss_acc[...] += (weight * nll).reshape(rb // 8, 8, tasks).sum(axis=0)
        for p in range(pieces):
            part2[p, span, :] = total[p * rb : (p + 1) * rb]

    def tg_add(st, blocks):
        zs = jnp.concatenate([zbuf[p, rows_of(st), :] for p in range(pieces)], axis=0)
        for b in blocks:
            dots = lax.dot_general(gbuf[b, st], zs, TN, preferred_element_type=F32)
            if st == 0:
                tg_acc[b] = dots
            else:
                tg_acc[b] += dots

    tg_copy = copy_to(tg_send, tg_recv, pair_ss.at[5], pair_rs.at[5], task=sib)
    bx = tasks // nx
    by = bx // ny
    left = pl.ds(0, width // 2)
    right = pl.ds(width // 2, width // 2)

    def to_x(j, src, dst, ss, rs):
        return copy_to(src, dst, ss.at[j - 1], rs.at[j - 1], row=(x + j) % nx)

    def to_y(j, src, dst, ss, rs):
        return copy_to(src, dst, ss.at[j - 1], rs.at[j - 1], section=(y + j) % ny)

    def xa(j):
        src = ta_send.at[:, ds((x + j) % nx * bx, bx), :]
        return to_x(j, src, ta_recv.at[j - 1], xa_ss, xa_rs)

    def yb(j):
        src = tb_send.at[:, ds((y + j) % ny * bx, bx), :]
        return to_y(j, src, tb_recv.at[j - 1], yb_ss, yb_rs)

    def ya(j):
        src = ua_send.at[:, ds((y + j) % ny * by, by), :]
        return to_y(j, src, ua_recv.at[j - 1], ya_ss, ya_rs)

    def xb(j):
        src = ub_send.at[:, ds((x + j) % nx * by, by), :]
        return to_x(j, src, ub_recv.at[j - 1], xb_ss, xb_rs)

    def tv(j):
        return copy_to(
            tv_send.at[j], tv_recv.at[QUAD - j - 1], tv_ss.at[j - 1], tv_rs.at[QUAD - j - 1],
            task=v_dev(j),
        )

    def tv_arrived(j):
        ref = tv_recv.at[j - 1]
        copy_to(ref, ref, tv_ss.at[j - 1], tv_rs.at[j - 1], task=v_dev(j)).wait_recv()

    def gya(j, arriving=False):
        at = (y + ny - j) % ny if arriving else y
        ref = fin_a.at[ds(x * bx + at * by, by), :]
        return to_y(j, ref, ref, gya_ss, gya_rs)

    def gxb(j, arriving=False):
        at = (x + nx - j) % nx if arriving else x
        ref = fin_b.at[ds(y * bx + at * by, by), :]
        return to_x(j, ref, ref, gxb_ss, gxb_rs)

    def gxa(j, arriving=False):
        at = (x + nx - j) % nx if arriving else x
        ref = fin_a.at[ds(at * bx, bx), :]
        return to_x(j, ref, ref, gxa_ss, gxa_rs)

    def gyb(j, arriving=False):
        at = (y + ny - j) % ny if arriving else y
        ref = fin_b.at[ds(at * bx, bx), :]
        return to_y(j, ref, ref, gyb_ss, gyb_rs)

    def lx(j, arriving=False):
        ref = loss_x.at[(x + nx - j) % nx if arriving else x]
        return to_x(j, ref, ref, lx_ss, lx_rs)

    def ly(j, arriving=False):
        ref = loss_y.at[(y + ny - j) % ny if arriving else y]
        return to_y(j, ref, ref, ly_ss, ly_rs)

    def lv(j, arriving=False):
        ref = loss_v.at[(v + QUAD - j) % QUAD if arriving else v]
        return copy_to(ref, ref, lv_ss.at[j - 1], lv_rs.at[j - 1], task=v_dev(j))

    def lu(j, arriving=False):
        ref = loss_u.at[(u + n_u - j) % n_u if arriving else u]
        return copy_to(ref, ref, lu_ss.at[j - 1], lu_rs.at[j - 1], task=z_dev(j * QUAD))

    def lp(arriving=False):
        ref = loss_pair.at[1 - core if arriving else core]
        return copy_to(ref, ref, pair_ss.at[6], pair_rs.at[6], task=sib)

    def start(copy, n):
        for j in range(1, n):
            copy(j).start()

    def finish(copy, n):
        for j in range(1, n):
            copy(j).wait_send()
            copy(j, True).wait_recv()

    def added(ref):
        return ref[0] + ref[1] + ref[2] + ref[3]

    def plane():
        loss_x[x] = loss_acc[:, :LANES] + loss_acc[:, LANES:]
        start(lx, nx)
        yield
        tg_copy.wait()
        for j in range(QUAD):
            total = (tg_acc[j] + tg_recv[j].astype(F32)).astype(BF16)
            ta_send[j] = total[:, : width // 2]
            tb_send[j] = total[:, width // 2 :]
        start(xa, nx)
        start(yb, ny)
        finish(lx, nx)
        loss_y[y] = added(loss_x)
        start(ly, ny)
        yield
        finish(ly, ny)
        loss_v[v] = added(loss_y)
        start(lv, QUAD)
        yield
        total = ta_send[:, ds(x * bx, bx), :].astype(F32)
        for j in range(1, nx):
            xa(j).wait()
            total += ta_recv[j - 1].astype(F32)
        ua_send[...] = total.astype(BF16)
        start(ya, ny)
        total = tb_send[:, ds(y * bx, bx), :].astype(F32)
        for j in range(1, ny):
            yb(j).wait()
            total += tb_recv[j - 1].astype(F32)
        ub_send[...] = total.astype(BF16)
        start(xb, nx)
        finish(lv, QUAD)
        loss_u[u] = added(loss_v)
        start(lu, n_u)
        yield
        total = ua_send[:, ds(y * by, by), :].astype(F32)
        for j in range(1, ny):
            ya(j).wait()
            total += ua_recv[j - 1].astype(F32)
        tv_send[:, 0] = total.astype(BF16)
        total = ub_send[:, ds(x * by, by), :].astype(F32)
        for j in range(1, nx):
            xb(j).wait()
            total += ub_recv[j - 1].astype(F32)
        tv_send[:, 1] = total.astype(BF16)
        start(tv, QUAD)
        finish(lu, n_u)
        loss_pair[core] = added(loss_u)
        lp().start()
        yield
        total = tv_send[0].astype(F32)
        for j in range(1, QUAD):
            tv(j).wait_send()
            tv_arrived(j)
            total += tv_recv[j - 1].astype(F32)
        total = (total * grad_scale).astype(BF16)
        fin_a[ds(x * bx + y * by, by), :] = total[0]
        fin_b[ds(y * bx + x * by, by), :] = total[1]
        start(gya, ny)
        start(gxb, nx)
        lp().wait_send()
        lp(True).wait_recv()
        loss_out[0, 0] = jnp.sum(loss_pair[0] + loss_pair[1]) * loss_scale
        yield
        finish(gya, ny)
        finish(gxb, nx)
        start(gxa, nx)
        start(gyb, ny)
        yield
        finish(gxa, nx)
        finish(gyb, ny)
        tg_out[:, left] = fin_a[...]
        tg_out[:, right] = fin_b[...]

    def add_chunk(off):
        c = wrap(z + off)
        for h, acc in ((0, acc_own), (1, acc_sib)):
            acc[c % QUAD] += lax.dot_general(
                pgf[c], pw[h, :, ds(c // QUAD * width, width)], NT, preferred_element_type=F32
            )

    hg_copy = copy_to(hg_send, hg_recv, pair_ss.at[7], pair_rs.at[7], task=sib)

    def stream(st):
        span = rows_of(st)
        n = len(CHAIN)
        last = st == STREAMS - 1
        d = long_way(st)
        for k in range(n):
            rs_stage(st, k)
            yield
            if st == 0:
                if k == 0:
                    pw_copy(2).wait_recv()
                fill(k + 1)
            yield
        zbuf[u, span, :] = rs_total(st).astype(BF16)
        a1_copy(d, st, 0).start()
        a1_copy(1 - d, st, 0).start()
        yield
        rs_sent(st)
        yield
        a1_copy(d, st, 0, True).wait_recv()
        a1_copy(d, st, 1).start()
        yield
        yield
        a1_copy(1 - d, st, 0, True).wait_recv()
        a1_copy(d, st, 1, True).wait_recv()
        if st == 0:
            gathered()
        head(st)
        q_send(d, st, 0, 2)
        q_send(1 - d, st, 1, 1)
        yield
        tg_add(st, range(QUAD, 2 * QUAD))
        if last:
            tg_send[...] = tg_acc[pl.ds(QUAD, QUAD)].astype(BF16)
            tg_copy.start()
        tg_add(st, range(QUAD))
        yield
        q_send(d, st, 1, 1)
        yield
        a1_sent(st)
        yield
        pgf[z, span, :] = q_total(st).astype(BF16)
        for k in range(n + 1):
            a2_stage(st, k)
            yield
            offs = [0] if k == 0 else [CHAIN[k - 1], -CHAIN[k - 1]]
            for off in between if k > 0 else []:
                if before(off) == ([0] + list(CHAIN))[k - 1]:
                    for side in sides(st):
                        a2_arrived(side, st, off)
                    offs += [off, -off]
            if last:
                for off in offs:
                    if off > -far:
                        add_chunk(off)
            if k == 1:
                q_sent(st)
            if k == n - 1:
                a2_sent(st, 1, CHAIN[n - 2])
            yield

    loads[0].wait()
    loads[1].wait()
    hid_rows[0] = hid[0].T
    hid_copy.wait_recv()
    hid_rows[1] = hid[1].T
    for m in (0, 1, -1):
        pw_copy(m).wait_recv()
    fill(0)
    head_slot = len(CHAIN) + 2
    last_slot = 2 * len(CHAIN) + 4
    running = {st: stream(st) for st in range(STREAMS)}
    beside = gather()
    slot = 0
    while running:
        active = [st for st in reversed(range(STREAMS)) if st in running and slot >= st * LAG]
        for st in active:
            next(running[st])
        for st in active:
            next(running[st])
        if slot == 0:
            prepare()
        if slot == head_slot + (STREAMS - 1) * LAG:
            beside = plane()
        if beside is not None and next(beside, True):
            beside = None
        for st in active:
            if slot - st * LAG == last_slot:
                for _ in running.pop(st):
                    pass
        slot += 1
    hg_send[...] = acc_sib[...].astype(BF16)
    hg_copy.start()
    for st in range(STREAMS):
        a2_sent(st, CHAIN[-2] + 1, far)
    if beside is not None:
        for _ in beside:
            pass
    hg_copy.wait()
    for i in range(QUAD):
        hg_out[pl.ds(i * rq, rq), :] = (acc_own[i] + hg_recv[i].astype(F32)).astype(BF16)


def shards(
    hidden, piece_weight, task_embed, task_bias, event_bin, censored, patient_id, patient_rows
):
    patients = patient_rows.shape[0]
    rows, depth = hidden.shape
    tasks, width = task_embed.shape
    pieces = task_bias.shape[1]
    n_task = lax.axis_size("task")
    nx, ny = lax.axis_size("row"), lax.axis_size("section")
    nz = n_task // 2
    far = nz // 2
    half = pieces * width // 2
    rq = rows // QUAD
    rb = rq // STREAMS
    bx = tasks // nx
    by = bx // ny
    hw = width // 2
    vmem = pl.BlockSpec(memory_space=pltpu.VMEM)
    in_hbm = pl.BlockSpec(memory_space=pltpu.HBM)
    dma = pltpu.SemaphoreType.DMA

    def pair(*shape):
        return [dma(shape), dma(shape)]

    def arrays(*shapes):
        return [pltpu.VMEM(shape, dtype) for shape, dtype in shapes]

    hg, tg, loss = pl.pallas_call(
        functools.partial(kernel, 1.0 / (patients * tasks * n_task), 1.0 / patients),
        out_shape=(
            jax.ShapeDtypeStruct((rows, depth), BF16),
            jax.ShapeDtypeStruct((tasks, width), BF16),
            jax.ShapeDtypeStruct((1, 1), F32),
        ),
        in_specs=[in_hbm] * 8,
        out_specs=(vmem, vmem, pl.BlockSpec(memory_space=pltpu.SMEM)),
        scratch_shapes=arrays(
            ((1, rows), jnp.int32),
            ((1, patients), jnp.int32),
            ((2, depth, rows), BF16),
            ((2, rows, depth), BF16),
            ((2, depth, half), BF16),
            ((2 * QUAD, tasks, width), BF16),
            ((2 * QUAD, pieces, tasks), F32),
            ((rows, tasks), jnp.int32),
            ((rows, tasks), jnp.int32),
            ((2, rows, tasks), BF16),
            ((2 * QUAD, 2, rq, tasks), BF16),
            ((rows, tasks), F32),
            ((nz, rq, width), F32),
            ((2, far, rq, width), BF16),
            ((2, far, rq, width), BF16),
            ((pieces // 2, rq, width), BF16),
            ((pieces // 2, rq, width), F32),
            ((2, 2, rq, width), BF16),
            ((2, 2, rq, width), BF16),
            ((nz, rq, width), BF16),
            ((2 * QUAD, STREAMS, pieces // 2 * rb, tasks), BF16),
            ((8, tasks), F32),
            ((nx, 8, LANES), F32),
            ((ny, 8, LANES), F32),
            ((QUAD, 8, LANES), F32),
            ((nz // QUAD, 8, LANES), F32),
            ((2, 8, LANES), F32),
            ((2 * QUAD, tasks, width), F32),
            ((QUAD, tasks, width), BF16),
            ((QUAD, tasks, width), BF16),
            ((QUAD, tasks, hw), BF16),
            ((QUAD, tasks, hw), BF16),
            ((nx - 1, QUAD, bx, hw), BF16),
            ((ny - 1, QUAD, bx, hw), BF16),
            ((QUAD, bx, hw), BF16),
            ((QUAD, bx, hw), BF16),
            ((ny - 1, QUAD, by, hw), BF16),
            ((nx - 1, QUAD, by, hw), BF16),
            ((QUAD, 2, by, hw), BF16),
            ((QUAD - 1, 2, by, hw), BF16),
            ((tasks, hw), BF16),
            ((tasks, hw), BF16),
            ((QUAD, rq, depth), F32),
            ((QUAD, rq, depth), F32),
            ((QUAD, rq, depth), BF16),
            ((QUAD, rq, depth), BF16),
        )
        + pair(2, STREAMS, far)
        + pair(2, STREAMS, 2)
        + pair(2, STREAMS, 2)
        + pair(2, STREAMS, far)
        + [dma((8,))]
        + pair(8)
        + pair(nz // QUAD)
        + pair(QUAD - 1) * 3
        + pair(ny - 1)
        + pair(nx - 1)
        + pair(nx - 1)
        + pair(ny - 1)
        + pair(QUAD - 1)
        + pair(nz // QUAD - 1)
        + pair(nx - 1) * 2
        + pair(ny - 1) * 2
        + pair(QUAD - 1)
        + pair(nx - 1) * 2
        + pair(ny - 1) * 2,
        compiler_params=pltpu.CompilerParams(
            collective_id=0, has_side_effects=True, vmem_limit_bytes=63 * 1024 * 1024
        ),
        cost_estimate=pl.CostEstimate(
            flops=2400000000, bytes_accessed=4000000, transcendentals=600000
        ),
    )(
        hidden.T,
        piece_weight,
        task_embed,
        task_bias.T,
        event_bin,
        censored,
        patient_id.reshape(1, rows),
        patient_rows.reshape(1, patients),
    )
    return hg, tg.astype(F32), loss.reshape(())


def solution(mesh):
    return jax.shard_map(
        shards,
        mesh=mesh,
        in_specs=(
            P(("section", "row"), "task"),
            P("task", None),
            P("task", None),
            P("task", None),
            P(("section", "row"), "task"),
            P(("section", "row"), "task"),
            P(("section", "row")),
            P(),
        ),
        out_specs=(P(("section", "row"), "task"), P("task", None), P()),
        check_vma=False,
    )
```

```python
import functools

import jax
import jax.numpy as jnp
from jax import lax
from jax.experimental import pallas as pl
from jax.experimental.pallas import tpu as pltpu
from jax.sharding import PartitionSpec as P

MESH = pl.DeviceIdType.MESH
F32 = jnp.float32
BF16 = jnp.bfloat16
LANES = 128
STREAMS = 2
CHAIN = (2, 4, 6, 8)
QUAD = 4
NT = (((1,), (1,)), ((), ()))
TN = (((0,), (0,)), ((), ()))


def kernel(
    loss_scale,
    grad_scale,
    hid_hbm,
    pw_hbm,
    te_hbm,
    bias_hbm,
    bins_hbm,
    cens_hbm,
    pid_hbm,
    prow_hbm,
    hg_out,
    tg_out,
    loss_out,
    pid_ref,
    prow_ref,
    hid,
    hid_rows,
    pw,
    te,
    bias,
    bins,
    cens,
    code_out,
    codes,
    wrow,
    part,
    rs_out,
    rs_in,
    zbuf,
    part2,
    q_out,
    q_in,
    pgf,
    gbuf,
    loss_acc,
    loss_x,
    loss_y,
    loss_v,
    loss_u,
    loss_pair,
    tg_acc,
    tg_send,
    tg_recv,
    ta_send,
    tb_send,
    ta_recv,
    tb_recv,
    ua_send,
    ub_send,
    ua_recv,
    ub_recv,
    tv_send,
    tv_recv,
    fin,
    acc_own,
    acc_sib,
    hg_send,
    hg_recv,
    rs_ss,
    rs_rs,
    a1_ss,
    a1_rs,
    q_ss,
    q_rs,
    a2_ss,
    a2_rs,
    local_sem,
    pair_ss,
    pair_rs,
    pw_ss,
    pw_rs,
    code_ss,
    code_rs,
    tez_ss,
    tez_rs,
    bz_ss,
    bz_rs,
    tey_ss,
    tey_rs,
    tex_ss,
    tex_rs,
    lx_ss,
    lx_rs,
    ly_ss,
    ly_rs,
    lv_ss,
    lv_rs,
    lu_ss,
    lu_rs,
    xa_ss,
    xa_rs,
    xb_ss,
    xb_rs,
    ya_ss,
    ya_rs,
    yb_ss,
    yb_rs,
    tv_ss,
    tv_rs,
    fin_ss,
    fin_rs,
):
    rows = hid.shape[2]
    half_cols = pw.shape[2]
    tasks = te.shape[1]
    width = te.shape[2]
    nz = part.shape[0]
    far = nz // 2
    pieces = half_cols // width
    rq = rows // QUAD
    rb = rq // STREAMS
    nx = lax.axis_size("row")
    ny = lax.axis_size("section")
    task = lax.axis_index("task")
    x = lax.axis_index("row")
    y = lax.axis_index("section")
    z = task // 2
    core = task % 2
    sib = z * 2 + 1 - core
    u = z // QUAD
    v = z % QUAD
    n_u = nz // QUAD

    def wrap(c):
        return (c + 2 * nz) % nz

    def z_dev(off):
        return wrap(z + off) * 2 + core

    def v_dev(j):
        return (u * QUAD + (v + j) % QUAD) * 2 + core

    def copy_to(src, dst, ss, rs, **where):
        return pltpu.make_async_remote_copy(
            src_ref=src,
            dst_ref=dst,
            send_sem=ss,
            recv_sem=rs,
            device_id=where,
            device_id_type=MESH,
        )

    def ds(start, size):
        return pl.ds(pl.multiple_of(start, size), size)

    mine = ds(core * half_cols, half_cols)
    loads = [
        (hid_hbm, hid.at[0]),
        (pw_hbm.at[:, mine], pw.at[0]),
        (te_hbm, te.at[0]),
        (bias_hbm, bias.at[0]),
        (bins_hbm, bins),
        (cens_hbm, cens),
        (pid_hbm, pid_ref),
        (prow_hbm, prow_ref),
    ]
    loads = [pltpu.make_async_copy(a, b, local_sem.at[i]) for i, (a, b) in enumerate(loads)]
    for load in loads:
        load.start()

    barrier = pltpu.get_barrier_semaphore()
    peers = [dict(task=sib), dict(task=z_dev(far))]
    peers += [dict(task=z_dev(s * n)) for n in (1, 2, QUAD) for s in (1, -1)]
    peers += [dict(task=v_dev(j)) for j in range(1, QUAD)]
    plane_steps = [(i, j) for i in range(nx) for j in range(ny) if i or j]
    peers += [dict(row=(x + i) % nx, section=(y + j) % ny) for i, j in plane_steps]
    for peer in peers:
        pl.semaphore_signal(barrier, inc=1, device_id=peer, device_id_type=MESH)
    loads[4].wait()
    loads[5].wait()
    code_out[0] = bins[...].astype(F32).astype(BF16)
    code_out[1] = cens[...].astype(F32).astype(BF16)
    codes[0] = code_out[:, ds(v * rq, rq), :]
    loads[2].wait()
    loads[3].wait()
    pl.semaphore_wait(barrier, len(peers))

    hid_copy = copy_to(hid_hbm, hid.at[1], pair_ss.at[0], pair_rs.at[0], task=sib)
    te_copy = copy_to(te_hbm, te.at[QUAD], pair_ss.at[1], pair_rs.at[1], task=sib)

    def pw_copy(n):
        q = (wrap(z + far) // QUAD + n + n_u) % n_u
        there = ds((1 - core) * half_cols + q * width, width)
        return copy_to(
            pw_hbm.at[:, there], pw.at[1, :, ds(q * width, width)], pw_ss.at[q], pw_rs.at[q],
            task=sib,
        )

    pw_order = [0, 1, -1, 2]
    hid_copy.start()
    for n in pw_order:
        pw_copy(n).start()
    te_copy.start()

    def code_copy(j):
        src = code_out.at[:, ds((v + j) % QUAD * rq, rq), :]
        return copy_to(
            src, codes.at[QUAD - j], code_ss.at[j - 1], code_rs.at[QUAD - j - 1], task=v_dev(j)
        )

    def code_arrived(j):
        ref = codes.at[j]
        copy_to(ref, ref, code_ss.at[j - 1], code_rs.at[j - 1], task=v_dev(j)).wait_recv()

    share = tasks // (nx * ny)

    def tez_copy(j):
        where = ds((x * ny + y) * share, share)
        return copy_to(
            te.at[0, where, :],
            te.at[QUAD - j, where, :],
            tez_ss.at[j - 1],
            tez_rs.at[QUAD - j - 1],
            task=v_dev(j),
        )

    def bz_copy(j):
        return copy_to(
            bias.at[0], bias.at[QUAD - j], bz_ss.at[j - 1], bz_rs.at[QUAD - j - 1], task=v_dev(j)
        )

    for j in (2, 1, 3):
        tez_copy(j).start()
        code_copy(j).start()
        bz_copy(j).start()

    def long_way(st):
        return 0 if st < STREAMS // 2 else 1

    def sides(st):
        return (long_way(st), 1 - long_way(st))

    def stops(d, st):
        return [c for c in CHAIN if c < far or d == long_way(st)]

    def before(off):
        return max([0] + [c for c in CHAIN if c < off])

    def behind(stop, d, st):
        last = far if d == long_way(st) else far - 1
        found = [off for off in range(1, last + 1) if before(off) == stop]
        return sorted(found, key=lambda off: off not in CHAIN)

    def rows_of(st):
        return pl.ds(st * rb, rb)

    def rs_copy(d, st, off):
        return copy_to(
            rs_out.at[d, off - 1, rows_of(st), :],
            rs_in.at[d, off - 1, rows_of(st), :],
            rs_ss.at[d, st, off - 1],
            rs_rs.at[d, st, off - 1],
            task=z_dev((1 - 2 * d) * (off - before(off))),
        )

    def fill(k):
        stop = ([0] + list(CHAIN))[-1 - k]
        offs = [stop] + list(range(before(stop) + 1, stop))
        if k == 0:
            offs = [far, far - 1]
        for off in offs:
            for c in [wrap(z + off)] if off in (0, far) else [wrap(z - off), wrap(z + off)]:
                total = None
                for h in range(2):
                    dots = jnp.dot(
                        hid_rows[h, ds(c % QUAD * rq, rq), :],
                        pw[h, :, ds(c // QUAD * width, width)],
                        preferred_element_type=F32,
                    )
                    total = dots if total is None else total + dots
                part[c] = total

    def rs_send(d, st, off):
        total = part[wrap(z + (1 - 2 * d) * off), rows_of(st), :]
        if off in stops(d, st):
            for other in behind(off, d, st):
                rs_copy(d, st, other).wait_recv()
                total += rs_in[d, other - 1, rows_of(st), :].astype(F32)
        rs_out[d, off - 1, rows_of(st), :] = total.astype(BF16)
        rs_copy(d, st, off).start()

    def rs_total(st):
        total = part[z, rows_of(st), :]
        for d in sides(st):
            for other in behind(0, d, st):
                rs_copy(d, st, other).wait_recv()
                total += rs_in[d, other - 1, rows_of(st), :].astype(F32)
        return total

    def rs_chain(st, k):
        stop = ([0] + list(CHAIN))[-1 - k]
        for d in sides(st):
            if k == 0:
                rs_send(d, st, far if d == long_way(st) else far - 1)
            elif stop != far - 1 or d == long_way(st):
                rs_send(d, st, stop)

    def rs_leaves(st, k):
        stop = ([0] + list(CHAIN))[-1 - k]
        for off in range(stop - 1, before(stop), -1):
            for d in sides(st):
                if off != far - 1 or d == long_way(st):
                    rs_send(d, st, off)

    def rs_sent(st):
        for d in range(2):
            for off in range(1, far + 1 if d == long_way(st) else far):
                rs_copy(d, st, off).wait_send()

    def a1_copy(d, st, step, arriving=False):
        sgn = 1 - 2 * d
        piece = (u - sgn * (step + (1 if arriving else 0)) + 2 * n_u) % n_u
        ref = zbuf.at[piece, rows_of(st), :]
        return copy_to(
            ref, ref, a1_ss.at[d, st, step], a1_rs.at[d, st, step], task=z_dev(sgn * QUAD)
        )

    def a1_sent(st):
        for d, step in ((0, 0), (1, 0), (long_way(st), 1)):
            a1_copy(d, st, step).wait_send()

    def q_copy(d, st, step):
        sgn = 1 - 2 * d
        return copy_to(
            q_out.at[d, step, rows_of(st), :],
            q_in.at[d, step, rows_of(st), :],
            q_ss.at[d, st, step],
            q_rs.at[d, st, step],
            task=z_dev(sgn * QUAD),
        )

    def q_send(d, st, step, ahead):
        sgn = 1 - 2 * d
        total = part2[(u + sgn * ahead + 2 * n_u) % n_u, rows_of(st), :]
        if step == 1 and d == long_way(st):
            q_copy(d, st, 0).wait_recv()
            total += q_in[d, 0, rows_of(st), :].astype(F32)
        q_out[d, step, rows_of(st), :] = total.astype(BF16)
        q_copy(d, st, step).start()

    def q_total(st):
        total = part2[u, rows_of(st), :]
        for d in range(2):
            q_copy(d, st, 1).wait_recv()
            total += q_in[d, 1, rows_of(st), :].astype(F32)
        return total

    def q_sent(st):
        for d, step in ((long_way(st), 0), (0, 1), (1, 1)):
            q_copy(d, st, step).wait_send()

    def a2_copy(d, st, off, arriving=False):
        sgn = 1 - 2 * d
        ref = pgf.at[wrap(z - sgn * (off if arriving else before(off))), rows_of(st), :]
        return copy_to(
            ref,
            ref,
            a2_ss.at[d, st, off - 1],
            a2_rs.at[d, st, off - 1],
            task=z_dev(sgn * (off - before(off))),
        )

    def a2_arrived(d, st, off):
        if off < far or d == long_way(st):
            a2_copy(d, st, off, True).wait_recv()

    def a2_chain(st, k):
        stop = ([0] + list(CHAIN))[k]
        for d in sides(st):
            if k > 0:
                a2_arrived(d, st, stop)
            for off in behind(stop, d, st)[:1]:
                a2_copy(d, st, off).start()

    def a2_leaves(st, k):
        stop = ([0] + list(CHAIN))[k]
        for d in sides(st):
            for off in behind(stop, d, st)[1:]:
                a2_copy(d, st, off).start()

    def a2_sent(st, first, last):
        for d in range(2):
            for off in range(first, last + 1):
                if off < far or d == long_way(st):
                    a2_copy(d, st, off).wait_send()

    between = [off for off in range(1, far) if off not in CHAIN]

    def prepare():
        loads[6].wait()
        loads[7].wait()
        ids = jnp.broadcast_to(pid_ref[...].astype(F32), (prow_ref.shape[1], rows)).T
        lane = lax.broadcasted_iota(jnp.int32, ids.shape, 1).astype(F32)
        record = jnp.where(ids == lane, prow_ref[...].astype(F32), 0.0)
        weight = 1.0 / jnp.sum(record, axis=1, keepdims=True)
        wrow[...] = jnp.broadcast_to(weight, wrow.shape)
        loss_acc[...] = jnp.zeros_like(loss_acc)
        acc_own[...] = jnp.zeros_like(acc_own)
        acc_sib[...] = jnp.zeros_like(acc_sib)

    def tez_arrived(j):
        ref = te.at[j, ds((x * ny + y) * share, share), :]
        copy_to(ref, ref, tez_ss.at[j - 1], tez_rs.at[j - 1], task=v_dev(j)).wait_recv()

    def bz_arrived(j):
        ref = bias.at[j]
        copy_to(ref, ref, bz_ss.at[j - 1], bz_rs.at[j - 1], task=v_dev(j)).wait_recv()

    others = pl.ds(1, QUAD - 1)

    def tey_copy(j, arriving=False):
        at = (y + ny - j) % ny if arriving else y
        ref = te.at[others, ds((x * ny + at) * share, share), :]
        return copy_to(ref, ref, tey_ss.at[j - 1], tey_rs.at[j - 1], section=(y + j) % ny)

    def tex_copy(j, arriving=False):
        at = (x + nx - j) % nx if arriving else x
        ref = te.at[others, ds(at * ny * share, ny * share), :]
        return copy_to(ref, ref, tex_ss.at[j - 1], tex_rs.at[j - 1], row=(x + j) % nx)

    te_sib = copy_to(
        te.at[others], te.at[pl.ds(QUAD + 1, QUAD - 1)], pair_ss.at[2], pair_rs.at[2], task=sib
    )
    first = pl.ds(0, QUAD)
    second = pl.ds(QUAD, QUAD)
    codes_sib = copy_to(codes.at[first], codes.at[second], pair_ss.at[3], pair_rs.at[3], task=sib)
    bias_sib = copy_to(bias.at[first], bias.at[second], pair_ss.at[4], pair_rs.at[4], task=sib)

    def gather():
        for j in range(1, QUAD):
            tez_arrived(j)
        for j in range(1, ny):
            tey_copy(j).start()
        yield
        for j in range(1, ny):
            tey_copy(j).wait_send()
            tey_copy(j, True).wait_recv()
        for j in range(1, nx):
            tex_copy(j).start()
        yield
        for j in range(1, QUAD):
            tez_copy(j).wait_send()
            code_copy(j).wait_send()
            bz_copy(j).wait_send()
        yield
        hid_copy.wait_send()
        te_copy.wait_send()
        for m in pw_order:
            pw_copy(m).wait_send()
        yield
        for j in range(1, QUAD):
            code_arrived(j)
            bz_arrived(j)
        codes_sib.start()
        bias_sib.start()
        for j in range(1, nx):
            tex_copy(j).wait_send()
            tex_copy(j, True).wait_recv()
        te_sib.start()

    def gathered():
        te_copy.wait_recv()
        codes_sib.wait()
        bias_sib.wait()
        te_sib.wait()

    def head(st):
        span = rows_of(st)
        zs = jnp.concatenate([zbuf[p, span, :] for p in range(pieces)], axis=0)
        weight = wrow[ds(v * rq + st * rb, rb), :]
        total = None
        nll = None
        for b in range(2 * QUAD):
            dots = lax.dot_general(zs, te[b], NT, preferred_element_type=F32)
            edge = codes[b, 0, span, :].astype(F32)
            alive = 1.0 - codes[b, 1, span, :].astype(F32)
            grads = []
            for p in range(pieces):
                piece = core * pieces + p
                at_piece = piece.astype(F32)
                logits = dots[p * rb : (p + 1) * rb] + bias[b, pl.ds(piece, 1), :]
                hazard = jnp.exp(logits)
                at = edge == at_piece
                hazard = jnp.where(edge > at_piece, hazard, jnp.where(at, 0.5 * hazard, 0.0))
                event = jnp.where(at, alive, 0.0)
                term = hazard - event * logits
                nll = term if nll is None else nll + term
                grads.append((weight * (hazard - event)).astype(BF16))
            grads = jnp.concatenate(grads, axis=0)
            gbuf[b, st] = grads
            dots = jnp.dot(grads, te[b], preferred_element_type=F32)
            total = dots if total is None else total + dots
        loss_acc[...] += (weight * nll).reshape(rb // 8, 8, tasks).sum(axis=0)
        for p in range(pieces):
            part2[p, span, :] = total[p * rb : (p + 1) * rb]

    def tg_product(b, zs):
        grads = gbuf[b].reshape(STREAMS * pieces * rb, tasks)
        return lax.dot_general(grads, zs, TN, preferred_element_type=F32)

    def tg_products():
        zs = jnp.concatenate(
            [zbuf[p, rows_of(st), :] for st in range(STREAMS) for p in range(pieces)], axis=0
        )
        for j in range(QUAD):
            tg_send[j] = tg_product(QUAD + j, zs).astype(BF16)
        tg_copy.start()
        for j in range(QUAD):
            tg_acc[j] = tg_product(j, zs)

    tg_copy = copy_to(tg_send, tg_recv, pair_ss.at[5], pair_rs.at[5], task=sib)
    by = tasks // (nx * ny)
    left = pl.ds(0, width // 2)
    right = pl.ds(width // 2, width // 2)

    def to_x(j, src, dst, ss, rs):
        return copy_to(src, dst, ss.at[j - 1], rs.at[j - 1], row=(x + j) % nx)

    def to_y(j, src, dst, ss, rs):
        return copy_to(src, dst, ss.at[j - 1], rs.at[j - 1], section=(y + j) % ny)

    def xa(j):
        src = ta_send.at[:, (x + j) % nx]
        return to_x(j, src, ta_recv.at[j - 1], xa_ss, xa_rs)

    def yb(j):
        src = tb_send.at[:, :, (y + j) % ny]
        return to_y(j, src, tb_recv.at[j - 1], yb_ss, yb_rs)

    def ya(j):
        src = ua_send.at[:, (y + j) % ny]
        return to_y(j, src, ua_recv.at[j - 1], ya_ss, ya_rs)

    def xb(j):
        src = ub_send.at[:, (x + j) % nx]
        return to_x(j, src, ub_recv.at[j - 1], xb_ss, xb_rs)

    def tv(j):
        return copy_to(
            tv_send.at[j], tv_recv.at[QUAD - j - 1], tv_ss.at[j - 1], tv_rs.at[QUAD - j - 1],
            task=v_dev(j),
        )

    def tv_arrived(j):
        ref = tv_recv.at[j - 1]
        copy_to(ref, ref, tv_ss.at[j - 1], tv_rs.at[j - 1], task=v_dev(j)).wait_recv()

    def fin_copy(i, j, arriving=False):
        at_x = (x + nx - i) % nx if arriving else x
        at_y = (y + ny - j) % ny if arriving else y
        ref = fin.at[ds((at_x * ny + at_y) * by, by), :]
        return copy_to(
            ref, ref, fin_ss.at[i, j], fin_rs.at[i, j], row=(x + i) % nx, section=(y + j) % ny
        )

    def lx(j, arriving=False):
        ref = loss_x.at[(x + nx - j) % nx if arriving else x]
        return to_x(j, ref, ref, lx_ss, lx_rs)

    def ly(j, arriving=False):
        ref = loss_y.at[(y + ny - j) % ny if arriving else y]
        return to_y(j, ref, ref, ly_ss, ly_rs)

    def lv(j, arriving=False):
        ref = loss_v.at[(v + QUAD - j) % QUAD if arriving else v]
        return copy_to(ref, ref, lv_ss.at[j - 1], lv_rs.at[j - 1], task=v_dev(j))

    def lu(j, arriving=False):
        ref = loss_u.at[(u + n_u - j) % n_u if arriving else u]
        return copy_to(ref, ref, lu_ss.at[j - 1], lu_rs.at[j - 1], task=z_dev(j * QUAD))

    def lp(arriving=False):
        ref = loss_pair.at[1 - core if arriving else core]
        return copy_to(ref, ref, pair_ss.at[6], pair_rs.at[6], task=sib)

    def start(copy, n):
        for j in range(1, n):
            copy(j).start()

    def finish(copy, n):
        for j in range(1, n):
            copy(j).wait_send()
            copy(j, True).wait_recv()

    def added(ref):
        return ref[0] + ref[1] + ref[2] + ref[3]

    def plane():
        loss_x[x] = loss_acc[:, :LANES] + loss_acc[:, LANES:]
        start(lx, nx)
        yield
        tg_copy.wait()
        for j in range(QUAD):
            total = (tg_acc[j] + tg_recv[j].astype(F32)).astype(BF16)
            ta_send[j] = total[:, : width // 2].reshape(nx, ny, by, width // 2)
            tb_send[j] = total[:, width // 2 :].reshape(nx, ny, by, width // 2)
        start(xa, nx)
        start(yb, ny)
        finish(lx, nx)
        loss_y[y] = added(loss_x)
        start(ly, ny)
        yield
        finish(ly, ny)
        loss_v[v] = added(loss_y)
        start(lv, QUAD)
        yield
        yield
        total = ta_send[:, x].astype(F32)
        for j in range(1, nx):
            xa(j).wait()
            total += ta_recv[j - 1].astype(F32)
        ua_send[...] = total.astype(BF16)
        start(ya, ny)
        total = tb_send[:, :, y].astype(F32)
        for j in range(1, ny):
            yb(j).wait()
            total += tb_recv[j - 1].astype(F32)
        ub_send[...] = total.astype(BF16)
        start(xb, nx)
        finish(lv, QUAD)
        loss_u[u] = added(loss_v)
        start(lu, n_u)
        yield
        total = ua_send[:, y].astype(F32)
        for j in range(1, ny):
            ya(j).wait()
            total += ua_recv[j - 1].astype(F32)
        tv_send[:, :, left] = total.astype(BF16)
        total = ub_send[:, x].astype(F32)
        for j in range(1, nx):
            xb(j).wait()
            total += ub_recv[j - 1].astype(F32)
        tv_send[:, :, right] = total.astype(BF16)
        start(tv, QUAD)
        finish(lu, n_u)
        loss_pair[core] = added(loss_u)
        lp().start()
        yield
        total = tv_send[0].astype(F32)
        for j in range(1, QUAD):
            tv(j).wait_send()
            tv_arrived(j)
            total += tv_recv[j - 1].astype(F32)
        fin[ds((x * ny + y) * by, by), :] = (total * grad_scale).astype(BF16)
        for i, j in plane_steps:
            fin_copy(i, j).start()
        lp().wait_send()
        lp(True).wait_recv()
        loss_out[0, 0] = jnp.sum(loss_pair[0] + loss_pair[1]) * loss_scale
        yield
        for i, j in plane_steps:
            fin_copy(i, j).wait_send()
            fin_copy(i, j, True).wait_recv()
        tg_out[...] = fin[...]

    def add_chunk(off):
        c = wrap(z + off)
        for h, acc in ((0, acc_own), (1, acc_sib)):
            acc[c % QUAD] += lax.dot_general(
                pgf[c], pw[h, :, ds(c // QUAD * width, width)], NT, preferred_element_type=F32
            )

    hg_copy = copy_to(hg_send, hg_recv, pair_ss.at[7], pair_rs.at[7], task=sib)

    def stream(st):
        span = rows_of(st)
        n = len(CHAIN)
        last = st == STREAMS - 1
        d = long_way(st)
        for k in range(n):
            rs_chain(st, k)
            yield
            rs_leaves(st, k)
            yield
            if last:
                if k == 0:
                    pw_copy(2).wait_recv()
                fill(k + 1)
            yield
        zbuf[u, span, :] = rs_total(st).astype(BF16)
        a1_copy(d, st, 0).start()
        yield
        a1_copy(1 - d, st, 0).start()
        yield
        rs_sent(st)
        yield
        a1_copy(d, st, 0, True).wait_recv()
        a1_copy(d, st, 1).start()
        yield
        yield
        yield
        a1_copy(1 - d, st, 0, True).wait_recv()
        a1_copy(d, st, 1, True).wait_recv()
        if st == 0:
            gathered()
        head(st)
        q_send(d, st, 0, 2)
        q_send(1 - d, st, 1, 1)
        yield
        yield
        if last:
            tg_products()
        yield
        q_send(d, st, 1, 1)
        yield
        yield
        a1_sent(st)
        yield
        pgf[z, span, :] = q_total(st).astype(BF16)
        for k in range(n + 1):
            a2_chain(st, k)
            yield
            a2_leaves(st, k)
            yield
            offs = [0] if k == 0 else [CHAIN[k - 1], -CHAIN[k - 1]]
            for off in between if k > 0 else []:
                if before(off) == ([0] + list(CHAIN))[k - 1]:
                    for side in sides(st):
                        a2_arrived(side, st, off)
                    offs += [off, -off]
            if last:
                for off in offs:
                    if off > -far:
                        add_chunk(off)
            if k == 1:
                q_sent(st)
            if k == n - 1:
                a2_sent(st, 1, CHAIN[n - 2])
            yield

    loads[0].wait()
    loads[1].wait()
    hid_rows[0] = hid[0].T
    hid_copy.wait_recv()
    hid_rows[1] = hid[1].T
    for m in (0, 1, -1):
        pw_copy(m).wait_recv()
    fill(0)
    head_slot = len(CHAIN) + 2
    last_slot = 2 * len(CHAIN) + 4
    running = [stream(st) for st in range(STREAMS)]
    beside = gather()
    for slot in range(last_slot + 1):
        for _ in range(3):
            for steps in running:
                next(steps)
        if slot == 0:
            prepare()
        if slot == head_slot:
            beside = plane()
        if beside is not None and next(beside, True):
            beside = None
    for steps in running:
        for _ in steps:
            pass
    hg_send[...] = acc_sib[...].astype(BF16)
    hg_copy.start()
    for st in range(STREAMS):
        a2_sent(st, CHAIN[-2] + 1, far)
    if beside is not None:
        for _ in beside:
            pass
    hg_copy.wait()
    for i in range(QUAD):
        hg_out[pl.ds(i * rq, rq), :] = (acc_own[i] + hg_recv[i].astype(F32)).astype(BF16)


def shards(
    hidden, piece_weight, task_embed, task_bias, event_bin, censored, patient_id, patient_rows
):
    patients = patient_rows.shape[0]
    rows, depth = hidden.shape
    tasks, width = task_embed.shape
    pieces = task_bias.shape[1]
    n_task = lax.axis_size("task")
    nx, ny = lax.axis_size("row"), lax.axis_size("section")
    nz = n_task // 2
    far = nz // 2
    half = pieces * width // 2
    rq = rows // QUAD
    rb = rq // STREAMS
    by = tasks // (nx * ny)
    hw = width // 2
    vmem = pl.BlockSpec(memory_space=pltpu.VMEM)
    in_hbm = pl.BlockSpec(memory_space=pltpu.HBM)
    dma = pltpu.SemaphoreType.DMA

    def pair(*shape):
        return [dma(shape), dma(shape)]

    def arrays(*shapes):
        return [pltpu.VMEM(shape, dtype) for shape, dtype in shapes]

    hg, tg, loss = pl.pallas_call(
        functools.partial(kernel, 1.0 / (patients * tasks * n_task), 1.0 / patients),
        out_shape=(
            jax.ShapeDtypeStruct((rows, depth), BF16),
            jax.ShapeDtypeStruct((tasks, width), BF16),
            jax.ShapeDtypeStruct((1, 1), F32),
        ),
        in_specs=[in_hbm] * 8,
        out_specs=(vmem, vmem, pl.BlockSpec(memory_space=pltpu.SMEM)),
        scratch_shapes=arrays(
            ((1, rows), jnp.int32),
            ((1, patients), jnp.int32),
            ((2, depth, rows), BF16),
            ((2, rows, depth), BF16),
            ((2, depth, half), BF16),
            ((2 * QUAD, tasks, width), BF16),
            ((2 * QUAD, pieces, tasks), F32),
            ((rows, tasks), jnp.int32),
            ((rows, tasks), jnp.int32),
            ((2, rows, tasks), BF16),
            ((2 * QUAD, 2, rq, tasks), BF16),
            ((rows, tasks), F32),
            ((nz, rq, width), F32),
            ((2, far, rq, width), BF16),
            ((2, far, rq, width), BF16),
            ((pieces // 2, rq, width), BF16),
            ((pieces // 2, rq, width), F32),
            ((2, 2, rq, width), BF16),
            ((2, 2, rq, width), BF16),
            ((nz, rq, width), BF16),
            ((2 * QUAD, STREAMS, pieces // 2 * rb, tasks), BF16),
            ((8, tasks), F32),
            ((nx, 8, LANES), F32),
            ((ny, 8, LANES), F32),
            ((QUAD, 8, LANES), F32),
            ((nz // QUAD, 8, LANES), F32),
            ((2, 8, LANES), F32),
            ((QUAD, tasks, width), F32),
            ((QUAD, tasks, width), BF16),
            ((QUAD, tasks, width), BF16),
            ((QUAD, nx, ny, by, hw), BF16),
            ((QUAD, nx, ny, by, hw), BF16),
            ((nx - 1, QUAD, ny, by, hw), BF16),
            ((ny - 1, QUAD, nx, by, hw), BF16),
            ((QUAD, ny, by, hw), BF16),
            ((QUAD, nx, by, hw), BF16),
            ((ny - 1, QUAD, by, hw), BF16),
            ((nx - 1, QUAD, by, hw), BF16),
            ((QUAD, by, width), BF16),
            ((QUAD - 1, by, width), BF16),
            ((tasks, width), BF16),
            ((QUAD, rq, depth), F32),
            ((QUAD, rq, depth), F32),
            ((QUAD, rq, depth), BF16),
            ((QUAD, rq, depth), BF16),
        )
        + pair(2, STREAMS, far)
        + pair(2, STREAMS, 2)
        + pair(2, STREAMS, 2)
        + pair(2, STREAMS, far)
        + [dma((8,))]
        + pair(8)
        + pair(nz // QUAD)
        + pair(QUAD - 1) * 3
        + pair(ny - 1)
        + pair(nx - 1)
        + pair(nx - 1)
        + pair(ny - 1)
        + pair(QUAD - 1)
        + pair(nz // QUAD - 1)
        + pair(nx - 1) * 2
        + pair(ny - 1) * 2
        + pair(QUAD - 1)
        + pair(nx, ny),
        compiler_params=pltpu.CompilerParams(
            collective_id=0, has_side_effects=True, vmem_limit_bytes=63 * 1024 * 1024
        ),
        cost_estimate=pl.CostEstimate(
            flops=2400000000, bytes_accessed=4000000, transcendentals=600000
        ),
    )(
        hidden.T,
        piece_weight,
        task_embed,
        task_bias.T,
        event_bin,
        censored,
        patient_id.reshape(1, rows),
        patient_rows.reshape(1, patients),
    )
    return hg, tg.astype(F32), loss.reshape(())


def solution(mesh):
    return jax.shard_map(
        shards,
        mesh=mesh,
        in_specs=(
            P(("section", "row"), "task"),
            P("task", None),
            P("task", None),
            P("task", None),
            P(("section", "row"), "task"),
            P(("section", "row"), "task"),
            P(("section", "row")),
            P(),
        ),
        out_specs=(P(("section", "row"), "task"), P("task", None), P()),
        check_vma=False,
    )
```

```python
import functools

import jax
import jax.numpy as jnp
from jax import lax
from jax.experimental import pallas as pl
from jax.experimental.pallas import tpu as pltpu
from jax.sharding import PartitionSpec as P

MESH = pl.DeviceIdType.MESH
F32 = jnp.float32
BF16 = jnp.bfloat16
LANES = 128
STREAMS = 2
CHAIN = (2, 4, 6, 8)
QUAD = 4
NT = (((1,), (1,)), ((), ()))
TN = (((0,), (0,)), ((), ()))


def kernel(
    loss_scale,
    grad_scale,
    hid_hbm,
    pw_hbm,
    te_hbm,
    bias_hbm,
    bins_hbm,
    cens_hbm,
    pid_hbm,
    prow_hbm,
    hg_out,
    tg_out,
    loss_out,
    pid_ref,
    prow_ref,
    hid,
    hid_rows,
    pw,
    te,
    bias,
    bins,
    cens,
    code_out,
    codes,
    wrow,
    part,
    rs_out,
    rs_in,
    zbuf,
    part2,
    q_out,
    q_in,
    pgf,
    gbuf,
    loss_acc,
    loss_x,
    loss_y,
    loss_v,
    loss_u,
    loss_pair,
    tg_send,
    tg_recv,
    ta_send,
    tb_send,
    ta_recv,
    tb_recv,
    ua_send,
    ub_send,
    ua_recv,
    ub_recv,
    tv_send,
    tv_recv,
    fin,
    acc_own,
    acc_sib,
    hg_send,
    hg_recv,
    rs_ss,
    rs_rs,
    a1_ss,
    a1_rs,
    q_ss,
    q_rs,
    a2_ss,
    a2_rs,
    local_sem,
    pair_ss,
    pair_rs,
    pw_ss,
    pw_rs,
    code_ss,
    code_rs,
    tez_ss,
    tez_rs,
    bz_ss,
    bz_rs,
    tey_ss,
    tey_rs,
    tex_ss,
    tex_rs,
    lx_ss,
    lx_rs,
    ly_ss,
    ly_rs,
    lv_ss,
    lv_rs,
    lu_ss,
    lu_rs,
    xa_ss,
    xa_rs,
    xb_ss,
    xb_rs,
    ya_ss,
    ya_rs,
    yb_ss,
    yb_rs,
    tv_ss,
    tv_rs,
    tg_ss,
    tg_rs,
    fin_ss,
    fin_rs,
):
    rows = hid.shape[2]
    half_cols = pw.shape[2]
    tasks = bins.shape[1]
    width = te.shape[4]
    nz = part.shape[0]
    far = nz // 2
    pieces = half_cols // width
    rq = rows // QUAD
    rb = rq // STREAMS
    nx = lax.axis_size("row")
    ny = lax.axis_size("section")
    task = lax.axis_index("task")
    x = lax.axis_index("row")
    y = lax.axis_index("section")
    z = task // 2
    core = task % 2
    sib = z * 2 + 1 - core
    u = z // QUAD
    v = z % QUAD
    n_u = nz // QUAD

    def wrap(c):
        return (c + 2 * nz) % nz

    def z_dev(off):
        return wrap(z + off) * 2 + core

    def v_dev(j):
        return (u * QUAD + (v + j) % QUAD) * 2 + core

    def copy_to(src, dst, ss, rs, **where):
        return pltpu.make_async_remote_copy(
            src_ref=src,
            dst_ref=dst,
            send_sem=ss,
            recv_sem=rs,
            device_id=where,
            device_id_type=MESH,
        )

    def ds(start, size):
        return pl.ds(pl.multiple_of(start, size), size)

    mine = ds(core * half_cols, half_cols)
    loads = [
        (hid_hbm, hid.at[0]),
        (pw_hbm.at[:, mine], pw.at[0]),
        (te_hbm, te.at[0]),
        (bias_hbm, bias.at[0]),
        (bins_hbm, bins),
        (cens_hbm, cens),
        (pid_hbm, pid_ref),
        (prow_hbm, prow_ref),
    ]
    loads = [pltpu.make_async_copy(a, b, local_sem.at[i]) for i, (a, b) in enumerate(loads)]
    for load in loads:
        load.start()

    barrier = pltpu.get_barrier_semaphore()
    peers = [dict(task=sib), dict(task=z_dev(far))]
    peers += [dict(task=z_dev(s * n)) for n in (1, 2, QUAD) for s in (1, -1)]
    peers += [dict(task=v_dev(j)) for j in range(1, QUAD)]
    plane_steps = [(i, j) for i in range(nx) for j in range(ny) if i or j]
    peers += [dict(row=(x + i) % nx, section=(y + j) % ny) for i, j in plane_steps]
    for peer in peers:
        pl.semaphore_signal(barrier, inc=1, device_id=peer, device_id_type=MESH)
    loads[4].wait()
    loads[5].wait()
    code_out[0] = bins[...].astype(F32).astype(BF16)
    code_out[1] = cens[...].astype(F32).astype(BF16)
    codes[0] = code_out[:, ds(v * rq, rq), :]
    loads[2].wait()
    loads[3].wait()
    pl.semaphore_wait(barrier, len(peers))

    hid_copy = copy_to(hid_hbm, hid.at[1], pair_ss.at[0], pair_rs.at[0], task=sib)
    te_copy = copy_to(te_hbm, te.at[QUAD], pair_ss.at[1], pair_rs.at[1], task=sib)

    def pw_copy(n):
        q = (wrap(z + far) // QUAD + n + n_u) % n_u
        there = ds((1 - core) * half_cols + q * width, width)
        return copy_to(
            pw_hbm.at[:, there], pw.at[1, :, ds(q * width, width)], pw_ss.at[q], pw_rs.at[q],
            task=sib,
        )

    pw_order = [0, 1, -1, 2]
    hid_copy.start()
    for n in pw_order:
        pw_copy(n).start()
    te_copy.start()

    def code_copy(j):
        src = code_out.at[:, ds((v + j) % QUAD * rq, rq), :]
        return copy_to(
            src, codes.at[QUAD - j], code_ss.at[j - 1], code_rs.at[QUAD - j - 1], task=v_dev(j)
        )

    def code_arrived(j):
        ref = codes.at[j]
        copy_to(ref, ref, code_ss.at[j - 1], code_rs.at[j - 1], task=v_dev(j)).wait_recv()

    def tez_copy(j):
        return copy_to(
            te.at[0, x, y],
            te.at[QUAD - j, x, y],
            tez_ss.at[j - 1],
            tez_rs.at[QUAD - j - 1],
            task=v_dev(j),
        )

    def bz_copy(j):
        return copy_to(
            bias.at[0], bias.at[QUAD - j], bz_ss.at[j - 1], bz_rs.at[QUAD - j - 1], task=v_dev(j)
        )

    for j in (2, 1, 3):
        tez_copy(j).start()
        code_copy(j).start()
        bz_copy(j).start()

    def long_way(st):
        return 0 if st < STREAMS // 2 else 1

    def sides(st):
        return (long_way(st), 1 - long_way(st))

    def stops(d, st):
        return [c for c in CHAIN if c < far or d == long_way(st)]

    def before(off):
        return max([0] + [c for c in CHAIN if c < off])

    def behind(stop, d, st):
        last = far if d == long_way(st) else far - 1
        found = [off for off in range(1, last + 1) if before(off) == stop]
        return sorted(found, key=lambda off: off not in CHAIN)

    def rows_of(st):
        return pl.ds(st * rb, rb)

    def rs_copy(d, st, off):
        return copy_to(
            rs_out.at[d, off - 1, rows_of(st), :],
            rs_in.at[d, off - 1, rows_of(st), :],
            rs_ss.at[d, st, off - 1],
            rs_rs.at[d, st, off - 1],
            task=z_dev((1 - 2 * d) * (off - before(off))),
        )

    def fill(k):
        stop = ([0] + list(CHAIN))[-1 - k]
        offs = [stop] + list(range(before(stop) + 1, stop))
        if k == 0:
            offs = [far, far - 1]
        for off in offs:
            for c in [wrap(z + off)] if off in (0, far) else [wrap(z - off), wrap(z + off)]:
                total = None
                for h in range(2):
                    dots = jnp.dot(
                        hid_rows[h, ds(c % QUAD * rq, rq), :],
                        pw[h, :, ds(c // QUAD * width, width)],
                        preferred_element_type=F32,
                    )
                    total = dots if total is None else total + dots
                part[c] = total

    def rs_send(d, st, off):
        total = part[wrap(z + (1 - 2 * d) * off), rows_of(st), :]
        if off in stops(d, st):
            for other in behind(off, d, st):
                rs_copy(d, st, other).wait_recv()
                total += rs_in[d, other - 1, rows_of(st), :].astype(F32)
        rs_out[d, off - 1, rows_of(st), :] = total.astype(BF16)
        rs_copy(d, st, off).start()

    def rs_total(st):
        total = part[z, rows_of(st), :]
        for d in sides(st):
            for other in behind(0, d, st):
                rs_copy(d, st, other).wait_recv()
                total += rs_in[d, other - 1, rows_of(st), :].astype(F32)
        return total

    def rs_chain(st, k):
        stop = ([0] + list(CHAIN))[-1 - k]
        for d in sides(st):
            if k == 0:
                rs_send(d, st, far if d == long_way(st) else far - 1)
            elif stop != far - 1 or d == long_way(st):
                rs_send(d, st, stop)

    def rs_leaves(st, k):
        stop = ([0] + list(CHAIN))[-1 - k]
        for off in range(stop - 1, before(stop), -1):
            for d in sides(st):
                if off != far - 1 or d == long_way(st):
                    rs_send(d, st, off)

    def rs_sent(st):
        for d in range(2):
            for off in range(1, far + 1 if d == long_way(st) else far):
                rs_copy(d, st, off).wait_send()

    def a1_copy(d, st, step, arriving=False):
        sgn = 1 - 2 * d
        piece = (u - sgn * (step + (1 if arriving else 0)) + 2 * n_u) % n_u
        ref = zbuf.at[piece, rows_of(st), :]
        return copy_to(
            ref, ref, a1_ss.at[d, st, step], a1_rs.at[d, st, step], task=z_dev(sgn * QUAD)
        )

    def a1_sent(st):
        for d, step in ((0, 0), (1, 0), (long_way(st), 1)):
            a1_copy(d, st, step).wait_send()

    def q_copy(d, st, step):
        sgn = 1 - 2 * d
        return copy_to(
            q_out.at[d, step, rows_of(st), :],
            q_in.at[d, step, rows_of(st), :],
            q_ss.at[d, st, step],
            q_rs.at[d, st, step],
            task=z_dev(sgn * QUAD),
        )

    def q_send(d, st, step, ahead):
        sgn = 1 - 2 * d
        total = part2[(u + sgn * ahead + 2 * n_u) % n_u, rows_of(st), :]
        if step == 1 and d == long_way(st):
            q_copy(d, st, 0).wait_recv()
            total += q_in[d, 0, rows_of(st), :].astype(F32)
        q_out[d, step, rows_of(st), :] = total.astype(BF16)
        q_copy(d, st, step).start()

    def q_total(st):
        total = part2[u, rows_of(st), :]
        for d in range(2):
            q_copy(d, st, 1).wait_recv()
            total += q_in[d, 1, rows_of(st), :].astype(F32)
        return total

    def q_sent(st):
        for d, step in ((long_way(st), 0), (0, 1), (1, 1)):
            q_copy(d, st, step).wait_send()

    def a2_copy(d, st, off, arriving=False):
        sgn = 1 - 2 * d
        ref = pgf.at[wrap(z - sgn * (off if arriving else before(off))), rows_of(st), :]
        return copy_to(
            ref,
            ref,
            a2_ss.at[d, st, off - 1],
            a2_rs.at[d, st, off - 1],
            task=z_dev(sgn * (off - before(off))),
        )

    def a2_arrived(d, st, off):
        if off < far or d == long_way(st):
            a2_copy(d, st, off, True).wait_recv()

    def a2_chain(st, k):
        stop = ([0] + list(CHAIN))[k]
        for d in sides(st):
            if k > 0:
                a2_arrived(d, st, stop)
            for off in behind(stop, d, st)[:1]:
                a2_copy(d, st, off).start()

    def a2_leaves(st, k):
        stop = ([0] + list(CHAIN))[k]
        for d in sides(st):
            for off in behind(stop, d, st)[1:]:
                a2_copy(d, st, off).start()

    def a2_sent(st, first, last):
        for d in range(2):
            for off in range(first, last + 1):
                if off < far or d == long_way(st):
                    a2_copy(d, st, off).wait_send()

    between = [off for off in range(1, far) if off not in CHAIN]

    def prepare():
        loads[6].wait()
        loads[7].wait()
        ids = jnp.broadcast_to(pid_ref[...].astype(F32), (prow_ref.shape[1], rows)).T
        lane = lax.broadcasted_iota(jnp.int32, ids.shape, 1).astype(F32)
        record = jnp.where(ids == lane, prow_ref[...].astype(F32), 0.0)
        weight = 1.0 / jnp.sum(record, axis=1, keepdims=True)
        wrow[...] = jnp.broadcast_to(weight, wrow.shape)
        acc_own[...] = jnp.zeros_like(acc_own)
        acc_sib[...] = jnp.zeros_like(acc_sib)

    def tez_arrived(j):
        ref = te.at[j, x, y]
        copy_to(ref, ref, tez_ss.at[j - 1], tez_rs.at[j - 1], task=v_dev(j)).wait_recv()

    def bz_arrived(j):
        ref = bias.at[j]
        copy_to(ref, ref, bz_ss.at[j - 1], bz_rs.at[j - 1], task=v_dev(j)).wait_recv()

    others = pl.ds(1, QUAD - 1)

    left = pl.ds(0, width // 2)
    right = pl.ds(width // 2, width // 2)

    def te_y(j, step, arriving=False):
        at = (y + ny - j) % ny if arriving else y
        ref = te.at[others, x, at, :, left] if step == 0 else te.at[others, :, at, :, right]
        return copy_to(
            ref, ref, tey_ss.at[step, j - 1], tey_rs.at[step, j - 1], section=(y + j) % ny
        )

    def te_x(j, step, arriving=False):
        at = (x + nx - j) % nx if arriving else x
        ref = te.at[others, at, y, :, right] if step == 0 else te.at[others, at, :, :, left]
        return copy_to(
            ref, ref, tex_ss.at[step, j - 1], tex_rs.at[step, j - 1], row=(x + j) % nx
        )

    te_sib = copy_to(
        te.at[others], te.at[pl.ds(QUAD + 1, QUAD - 1)], pair_ss.at[2], pair_rs.at[2], task=sib
    )
    first = pl.ds(0, QUAD)
    second = pl.ds(QUAD, QUAD)
    codes_sib = copy_to(codes.at[first], codes.at[second], pair_ss.at[3], pair_rs.at[3], task=sib)
    bias_sib = copy_to(bias.at[first], bias.at[second], pair_ss.at[4], pair_rs.at[4], task=sib)

    def te_start(step):
        for j in range(1, ny):
            te_y(j, step).start()
        for j in range(1, nx):
            te_x(j, step).start()

    def te_finish(step):
        for j in range(1, ny):
            te_y(j, step).wait_send()
            te_y(j, step, True).wait_recv()
        for j in range(1, nx):
            te_x(j, step).wait_send()
            te_x(j, step, True).wait_recv()

    def gather():
        for j in range(1, QUAD):
            tez_arrived(j)
        te_start(0)
        yield
        te_finish(0)
        te_start(1)
        yield
        for j in range(1, QUAD):
            tez_copy(j).wait_send()
            code_copy(j).wait_send()
            bz_copy(j).wait_send()
        hid_copy.wait_send()
        te_copy.wait_send()
        for m in pw_order:
            pw_copy(m).wait_send()
        yield
        for j in range(1, QUAD):
            code_arrived(j)
            bz_arrived(j)
        codes_sib.start()
        bias_sib.start()
        yield
        te_finish(1)
        te_sib.start()

    def gathered():
        te_copy.wait_recv()
        codes_sib.wait()
        bias_sib.wait()
        te_sib.wait()

    def head():
        zs = zbuf[...].reshape(pieces * rq, width)
        weight = wrow[ds(v * rq, rq), :]
        total = None
        nll = None
        for b in [*range(QUAD, 2 * QUAD), *range(QUAD)]:
            embed = te[b].reshape(tasks, width)
            dots = lax.dot_general(zs, embed, NT, preferred_element_type=F32)
            edge = codes[b, 0].astype(F32)
            alive = 1.0 - codes[b, 1].astype(F32)
            terms = None
            for p in range(pieces):
                piece = core * pieces + p
                at_piece = piece.astype(F32)
                logits = dots[p * rq : (p + 1) * rq] + bias[b, pl.ds(piece, 1), :]
                hazard = jnp.exp(logits)
                at = edge == at_piece
                hazard = jnp.where(edge > at_piece, hazard, jnp.where(at, 0.5 * hazard, 0.0))
                event = jnp.where(at, alive, 0.0)
                term = hazard - event * logits
                terms = term if terms is None else terms + term
                gbuf[b, p] = (weight * (hazard - event)).astype(BF16)
            terms = (weight * terms).reshape(rq // 8, 8, tasks).sum(axis=0)
            nll = terms if nll is None else nll + terms
            grads = gbuf[b].reshape(pieces * rq, tasks)
            dots = jnp.dot(grads, embed, preferred_element_type=F32)
            if total is None:
                part2[...] = dots.reshape(pieces, rq, width)
                total = part2
            else:
                part2[...] += dots.reshape(pieces, rq, width)
            if b >= QUAD:
                tg_send[b - QUAD] = tg_product(b, zs).astype(BF16)
                tg_copy(b - QUAD).start()
        loss_acc[...] = nll

    def tg_product(b, zs):
        grads = gbuf[b].reshape(pieces * rq, tasks)
        return lax.dot_general(grads, zs, TN, preferred_element_type=F32)

    def tg_copy(j):
        return copy_to(tg_send.at[j], tg_recv.at[j], tg_ss.at[j], tg_rs.at[j], task=sib)

    by = tasks // (nx * ny)
    def to_x(j, src, dst, ss, rs):
        return copy_to(src, dst, ss.at[j - 1], rs.at[j - 1], row=(x + j) % nx)

    def to_y(j, src, dst, ss, rs):
        return copy_to(src, dst, ss.at[j - 1], rs.at[j - 1], section=(y + j) % ny)

    def xa(j):
        src = ta_send.at[:, (x + j) % nx]
        return to_x(j, src, ta_recv.at[j - 1], xa_ss, xa_rs)

    def yb(j):
        src = tb_send.at[:, :, (y + j) % ny]
        return to_y(j, src, tb_recv.at[j - 1], yb_ss, yb_rs)

    def ya(j):
        src = ua_send.at[:, (y + j) % ny]
        return to_y(j, src, ua_recv.at[j - 1], ya_ss, ya_rs)

    def xb(j):
        src = ub_send.at[:, (x + j) % nx]
        return to_x(j, src, ub_recv.at[j - 1], xb_ss, xb_rs)

    def tv(j):
        return copy_to(
            tv_send.at[j], tv_recv.at[QUAD - j - 1], tv_ss.at[j - 1], tv_rs.at[QUAD - j - 1],
            task=v_dev(j),
        )

    def tv_arrived(j):
        ref = tv_recv.at[j - 1]
        copy_to(ref, ref, tv_ss.at[j - 1], tv_rs.at[j - 1], task=v_dev(j)).wait_recv()

    def fin_copy(i, j, arriving=False):
        at_x = (x + nx - i) % nx if arriving else x
        at_y = (y + ny - j) % ny if arriving else y
        ref = fin.at[ds((at_x * ny + at_y) * by, by), :]
        return copy_to(
            ref, ref, fin_ss.at[i, j], fin_rs.at[i, j], row=(x + i) % nx, section=(y + j) % ny
        )

    def lx(j, arriving=False):
        ref = loss_x.at[(x + nx - j) % nx if arriving else x]
        return to_x(j, ref, ref, lx_ss, lx_rs)

    def ly(j, arriving=False):
        ref = loss_y.at[(y + ny - j) % ny if arriving else y]
        return to_y(j, ref, ref, ly_ss, ly_rs)

    def lv(j, arriving=False):
        ref = loss_v.at[(v + QUAD - j) % QUAD if arriving else v]
        return copy_to(ref, ref, lv_ss.at[j - 1], lv_rs.at[j - 1], task=v_dev(j))

    def lu(j, arriving=False):
        ref = loss_u.at[(u + n_u - j) % n_u if arriving else u]
        return copy_to(ref, ref, lu_ss.at[j - 1], lu_rs.at[j - 1], task=z_dev(j * QUAD))

    def lp(arriving=False):
        ref = loss_pair.at[1 - core if arriving else core]
        return copy_to(ref, ref, pair_ss.at[6], pair_rs.at[6], task=sib)

    def start(copy, n):
        for j in range(1, n):
            copy(j).start()

    def finish(copy, n):
        for j in range(1, n):
            copy(j).wait_send()
            copy(j, True).wait_recv()

    def added(ref):
        return ref[0] + ref[1] + ref[2] + ref[3]

    def plane():
        loss_x[x] = loss_acc[:, :LANES] + loss_acc[:, LANES:]
        start(lx, nx)
        zs = zbuf[...].reshape(pieces * rq, width)
        for j in range(QUAD):
            total = tg_product(j, zs)
            tg_copy(j).wait()
            total = (total + tg_recv[j].astype(F32)).astype(BF16)
            ta_send[j] = total[:, : width // 2].reshape(nx, ny, by, width // 2)
            tb_send[j] = total[:, width // 2 :].reshape(nx, ny, by, width // 2)
        start(xa, nx)
        start(yb, ny)
        yield
        finish(lx, nx)
        loss_y[y] = added(loss_x)
        start(ly, ny)
        yield
        finish(ly, ny)
        loss_v[v] = added(loss_y)
        start(lv, QUAD)
        yield
        total = ta_send[:, x].astype(F32)
        for j in range(1, nx):
            xa(j).wait()
            total += ta_recv[j - 1].astype(F32)
        ua_send[...] = total.astype(BF16)
        start(ya, ny)
        total = tb_send[:, :, y].astype(F32)
        for j in range(1, ny):
            yb(j).wait()
            total += tb_recv[j - 1].astype(F32)
        ub_send[...] = total.astype(BF16)
        start(xb, nx)
        finish(lv, QUAD)
        loss_u[u] = added(loss_v)
        start(lu, n_u)
        yield
        total = ua_send[:, y].astype(F32)
        for j in range(1, ny):
            ya(j).wait()
            total += ua_recv[j - 1].astype(F32)
        tv_send[:, :, left] = total.astype(BF16)
        total = ub_send[:, x].astype(F32)
        for j in range(1, nx):
            xb(j).wait()
            total += ub_recv[j - 1].astype(F32)
        tv_send[:, :, right] = total.astype(BF16)
        start(tv, QUAD)
        finish(lu, n_u)
        loss_pair[core] = added(loss_u)
        lp().start()
        yield
        total = tv_send[0].astype(F32)
        for j in range(1, QUAD):
            tv(j).wait_send()
            tv_arrived(j)
            total += tv_recv[j - 1].astype(F32)
        fin[ds((x * ny + y) * by, by), :] = (total * grad_scale).astype(BF16)
        for i, j in plane_steps:
            fin_copy(i, j).start()
        lp().wait_send()
        lp(True).wait_recv()
        loss_out[0, 0] = jnp.sum(loss_pair[0] + loss_pair[1]) * loss_scale
        yield
        for i, j in plane_steps:
            fin_copy(i, j).wait_send()
            fin_copy(i, j, True).wait_recv()
        tg_out[...] = fin[...]

    def add_chunk(off):
        c = wrap(z + off)
        for h, acc in ((0, acc_own), (1, acc_sib)):
            acc[c % QUAD] += lax.dot_general(
                pgf[c], pw[h, :, ds(c // QUAD * width, width)], NT, preferred_element_type=F32
            )

    hg_copy = copy_to(hg_send, hg_recv, pair_ss.at[7], pair_rs.at[7], task=sib)

    def stream(st):
        span = rows_of(st)
        n = len(CHAIN)
        last = st == STREAMS - 1
        d = long_way(st)
        for k in range(n):
            rs_chain(st, k)
            yield
            rs_leaves(st, k)
            yield
            if last:
                if k == 0:
                    pw_copy(2).wait_recv()
                fill(k + 1)
            yield
        zbuf[u, span, :] = rs_total(st).astype(BF16)
        a1_copy(d, st, 0).start()
        yield
        a1_copy(1 - d, st, 0).start()
        yield
        rs_sent(st)
        yield
        a1_copy(d, st, 0, True).wait_recv()
        a1_copy(d, st, 1).start()
        yield
        yield
        yield
        a1_copy(1 - d, st, 0, True).wait_recv()
        a1_copy(d, st, 1, True).wait_recv()
        yield
        if st == 0:
            gathered()
            head()
        q_send(d, st, 0, 2)
        yield
        q_send(1 - d, st, 1, 1)
        yield
        q_send(d, st, 1, 1)
        yield
        yield
        a1_sent(st)
        yield
        pgf[z, span, :] = q_total(st).astype(BF16)
        for k in range(n + 1):
            a2_chain(st, k)
            yield
            a2_leaves(st, k)
            yield
            offs = [0] if k == 0 else [CHAIN[k - 1], -CHAIN[k - 1]]
            for off in between if k > 0 else []:
                if before(off) == ([0] + list(CHAIN))[k - 1]:
                    for side in sides(st):
                        a2_arrived(side, st, off)
                    offs += [off, -off]
            if last:
                for off in offs:
                    if off > -far:
                        add_chunk(off)
            if k == 1:
                q_sent(st)
            if k == n - 1:
                a2_sent(st, 1, CHAIN[n - 2])
            yield

    loads[0].wait()
    loads[1].wait()
    hid_rows[0] = hid[0].T
    hid_copy.wait_recv()
    hid_rows[1] = hid[1].T
    for m in (0, 1, -1):
        pw_copy(m).wait_recv()
    fill(0)
    head_slot = len(CHAIN) + 2
    last_slot = 2 * len(CHAIN) + 4
    running = [stream(st) for st in range(STREAMS)]
    beside = gather()
    for slot in range(last_slot + 1):
        for _ in range(3):
            for steps in running:
                next(steps)
        if slot == 0:
            prepare()
        if slot == head_slot:
            beside = plane()
        if slot < last_slot and beside is not None and next(beside, True):
            beside = None
    for steps in running:
        for _ in steps:
            pass
    hg_send[...] = acc_sib[...].astype(BF16)
    hg_copy.start()
    for st in range(STREAMS):
        a2_sent(st, CHAIN[-2] + 1, far)
    if beside is not None:
        for _ in beside:
            pass
    hg_copy.wait()
    for i in range(QUAD):
        hg_out[pl.ds(i * rq, rq), :] = (acc_own[i] + hg_recv[i].astype(F32)).astype(BF16)


def shards(
    hidden, piece_weight, task_embed, task_bias, event_bin, censored, patient_id, patient_rows
):
    patients = patient_rows.shape[0]
    rows, depth = hidden.shape
    tasks, width = task_embed.shape
    pieces = task_bias.shape[1]
    n_task = lax.axis_size("task")
    nx, ny = lax.axis_size("row"), lax.axis_size("section")
    nz = n_task // 2
    far = nz // 2
    half = pieces * width // 2
    rq = rows // QUAD
    rb = rq // STREAMS
    by = tasks // (nx * ny)
    hw = width // 2
    vmem = pl.BlockSpec(memory_space=pltpu.VMEM)
    in_hbm = pl.BlockSpec(memory_space=pltpu.HBM)
    dma = pltpu.SemaphoreType.DMA

    def pair(*shape):
        return [dma(shape), dma(shape)]

    def arrays(*shapes):
        return [pltpu.VMEM(shape, dtype) for shape, dtype in shapes]

    hg, tg, loss = pl.pallas_call(
        functools.partial(kernel, 1.0 / (patients * tasks * n_task), 1.0 / patients),
        out_shape=(
            jax.ShapeDtypeStruct((rows, depth), BF16),
            jax.ShapeDtypeStruct((tasks, width), BF16),
            jax.ShapeDtypeStruct((1, 1), F32),
        ),
        in_specs=[in_hbm] * 8,
        out_specs=(vmem, vmem, pl.BlockSpec(memory_space=pltpu.SMEM)),
        scratch_shapes=arrays(
            ((1, rows), jnp.int32),
            ((1, patients), jnp.int32),
            ((2, depth, rows), BF16),
            ((2, rows, depth), BF16),
            ((2, depth, half), BF16),
            ((2 * QUAD, nx, ny, by, width), BF16),
            ((2 * QUAD, pieces, tasks), F32),
            ((rows, tasks), jnp.int32),
            ((rows, tasks), jnp.int32),
            ((2, rows, tasks), BF16),
            ((2 * QUAD, 2, rq, tasks), BF16),
            ((rows, tasks), F32),
            ((nz, rq, width), F32),
            ((2, far, rq, width), BF16),
            ((2, far, rq, width), BF16),
            ((pieces // 2, rq, width), BF16),
            ((pieces // 2, rq, width), F32),
            ((2, 2, rq, width), BF16),
            ((2, 2, rq, width), BF16),
            ((nz, rq, width), BF16),
            ((2 * QUAD, pieces // 2, rq, tasks), BF16),
            ((8, tasks), F32),
            ((nx, 8, LANES), F32),
            ((ny, 8, LANES), F32),
            ((QUAD, 8, LANES), F32),
            ((nz // QUAD, 8, LANES), F32),
            ((2, 8, LANES), F32),
            ((QUAD, tasks, width), BF16),
            ((QUAD, tasks, width), BF16),
            ((QUAD, nx, ny, by, hw), BF16),
            ((QUAD, nx, ny, by, hw), BF16),
            ((nx - 1, QUAD, ny, by, hw), BF16),
            ((ny - 1, QUAD, nx, by, hw), BF16),
            ((QUAD, ny, by, hw), BF16),
            ((QUAD, nx, by, hw), BF16),
            ((ny - 1, QUAD, by, hw), BF16),
            ((nx - 1, QUAD, by, hw), BF16),
            ((QUAD, by, width), BF16),
            ((QUAD - 1, by, width), BF16),
            ((tasks, width), BF16),
            ((QUAD, rq, depth), F32),
            ((QUAD, rq, depth), F32),
            ((QUAD, rq, depth), BF16),
            ((QUAD, rq, depth), BF16),
        )
        + pair(2, STREAMS, far)
        + pair(2, STREAMS, 2)
        + pair(2, STREAMS, 2)
        + pair(2, STREAMS, far)
        + [dma((8,))]
        + pair(8)
        + pair(nz // QUAD)
        + pair(QUAD - 1) * 3
        + pair(2, ny - 1)
        + pair(2, nx - 1)
        + pair(nx - 1)
        + pair(ny - 1)
        + pair(QUAD - 1)
        + pair(nz // QUAD - 1)
        + pair(nx - 1) * 2
        + pair(ny - 1) * 2
        + pair(QUAD - 1)
        + pair(QUAD)
        + pair(nx, ny),
        compiler_params=pltpu.CompilerParams(
            collective_id=0, has_side_effects=True, vmem_limit_bytes=63 * 1024 * 1024
        ),
        cost_estimate=pl.CostEstimate(
            flops=2400000000, bytes_accessed=4000000, transcendentals=600000
        ),
    )(
        hidden.T,
        piece_weight,
        task_embed.reshape(nx, ny, by, width),
        task_bias.T,
        event_bin,
        censored,
        patient_id.reshape(1, rows),
        patient_rows.reshape(1, patients),
    )
    return hg, tg.astype(F32), loss.reshape(())


def solution(mesh):
    return jax.shard_map(
        shards,
        mesh=mesh,
        in_specs=(
            P(("section", "row"), "task"),
            P("task", None),
            P("task", None),
            P("task", None),
            P(("section", "row"), "task"),
            P(("section", "row"), "task"),
            P(("section", "row")),
            P(),
        ),
        out_specs=(P(("section", "row"), "task"), P("task", None), P()),
        check_vma=False,
    )
```

```python
import functools

import jax
import jax.numpy as jnp
from jax import lax
from jax.experimental import pallas as pl
from jax.experimental.pallas import tpu as pltpu
from jax.sharding import PartitionSpec as P

MESH = pl.DeviceIdType.MESH
F32 = jnp.float32
BF16 = jnp.bfloat16
LANES = 128
STREAMS = 2
CHAIN = (2, 4, 6, 8)
NT = (((1,), (1,)), ((), ()))
TN = (((0,), (0,)), ((), ()))


def kernel(
    loss_scale,
    grad_scale,
    hid_hbm,
    pw_hbm,
    te_hbm,
    bias_hbm,
    bins_hbm,
    cens_hbm,
    pid_hbm,
    prow_hbm,
    hg_out,
    tg_out,
    loss_out,
    pid_ref,
    prow_ref,
    hid,
    hid_rows,
    pw,
    te,
    bias,
    bins,
    cens,
    wrow,
    part,
    rs_out,
    rs_in,
    zbuf,
    pgf,
    gbuf,
    loss_acc,
    loss_x,
    loss_y,
    loss_pair,
    tg_acc,
    tg_send,
    tg_recv,
    tx_send,
    tx_recv,
    ty_send,
    ty_recv,
    tg_fin,
    acc_own,
    acc_sib,
    hg_send,
    hg_recv,
    send_sem,
    recv_sem,
    local_sem,
    pair_send,
    pair_recv,
    pw_send,
    pw_recv,
    px_send,
    px_recv,
    py_send,
    py_recv,
):
    rows = hid.shape[2]
    half_cols = pw.shape[2]
    tasks = te.shape[1]
    nz = part.shape[0]
    far = nz // 2
    pieces = half_cols // te.shape[2]
    per_piece = nz // pieces
    rb = rows // STREAMS
    nx = lax.axis_size("row")
    ny = lax.axis_size("section")
    task = lax.axis_index("task")
    x = lax.axis_index("row")
    y = lax.axis_index("section")
    z = task // 2
    core = task % 2
    sib = z * 2 + 1 - core

    def wrap(v):
        return (v + 2 * nz) % nz

    def z_dev(off):
        return wrap(z + off) * 2 + core

    def copy_to(src, dst, ss, rs, **where):
        return pltpu.make_async_remote_copy(
            src_ref=src,
            dst_ref=dst,
            send_sem=ss,
            recv_sem=rs,
            device_id=where,
            device_id_type=MESH,
        )

    mine = pl.ds(pl.multiple_of(core * half_cols, half_cols), half_cols)
    loads = [
        (hid_hbm, hid.at[0]),
        (pw_hbm.at[:, mine], pw.at[0]),
        (te_hbm, te.at[0]),
        (bias_hbm, bias.at[0]),
        (bins_hbm, bins.at[0]),
        (cens_hbm, cens.at[0]),
        (pid_hbm, pid_ref),
        (prow_hbm, prow_ref),
    ]
    loads = [pltpu.make_async_copy(a, b, local_sem.at[i]) for i, (a, b) in enumerate(loads)]
    for load in loads:
        load.start()

    barrier = pltpu.get_barrier_semaphore()
    strides = sorted({b - a for a, b in zip((0,) + CHAIN, CHAIN)} | {1})
    peers = [dict(task=sib)] + [dict(task=z_dev(s * n)) for n in strides for s in (1, -1)]
    peers += [dict(row=(x + j) % nx) for j in range(1, nx)]
    peers += [dict(section=(y + j) % ny) for j in range(1, ny)]
    for peer in peers:
        pl.semaphore_signal(barrier, inc=1, device_id=peer, device_id_type=MESH)
    pl.semaphore_wait(barrier, len(peers))

    pair = [
        (hid_hbm, hid.at[1]),
        (te_hbm, te.at[1]),
        (bias_hbm, bias.at[1]),
        (bins_hbm, bins.at[1]),
        (cens_hbm, cens.at[1]),
    ]
    pair = [
        copy_to(a, b, pair_send.at[i], pair_recv.at[i], task=sib) for i, (a, b) in enumerate(pair)
    ]

    part_cols = half_cols // far

    def pw_copy(n):
        q = (wrap(z + far) // 2 + n + far) % far
        there = pl.ds(
            pl.multiple_of((1 - core) * half_cols + q * part_cols, part_cols), part_cols
        )
        here = pl.ds(pl.multiple_of(q * part_cols, part_cols), part_cols)
        return copy_to(
            pw_hbm.at[:, there], pw.at[1, :, here], pw_send.at[q], pw_recv.at[q], task=sib
        )

    pw_order = [0] + [s * n for n in range(1, far // 2) for s in (1, -1)] + [far // 2]
    pair[0].start()
    for n in pw_order:
        pw_copy(n).start()
    for copy in pair[1:]:
        copy.start()

    def long_way(st):
        return 0 if st < STREAMS // 2 else 1

    def stops(d, st):
        return [c for c in CHAIN if c < far or d == long_way(st)]

    def before(off):
        return max([0] + [c for c in CHAIN if c < off])

    def behind(stop, d, st):
        last = far if d == long_way(st) else far - 1
        found = [off for off in range(1, last + 1) if before(off) == stop]
        return sorted(found, key=lambda off: off not in CHAIN)

    def sides(st):
        return (long_way(st), 1 - long_way(st))

    def rs_copy(ph, d, st, off):
        span = pl.ds(st * rb, rb)
        return copy_to(
            rs_out.at[ph, d, off - 1, span, :],
            rs_in.at[ph, d, off - 1, span, :],
            send_sem.at[2 * ph, d, st, off - 1],
            recv_sem.at[2 * ph, d, st, off - 1],
            task=z_dev((1 - 2 * d) * (off - before(off))),
        )

    def cols(c):
        return pl.ds(pl.multiple_of(c * LANES, LANES), LANES)

    def fill(k):
        stop = ([0] + list(CHAIN))[-1 - k]
        for off in [stop] + list(range(before(stop) + 1, stop)):
            chunks = [wrap(z + off)] if off in (0, far) else [wrap(z - off), wrap(z + off)]
            total = None
            for h in range(2):
                w = jnp.concatenate([pw[h, :, cols(c)] for c in chunks], axis=1)
                dots = jnp.dot(hid_rows[h], w, preferred_element_type=F32)
                total = dots if total is None else total + dots
            for i, c in enumerate(chunks):
                part[c] = total[:, i * LANES : (i + 1) * LANES]

    def rs_send(ph, d, st, off):
        span = pl.ds(st * rb, rb)
        total = part[wrap(z + (1 - 2 * d) * off), span, :]
        if off in stops(d, st):
            for other in behind(off, d, st):
                rs_copy(ph, d, st, other).wait_recv()
                total += rs_in[ph, d, other - 1, span, :].astype(F32)
        rs_out[ph, d, off - 1, span, :] = total.astype(BF16)
        rs_copy(ph, d, st, off).start()

    def rs_total(ph, st):
        span = pl.ds(st * rb, rb)
        total = part[z, span, :]
        for d in sides(st):
            for other in behind(0, d, st):
                rs_copy(ph, d, st, other).wait_recv()
                total += rs_in[ph, d, other - 1, span, :].astype(F32)
        return total

    def rs_chain(ph, st, k):
        stop = ([0] + list(CHAIN))[-1 - k]
        for d in sides(st):
            if k == 0:
                rs_send(ph, d, st, far if d == long_way(st) else far - 1)
            elif stop != far - 1 or d == long_way(st):
                rs_send(ph, d, st, stop)
        if k == 0:
            rs_leaves(ph, st, 0)

    def rs_leaves(ph, st, k):
        stop = ([0] + list(CHAIN))[-1 - k]
        for off in range(stop - 1, before(stop), -1):
            for d in sides(st):
                if off != far - 1 or d == long_way(st):
                    rs_send(ph, d, st, off)

    def rs_sent(ph, st):
        for d in range(2):
            for off in range(1, far + 1 if d == long_way(st) else far):
                rs_copy(ph, d, st, off).wait_send()

    def ag_copy(ph, d, st, off):
        buf = zbuf if ph == 0 else pgf
        extra = 16 if ph == 1 and st == STREAMS - 1 else 0
        sgn = 1 - 2 * d
        ref = buf.at[wrap(z - sgn * before(off)), pl.ds(st * rb, rb + extra), :]
        return copy_to(
            ref,
            ref,
            send_sem.at[2 * ph + 1, d, st, off - 1],
            recv_sem.at[2 * ph + 1, d, st, off - 1],
            task=z_dev(sgn * (off - before(off))),
        )

    def ag_arrived(ph, d, st, off):
        buf = zbuf if ph == 0 else pgf
        extra = 16 if ph == 1 and st == STREAMS - 1 else 0
        sgn = 1 - 2 * d
        if off < far or d == long_way(st):
            ref = buf.at[wrap(z - sgn * off), pl.ds(st * rb, rb + extra), :]
            copy_to(
                ref,
                ref,
                send_sem.at[2 * ph + 1, d, st, off - 1],
                recv_sem.at[2 * ph + 1, d, st, off - 1],
                task=z_dev(sgn * (off - before(off))),
            ).wait_recv()

    def ag_chain(ph, st, k):
        stop = ([0] + list(CHAIN))[k]
        for d in sides(st):
            if k > 0:
                ag_arrived(ph, d, st, stop)
            for off in behind(stop, d, st)[:1]:
                ag_copy(ph, d, st, off).start()

    def ag_leaves(ph, st, k):
        stop = ([0] + list(CHAIN))[k]
        for d in sides(st):
            for off in behind(stop, d, st)[1:]:
                ag_copy(ph, d, st, off).start()

    def ag_sent(ph, st, first, last):
        for d in range(2):
            for off in range(first, last + 1):
                if off < far or d == long_way(st):
                    ag_copy(ph, d, st, off).wait_send()

    between = [off for off in range(1, far) if off not in CHAIN]

    def prepare():
        loads[6].wait()
        loads[7].wait()
        ids = jnp.broadcast_to(pid_ref[...].astype(F32), (prow_ref.shape[1], rows)).T
        lane = lax.broadcasted_iota(jnp.int32, ids.shape, 1).astype(F32)
        record = jnp.where(ids == lane, prow_ref[...].astype(F32), 0.0)
        weight = 1.0 / jnp.sum(record, axis=1, keepdims=True)
        wrow[...] = jnp.broadcast_to(weight, wrow.shape)
        loss_acc[...] = jnp.zeros_like(loss_acc)
        tg_acc[...] = jnp.zeros_like(tg_acc)
        acc_own[...] = jnp.zeros_like(acc_own)
        acc_sib[...] = jnp.zeros_like(acc_sib)

    def head(st):
        span = pl.ds(pl.multiple_of(st * rb, rb), rb)
        zs = jnp.concatenate(
            [
                jnp.concatenate(
                    [zbuf[p * per_piece + k, span, :] for k in range(per_piece)], axis=1
                )
                for p in range(pieces)
            ],
            axis=0,
        )
        total = None
        for h in range(2):
            dots = lax.dot_general(zs, te[h], NT, preferred_element_type=F32)
            edge = bins[h, span, :]
            alive = (1 - cens[h, span, :]).astype(F32)
            weight = wrow[span, :]
            grads = []
            nll = None
            for p in range(pieces):
                piece = core * pieces + p
                logits = dots[p * rb : (p + 1) * rb] + bias[h, pl.ds(piece, 1), :]
                hazard = jnp.exp(logits)
                at = edge == piece
                hazard = jnp.where(edge > piece, hazard, jnp.where(at, 0.5 * hazard, 0.0))
                event = jnp.where(at, alive, 0.0)
                term = hazard - event * logits
                nll = term if nll is None else nll + term
                grad = (weight * (hazard - event)).astype(BF16)
                gbuf[h, p, span, :] = grad
                grads.append(grad)
            nll = (weight * nll).reshape(rb // 8, 8, tasks).sum(axis=0)
            loss_acc[...] += nll
            grads = jnp.concatenate(grads, axis=0)
            dots = jnp.dot(grads, te[h], preferred_element_type=F32)
            total = dots if total is None else total + dots
        for p in range(pieces):
            for k in range(per_piece):
                part[p * per_piece + k, span, :] = total[
                    p * rb : (p + 1) * rb, k * LANES : (k + 1) * LANES
                ]

    def x_copy(j, src, dst, k):
        return copy_to(
            src, dst, px_send.at[k, j - 1], px_recv.at[k, j - 1], row=(x + j) % nx
        )

    def y_copy(j, src, dst, k):
        return copy_to(
            src, dst, py_send.at[k, j - 1], py_recv.at[k, j - 1], section=(y + j) % ny
        )

    def loss_x_copy(j):
        return x_copy(j, loss_x.at[x], loss_x.at[x], 0)

    def loss_y_copy(j):
        return y_copy(j, loss_y.at[y], loss_y.at[y], 0)

    bx = tasks // nx
    by = bx // ny

    def tgx_copy(j):
        peer = (x + j) % nx
        src = tx_send.at[pl.ds(pl.multiple_of(peer * bx, bx), bx), :]
        return x_copy(j, src, tx_recv.at[j - 1], 1)

    def tgy_copy(j):
        peer = (y + j) % ny
        src = ty_send.at[pl.ds(pl.multiple_of(peer * by, by), by), :]
        return y_copy(j, src, ty_recv.at[j - 1], 1)

    def agy_copy(j):
        ref = tg_fin.at[pl.ds(pl.multiple_of(x * bx + y * by, by), by), :]
        return y_copy(j, ref, ref, 2)

    def agx_copy(j):
        ref = tg_fin.at[pl.ds(pl.multiple_of(x * bx, bx), bx), :]
        return x_copy(j, ref, ref, 2)

    tg_copy = copy_to(tg_send, tg_recv, pair_send.at[5], pair_recv.at[5], task=sib)

    def tg_piece(p):
        zp = jnp.concatenate([zbuf[p * per_piece + k] for k in range(per_piece)], axis=1)
        for h in range(2):
            tg_acc[h] += lax.dot_general(gbuf[h, p], zp, TN, preferred_element_type=F32)

    def loss_terms():
        own = sum(loss_y[i] for i in range(1, ny)) + loss_y[0]
        own = jnp.sum(jnp.sum(own, axis=0, keepdims=True), axis=1, keepdims=True)
        own = jnp.broadcast_to(own, (16, LANES))
        place = lax.broadcasted_iota(jnp.int32, own.shape, 1)
        place += LANES * lax.broadcasted_iota(jnp.int32, own.shape, 0)
        high = own.astype(BF16).astype(F32)
        rest = own - high
        middle = rest.astype(BF16).astype(F32)
        low = rest - middle
        terms = jnp.where(
            place == 0, high, jnp.where(place == 1, middle, jnp.where(place == 2, low, 0.0))
        )
        pgf[z, pl.ds(rows, 16), :] = terms.astype(BF16)

    def plane():
        loss_x[x] = loss_acc[:, :LANES] + loss_acc[:, LANES:]
        for j in range(1, nx):
            loss_x_copy(j).start()
        for p in range(pieces // 2):
            tg_piece(p)
        yield
        for p in range(pieces // 2, pieces):
            tg_piece(p)
        tg_send[...] = tg_acc[1].astype(BF16)
        tg_copy.start()
        for j in range(1, nx):
            loss_x_copy(j).wait()
        loss_y[y] = sum(loss_x[i] for i in range(1, nx)) + loss_x[0]
        for j in range(1, ny):
            loss_y_copy(j).start()
        yield
        tg_copy.wait()
        tg_acc[0] += tg_recv[...].astype(F32)
        tx_send[...] = tg_acc[0].astype(BF16)
        for j in range(1, nx):
            tgx_copy(j).start()
        for j in range(1, ny):
            loss_y_copy(j).wait()
        loss_terms()
        yield
        total = tg_acc[0, pl.ds(pl.multiple_of(x * bx, bx), bx), :]
        for j in range(1, nx):
            tgx_copy(j).wait()
            total += tx_recv[j - 1].astype(F32)
        tg_acc[0, pl.ds(0, bx), :] = total
        ty_send[...] = total.astype(BF16)
        for j in range(1, ny):
            tgy_copy(j).start()
        yield
        total = tg_acc[0, pl.ds(pl.multiple_of(y * by, by), by), :]
        for j in range(1, ny):
            tgy_copy(j).wait()
            total += ty_recv[j - 1].astype(F32)
        place = pl.ds(pl.multiple_of(x * bx + y * by, by), by)
        tg_fin[place, :] = (total * grad_scale).astype(BF16)
        for j in range(1, ny):
            agy_copy(j).start()
        yield
        for j in range(1, ny):
            agy_copy(j).wait_send()
            from_y = (y + ny - j) % ny
            ref = tg_fin.at[pl.ds(pl.multiple_of(x * bx + from_y * by, by), by), :]
            y_copy(j, ref, ref, 2).wait_recv()
        for j in range(1, nx):
            agx_copy(j).start()
        yield
        for j in range(1, nx):
            agx_copy(j).wait_send()
            from_x = (x + nx - j) % nx
            ref = tg_fin.at[pl.ds(pl.multiple_of(from_x * bx, bx), bx), :]
            x_copy(j, ref, ref, 2).wait_recv()
        tg_out[...] = tg_fin[...]

    def add_chunks(st, offs):
        span = pl.ds(st * rb, rb)
        chunks = [wrap(z + off) for off in offs]
        value = jnp.concatenate([pgf[c, span, :] for c in chunks], axis=1)
        for h, acc in ((0, acc_own), (1, acc_sib)):
            w = jnp.concatenate([pw[h, :, cols(c)] for c in chunks], axis=1)
            acc[:, span] += lax.dot_general(w, value, NT, preferred_element_type=F32)

    def hg_copy(st):
        return copy_to(
            hg_send.at[st], hg_recv.at[st], pair_send.at[6 + st], pair_recv.at[6 + st], task=sib
        )

    def pw_arrived(*order):
        for m in order:
            pw_copy(m).wait_recv()

    def stream(st):
        span = pl.ds(st * rb, rb)
        n = len(CHAIN)
        for k in range(n):
            rs_chain(0, st, k)
            yield
            if st == 0 and k == 0:
                pw_arrived(2, -2)
                fill(1)
            if k < n - 1:
                rs_leaves(0, st, k + 1)
            yield
            if st == 0 and k < n - 1:
                pw_arrived(*{0: (3, -3), 1: (4,)}.get(k, ()))
                fill(k + 2)
            yield
        zbuf[z, span, :] = rs_total(0, st).astype(BF16)
        for k in range(n):
            ag_chain(0, st, k)
            yield
            ag_leaves(0, st, k)
            yield
            if k == 1:
                rs_sent(0, st)
            if st == 0 and k == 2:
                for copy in pair:
                    copy.wait_send()
                for m in pw_order:
                    pw_copy(m).wait_send()
            yield
        ag_chain(0, st, n)
        for off in between:
            for d in sides(st):
                ag_arrived(0, d, st, off)
        if st == 0:
            for i in range(1, 5):
                loads[1 + i].wait()
                pair[i].wait_recv()
        head(st)
        for k in range(n):
            rs_chain(1, st, k)
            yield
            if k < n - 1:
                rs_leaves(1, st, k + 1)
            yield
            if k == 1:
                ag_sent(0, st, 1, far)
            yield
        pgf[z, span, :] = rs_total(1, st).astype(BF16)
        for k in range(n + 1):
            ag_chain(1, st, k)
            yield
            ag_leaves(1, st, k)
            yield
            if k == 0:
                add_chunks(st, [0])
            else:
                offs = [CHAIN[k - 1]]
                for off in between:
                    if before(off) == ([0] + list(CHAIN))[k - 1]:
                        for d in sides(st):
                            ag_arrived(1, d, st, off)
                        offs.append(off)
                add_chunks(st, [s * off for off in offs for s in (1, -1) if s * off > -far])
            if k == 1:
                rs_sent(1, st)
            if k == n - 1:
                ag_sent(1, st, 1, CHAIN[n - 2])
            if k == n:
                hg_send[st] = acc_sib[:, span].astype(BF16)
                hg_copy(st).start()
            yield

    loads[0].wait()
    loads[1].wait()
    hid_rows[0] = hid[0].T
    pair[0].wait_recv()
    hid_rows[1] = hid[1].T
    pw_arrived(0, 1, -1)
    fill(0)
    head_slot = len(CHAIN) * 2
    last_slot = len(CHAIN) * 4
    running = [stream(st) for st in range(STREAMS)]
    beside = None
    for slot in range(last_slot + 1):
        for _ in range(3):
            for steps in running:
                next(steps)
        if slot == 0:
            prepare()
        if slot == head_slot:
            beside = plane()
        if beside is not None and next(beside, True):
            beside = None
    for steps in running:
        for _ in steps:
            pass
    if beside is not None:
        for _ in beside:
            pass

    total = pgf[0, pl.ds(rows, 16), :].astype(F32)
    for c in range(1, nz):
        total += pgf[c, pl.ds(rows, 16), :].astype(F32)
    loss_pair[core] = total
    ref = loss_pair.at[core]
    last = 6 + STREAMS
    loss_copy = copy_to(ref, ref, pair_send.at[last], pair_recv.at[last], task=sib)
    loss_copy.start()
    for st in range(STREAMS):
        ag_sent(1, st, CHAIN[-2] + 1, far)
    loss_copy.wait()
    total = loss_pair[0] + loss_pair[1]
    loss_out[0, 0] = jnp.sum(total) * loss_scale
    for st in range(STREAMS):
        span = pl.ds(st * rb, rb)
        hg_copy(st).wait()
        hg_out[:, span] = (acc_own[:, span] + hg_recv[st].astype(F32)).astype(BF16)


def shards(
    hidden, piece_weight, task_embed, task_bias, event_bin, censored, patient_id, patient_rows
):
    patients = patient_rows.shape[0]
    rows, depth = hidden.shape
    tasks, width = task_embed.shape
    pieces = task_bias.shape[1]
    n_task = lax.axis_size("task")
    nx, ny = lax.axis_size("row"), lax.axis_size("section")
    nz = n_task // 2
    half = pieces * width // 2
    bx = tasks // nx
    by = bx // ny
    vmem = pl.BlockSpec(memory_space=pltpu.VMEM)
    in_hbm = pl.BlockSpec(memory_space=pltpu.HBM)
    dma = pltpu.SemaphoreType.DMA
    hg, tg, loss = pl.pallas_call(
        functools.partial(kernel, 1.0 / (patients * tasks * n_task), 1.0 / patients),
        out_shape=(
            jax.ShapeDtypeStruct((depth, rows), BF16),
            jax.ShapeDtypeStruct((tasks, width), BF16),
            jax.ShapeDtypeStruct((1, 1), F32),
        ),
        in_specs=[in_hbm] * 8,
        out_specs=(vmem, vmem, pl.BlockSpec(memory_space=pltpu.SMEM)),
        scratch_shapes=[
            pltpu.VMEM((1, rows), jnp.int32),
            pltpu.VMEM((1, patients), jnp.int32),
            pltpu.VMEM((2, depth, rows), BF16),
            pltpu.VMEM((2, rows, depth), BF16),
            pltpu.VMEM((2, depth, half), BF16),
            pltpu.VMEM((2, tasks, width), BF16),
            pltpu.VMEM((2, pieces, tasks), F32),
            pltpu.VMEM((2, rows, tasks), jnp.int32),
            pltpu.VMEM((2, rows, tasks), jnp.int32),
            pltpu.VMEM((rows, tasks), F32),
            pltpu.VMEM((nz, rows, LANES), F32),
            pltpu.VMEM((2, 2, nz // 2, rows, LANES), BF16),
            pltpu.VMEM((2, 2, nz // 2, rows, LANES), BF16),
            pltpu.VMEM((nz, rows, LANES), BF16),
            pltpu.VMEM((nz, rows + 16, LANES), BF16),
            pltpu.VMEM((2, pieces // 2, rows, tasks), BF16),
            pltpu.VMEM((8, tasks), F32),
            pltpu.VMEM((nx, 8, LANES), F32),
            pltpu.VMEM((ny, 8, LANES), F32),
            pltpu.VMEM((2, 16, LANES), F32),
            pltpu.VMEM((2, tasks, width), F32),
            pltpu.VMEM((tasks, width), BF16),
            pltpu.VMEM((tasks, width), BF16),
            pltpu.VMEM((tasks, width), BF16),
            pltpu.VMEM((nx - 1, bx, width), BF16),
            pltpu.VMEM((bx, width), BF16),
            pltpu.VMEM((ny - 1, by, width), BF16),
            pltpu.VMEM((tasks, width), BF16),
            pltpu.VMEM((depth, rows), F32),
            pltpu.VMEM((depth, rows), F32),
            pltpu.VMEM((STREAMS, depth, rows // STREAMS), BF16),
            pltpu.VMEM((STREAMS, depth, rows // STREAMS), BF16),
            dma((4, 2, STREAMS, nz // 2)),
            dma((4, 2, STREAMS, nz // 2)),
            dma((8,)),
            dma((7 + STREAMS,)),
            dma((7 + STREAMS,)),
            dma((nz // 2,)),
            dma((nz // 2,)),
            dma((3, nx - 1)),
            dma((3, nx - 1)),
            dma((3, ny - 1)),
            dma((3, ny - 1)),
        ],
        compiler_params=pltpu.CompilerParams(
            collective_id=0, has_side_effects=True, vmem_limit_bytes=63 * 1024 * 1024
        ),
        cost_estimate=pl.CostEstimate(
            flops=2400000000, bytes_accessed=4000000, transcendentals=600000
        ),
    )(
        hidden.T,
        piece_weight,
        task_embed,
        task_bias.T,
        event_bin,
        censored,
        patient_id.reshape(1, rows),
        patient_rows.reshape(1, patients),
    )
    return hg.T, tg.astype(F32), loss.reshape(())


def solution(mesh):
    return jax.shard_map(
        shards,
        mesh=mesh,
        in_specs=(
            P(("section", "row"), "task"),
            P("task", None),
            P("task", None),
            P("task", None),
            P(("section", "row"), "task"),
            P(("section", "row"), "task"),
            P(("section", "row")),
            P(),
        ),
        out_specs=(P(("section", "row"), "task"), P("task", None), P()),
        check_vma=False,
    )
```

```python
import functools

import jax
import jax.numpy as jnp
from jax import lax
from jax.experimental import pallas as pl
from jax.experimental.pallas import tpu as pltpu
from jax.sharding import PartitionSpec as P

MESH = pl.DeviceIdType.MESH
F32 = jnp.float32
BF16 = jnp.bfloat16
LANES = 128
STREAMS = 2
CHAIN = (2, 4, 6, 8)
NT = (((1,), (1,)), ((), ()))
TN = (((0,), (0,)), ((), ()))


def kernel(
    loss_scale,
    grad_scale,
    hid_hbm,
    pw_hbm,
    te_hbm,
    bias_hbm,
    bins_hbm,
    cens_hbm,
    pid_hbm,
    prow_hbm,
    hg_out,
    tg_out,
    loss_out,
    pid_ref,
    prow_ref,
    hid,
    hid_rows,
    pw,
    te,
    bias,
    bins,
    cens,
    wrow,
    part,
    rs_out,
    rs_in,
    zbuf,
    pgf,
    gbuf,
    loss_acc,
    loss_x,
    loss_y,
    loss_pair,
    tg_acc,
    tg_send,
    tg_recv,
    tx_send,
    tx_recv,
    ty_send,
    ty_recv,
    tg_fin,
    acc_own,
    acc_sib,
    hg_send,
    hg_recv,
    send_sem,
    recv_sem,
    local_sem,
    pair_send,
    pair_recv,
    pw_send,
    pw_recv,
    px_send,
    px_recv,
    py_send,
    py_recv,
):
    rows = hid.shape[2]
    half_cols = pw.shape[2]
    tasks = te.shape[1]
    nz = part.shape[0]
    far = nz // 2
    pieces = half_cols // te.shape[2]
    per_piece = nz // pieces
    rb = rows // STREAMS
    nx = lax.axis_size("row")
    ny = lax.axis_size("section")
    task = lax.axis_index("task")
    x = lax.axis_index("row")
    y = lax.axis_index("section")
    z = task // 2
    core = task % 2
    sib = z * 2 + 1 - core

    def wrap(v):
        return (v + 2 * nz) % nz

    def z_dev(off):
        return wrap(z + off) * 2 + core

    def copy_to(src, dst, ss, rs, **where):
        return pltpu.make_async_remote_copy(
            src_ref=src,
            dst_ref=dst,
            send_sem=ss,
            recv_sem=rs,
            device_id=where,
            device_id_type=MESH,
        )

    mine = pl.ds(pl.multiple_of(core * half_cols, half_cols), half_cols)
    loads = [
        (hid_hbm, hid.at[0]),
        (pw_hbm.at[:, mine], pw.at[0]),
        (te_hbm, te.at[0]),
        (bias_hbm, bias.at[0]),
        (bins_hbm, bins.at[0]),
        (cens_hbm, cens.at[0]),
        (pid_hbm, pid_ref),
        (prow_hbm, prow_ref),
    ]
    loads = [pltpu.make_async_copy(a, b, local_sem.at[i]) for i, (a, b) in enumerate(loads)]
    for load in loads:
        load.start()

    barrier = pltpu.get_barrier_semaphore()
    strides = sorted({b - a for a, b in zip((0,) + CHAIN, CHAIN)} | {1})
    peers = [dict(task=sib)] + [dict(task=z_dev(s * n)) for n in strides for s in (1, -1)]
    peers += [dict(row=(x + j) % nx) for j in range(1, nx)]
    peers += [dict(section=(y + j) % ny) for j in range(1, ny)]
    for peer in peers:
        pl.semaphore_signal(barrier, inc=1, device_id=peer, device_id_type=MESH)
    pl.semaphore_wait(barrier, len(peers))

    pair = [
        (hid_hbm, hid.at[1]),
        (te_hbm, te.at[1]),
        (bias_hbm, bias.at[1]),
        (bins_hbm, bins.at[1]),
        (cens_hbm, cens.at[1]),
    ]
    pair = [
        copy_to(a, b, pair_send.at[i], pair_recv.at[i], task=sib) for i, (a, b) in enumerate(pair)
    ]

    part_cols = half_cols // far

    def pw_copy(n):
        q = (wrap(z + far) // 2 + n + far) % far
        there = pl.ds(
            pl.multiple_of((1 - core) * half_cols + q * part_cols, part_cols), part_cols
        )
        here = pl.ds(pl.multiple_of(q * part_cols, part_cols), part_cols)
        return copy_to(
            pw_hbm.at[:, there], pw.at[1, :, here], pw_send.at[q], pw_recv.at[q], task=sib
        )

    pw_order = [0] + [s * n for n in range(1, far // 2) for s in (1, -1)] + [far // 2]
    pair[0].start()
    for n in pw_order:
        pw_copy(n).start()
    for copy in pair[1:]:
        copy.start()

    def long_way(st):
        return 0 if st < STREAMS // 2 else 1

    def stops(d, st):
        return [c for c in CHAIN if c < far or d == long_way(st)]

    def before(off):
        return max([0] + [c for c in CHAIN if c < off])

    def behind(stop, d, st):
        last = far if d == long_way(st) else far - 1
        found = [off for off in range(1, last + 1) if before(off) == stop]
        return sorted(found, key=lambda off: off not in CHAIN)

    def sides(st):
        return (long_way(st), 1 - long_way(st))

    def rs_copy(ph, d, st, off):
        span = pl.ds(st * rb, rb)
        return copy_to(
            rs_out.at[ph, d, off - 1, span, :],
            rs_in.at[ph, d, off - 1, span, :],
            send_sem.at[2 * ph, d, st, off - 1],
            recv_sem.at[2 * ph, d, st, off - 1],
            task=z_dev((1 - 2 * d) * (off - before(off))),
        )

    def cols(c):
        return pl.ds(pl.multiple_of(c * LANES, LANES), LANES)

    def fill(k):
        stop = ([0] + list(CHAIN))[-1 - k]
        for off in [stop] + list(range(before(stop) + 1, stop)):
            chunks = [wrap(z + off)] if off in (0, far) else [wrap(z - off), wrap(z + off)]
            total = None
            for h in range(2):
                w = jnp.concatenate([pw[h, :, cols(c)] for c in chunks], axis=1)
                dots = jnp.dot(hid_rows[h], w, preferred_element_type=F32)
                total = dots if total is None else total + dots
            for i, c in enumerate(chunks):
                part[c] = total[:, i * LANES : (i + 1) * LANES]

    def rs_send(ph, d, st, off):
        span = pl.ds(st * rb, rb)
        total = part[wrap(z + (1 - 2 * d) * off), span, :]
        if off in stops(d, st):
            for other in behind(off, d, st):
                rs_copy(ph, d, st, other).wait_recv()
                total += rs_in[ph, d, other - 1, span, :].astype(F32)
        rs_out[ph, d, off - 1, span, :] = total.astype(BF16)
        rs_copy(ph, d, st, off).start()

    def rs_total(ph, st):
        span = pl.ds(st * rb, rb)
        total = part[z, span, :]
        for d in sides(st):
            for other in behind(0, d, st):
                rs_copy(ph, d, st, other).wait_recv()
                total += rs_in[ph, d, other - 1, span, :].astype(F32)
        return total

    def rs_chain(ph, st, k):
        stop = ([0] + list(CHAIN))[-1 - k]
        for d in sides(st):
            if k == 0:
                rs_send(ph, d, st, far if d == long_way(st) else far - 1)
            elif stop != far - 1 or d == long_way(st):
                rs_send(ph, d, st, stop)
        if k == 0:
            rs_leaves(ph, st, 0)

    def rs_leaves(ph, st, k):
        stop = ([0] + list(CHAIN))[-1 - k]
        for off in range(stop - 1, before(stop), -1):
            for d in sides(st):
                if off != far - 1 or d == long_way(st):
                    rs_send(ph, d, st, off)

    def rs_sent(ph, st):
        for d in range(2):
            for off in range(1, far + 1 if d == long_way(st) else far):
                rs_copy(ph, d, st, off).wait_send()

    def ag_copy(ph, d, st, off):
        buf = zbuf if ph == 0 else pgf
        extra = 16 if ph == 1 and st == STREAMS - 1 else 0
        sgn = 1 - 2 * d
        ref = buf.at[wrap(z - sgn * before(off)), pl.ds(st * rb, rb + extra), :]
        return copy_to(
            ref,
            ref,
            send_sem.at[2 * ph + 1, d, st, off - 1],
            recv_sem.at[2 * ph + 1, d, st, off - 1],
            task=z_dev(sgn * (off - before(off))),
        )

    def ag_arrived(ph, d, st, off):
        buf = zbuf if ph == 0 else pgf
        extra = 16 if ph == 1 and st == STREAMS - 1 else 0
        sgn = 1 - 2 * d
        if off < far or d == long_way(st):
            ref = buf.at[wrap(z - sgn * off), pl.ds(st * rb, rb + extra), :]
            copy_to(
                ref,
                ref,
                send_sem.at[2 * ph + 1, d, st, off - 1],
                recv_sem.at[2 * ph + 1, d, st, off - 1],
                task=z_dev(sgn * (off - before(off))),
            ).wait_recv()

    def ag_chain(ph, st, k):
        stop = ([0] + list(CHAIN))[k]
        for d in sides(st):
            if k > 0:
                ag_arrived(ph, d, st, stop)
            for off in behind(stop, d, st)[:1]:
                ag_copy(ph, d, st, off).start()

    def ag_leaves(ph, st, k):
        stop = ([0] + list(CHAIN))[k]
        for d in sides(st):
            for off in behind(stop, d, st)[1:]:
                ag_copy(ph, d, st, off).start()

    def ag_sent(ph, st, first, last):
        for d in range(2):
            for off in range(first, last + 1):
                if off < far or d == long_way(st):
                    ag_copy(ph, d, st, off).wait_send()

    between = [off for off in range(1, far) if off not in CHAIN]

    def prepare():
        loads[6].wait()
        loads[7].wait()
        ids = jnp.broadcast_to(pid_ref[...].astype(F32), (prow_ref.shape[1], rows)).T
        lane = lax.broadcasted_iota(jnp.int32, ids.shape, 1).astype(F32)
        record = jnp.where(ids == lane, prow_ref[...].astype(F32), 0.0)
        weight = 1.0 / jnp.sum(record, axis=1, keepdims=True)
        wrow[...] = jnp.broadcast_to(weight, wrow.shape)
        loss_acc[...] = jnp.zeros_like(loss_acc)
        tg_acc[...] = jnp.zeros_like(tg_acc)
        acc_own[...] = jnp.zeros_like(acc_own)
        acc_sib[...] = jnp.zeros_like(acc_sib)

    late = (wrap(z + far + 1) // per_piece) % pieces

    def head(st, first, last):
        span = pl.ds(st * rb, rb)
        order = [(late + 1 + i) % pieces for i in range(first, last)]
        zs = jnp.concatenate(
            [
                jnp.concatenate(
                    [zbuf[p * per_piece + k, span, :] for k in range(per_piece)], axis=1
                )
                for p in order
            ],
            axis=0,
        )
        total = None
        for h in range(2):
            dots = lax.dot_general(zs, te[h], NT, preferred_element_type=F32)
            edge = bins[h, span, :]
            alive = (1 - cens[h, span, :]).astype(F32)
            weight = wrow[span, :]
            grads = []
            nll = None
            for i, p in enumerate(order):
                piece = core * pieces + p
                logits = dots[i * rb : (i + 1) * rb] + bias[h, pl.ds(piece, 1), :]
                hazard = jnp.exp(logits)
                at = edge == piece
                hazard = jnp.where(edge > piece, hazard, jnp.where(at, 0.5 * hazard, 0.0))
                event = jnp.where(at, alive, 0.0)
                term = hazard - event * logits
                nll = term if nll is None else nll + term
                grad = (weight * (hazard - event)).astype(BF16)
                gbuf[h, p, span, :] = grad
                grads.append(grad)
            nll = (weight * nll).reshape(rb // 8, 8, tasks).sum(axis=0)
            loss_acc[...] += nll
            grads = jnp.concatenate(grads, axis=0)
            dots = jnp.dot(grads, te[h], preferred_element_type=F32)
            total = dots if total is None else total + dots
        for i, p in enumerate(order):
            for k in range(per_piece):
                part[p * per_piece + k, span, :] = total[
                    i * rb : (i + 1) * rb, k * LANES : (k + 1) * LANES
                ]

    def x_copy(j, src, dst, k):
        return copy_to(
            src, dst, px_send.at[k, j - 1], px_recv.at[k, j - 1], row=(x + j) % nx
        )

    def y_copy(j, src, dst, k):
        return copy_to(
            src, dst, py_send.at[k, j - 1], py_recv.at[k, j - 1], section=(y + j) % ny
        )

    def loss_x_copy(j):
        return x_copy(j, loss_x.at[x], loss_x.at[x], 0)

    def loss_y_copy(j):
        return y_copy(j, loss_y.at[y], loss_y.at[y], 0)

    bx = tasks // nx
    by = bx // ny

    def tgx_copy(j):
        peer = (x + j) % nx
        src = tx_send.at[pl.ds(pl.multiple_of(peer * bx, bx), bx), :]
        return x_copy(j, src, tx_recv.at[j - 1], 1)

    def tgy_copy(j):
        peer = (y + j) % ny
        src = ty_send.at[pl.ds(pl.multiple_of(peer * by, by), by), :]
        return y_copy(j, src, ty_recv.at[j - 1], 1)

    def agy_copy(j):
        ref = tg_fin.at[pl.ds(pl.multiple_of(x * bx + y * by, by), by), :]
        return y_copy(j, ref, ref, 2)

    def agx_copy(j):
        ref = tg_fin.at[pl.ds(pl.multiple_of(x * bx, bx), bx), :]
        return x_copy(j, ref, ref, 2)

    tg_copy = copy_to(tg_send, tg_recv, pair_send.at[5], pair_recv.at[5], task=sib)

    def tg_piece(p):
        zp = jnp.concatenate([zbuf[p * per_piece + k] for k in range(per_piece)], axis=1)
        for h in range(2):
            tg_acc[h] += lax.dot_general(gbuf[h, p], zp, TN, preferred_element_type=F32)

    def loss_terms():
        own = sum(loss_y[i] for i in range(1, ny)) + loss_y[0]
        own = jnp.sum(jnp.sum(own, axis=0, keepdims=True), axis=1, keepdims=True)
        own = jnp.broadcast_to(own, (16, LANES))
        place = lax.broadcasted_iota(jnp.int32, own.shape, 1)
        place += LANES * lax.broadcasted_iota(jnp.int32, own.shape, 0)
        high = own.astype(BF16).astype(F32)
        rest = own - high
        middle = rest.astype(BF16).astype(F32)
        low = rest - middle
        terms = jnp.where(
            place == 0, high, jnp.where(place == 1, middle, jnp.where(place == 2, low, 0.0))
        )
        pgf[z, pl.ds(rows, 16), :] = terms.astype(BF16)

    def plane():
        loss_x[x] = loss_acc[:, :LANES] + loss_acc[:, LANES:]
        for j in range(1, nx):
            loss_x_copy(j).start()
        for p in range(pieces // 2):
            tg_piece(p)
        yield
        for p in range(pieces // 2, pieces):
            tg_piece(p)
        tg_send[...] = tg_acc[1].astype(BF16)
        tg_copy.start()
        for j in range(1, nx):
            loss_x_copy(j).wait()
        loss_y[y] = sum(loss_x[i] for i in range(1, nx)) + loss_x[0]
        for j in range(1, ny):
            loss_y_copy(j).start()
        yield
        tg_copy.wait()
        tg_acc[0] += tg_recv[...].astype(F32)
        tx_send[...] = tg_acc[0].astype(BF16)
        for j in range(1, nx):
            tgx_copy(j).start()
        for j in range(1, ny):
            loss_y_copy(j).wait()
        loss_terms()
        yield
        total = tg_acc[0, pl.ds(pl.multiple_of(x * bx, bx), bx), :]
        for j in range(1, nx):
            tgx_copy(j).wait()
            total += tx_recv[j - 1].astype(F32)
        tg_acc[0, pl.ds(0, bx), :] = total
        ty_send[...] = total.astype(BF16)
        for j in range(1, ny):
            tgy_copy(j).start()
        yield
        total = tg_acc[0, pl.ds(pl.multiple_of(y * by, by), by), :]
        for j in range(1, ny):
            tgy_copy(j).wait()
            total += ty_recv[j - 1].astype(F32)
        place = pl.ds(pl.multiple_of(x * bx + y * by, by), by)
        tg_fin[place, :] = (total * grad_scale).astype(BF16)
        for j in range(1, ny):
            agy_copy(j).start()
        yield
        for j in range(1, ny):
            agy_copy(j).wait_send()
            from_y = (y + ny - j) % ny
            ref = tg_fin.at[pl.ds(pl.multiple_of(x * bx + from_y * by, by), by), :]
            y_copy(j, ref, ref, 2).wait_recv()
        for j in range(1, nx):
            agx_copy(j).start()
        yield
        for j in range(1, nx):
            agx_copy(j).wait_send()
            from_x = (x + nx - j) % nx
            ref = tg_fin.at[pl.ds(pl.multiple_of(from_x * bx, bx), bx), :]
            x_copy(j, ref, ref, 2).wait_recv()
        tg_out[...] = tg_fin[...]

    def add_chunks(st, offs):
        span = pl.ds(st * rb, rb)
        chunks = [wrap(z + off) for off in offs]
        value = jnp.concatenate([pgf[c, span, :] for c in chunks], axis=1)
        for h, acc in ((0, acc_own), (1, acc_sib)):
            w = jnp.concatenate([pw[h, :, cols(c)] for c in chunks], axis=1)
            acc[:, span] += lax.dot_general(w, value, NT, preferred_element_type=F32)

    def hg_copy(st):
        return copy_to(
            hg_send.at[st], hg_recv.at[st], pair_send.at[6 + st], pair_recv.at[6 + st], task=sib
        )

    def pw_arrived(*order):
        for m in order:
            pw_copy(m).wait_recv()

    def stream(st):
        span = pl.ds(st * rb, rb)
        n = len(CHAIN)
        for k in range(n):
            rs_chain(0, st, k)
            yield
            if st == 0 and k == 0:
                pw_arrived(2, -2)
                fill(1)
            if k < n - 1:
                rs_leaves(0, st, k + 1)
            yield
            if st == 0 and k < n - 1:
                pw_arrived(*{0: (3, -3), 1: (4,)}.get(k, ()))
                fill(k + 2)
            yield
        zbuf[z, span, :] = rs_total(0, st).astype(BF16)
        for k in range(n):
            ag_chain(0, st, k)
            yield
            ag_leaves(0, st, k)
            yield
            if k == 1:
                rs_sent(0, st)
            if st == 0 and k == 2:
                for copy in pair:
                    copy.wait_send()
                for m in pw_order:
                    pw_copy(m).wait_send()
            if k == n - 1:
                if st == 0:
                    for i in range(1, 5):
                        loads[1 + i].wait()
                        pair[i].wait_recv()
                for off in between[:-1]:
                    for d in sides(st):
                        ag_arrived(0, d, st, off)
                head(st, 0, pieces // 2)
            yield
        ag_chain(0, st, n)
        for d in sides(st):
            ag_arrived(0, d, st, far - 1)
        head(st, pieces // 2, pieces)
        for k in range(n):
            rs_chain(1, st, k)
            yield
            if k < n - 1:
                rs_leaves(1, st, k + 1)
            yield
            if k == 1:
                ag_sent(0, st, 1, far)
            yield
        pgf[z, span, :] = rs_total(1, st).astype(BF16)
        for k in range(n + 1):
            ag_chain(1, st, k)
            yield
            ag_leaves(1, st, k)
            yield
            if k == 0:
                add_chunks(st, [0])
            else:
                offs = [CHAIN[k - 1]]
                for off in between:
                    if before(off) == ([0] + list(CHAIN))[k - 1]:
                        for d in sides(st):
                            ag_arrived(1, d, st, off)
                        offs.append(off)
                add_chunks(st, [s * off for off in offs for s in (1, -1) if s * off > -far])
            if k == 1:
                rs_sent(1, st)
            if k == n - 1:
                ag_sent(1, st, 1, CHAIN[n - 2])
            if k == n:
                hg_send[st] = acc_sib[:, span].astype(BF16)
                hg_copy(st).start()
            yield

    loads[0].wait()
    loads[1].wait()
    hid_rows[0] = hid[0].T
    pair[0].wait_recv()
    hid_rows[1] = hid[1].T
    pw_arrived(0, 1, -1)
    fill(0)
    head_slot = len(CHAIN) * 2
    last_slot = len(CHAIN) * 4
    running = [stream(st) for st in range(STREAMS)]
    beside = None
    for slot in range(last_slot + 1):
        for _ in range(3):
            for steps in running:
                next(steps)
        if slot == 0:
            prepare()
        if slot == head_slot:
            beside = plane()
        if beside is not None and next(beside, True):
            beside = None
    for steps in running:
        for _ in steps:
            pass
    if beside is not None:
        for _ in beside:
            pass

    total = pgf[0, pl.ds(rows, 16), :].astype(F32)
    for c in range(1, nz):
        total += pgf[c, pl.ds(rows, 16), :].astype(F32)
    loss_pair[core] = total
    ref = loss_pair.at[core]
    last = 6 + STREAMS
    loss_copy = copy_to(ref, ref, pair_send.at[last], pair_recv.at[last], task=sib)
    loss_copy.start()
    for st in range(STREAMS):
        ag_sent(1, st, CHAIN[-2] + 1, far)
    loss_copy.wait()
    total = loss_pair[0] + loss_pair[1]
    loss_out[0, 0] = jnp.sum(total) * loss_scale
    for st in range(STREAMS):
        span = pl.ds(st * rb, rb)
        hg_copy(st).wait()
        hg_out[:, span] = (acc_own[:, span] + hg_recv[st].astype(F32)).astype(BF16)


def shards(
    hidden, piece_weight, task_embed, task_bias, event_bin, censored, patient_id, patient_rows
):
    patients = patient_rows.shape[0]
    rows, depth = hidden.shape
    tasks, width = task_embed.shape
    pieces = task_bias.shape[1]
    n_task = lax.axis_size("task")
    nx, ny = lax.axis_size("row"), lax.axis_size("section")
    nz = n_task // 2
    half = pieces * width // 2
    bx = tasks // nx
    by = bx // ny
    vmem = pl.BlockSpec(memory_space=pltpu.VMEM)
    in_hbm = pl.BlockSpec(memory_space=pltpu.HBM)
    dma = pltpu.SemaphoreType.DMA
    hg, tg, loss = pl.pallas_call(
        functools.partial(kernel, 1.0 / (patients * tasks * n_task), 1.0 / patients),
        out_shape=(
            pltpu.VMEM((depth, rows), BF16),
            pltpu.VMEM((tasks, width), BF16),
            jax.ShapeDtypeStruct((1, 1), F32),
        ),
        in_specs=[in_hbm] * 8,
        out_specs=(vmem, vmem, pl.BlockSpec(memory_space=pltpu.SMEM)),
        scratch_shapes=[
            pltpu.VMEM((1, rows), jnp.int32),
            pltpu.VMEM((1, patients), jnp.int32),
            pltpu.VMEM((2, depth, rows), BF16),
            pltpu.VMEM((2, rows, depth), BF16),
            pltpu.VMEM((2, depth, half), BF16),
            pltpu.VMEM((2, tasks, width), BF16),
            pltpu.VMEM((2, pieces, tasks), F32),
            pltpu.VMEM((2, rows, tasks), jnp.int32),
            pltpu.VMEM((2, rows, tasks), jnp.int32),
            pltpu.VMEM((rows, tasks), F32),
            pltpu.VMEM((nz, rows, LANES), F32),
            pltpu.VMEM((2, 2, nz // 2, rows, LANES), BF16),
            pltpu.VMEM((2, 2, nz // 2, rows, LANES), BF16),
            pltpu.VMEM((nz, rows, LANES), BF16),
            pltpu.VMEM((nz, rows + 16, LANES), BF16),
            pltpu.VMEM((2, pieces // 2, rows, tasks), BF16),
            pltpu.VMEM((8, tasks), F32),
            pltpu.VMEM((nx, 8, LANES), F32),
            pltpu.VMEM((ny, 8, LANES), F32),
            pltpu.VMEM((2, 16, LANES), F32),
            pltpu.VMEM((2, tasks, width), F32),
            pltpu.VMEM((tasks, width), BF16),
            pltpu.VMEM((tasks, width), BF16),
            pltpu.VMEM((tasks, width), BF16),
            pltpu.VMEM((nx - 1, bx, width), BF16),
            pltpu.VMEM((bx, width), BF16),
            pltpu.VMEM((ny - 1, by, width), BF16),
            pltpu.VMEM((tasks, width), BF16),
            pltpu.VMEM((depth, rows), F32),
            pltpu.VMEM((depth, rows), F32),
            pltpu.VMEM((STREAMS, depth, rows // STREAMS), BF16),
            pltpu.VMEM((STREAMS, depth, rows // STREAMS), BF16),
            dma((4, 2, STREAMS, nz // 2)),
            dma((4, 2, STREAMS, nz // 2)),
            dma((8,)),
            dma((7 + STREAMS,)),
            dma((7 + STREAMS,)),
            dma((nz // 2,)),
            dma((nz // 2,)),
            dma((3, nx - 1)),
            dma((3, nx - 1)),
            dma((3, ny - 1)),
            dma((3, ny - 1)),
        ],
        compiler_params=pltpu.CompilerParams(
            collective_id=0, has_side_effects=True, vmem_limit_bytes=60 * 1024 * 1024
        ),
        cost_estimate=pl.CostEstimate(
            flops=2400000000, bytes_accessed=4000000, transcendentals=600000
        ),
    )(
        hidden.T,
        piece_weight,
        task_embed,
        task_bias.T,
        event_bin,
        censored,
        patient_id.reshape(1, rows),
        patient_rows.reshape(1, patients),
    )
    return hg.T, tg.astype(F32), loss.reshape(())


def solution(mesh):
    return jax.shard_map(
        shards,
        mesh=mesh,
        in_specs=(
            P(("section", "row"), "task"),
            P("task", None),
            P("task", None),
            P("task", None),
            P(("section", "row"), "task"),
            P(("section", "row"), "task"),
            P(("section", "row")),
            P(),
        ),
        out_specs=(P(("section", "row"), "task"), P("task", None), P()),
        check_vma=False,
    )
```

```python
import functools

import jax
import jax.numpy as jnp
from jax import lax
from jax.experimental import pallas as pl
from jax.experimental.pallas import tpu as pltpu
from jax.sharding import PartitionSpec as P

MESH = pl.DeviceIdType.MESH
F32 = jnp.float32
BF16 = jnp.bfloat16
LANES = 128
STREAMS = 2
CHAIN = (2, 4, 6, 8)
LAG = 1
NT = (((1,), (1,)), ((), ()))
TN = (((0,), (0,)), ((), ()))


def kernel(
    loss_scale,
    grad_scale,
    hid_hbm,
    pw_hbm,
    te_hbm,
    bias_hbm,
    bins_hbm,
    cens_hbm,
    pid_hbm,
    prow_hbm,
    hg_out,
    tg_out,
    loss_out,
    pid_ref,
    prow_ref,
    hid,
    hid_rows,
    pw,
    te,
    bias,
    bins,
    cens,
    wrow,
    part,
    rs_out,
    rs_in,
    zbuf,
    pgf,
    gbuf,
    loss_acc,
    loss_x,
    loss_y,
    loss_pair,
    tg_acc,
    tg_send,
    tg_recv,
    tx_send,
    tx_recv,
    ty_send,
    ty_recv,
    tg_fin,
    acc_own,
    acc_sib,
    hg_send,
    hg_recv,
    send_sem,
    recv_sem,
    local_sem,
    pair_send,
    pair_recv,
    pw_send,
    pw_recv,
    px_send,
    px_recv,
    py_send,
    py_recv,
):
    rows = hid.shape[2]
    half_cols = pw.shape[2]
    tasks = te.shape[1]
    nz = part.shape[0]
    far = nz // 2
    pieces = half_cols // te.shape[2]
    per_piece = nz // pieces
    rb = rows // STREAMS
    nx = lax.axis_size("row")
    ny = lax.axis_size("section")
    task = lax.axis_index("task")
    x = lax.axis_index("row")
    y = lax.axis_index("section")
    z = task // 2
    core = task % 2
    sib = z * 2 + 1 - core

    def wrap(v):
        return (v + 2 * nz) % nz

    def z_dev(off):
        return wrap(z + off) * 2 + core

    def copy_to(src, dst, ss, rs, **where):
        return pltpu.make_async_remote_copy(
            src_ref=src,
            dst_ref=dst,
            send_sem=ss,
            recv_sem=rs,
            device_id=where,
            device_id_type=MESH,
        )

    mine = pl.ds(pl.multiple_of(core * half_cols, half_cols), half_cols)
    loads = [
        (hid_hbm, hid.at[0]),
        (pw_hbm.at[:, mine], pw.at[0]),
        (te_hbm, te.at[0]),
        (bias_hbm, bias.at[0]),
        (bins_hbm, bins.at[0]),
        (cens_hbm, cens.at[0]),
        (pid_hbm, pid_ref),
        (prow_hbm, prow_ref),
    ]
    loads = [pltpu.make_async_copy(a, b, local_sem.at[i]) for i, (a, b) in enumerate(loads)]
    for load in loads:
        load.start()

    barrier = pltpu.get_barrier_semaphore()
    strides = sorted({b - a for a, b in zip((0,) + CHAIN, CHAIN)} | {1})
    peers = [dict(task=sib)] + [dict(task=z_dev(s * n)) for n in strides for s in (1, -1)]
    peers += [dict(row=(x + j) % nx) for j in range(1, nx)]
    peers += [dict(section=(y + j) % ny) for j in range(1, ny)]
    for peer in peers:
        pl.semaphore_signal(barrier, inc=1, device_id=peer, device_id_type=MESH)
    pl.semaphore_wait(barrier, len(peers))

    pair = [
        (hid_hbm, hid.at[1]),
        (te_hbm, te.at[1]),
        (bias_hbm, bias.at[1]),
        (bins_hbm, bins.at[1]),
        (cens_hbm, cens.at[1]),
    ]
    pair = [
        copy_to(a, b, pair_send.at[i], pair_recv.at[i], task=sib) for i, (a, b) in enumerate(pair)
    ]

    part_cols = half_cols // far

    def pw_copy(n):
        q = (wrap(z + far) // 2 + n + far) % far
        there = pl.ds(
            pl.multiple_of((1 - core) * half_cols + q * part_cols, part_cols), part_cols
        )
        here = pl.ds(pl.multiple_of(q * part_cols, part_cols), part_cols)
        return copy_to(
            pw_hbm.at[:, there], pw.at[1, :, here], pw_send.at[q], pw_recv.at[q], task=sib
        )

    pw_order = [0] + [s * n for n in range(1, far // 2) for s in (1, -1)] + [far // 2]
    pair[0].start()
    for n in pw_order:
        pw_copy(n).start()
    for copy in pair[1:]:
        copy.start()

    def long_way(st):
        return 0 if st < STREAMS // 2 else 1

    def stops(d, st):
        return [c for c in CHAIN if c < far or d == long_way(st)]

    def before(off):
        return max([0] + [c for c in CHAIN if c < off])

    def behind(stop, d, st):
        last = far if d == long_way(st) else far - 1
        found = [off for off in range(1, last + 1) if before(off) == stop]
        return sorted(found, key=lambda off: off not in CHAIN)

    def sides(st):
        return (long_way(st), 1 - long_way(st))

    def rs_copy(ph, d, st, off):
        span = pl.ds(st * rb, rb)
        return copy_to(
            rs_out.at[ph, d, off - 1, span, :],
            rs_in.at[ph, d, off - 1, span, :],
            send_sem.at[2 * ph, d, st, off - 1],
            recv_sem.at[2 * ph, d, st, off - 1],
            task=z_dev((1 - 2 * d) * (off - before(off))),
        )

    def cols(c):
        return pl.ds(pl.multiple_of(c * LANES, LANES), LANES)

    def fill(k):
        stop = ([0] + list(CHAIN))[-1 - k]
        for off in [stop] + list(range(before(stop) + 1, stop)):
            chunks = [wrap(z + off)] if off in (0, far) else [wrap(z - off), wrap(z + off)]
            total = None
            for h in range(2):
                w = jnp.concatenate([pw[h, :, cols(c)] for c in chunks], axis=1)
                dots = jnp.dot(hid_rows[h], w, preferred_element_type=F32)
                total = dots if total is None else total + dots
            for i, c in enumerate(chunks):
                part[c] = total[:, i * LANES : (i + 1) * LANES]

    def rs_send(ph, d, st, off):
        span = pl.ds(st * rb, rb)
        total = part[wrap(z + (1 - 2 * d) * off), span, :]
        if off in stops(d, st):
            for other in behind(off, d, st):
                rs_copy(ph, d, st, other).wait_recv()
                total += rs_in[ph, d, other - 1, span, :].astype(F32)
        rs_out[ph, d, off - 1, span, :] = total.astype(BF16)
        rs_copy(ph, d, st, off).start()

    def rs_total(ph, st):
        span = pl.ds(st * rb, rb)
        total = part[z, span, :]
        for d in sides(st):
            for other in behind(0, d, st):
                rs_copy(ph, d, st, other).wait_recv()
                total += rs_in[ph, d, other - 1, span, :].astype(F32)
        return total

    def rs_chain(ph, st, k):
        stop = ([0] + list(CHAIN))[-1 - k]
        for d in sides(st):
            if k == 0:
                rs_send(ph, d, st, far if d == long_way(st) else far - 1)
            elif stop != far - 1 or d == long_way(st):
                rs_send(ph, d, st, stop)
        if k == 0:
            rs_leaves(ph, st, 0)

    def rs_leaves(ph, st, k):
        stop = ([0] + list(CHAIN))[-1 - k]
        for off in range(stop - 1, before(stop), -1):
            for d in sides(st):
                if off != far - 1 or d == long_way(st):
                    rs_send(ph, d, st, off)

    def rs_sent(ph, st):
        for d in range(2):
            for off in range(1, far + 1 if d == long_way(st) else far):
                rs_copy(ph, d, st, off).wait_send()

    def ag_copy(ph, d, st, off):
        buf = zbuf if ph == 0 else pgf
        extra = 16 if ph == 1 and st == STREAMS - 1 else 0
        sgn = 1 - 2 * d
        ref = buf.at[wrap(z - sgn * before(off)), pl.ds(st * rb, rb + extra), :]
        return copy_to(
            ref,
            ref,
            send_sem.at[2 * ph + 1, d, st, off - 1],
            recv_sem.at[2 * ph + 1, d, st, off - 1],
            task=z_dev(sgn * (off - before(off))),
        )

    def ag_arrived(ph, d, st, off):
        buf = zbuf if ph == 0 else pgf
        extra = 16 if ph == 1 and st == STREAMS - 1 else 0
        sgn = 1 - 2 * d
        if off < far or d == long_way(st):
            ref = buf.at[wrap(z - sgn * off), pl.ds(st * rb, rb + extra), :]
            copy_to(
                ref,
                ref,
                send_sem.at[2 * ph + 1, d, st, off - 1],
                recv_sem.at[2 * ph + 1, d, st, off - 1],
                task=z_dev(sgn * (off - before(off))),
            ).wait_recv()

    def ag_chain(ph, st, k):
        stop = ([0] + list(CHAIN))[k]
        for d in sides(st):
            if k > 0:
                ag_arrived(ph, d, st, stop)
            for off in behind(stop, d, st)[:1]:
                ag_copy(ph, d, st, off).start()

    def ag_leaves(ph, st, k):
        stop = ([0] + list(CHAIN))[k]
        for d in sides(st):
            for off in behind(stop, d, st)[1:]:
                ag_copy(ph, d, st, off).start()

    def ag_sent(ph, st, first, last):
        for d in range(2):
            for off in range(first, last + 1):
                if off < far or d == long_way(st):
                    ag_copy(ph, d, st, off).wait_send()

    between = [off for off in range(1, far) if off not in CHAIN]

    def prepare():
        loads[6].wait()
        loads[7].wait()
        ids = jnp.broadcast_to(pid_ref[...].astype(F32), (prow_ref.shape[1], rows)).T
        lane = lax.broadcasted_iota(jnp.int32, ids.shape, 1).astype(F32)
        record = jnp.where(ids == lane, prow_ref[...].astype(F32), 0.0)
        weight = 1.0 / jnp.sum(record, axis=1, keepdims=True)
        wrow[...] = jnp.broadcast_to(weight, wrow.shape)
        loss_acc[...] = jnp.zeros_like(loss_acc)
        tg_acc[...] = jnp.zeros_like(tg_acc)
        acc_own[...] = jnp.zeros_like(acc_own)
        acc_sib[...] = jnp.zeros_like(acc_sib)

    late = (wrap(z + far + 1) // per_piece) % pieces

    def head(st, first, last):
        span = pl.ds(st * rb, rb)
        order = [(late + 1 + i) % pieces for i in range(first, last)]
        zs = jnp.concatenate(
            [
                jnp.concatenate(
                    [zbuf[p * per_piece + k, span, :] for k in range(per_piece)], axis=1
                )
                for p in order
            ],
            axis=0,
        )
        total = None
        for h in range(2):
            dots = lax.dot_general(zs, te[h], NT, preferred_element_type=F32)
            edge = bins[h, span, :]
            alive = (1 - cens[h, span, :]).astype(F32)
            weight = wrow[span, :]
            grads = []
            nll = None
            for i, p in enumerate(order):
                piece = core * pieces + p
                logits = dots[i * rb : (i + 1) * rb] + bias[h, pl.ds(piece, 1), :]
                hazard = jnp.exp(logits)
                at = edge == piece
                hazard = jnp.where(edge > piece, hazard, jnp.where(at, 0.5 * hazard, 0.0))
                event = jnp.where(at, alive, 0.0)
                term = hazard - event * logits
                nll = term if nll is None else nll + term
                grad = (weight * (hazard - event)).astype(BF16)
                gbuf[h, p, span, :] = grad
                grads.append(grad)
            nll = (weight * nll).reshape(rb // 8, 8, tasks).sum(axis=0)
            loss_acc[...] += nll
            grads = jnp.concatenate(grads, axis=0)
            dots = jnp.dot(grads, te[h], preferred_element_type=F32)
            total = dots if total is None else total + dots
        for i, p in enumerate(order):
            for k in range(per_piece):
                part[p * per_piece + k, span, :] = total[
                    i * rb : (i + 1) * rb, k * LANES : (k + 1) * LANES
                ]

    def x_copy(j, src, dst, k):
        return copy_to(
            src, dst, px_send.at[k, j - 1], px_recv.at[k, j - 1], row=(x + j) % nx
        )

    def y_copy(j, src, dst, k):
        return copy_to(
            src, dst, py_send.at[k, j - 1], py_recv.at[k, j - 1], section=(y + j) % ny
        )

    def loss_x_copy(j):
        return x_copy(j, loss_x.at[x], loss_x.at[x], 0)

    def loss_y_copy(j):
        return y_copy(j, loss_y.at[y], loss_y.at[y], 0)

    bx = tasks // nx
    by = bx // ny

    def tgx_copy(j):
        peer = (x + j) % nx
        src = tx_send.at[pl.ds(pl.multiple_of(peer * bx, bx), bx), :]
        return x_copy(j, src, tx_recv.at[j - 1], 1)

    def tgy_copy(j):
        peer = (y + j) % ny
        src = ty_send.at[pl.ds(pl.multiple_of(peer * by, by), by), :]
        return y_copy(j, src, ty_recv.at[j - 1], 1)

    def agy_copy(j):
        ref = tg_fin.at[pl.ds(pl.multiple_of(x * bx + y * by, by), by), :]
        return y_copy(j, ref, ref, 2)

    def agx_copy(j):
        ref = tg_fin.at[pl.ds(pl.multiple_of(x * bx, bx), bx), :]
        return x_copy(j, ref, ref, 2)

    tg_copy = copy_to(tg_send, tg_recv, pair_send.at[5], pair_recv.at[5], task=sib)

    def tg_piece(p):
        zp = jnp.concatenate([zbuf[p * per_piece + k] for k in range(per_piece)], axis=1)
        for h in range(2):
            tg_acc[h] += lax.dot_general(gbuf[h, p], zp, TN, preferred_element_type=F32)

    def loss_terms():
        own = sum(loss_y[i] for i in range(1, ny)) + loss_y[0]
        own = jnp.sum(jnp.sum(own, axis=0, keepdims=True), axis=1, keepdims=True)
        own = jnp.broadcast_to(own, (16, LANES))
        place = lax.broadcasted_iota(jnp.int32, own.shape, 1)
        place += LANES * lax.broadcasted_iota(jnp.int32, own.shape, 0)
        high = own.astype(BF16).astype(F32)
        rest = own - high
        middle = rest.astype(BF16).astype(F32)
        low = rest - middle
        terms = jnp.where(
            place == 0, high, jnp.where(place == 1, middle, jnp.where(place == 2, low, 0.0))
        )
        pgf[z, pl.ds(rows, 16), :] = terms.astype(BF16)

    def plane():
        loss_x[x] = loss_acc[:, :LANES] + loss_acc[:, LANES:]
        for j in range(1, nx):
            loss_x_copy(j).start()
        for p in range(pieces // 2):
            tg_piece(p)
        yield
        for p in range(pieces // 2, pieces):
            tg_piece(p)
        tg_send[...] = tg_acc[1].astype(BF16)
        tg_copy.start()
        for j in range(1, nx):
            loss_x_copy(j).wait()
        loss_y[y] = sum(loss_x[i] for i in range(1, nx)) + loss_x[0]
        for j in range(1, ny):
            loss_y_copy(j).start()
        yield
        tg_copy.wait()
        tg_acc[0] += tg_recv[...].astype(F32)
        tx_send[...] = tg_acc[0].astype(BF16)
        for j in range(1, nx):
            tgx_copy(j).start()
        for j in range(1, ny):
            loss_y_copy(j).wait()
        loss_terms()
        yield
        total = tg_acc[0, pl.ds(pl.multiple_of(x * bx, bx), bx), :]
        for j in range(1, nx):
            tgx_copy(j).wait()
            total += tx_recv[j - 1].astype(F32)
        tg_acc[0, pl.ds(0, bx), :] = total
        ty_send[...] = total.astype(BF16)
        for j in range(1, ny):
            tgy_copy(j).start()
        yield
        total = tg_acc[0, pl.ds(pl.multiple_of(y * by, by), by), :]
        for j in range(1, ny):
            tgy_copy(j).wait()
            total += ty_recv[j - 1].astype(F32)
        place = pl.ds(pl.multiple_of(x * bx + y * by, by), by)
        tg_fin[place, :] = (total * grad_scale).astype(BF16)
        for j in range(1, ny):
            agy_copy(j).start()
        yield
        for j in range(1, ny):
            agy_copy(j).wait_send()
            from_y = (y + ny - j) % ny
            ref = tg_fin.at[pl.ds(pl.multiple_of(x * bx + from_y * by, by), by), :]
            y_copy(j, ref, ref, 2).wait_recv()
        for j in range(1, nx):
            agx_copy(j).start()
        yield
        for j in range(1, nx):
            agx_copy(j).wait_send()
            from_x = (x + nx - j) % nx
            ref = tg_fin.at[pl.ds(pl.multiple_of(from_x * bx, bx), bx), :]
            x_copy(j, ref, ref, 2).wait_recv()
        tg_out[...] = tg_fin[...]

    def add_chunks(st, offs):
        span = pl.ds(st * rb, rb)
        chunks = [wrap(z + off) for off in offs]
        value = jnp.concatenate([pgf[c, span, :] for c in chunks], axis=1)
        for h, acc in ((0, acc_own), (1, acc_sib)):
            w = jnp.concatenate([pw[h, :, cols(c)] for c in chunks], axis=1)
            acc[:, span] += lax.dot_general(w, value, NT, preferred_element_type=F32)

    def hg_copy(st):
        return copy_to(
            hg_send.at[st], hg_recv.at[st], pair_send.at[6 + st], pair_recv.at[6 + st], task=sib
        )

    def pw_arrived(*order):
        for m in order:
            pw_copy(m).wait_recv()

    def stream(st):
        span = pl.ds(st * rb, rb)
        n = len(CHAIN)
        for k in range(n):
            rs_chain(0, st, k)
            yield
            if st == 0 and k == 0:
                pw_arrived(2, -2)
                fill(1)
            if k < n - 1:
                rs_leaves(0, st, k + 1)
            yield
            if st == 0 and k < n - 1:
                pw_arrived(*{0: (3, -3), 1: (4,)}.get(k, ()))
                fill(k + 2)
            yield
        zbuf[z, span, :] = rs_total(0, st).astype(BF16)
        for k in range(n):
            ag_chain(0, st, k)
            yield
            ag_leaves(0, st, k)
            yield
            if k == 1:
                rs_sent(0, st)
            if st == 0 and k == 2:
                for copy in pair:
                    copy.wait_send()
                for m in pw_order:
                    pw_copy(m).wait_send()
            if k == n - 1:
                if st == 0:
                    for i in range(1, 5):
                        loads[1 + i].wait()
                        pair[i].wait_recv()
                for off in between[:-1]:
                    for d in sides(st):
                        ag_arrived(0, d, st, off)
                head(st, 0, pieces // 2)
            yield
        ag_chain(0, st, n)
        for d in sides(st):
            ag_arrived(0, d, st, far - 1)
        head(st, pieces // 2, pieces)
        for k in range(n):
            rs_chain(1, st, k)
            yield
            if k < n - 1:
                rs_leaves(1, st, k + 1)
            yield
            if k == 1:
                ag_sent(0, st, 1, far)
            yield
        pgf[z, span, :] = rs_total(1, st).astype(BF16)
        for k in range(n + 1):
            ag_chain(1, st, k)
            yield
            ag_leaves(1, st, k)
            yield
            if k == 0:
                add_chunks(st, [0])
            else:
                offs = [CHAIN[k - 1]]
                for off in between:
                    if before(off) == ([0] + list(CHAIN))[k - 1]:
                        for d in sides(st):
                            ag_arrived(1, d, st, off)
                        offs.append(off)
                add_chunks(st, [s * off for off in offs for s in (1, -1) if s * off > -far])
            if k == 1:
                rs_sent(1, st)
            if k == n - 1:
                ag_sent(1, st, 1, CHAIN[n - 2])
            if k == n:
                hg_send[st] = acc_sib[:, span].astype(BF16)
                hg_copy(st).start()
            yield

    loads[0].wait()
    loads[1].wait()
    hid_rows[0] = hid[0].T
    pair[0].wait_recv()
    hid_rows[1] = hid[1].T
    pw_arrived(0, 1, -1)
    fill(0)
    head_slot = len(CHAIN) * 2
    last_slot = len(CHAIN) * 4
    running = [stream(st) for st in range(STREAMS)]
    beside = None
    for slot in range(last_slot + (STREAMS - 1) * LAG + 1):
        active = [st for st in range(STREAMS) if 0 <= slot - st * LAG <= last_slot]
        for _ in range(3):
            for st in reversed(active):
                next(running[st])
        if slot == 0:
            prepare()
        if slot == head_slot + (STREAMS - 1) * LAG:
            beside = plane()
        if beside is not None and next(beside, True):
            beside = None
    for steps in running:
        for _ in steps:
            pass
    if beside is not None:
        for _ in beside:
            pass

    total = pgf[0, pl.ds(rows, 16), :].astype(F32)
    for c in range(1, nz):
        total += pgf[c, pl.ds(rows, 16), :].astype(F32)
    loss_pair[core] = total
    ref = loss_pair.at[core]
    last = 6 + STREAMS
    loss_copy = copy_to(ref, ref, pair_send.at[last], pair_recv.at[last], task=sib)
    loss_copy.start()
    for st in range(STREAMS):
        ag_sent(1, st, CHAIN[-2] + 1, far)
    loss_copy.wait()
    total = loss_pair[0] + loss_pair[1]
    loss_out[0, 0] = jnp.sum(total) * loss_scale
    for st in range(STREAMS):
        span = pl.ds(st * rb, rb)
        hg_copy(st).wait()
        hg_out[:, span] = (acc_own[:, span] + hg_recv[st].astype(F32)).astype(BF16)


def shards(
    hidden, piece_weight, task_embed, task_bias, event_bin, censored, patient_id, patient_rows
):
    patients = patient_rows.shape[0]
    rows, depth = hidden.shape
    tasks, width = task_embed.shape
    pieces = task_bias.shape[1]
    n_task = lax.axis_size("task")
    nx, ny = lax.axis_size("row"), lax.axis_size("section")
    nz = n_task // 2
    half = pieces * width // 2
    bx = tasks // nx
    by = bx // ny
    vmem = pl.BlockSpec(memory_space=pltpu.VMEM)
    in_hbm = pl.BlockSpec(memory_space=pltpu.HBM)
    dma = pltpu.SemaphoreType.DMA
    hg, tg, loss = pl.pallas_call(
        functools.partial(kernel, 1.0 / (patients * tasks * n_task), 1.0 / patients),
        out_shape=(
            pltpu.VMEM((depth, rows), BF16),
            pltpu.VMEM((tasks, width), BF16),
            jax.ShapeDtypeStruct((1, 1), F32),
        ),
        in_specs=[in_hbm] * 8,
        out_specs=(vmem, vmem, pl.BlockSpec(memory_space=pltpu.SMEM)),
        scratch_shapes=[
            pltpu.VMEM((1, rows), jnp.int32),
            pltpu.VMEM((1, patients), jnp.int32),
            pltpu.VMEM((2, depth, rows), BF16),
            pltpu.VMEM((2, rows, depth), BF16),
            pltpu.VMEM((2, depth, half), BF16),
            pltpu.VMEM((2, tasks, width), BF16),
            pltpu.VMEM((2, pieces, tasks), F32),
            pltpu.VMEM((2, rows, tasks), jnp.int32),
            pltpu.VMEM((2, rows, tasks), jnp.int32),
            pltpu.VMEM((rows, tasks), F32),
            pltpu.VMEM((nz, rows, LANES), F32),
            pltpu.VMEM((2, 2, nz // 2, rows, LANES), BF16),
            pltpu.VMEM((2, 2, nz // 2, rows, LANES), BF16),
            pltpu.VMEM((nz, rows, LANES), BF16),
            pltpu.VMEM((nz, rows + 16, LANES), BF16),
            pltpu.VMEM((2, pieces // 2, rows, tasks), BF16),
            pltpu.VMEM((8, tasks), F32),
            pltpu.VMEM((nx, 8, LANES), F32),
            pltpu.VMEM((ny, 8, LANES), F32),
            pltpu.VMEM((2, 16, LANES), F32),
            pltpu.VMEM((2, tasks, width), F32),
            pltpu.VMEM((tasks, width), BF16),
            pltpu.VMEM((tasks, width), BF16),
            pltpu.VMEM((tasks, width), BF16),
            pltpu.VMEM((nx - 1, bx, width), BF16),
            pltpu.VMEM((bx, width), BF16),
            pltpu.VMEM((ny - 1, by, width), BF16),
            pltpu.VMEM((tasks, width), BF16),
            pltpu.VMEM((depth, rows), F32),
            pltpu.VMEM((depth, rows), F32),
            pltpu.VMEM((STREAMS, depth, rows // STREAMS), BF16),
            pltpu.VMEM((STREAMS, depth, rows // STREAMS), BF16),
            dma((4, 2, STREAMS, nz // 2)),
            dma((4, 2, STREAMS, nz // 2)),
            dma((8,)),
            dma((7 + STREAMS,)),
            dma((7 + STREAMS,)),
            dma((nz // 2,)),
            dma((nz // 2,)),
            dma((3, nx - 1)),
            dma((3, nx - 1)),
            dma((3, ny - 1)),
            dma((3, ny - 1)),
        ],
        compiler_params=pltpu.CompilerParams(
            collective_id=0, has_side_effects=True, vmem_limit_bytes=60 * 1024 * 1024
        ),
        cost_estimate=pl.CostEstimate(
            flops=2400000000, bytes_accessed=4000000, transcendentals=600000
        ),
    )(
        hidden.T,
        piece_weight,
        task_embed,
        task_bias.T,
        event_bin,
        censored,
        patient_id.reshape(1, rows),
        patient_rows.reshape(1, patients),
    )
    return hg.T, tg.astype(F32), loss.reshape(())


def solution(mesh):
    return jax.shard_map(
        shards,
        mesh=mesh,
        in_specs=(
            P(("section", "row"), "task"),
            P("task", None),
            P("task", None),
            P("task", None),
            P(("section", "row"), "task"),
            P(("section", "row"), "task"),
            P(("section", "row")),
            P(),
        ),
        out_specs=(P(("section", "row"), "task"), P("task", None), P()),
        check_vma=False,
    )
```

```python
import functools

import jax
import jax.numpy as jnp
from jax import lax
from jax.experimental import pallas as pl
from jax.experimental.pallas import tpu as pltpu
from jax.sharding import PartitionSpec as P

MESH = pl.DeviceIdType.MESH
F32 = jnp.float32
BF16 = jnp.bfloat16
LANES = 128
STREAMS = 2
CHAIN = (2, 4, 6, 8)
NT = (((1,), (1,)), ((), ()))
TN = (((0,), (0,)), ((), ()))


def kernel(
    loss_scale,
    grad_scale,
    hid_hbm,
    pw_hbm,
    te_hbm,
    bias_hbm,
    bins_hbm,
    cens_hbm,
    pid_hbm,
    prow_hbm,
    hg_out,
    tg_out,
    loss_out,
    pid_ref,
    prow_ref,
    hid,
    hid_rows,
    pw,
    te,
    bias,
    bins,
    cens,
    wrow,
    part,
    rs_out,
    rs_in,
    zbuf,
    pgf,
    gbuf,
    loss_acc,
    loss_x,
    loss_y,
    loss_pair,
    tg_acc,
    tg_send,
    tg_recv,
    tx_send,
    tx_recv,
    ty_send,
    ty_recv,
    tg_fin,
    acc_own,
    acc_sib,
    hg_send,
    hg_recv,
    send_sem,
    recv_sem,
    local_sem,
    pair_send,
    pair_recv,
    pw_send,
    pw_recv,
    px_send,
    px_recv,
    py_send,
    py_recv,
):
    rows = hid.shape[2]
    half_cols = pw.shape[2]
    tasks = te.shape[1]
    nz = part.shape[0]
    far = nz // 2
    pieces = half_cols // te.shape[2]
    per_piece = nz // pieces
    rb = rows // STREAMS
    nx = lax.axis_size("row")
    ny = lax.axis_size("section")
    task = lax.axis_index("task")
    x = lax.axis_index("row")
    y = lax.axis_index("section")
    z = task // 2
    core = task % 2
    sib = z * 2 + 1 - core

    def wrap(v):
        return (v + 2 * nz) % nz

    def z_dev(off):
        return wrap(z + off) * 2 + core

    def copy_to(src, dst, ss, rs, **where):
        return pltpu.make_async_remote_copy(
            src_ref=src,
            dst_ref=dst,
            send_sem=ss,
            recv_sem=rs,
            device_id=where,
            device_id_type=MESH,
        )

    mine = pl.ds(pl.multiple_of(core * half_cols, half_cols), half_cols)
    loads = [
        (hid_hbm, hid.at[0]),
        (pw_hbm.at[:, mine], pw.at[0]),
        (te_hbm, te.at[0]),
        (bias_hbm, bias.at[0]),
        (bins_hbm, bins.at[0]),
        (cens_hbm, cens.at[0]),
        (pid_hbm, pid_ref),
        (prow_hbm, prow_ref),
    ]
    loads = [pltpu.make_async_copy(a, b, local_sem.at[i]) for i, (a, b) in enumerate(loads)]
    for load in loads[:2]:
        load.start()

    barrier = pltpu.get_barrier_semaphore()
    strides = sorted({b - a for a, b in zip((0,) + CHAIN, CHAIN)} | {1})
    peers = [dict(task=sib)] + [dict(task=z_dev(s * n)) for n in strides for s in (1, -1)]
    peers += [dict(row=(x + j) % nx) for j in range(1, nx)]
    peers += [dict(section=(y + j) % ny) for j in range(1, ny)]
    for peer in peers:
        pl.semaphore_signal(barrier, inc=1, device_id=peer, device_id_type=MESH)
    pl.semaphore_wait(barrier, len(peers))

    pair = [
        (hid_hbm, hid.at[1]),
        (te_hbm, te.at[1]),
        (bias_hbm, bias.at[1]),
        (bins_hbm, bins.at[1]),
        (cens_hbm, cens.at[1]),
    ]
    pair = [
        copy_to(a, b, pair_send.at[i], pair_recv.at[i], task=sib) for i, (a, b) in enumerate(pair)
    ]

    part_cols = half_cols // far

    def pw_copy(n):
        q = (wrap(z + far) // 2 + n + far) % far
        there = pl.ds(
            pl.multiple_of((1 - core) * half_cols + q * part_cols, part_cols), part_cols
        )
        here = pl.ds(pl.multiple_of(q * part_cols, part_cols), part_cols)
        return copy_to(
            pw_hbm.at[:, there], pw.at[1, :, here], pw_send.at[q], pw_recv.at[q], task=sib
        )

    pw_order = [0] + [s * n for n in range(1, far // 2) for s in (1, -1)] + [far // 2]
    pair[0].start()
    for n in pw_order[:5]:
        pw_copy(n).start()
    for load in loads[2:]:
        load.start()

    def long_way(st):
        return 0 if st < STREAMS // 2 else 1

    def stops(d, st):
        return [c for c in CHAIN if c < far or d == long_way(st)]

    def before(off):
        return max([0] + [c for c in CHAIN if c < off])

    def behind(stop, d, st):
        last = far if d == long_way(st) else far - 1
        found = [off for off in range(1, last + 1) if before(off) == stop]
        return sorted(found, key=lambda off: off not in CHAIN)

    def sides(st):
        return (long_way(st), 1 - long_way(st))

    def rs_copy(ph, d, st, off):
        span = pl.ds(st * rb, rb)
        return copy_to(
            rs_out.at[ph, d, off - 1, span, :],
            rs_in.at[ph, d, off - 1, span, :],
            send_sem.at[2 * ph, d, st, off - 1],
            recv_sem.at[2 * ph, d, st, off - 1],
            task=z_dev((1 - 2 * d) * (off - before(off))),
        )

    def cols(c):
        return pl.ds(pl.multiple_of(c * LANES, LANES), LANES)

    def fill(k):
        stop = ([0] + list(CHAIN))[-1 - k]
        for off in [stop] + list(range(before(stop) + 1, stop)):
            chunks = [wrap(z + off)] if off in (0, far) else [wrap(z - off), wrap(z + off)]
            total = None
            for h in range(2):
                w = jnp.concatenate([pw[h, :, cols(c)] for c in chunks], axis=1)
                dots = jnp.dot(hid_rows[h], w, preferred_element_type=F32)
                total = dots if total is None else total + dots
            for i, c in enumerate(chunks):
                part[c] = total[:, i * LANES : (i + 1) * LANES]

    def rs_send(ph, d, st, off):
        span = pl.ds(st * rb, rb)
        total = part[wrap(z + (1 - 2 * d) * off), span, :]
        if off in stops(d, st):
            for other in behind(off, d, st):
                rs_copy(ph, d, st, other).wait_recv()
                total += rs_in[ph, d, other - 1, span, :].astype(F32)
        rs_out[ph, d, off - 1, span, :] = total.astype(BF16)
        rs_copy(ph, d, st, off).start()

    def rs_total(ph, st):
        span = pl.ds(st * rb, rb)
        total = part[z, span, :]
        for d in sides(st):
            for other in behind(0, d, st):
                rs_copy(ph, d, st, other).wait_recv()
                total += rs_in[ph, d, other - 1, span, :].astype(F32)
        return total

    def rs_chain(ph, st, k):
        stop = ([0] + list(CHAIN))[-1 - k]
        for d in sides(st):
            if k == 0:
                rs_send(ph, d, st, far if d == long_way(st) else far - 1)
            elif stop != far - 1 or d == long_way(st):
                rs_send(ph, d, st, stop)
        if k == 0:
            rs_leaves(ph, st, 0)

    def rs_leaves(ph, st, k):
        stop = ([0] + list(CHAIN))[-1 - k]
        for off in range(stop - 1, before(stop), -1):
            for d in sides(st):
                if off != far - 1 or d == long_way(st):
                    rs_send(ph, d, st, off)

    def rs_sent(ph, st):
        for d in range(2):
            for off in range(1, far + 1 if d == long_way(st) else far):
                rs_copy(ph, d, st, off).wait_send()

    def ag_copy(ph, d, st, off):
        buf = zbuf if ph == 0 else pgf
        extra = 16 if ph == 1 and st == STREAMS - 1 else 0
        sgn = 1 - 2 * d
        ref = buf.at[wrap(z - sgn * before(off)), pl.ds(st * rb, rb + extra), :]
        return copy_to(
            ref,
            ref,
            send_sem.at[2 * ph + 1, d, st, off - 1],
            recv_sem.at[2 * ph + 1, d, st, off - 1],
            task=z_dev(sgn * (off - before(off))),
        )

    def ag_arrived(ph, d, st, off):
        buf = zbuf if ph == 0 else pgf
        extra = 16 if ph == 1 and st == STREAMS - 1 else 0
        sgn = 1 - 2 * d
        if off < far or d == long_way(st):
            ref = buf.at[wrap(z - sgn * off), pl.ds(st * rb, rb + extra), :]
            copy_to(
                ref,
                ref,
                send_sem.at[2 * ph + 1, d, st, off - 1],
                recv_sem.at[2 * ph + 1, d, st, off - 1],
                task=z_dev(sgn * (off - before(off))),
            ).wait_recv()

    def ag_chain(ph, st, k):
        stop = ([0] + list(CHAIN))[k]
        for d in sides(st):
            if k > 0:
                ag_arrived(ph, d, st, stop)
            for off in behind(stop, d, st)[:1]:
                ag_copy(ph, d, st, off).start()

    def ag_leaves(ph, st, k):
        stop = ([0] + list(CHAIN))[k]
        for d in sides(st):
            for off in behind(stop, d, st)[1:]:
                ag_copy(ph, d, st, off).start()

    def ag_sent(ph, st, first, last):
        for d in range(2):
            for off in range(first, last + 1):
                if off < far or d == long_way(st):
                    ag_copy(ph, d, st, off).wait_send()

    between = [off for off in range(1, far) if off not in CHAIN]

    def prepare():
        loads[6].wait()
        loads[7].wait()
        ids = jnp.broadcast_to(pid_ref[...].astype(F32), (prow_ref.shape[1], rows)).T
        lane = lax.broadcasted_iota(jnp.int32, ids.shape, 1).astype(F32)
        record = jnp.where(ids == lane, prow_ref[...].astype(F32), 0.0)
        weight = 1.0 / jnp.sum(record, axis=1, keepdims=True)
        wrow[...] = jnp.broadcast_to(weight, wrow.shape)
        loss_acc[...] = jnp.zeros_like(loss_acc)
        tg_acc[...] = jnp.zeros_like(tg_acc)
        acc_own[...] = jnp.zeros_like(acc_own)
        acc_sib[...] = jnp.zeros_like(acc_sib)

    late = (wrap(z + far + 1) // per_piece) % pieces

    def head(st, first, last):
        span = pl.ds(st * rb, rb)
        order = [(late + 1 + i) % pieces for i in range(first, last)]
        zs = jnp.concatenate(
            [
                jnp.concatenate(
                    [zbuf[p * per_piece + k, span, :] for k in range(per_piece)], axis=1
                )
                for p in order
            ],
            axis=0,
        )
        total = None
        for h in range(2):
            dots = lax.dot_general(zs, te[h], NT, preferred_element_type=F32)
            edge = bins[h, span, :]
            alive = (1 - cens[h, span, :]).astype(F32)
            weight = wrow[span, :]
            grads = []
            nll = None
            for i, p in enumerate(order):
                piece = core * pieces + p
                logits = dots[i * rb : (i + 1) * rb] + bias[h, pl.ds(piece, 1), :]
                hazard = jnp.exp(logits)
                at = edge == piece
                hazard = jnp.where(edge > piece, hazard, jnp.where(at, 0.5 * hazard, 0.0))
                event = jnp.where(at, alive, 0.0)
                term = hazard - event * logits
                nll = term if nll is None else nll + term
                grad = (weight * (hazard - event)).astype(BF16)
                gbuf[h, p, span, :] = grad
                grads.append(grad)
            nll = (weight * nll).reshape(rb // 8, 8, tasks).sum(axis=0)
            loss_acc[...] += nll
            grads = jnp.concatenate(grads, axis=0)
            dots = jnp.dot(grads, te[h], preferred_element_type=F32)
            total = dots if total is None else total + dots
        for i, p in enumerate(order):
            for k in range(per_piece):
                part[p * per_piece + k, span, :] = total[
                    i * rb : (i + 1) * rb, k * LANES : (k + 1) * LANES
                ]

    def x_copy(j, src, dst, k):
        return copy_to(
            src, dst, px_send.at[k, j - 1], px_recv.at[k, j - 1], row=(x + j) % nx
        )

    def y_copy(j, src, dst, k):
        return copy_to(
            src, dst, py_send.at[k, j - 1], py_recv.at[k, j - 1], section=(y + j) % ny
        )

    def loss_x_copy(j):
        return x_copy(j, loss_x.at[x], loss_x.at[x], 0)

    def loss_y_copy(j):
        return y_copy(j, loss_y.at[y], loss_y.at[y], 0)

    bx = tasks // nx
    by = bx // ny

    def tgx_copy(j):
        peer = (x + j) % nx
        src = tx_send.at[pl.ds(pl.multiple_of(peer * bx, bx), bx), :]
        return x_copy(j, src, tx_recv.at[j - 1], 1)

    def tgy_copy(j):
        peer = (y + j) % ny
        src = ty_send.at[pl.ds(pl.multiple_of(peer * by, by), by), :]
        return y_copy(j, src, ty_recv.at[j - 1], 1)

    def agy_copy(j):
        ref = tg_fin.at[pl.ds(pl.multiple_of(x * bx + y * by, by), by), :]
        return y_copy(j, ref, ref, 2)

    def agx_copy(j):
        ref = tg_fin.at[pl.ds(pl.multiple_of(x * bx, bx), bx), :]
        return x_copy(j, ref, ref, 2)

    tg_copy = copy_to(tg_send, tg_recv, pair_send.at[5], pair_recv.at[5], task=sib)

    def tg_piece(p):
        zp = jnp.concatenate([zbuf[p * per_piece + k] for k in range(per_piece)], axis=1)
        for h in range(2):
            tg_acc[h] += lax.dot_general(gbuf[h, p], zp, TN, preferred_element_type=F32)

    def loss_terms():
        own = sum(loss_y[i] for i in range(1, ny)) + loss_y[0]
        own = jnp.sum(jnp.sum(own, axis=0, keepdims=True), axis=1, keepdims=True)
        own = jnp.broadcast_to(own, (16, LANES))
        place = lax.broadcasted_iota(jnp.int32, own.shape, 1)
        place += LANES * lax.broadcasted_iota(jnp.int32, own.shape, 0)
        high = own.astype(BF16).astype(F32)
        rest = own - high
        middle = rest.astype(BF16).astype(F32)
        low = rest - middle
        terms = jnp.where(
            place == 0, high, jnp.where(place == 1, middle, jnp.where(place == 2, low, 0.0))
        )
        pgf[z, pl.ds(rows, 16), :] = terms.astype(BF16)

    def plane():
        loss_x[x] = loss_acc[:, :LANES] + loss_acc[:, LANES:]
        for j in range(1, nx):
            loss_x_copy(j).start()
        for p in range(pieces // 2):
            tg_piece(p)
        yield
        for p in range(pieces // 2, pieces):
            tg_piece(p)
        tg_send[...] = tg_acc[1].astype(BF16)
        tg_copy.start()
        for j in range(1, nx):
            loss_x_copy(j).wait()
        loss_y[y] = sum(loss_x[i] for i in range(1, nx)) + loss_x[0]
        for j in range(1, ny):
            loss_y_copy(j).start()
        yield
        tg_copy.wait()
        tg_acc[0] += tg_recv[...].astype(F32)
        tx_send[...] = tg_acc[0].astype(BF16)
        for j in range(1, nx):
            tgx_copy(j).start()
        for j in range(1, ny):
            loss_y_copy(j).wait()
        loss_terms()
        yield
        total = tg_acc[0, pl.ds(pl.multiple_of(x * bx, bx), bx), :]
        for j in range(1, nx):
            tgx_copy(j).wait()
            total += tx_recv[j - 1].astype(F32)
        tg_acc[0, pl.ds(0, bx), :] = total
        ty_send[...] = total.astype(BF16)
        for j in range(1, ny):
            tgy_copy(j).start()
        yield
        total = tg_acc[0, pl.ds(pl.multiple_of(y * by, by), by), :]
        for j in range(1, ny):
            tgy_copy(j).wait()
            total += ty_recv[j - 1].astype(F32)
        place = pl.ds(pl.multiple_of(x * bx + y * by, by), by)
        tg_fin[place, :] = (total * grad_scale).astype(BF16)
        for j in range(1, ny):
            agy_copy(j).start()
        yield
        for j in range(1, ny):
            agy_copy(j).wait_send()
            from_y = (y + ny - j) % ny
            ref = tg_fin.at[pl.ds(pl.multiple_of(x * bx + from_y * by, by), by), :]
            y_copy(j, ref, ref, 2).wait_recv()
        for j in range(1, nx):
            agx_copy(j).start()
        yield
        for j in range(1, nx):
            agx_copy(j).wait_send()
            from_x = (x + nx - j) % nx
            ref = tg_fin.at[pl.ds(pl.multiple_of(from_x * bx, bx), bx), :]
            x_copy(j, ref, ref, 2).wait_recv()
        tg_out[...] = tg_fin[...]

    def add_chunks(st, offs):
        span = pl.ds(st * rb, rb)
        chunks = [wrap(z + off) for off in offs]
        value = jnp.concatenate([pgf[c, span, :] for c in chunks], axis=1)
        for h, acc in ((0, acc_own), (1, acc_sib)):
            w = jnp.concatenate([pw[h, :, cols(c)] for c in chunks], axis=1)
            acc[:, span] += lax.dot_general(w, value, NT, preferred_element_type=F32)

    def hg_copy(st):
        return copy_to(
            hg_send.at[st], hg_recv.at[st], pair_send.at[6 + st], pair_recv.at[6 + st], task=sib
        )

    def pw_arrived(*order):
        for m in order:
            pw_copy(m).wait_recv()

    def stream(st):
        span = pl.ds(st * rb, rb)
        n = len(CHAIN)
        for k in range(n):
            rs_chain(0, st, k)
            yield
            if st == 0 and k == 0:
                for m in pw_order[5:]:
                    pw_copy(m).start()
                pw_arrived(2, -2)
                fill(1)
            if k < n - 1:
                rs_leaves(0, st, k + 1)
            yield
            if st == 0 and k < n - 1:
                pw_arrived(*{0: (3, -3), 1: (4,)}.get(k, ()))
                fill(k + 2)
            if st == 0 and k > 0:
                for copy in {1: pair[1:3], 2: pair[3:4], 3: pair[4:5]}[k]:
                    copy.start()
            yield
        zbuf[z, span, :] = rs_total(0, st).astype(BF16)
        for k in range(n):
            ag_chain(0, st, k)
            yield
            ag_leaves(0, st, k)
            yield
            if k == 1:
                rs_sent(0, st)
            if st == 0 and k == 2:
                for copy in pair:
                    copy.wait_send()
                for m in pw_order:
                    pw_copy(m).wait_send()
            if k == n - 1:
                if st == 0:
                    for i in range(1, 5):
                        loads[1 + i].wait()
                        pair[i].wait_recv()
                for off in between[:-1]:
                    for d in sides(st):
                        ag_arrived(0, d, st, off)
                head(st, 0, pieces // 2)
            yield
        ag_chain(0, st, n)
        for d in sides(st):
            ag_arrived(0, d, st, far - 1)
        head(st, pieces // 2, pieces)
        for k in range(n):
            rs_chain(1, st, k)
            yield
            if k < n - 1:
                rs_leaves(1, st, k + 1)
            yield
            if k == 1:
                ag_sent(0, st, 1, far)
            yield
        pgf[z, span, :] = rs_total(1, st).astype(BF16)
        for k in range(n + 1):
            ag_chain(1, st, k)
            yield
            ag_leaves(1, st, k)
            yield
            if k == 0:
                add_chunks(st, [0])
            else:
                offs = [CHAIN[k - 1]]
                for off in between:
                    if before(off) == ([0] + list(CHAIN))[k - 1]:
                        for d in sides(st):
                            ag_arrived(1, d, st, off)
                        offs.append(off)
                add_chunks(st, [s * off for off in offs for s in (1, -1) if s * off > -far])
            if k == 1:
                rs_sent(1, st)
            if k == n - 1:
                ag_sent(1, st, 1, CHAIN[n - 2])
            if k == n:
                hg_send[st] = acc_sib[:, span].astype(BF16)
                hg_copy(st).start()
            yield

    loads[0].wait()
    loads[1].wait()
    hid_rows[0] = hid[0].T
    pair[0].wait_recv()
    hid_rows[1] = hid[1].T
    pw_arrived(0, 1, -1)
    fill(0)
    head_slot = len(CHAIN) * 2
    last_slot = len(CHAIN) * 4
    running = [stream(st) for st in range(STREAMS)]
    beside = None
    for slot in range(last_slot + 1):
        for _ in range(3):
            for steps in running:
                next(steps)
        if slot == 0:
            prepare()
        if slot == head_slot:
            beside = plane()
        if beside is not None and next(beside, True):
            beside = None
    for steps in running:
        for _ in steps:
            pass
    if beside is not None:
        for _ in beside:
            pass

    total = pgf[0, pl.ds(rows, 16), :].astype(F32)
    for c in range(1, nz):
        total += pgf[c, pl.ds(rows, 16), :].astype(F32)
    loss_pair[core] = total
    ref = loss_pair.at[core]
    last = 6 + STREAMS
    loss_copy = copy_to(ref, ref, pair_send.at[last], pair_recv.at[last], task=sib)
    loss_copy.start()
    for st in range(STREAMS):
        ag_sent(1, st, CHAIN[-2] + 1, far)
    loss_copy.wait()
    total = loss_pair[0] + loss_pair[1]
    loss_out[0, 0] = jnp.sum(total) * loss_scale
    for st in range(STREAMS):
        span = pl.ds(st * rb, rb)
        hg_copy(st).wait()
        hg_out[:, span] = (acc_own[:, span] + hg_recv[st].astype(F32)).astype(BF16)


def shards(
    hidden, piece_weight, task_embed, task_bias, event_bin, censored, patient_id, patient_rows
):
    patients = patient_rows.shape[0]
    rows, depth = hidden.shape
    tasks, width = task_embed.shape
    pieces = task_bias.shape[1]
    n_task = lax.axis_size("task")
    nx, ny = lax.axis_size("row"), lax.axis_size("section")
    nz = n_task // 2
    half = pieces * width // 2
    bx = tasks // nx
    by = bx // ny
    vmem = pl.BlockSpec(memory_space=pltpu.VMEM)
    in_hbm = pl.BlockSpec(memory_space=pltpu.HBM)
    dma = pltpu.SemaphoreType.DMA
    hg, tg, loss = pl.pallas_call(
        functools.partial(kernel, 1.0 / (patients * tasks * n_task), 1.0 / patients),
        out_shape=(
            pltpu.VMEM((depth, rows), BF16),
            pltpu.VMEM((tasks, width), BF16),
            jax.ShapeDtypeStruct((1, 1), F32),
        ),
        in_specs=[in_hbm] * 8,
        out_specs=(vmem, vmem, pl.BlockSpec(memory_space=pltpu.SMEM)),
        scratch_shapes=[
            pltpu.VMEM((1, rows), jnp.int32),
            pltpu.VMEM((1, patients), jnp.int32),
            pltpu.VMEM((2, depth, rows), BF16),
            pltpu.VMEM((2, rows, depth), BF16),
            pltpu.VMEM((2, depth, half), BF16),
            pltpu.VMEM((2, tasks, width), BF16),
            pltpu.VMEM((2, pieces, tasks), F32),
            pltpu.VMEM((2, rows, tasks), jnp.int32),
            pltpu.VMEM((2, rows, tasks), jnp.int32),
            pltpu.VMEM((rows, tasks), F32),
            pltpu.VMEM((nz, rows, LANES), F32),
            pltpu.VMEM((2, 2, nz // 2, rows, LANES), BF16),
            pltpu.VMEM((2, 2, nz // 2, rows, LANES), BF16),
            pltpu.VMEM((nz, rows, LANES), BF16),
            pltpu.VMEM((nz, rows + 16, LANES), BF16),
            pltpu.VMEM((2, pieces // 2, rows, tasks), BF16),
            pltpu.VMEM((8, tasks), F32),
            pltpu.VMEM((nx, 8, LANES), F32),
            pltpu.VMEM((ny, 8, LANES), F32),
            pltpu.VMEM((2, 16, LANES), F32),
            pltpu.VMEM((2, tasks, width), F32),
            pltpu.VMEM((tasks, width), BF16),
            pltpu.VMEM((tasks, width), BF16),
            pltpu.VMEM((tasks, width), BF16),
            pltpu.VMEM((nx - 1, bx, width), BF16),
            pltpu.VMEM((bx, width), BF16),
            pltpu.VMEM((ny - 1, by, width), BF16),
            pltpu.VMEM((tasks, width), BF16),
            pltpu.VMEM((depth, rows), F32),
            pltpu.VMEM((depth, rows), F32),
            pltpu.VMEM((STREAMS, depth, rows // STREAMS), BF16),
            pltpu.VMEM((STREAMS, depth, rows // STREAMS), BF16),
            dma((4, 2, STREAMS, nz // 2)),
            dma((4, 2, STREAMS, nz // 2)),
            dma((8,)),
            dma((7 + STREAMS,)),
            dma((7 + STREAMS,)),
            dma((nz // 2,)),
            dma((nz // 2,)),
            dma((3, nx - 1)),
            dma((3, nx - 1)),
            dma((3, ny - 1)),
            dma((3, ny - 1)),
        ],
        compiler_params=pltpu.CompilerParams(
            collective_id=0, has_side_effects=True, vmem_limit_bytes=60 * 1024 * 1024
        ),
        cost_estimate=pl.CostEstimate(
            flops=2400000000, bytes_accessed=4000000, transcendentals=600000
        ),
    )(
        hidden.T,
        piece_weight,
        task_embed,
        task_bias.T,
        event_bin,
        censored,
        patient_id.reshape(1, rows),
        patient_rows.reshape(1, patients),
    )
    return hg.T, tg.astype(F32), loss.reshape(())


def solution(mesh):
    return jax.shard_map(
        shards,
        mesh=mesh,
        in_specs=(
            P(("section", "row"), "task"),
            P("task", None),
            P("task", None),
            P("task", None),
            P(("section", "row"), "task"),
            P(("section", "row"), "task"),
            P(("section", "row")),
            P(),
        ),
        out_specs=(P(("section", "row"), "task"), P("task", None), P()),
        check_vma=False,
    )
```

```python
import functools

import jax
import jax.numpy as jnp
from jax import lax
from jax.experimental import pallas as pl
from jax.experimental.pallas import tpu as pltpu
from jax.sharding import PartitionSpec as P

MESH = pl.DeviceIdType.MESH
F32 = jnp.float32
BF16 = jnp.bfloat16
LANES = 128
STREAMS = 2
CHAIN = (2, 4, 6, 8)
NT = (((1,), (1,)), ((), ()))
TN = (((0,), (0,)), ((), ()))


def kernel(
    loss_scale,
    grad_scale,
    hid_hbm,
    pw_hbm,
    te_hbm,
    bias_hbm,
    bins_hbm,
    cens_hbm,
    pid_hbm,
    prow_hbm,
    hg_out,
    tg_out,
    loss_out,
    pid_ref,
    prow_ref,
    hid,
    hid_rows,
    pw,
    te,
    bias,
    bins,
    cens,
    wrow,
    part,
    rs_out,
    rs_in,
    zbuf,
    pgf,
    gbuf,
    loss_acc,
    loss_x,
    loss_y,
    loss_pair,
    tg_acc,
    tg_send,
    tg_recv,
    tx_send,
    tx_recv,
    ty_send,
    ty_recv,
    tg_fin,
    acc_own,
    acc_sib,
    hg_send,
    hg_recv,
    send_sem,
    recv_sem,
    local_sem,
    pair_send,
    pair_recv,
    pw_send,
    pw_recv,
    px_send,
    px_recv,
    py_send,
    py_recv,
):
    rows = hid.shape[2]
    half_cols = pw.shape[2]
    tasks = te.shape[1]
    nz = part.shape[0]
    far = nz // 2
    pieces = half_cols // te.shape[2]
    per_piece = nz // pieces
    rb = rows // STREAMS
    nx = lax.axis_size("row")
    ny = lax.axis_size("section")
    task = lax.axis_index("task")
    x = lax.axis_index("row")
    y = lax.axis_index("section")
    z = task // 2
    core = task % 2
    sib = z * 2 + 1 - core

    def wrap(v):
        return (v + 2 * nz) % nz

    def z_dev(off):
        return wrap(z + off) * 2 + core

    def copy_to(src, dst, ss, rs, **where):
        return pltpu.make_async_remote_copy(
            src_ref=src,
            dst_ref=dst,
            send_sem=ss,
            recv_sem=rs,
            device_id=where,
            device_id_type=MESH,
        )

    mine = pl.ds(pl.multiple_of(core * half_cols, half_cols), half_cols)
    loads = [
        (hid_hbm, hid.at[0]),
        (pw_hbm.at[:, mine], pw.at[0]),
        (te_hbm, te.at[0]),
        (bias_hbm, bias.at[0]),
        (bins_hbm, bins.at[0]),
        (cens_hbm, cens.at[0]),
        (pid_hbm, pid_ref),
        (prow_hbm, prow_ref),
    ]
    loads = [pltpu.make_async_copy(a, b, local_sem.at[i]) for i, (a, b) in enumerate(loads)]
    for load in loads[:2]:
        load.start()

    barrier = pltpu.get_barrier_semaphore()
    strides = sorted({b - a for a, b in zip((0,) + CHAIN, CHAIN)} | {1})
    peers = [dict(task=sib)] + [dict(task=z_dev(s * n)) for n in strides for s in (1, -1)]
    peers += [dict(row=(x + j) % nx) for j in range(1, nx)]
    peers += [dict(section=(y + j) % ny) for j in range(1, ny)]
    for peer in peers:
        pl.semaphore_signal(barrier, inc=1, device_id=peer, device_id_type=MESH)
    pl.semaphore_wait(barrier, len(peers))

    pair = [
        (hid_hbm, hid.at[1]),
        (te_hbm, te.at[1]),
        (bias_hbm, bias.at[1]),
        (bins_hbm, bins.at[1]),
        (cens_hbm, cens.at[1]),
    ]
    pair = [
        copy_to(a, b, pair_send.at[i], pair_recv.at[i], task=sib) for i, (a, b) in enumerate(pair)
    ]

    part_cols = half_cols // far

    def pw_copy(n):
        q = (wrap(z + far) // 2 + n + far) % far
        there = pl.ds(
            pl.multiple_of((1 - core) * half_cols + q * part_cols, part_cols), part_cols
        )
        here = pl.ds(pl.multiple_of(q * part_cols, part_cols), part_cols)
        return copy_to(
            pw_hbm.at[:, there], pw.at[1, :, here], pw_send.at[q], pw_recv.at[q], task=sib
        )

    pw_order = [0] + [s * n for n in range(1, far // 2) for s in (1, -1)] + [far // 2]
    pair[0].start()
    for n in pw_order[:5]:
        pw_copy(n).start()
    for load in loads[2:]:
        load.start()

    def long_way(st):
        return 0 if st < STREAMS // 2 else 1

    def stops(d, st):
        return [c for c in CHAIN if c < far or d == long_way(st)]

    def before(off):
        return max([0] + [c for c in CHAIN if c < off])

    def behind(stop, d, st):
        last = far if d == long_way(st) else far - 1
        found = [off for off in range(1, last + 1) if before(off) == stop]
        return sorted(found, key=lambda off: off not in CHAIN)

    def sides(st):
        return (long_way(st), 1 - long_way(st))

    def rs_copy(ph, d, st, off):
        span = pl.ds(st * rb, rb)
        return copy_to(
            rs_out.at[ph, d, off - 1, span, :],
            rs_in.at[ph, d, off - 1, span, :],
            send_sem.at[2 * ph, d, st, off - 1],
            recv_sem.at[2 * ph, d, st, off - 1],
            task=z_dev((1 - 2 * d) * (off - before(off))),
        )

    def cols(c):
        return pl.ds(pl.multiple_of(c * LANES, LANES), LANES)

    def fill(k):
        stop = ([0] + list(CHAIN))[-1 - k]
        for off in [stop] + list(range(before(stop) + 1, stop)):
            chunks = [wrap(z + off)] if off in (0, far) else [wrap(z - off), wrap(z + off)]
            total = None
            for h in range(2):
                w = jnp.concatenate([pw[h, :, cols(c)] for c in chunks], axis=1)
                dots = jnp.dot(hid_rows[h], w, preferred_element_type=F32)
                total = dots if total is None else total + dots
            for i, c in enumerate(chunks):
                part[c] = total[:, i * LANES : (i + 1) * LANES]

    def rs_send(ph, d, st, off):
        span = pl.ds(st * rb, rb)
        total = part[wrap(z + (1 - 2 * d) * off), span, :]
        if off in stops(d, st):
            for other in behind(off, d, st):
                rs_copy(ph, d, st, other).wait_recv()
                total += rs_in[ph, d, other - 1, span, :].astype(F32)
        rs_out[ph, d, off - 1, span, :] = total.astype(BF16)
        rs_copy(ph, d, st, off).start()

    def rs_total(ph, st):
        span = pl.ds(st * rb, rb)
        total = part[z, span, :]
        for d in sides(st):
            for other in behind(0, d, st):
                rs_copy(ph, d, st, other).wait_recv()
                total += rs_in[ph, d, other - 1, span, :].astype(F32)
        return total

    def rs_chain(ph, st, k):
        stop = ([0] + list(CHAIN))[-1 - k]
        for d in sides(st):
            if k == 0:
                rs_send(ph, d, st, far if d == long_way(st) else far - 1)
            elif stop != far - 1 or d == long_way(st):
                rs_send(ph, d, st, stop)
        if k == 0:
            rs_leaves(ph, st, 0)

    def rs_leaves(ph, st, k):
        stop = ([0] + list(CHAIN))[-1 - k]
        for off in range(stop - 1, before(stop), -1):
            for d in sides(st):
                if off != far - 1 or d == long_way(st):
                    rs_send(ph, d, st, off)

    def rs_sent(ph, st):
        for d in range(2):
            for off in range(1, far + 1 if d == long_way(st) else far):
                rs_copy(ph, d, st, off).wait_send()

    def ag_copy(ph, d, st, off):
        buf = zbuf if ph == 0 else pgf
        extra = 16 if ph == 1 and st == STREAMS - 1 else 0
        sgn = 1 - 2 * d
        ref = buf.at[wrap(z - sgn * before(off)), pl.ds(st * rb, rb + extra), :]
        return copy_to(
            ref,
            ref,
            send_sem.at[2 * ph + 1, d, st, off - 1],
            recv_sem.at[2 * ph + 1, d, st, off - 1],
            task=z_dev(sgn * (off - before(off))),
        )

    def ag_arrived(ph, d, st, off):
        buf = zbuf if ph == 0 else pgf
        extra = 16 if ph == 1 and st == STREAMS - 1 else 0
        sgn = 1 - 2 * d
        if off < far or d == long_way(st):
            ref = buf.at[wrap(z - sgn * off), pl.ds(st * rb, rb + extra), :]
            copy_to(
                ref,
                ref,
                send_sem.at[2 * ph + 1, d, st, off - 1],
                recv_sem.at[2 * ph + 1, d, st, off - 1],
                task=z_dev(sgn * (off - before(off))),
            ).wait_recv()

    def ag_chain(ph, st, k):
        stop = ([0] + list(CHAIN))[k]
        for d in sides(st):
            if k > 0:
                ag_arrived(ph, d, st, stop)
            for off in behind(stop, d, st)[:1]:
                ag_copy(ph, d, st, off).start()

    def ag_leaves(ph, st, k):
        stop = ([0] + list(CHAIN))[k]
        for d in sides(st):
            for off in behind(stop, d, st)[1:]:
                ag_copy(ph, d, st, off).start()

    def ag_sent(ph, st, first, last):
        for d in range(2):
            for off in range(first, last + 1):
                if off < far or d == long_way(st):
                    ag_copy(ph, d, st, off).wait_send()

    between = [off for off in range(1, far) if off not in CHAIN]

    def prepare():
        loads[6].wait()
        loads[7].wait()
        ids = jnp.broadcast_to(pid_ref[...].astype(F32), (prow_ref.shape[1], rows)).T
        lane = lax.broadcasted_iota(jnp.int32, ids.shape, 1).astype(F32)
        record = jnp.where(ids == lane, prow_ref[...].astype(F32), 0.0)
        weight = 1.0 / jnp.sum(record, axis=1, keepdims=True)
        wrow[...] = jnp.broadcast_to(weight, wrow.shape)
        loss_acc[...] = jnp.zeros_like(loss_acc)
        tg_acc[...] = jnp.zeros_like(tg_acc)
        acc_own[...] = jnp.zeros_like(acc_own)
        acc_sib[...] = jnp.zeros_like(acc_sib)

    late = (wrap(z + far + 1) // per_piece) % pieces
    near = z // per_piece
    aside = (2 * late + 3 - near + pieces) % pieces
    rest = [(late + 3) % pieces, late]

    def head(st, order):
        span = pl.ds(st * rb, rb)
        zs = jnp.concatenate(
            [
                jnp.concatenate(
                    [zbuf[p * per_piece + k, span, :] for k in range(per_piece)], axis=1
                )
                for p in order
            ],
            axis=0,
        )
        total = None
        for h in range(2):
            dots = lax.dot_general(zs, te[h], NT, preferred_element_type=F32)
            edge = bins[h, span, :]
            alive = (1 - cens[h, span, :]).astype(F32)
            weight = wrow[span, :]
            grads = []
            nll = None
            for i, p in enumerate(order):
                piece = core * pieces + p
                logits = dots[i * rb : (i + 1) * rb] + bias[h, pl.ds(piece, 1), :]
                hazard = jnp.exp(logits)
                at = edge == piece
                hazard = jnp.where(edge > piece, hazard, jnp.where(at, 0.5 * hazard, 0.0))
                event = jnp.where(at, alive, 0.0)
                term = hazard - event * logits
                nll = term if nll is None else nll + term
                grad = (weight * (hazard - event)).astype(BF16)
                gbuf[h, p, span, :] = grad
                grads.append(grad)
            nll = (weight * nll).reshape(rb // 8, 8, tasks).sum(axis=0)
            loss_acc[...] += nll
            grads = jnp.concatenate(grads, axis=0)
            dots = jnp.dot(grads, te[h], preferred_element_type=F32)
            total = dots if total is None else total + dots
        for i, p in enumerate(order):
            for k in range(per_piece):
                part[p * per_piece + k, span, :] = total[
                    i * rb : (i + 1) * rb, k * LANES : (k + 1) * LANES
                ]

    def x_copy(j, src, dst, k):
        return copy_to(
            src, dst, px_send.at[k, j - 1], px_recv.at[k, j - 1], row=(x + j) % nx
        )

    def y_copy(j, src, dst, k):
        return copy_to(
            src, dst, py_send.at[k, j - 1], py_recv.at[k, j - 1], section=(y + j) % ny
        )

    def loss_x_copy(j):
        return x_copy(j, loss_x.at[x], loss_x.at[x], 0)

    def loss_y_copy(j):
        return y_copy(j, loss_y.at[y], loss_y.at[y], 0)

    bx = tasks // nx
    by = bx // ny

    def tgx_copy(j):
        peer = (x + j) % nx
        src = tx_send.at[pl.ds(pl.multiple_of(peer * bx, bx), bx), :]
        return x_copy(j, src, tx_recv.at[j - 1], 1)

    def tgy_copy(j):
        peer = (y + j) % ny
        src = ty_send.at[pl.ds(pl.multiple_of(peer * by, by), by), :]
        return y_copy(j, src, ty_recv.at[j - 1], 1)

    def agy_copy(j):
        ref = tg_fin.at[pl.ds(pl.multiple_of(x * bx + y * by, by), by), :]
        return y_copy(j, ref, ref, 2)

    def agx_copy(j):
        ref = tg_fin.at[pl.ds(pl.multiple_of(x * bx, bx), bx), :]
        return x_copy(j, ref, ref, 2)

    tg_copy = copy_to(tg_send, tg_recv, pair_send.at[5], pair_recv.at[5], task=sib)

    def tg_piece(p):
        zp = jnp.concatenate([zbuf[p * per_piece + k] for k in range(per_piece)], axis=1)
        for h in range(2):
            tg_acc[h] += lax.dot_general(gbuf[h, p], zp, TN, preferred_element_type=F32)

    def loss_terms():
        own = sum(loss_y[i] for i in range(1, ny)) + loss_y[0]
        own = jnp.sum(jnp.sum(own, axis=0, keepdims=True), axis=1, keepdims=True)
        own = jnp.broadcast_to(own, (16, LANES))
        place = lax.broadcasted_iota(jnp.int32, own.shape, 1)
        place += LANES * lax.broadcasted_iota(jnp.int32, own.shape, 0)
        high = own.astype(BF16).astype(F32)
        rest = own - high
        middle = rest.astype(BF16).astype(F32)
        low = rest - middle
        terms = jnp.where(
            place == 0, high, jnp.where(place == 1, middle, jnp.where(place == 2, low, 0.0))
        )
        pgf[z, pl.ds(rows, 16), :] = terms.astype(BF16)

    def plane():
        loss_x[x] = loss_acc[:, :LANES] + loss_acc[:, LANES:]
        for j in range(1, nx):
            loss_x_copy(j).start()
        tg_piece(0)
        yield
        for j in range(1, nx):
            loss_x_copy(j).wait()
        loss_y[y] = sum(loss_x[i] for i in range(1, nx)) + loss_x[0]
        for j in range(1, ny):
            loss_y_copy(j).start()
        tg_piece(1)
        yield
        tg_piece(2)
        for j in range(1, ny):
            loss_y_copy(j).wait()
        loss_terms()
        yield
        tg_piece(3)
        tg_send[...] = tg_acc[1].astype(BF16)
        tg_copy.start()
        yield
        tg_copy.wait()
        tg_acc[0] += tg_recv[...].astype(F32)
        tx_send[...] = tg_acc[0].astype(BF16)
        for j in range(1, nx):
            tgx_copy(j).start()
        yield
        total = tg_acc[0, pl.ds(pl.multiple_of(x * bx, bx), bx), :]
        for j in range(1, nx):
            tgx_copy(j).wait()
            total += tx_recv[j - 1].astype(F32)
        tg_acc[0, pl.ds(0, bx), :] = total
        ty_send[...] = total.astype(BF16)
        for j in range(1, ny):
            tgy_copy(j).start()
        yield
        total = tg_acc[0, pl.ds(pl.multiple_of(y * by, by), by), :]
        for j in range(1, ny):
            tgy_copy(j).wait()
            total += ty_recv[j - 1].astype(F32)
        place = pl.ds(pl.multiple_of(x * bx + y * by, by), by)
        tg_fin[place, :] = (total * grad_scale).astype(BF16)
        for j in range(1, ny):
            agy_copy(j).start()
        yield
        for j in range(1, ny):
            agy_copy(j).wait_send()
            from_y = (y + ny - j) % ny
            ref = tg_fin.at[pl.ds(pl.multiple_of(x * bx + from_y * by, by), by), :]
            y_copy(j, ref, ref, 2).wait_recv()
        for j in range(1, nx):
            agx_copy(j).start()
        yield
        for j in range(1, nx):
            agx_copy(j).wait_send()
            from_x = (x + nx - j) % nx
            ref = tg_fin.at[pl.ds(pl.multiple_of(from_x * bx, bx), bx), :]
            x_copy(j, ref, ref, 2).wait_recv()
        tg_out[...] = tg_fin[...]

    def add_chunks(st, offs):
        span = pl.ds(st * rb, rb)
        chunks = [wrap(z + off) for off in offs]
        value = jnp.concatenate([pgf[c, span, :] for c in chunks], axis=1)
        for h, acc in ((0, acc_own), (1, acc_sib)):
            w = jnp.concatenate([pw[h, :, cols(c)] for c in chunks], axis=1)
            acc[:, span] += lax.dot_general(w, value, NT, preferred_element_type=F32)

    def hg_copy(st):
        return copy_to(
            hg_send.at[st], hg_recv.at[st], pair_send.at[6 + st], pair_recv.at[6 + st], task=sib
        )

    def pw_arrived(*order):
        for m in order:
            pw_copy(m).wait_recv()

    def stream(st):
        span = pl.ds(st * rb, rb)
        n = len(CHAIN)
        for k in range(n):
            rs_chain(0, st, k)
            yield
            if st == 0 and k == 0:
                for m in pw_order[5:]:
                    pw_copy(m).start()
                pw_arrived(2, -2)
                fill(1)
            if k < n - 1:
                rs_leaves(0, st, k + 1)
            yield
            if st == 0 and k < n - 1:
                pw_arrived(*{0: (3, -3), 1: (4,)}.get(k, ()))
                fill(k + 2)
            if st == 0 and k > 0:
                for copy in {1: pair[1:3], 2: pair[3:4], 3: pair[4:5]}[k]:
                    copy.start()
            yield
        zbuf[z, span, :] = rs_total(0, st).astype(BF16)
        for k in range(n):
            ag_chain(0, st, k)
            yield
            ag_leaves(0, st, k)
            yield
            if k == 1:
                rs_sent(0, st)
            if st == 0 and k == 2:
                for copy in pair:
                    copy.wait_send()
                for m in pw_order:
                    pw_copy(m).wait_send()
            if k == n - 2:
                if st == 0:
                    for i in range(1, 5):
                        loads[1 + i].wait()
                        pair[i].wait_recv()
                for off in between[:-2]:
                    for d in sides(st):
                        ag_arrived(0, d, st, off)
                head(st, [near])
            if k == n - 1:
                for d in sides(st):
                    ag_arrived(0, d, st, between[-2])
                head(st, [aside])
            yield
        ag_chain(0, st, n)
        for d in sides(st):
            ag_arrived(0, d, st, far - 1)
        head(st, rest)
        for k in range(n):
            rs_chain(1, st, k)
            yield
            if k < n - 1:
                rs_leaves(1, st, k + 1)
            yield
            if k == 1:
                ag_sent(0, st, 1, far)
            yield
        pgf[z, span, :] = rs_total(1, st).astype(BF16)
        for k in range(n + 1):
            ag_chain(1, st, k)
            yield
            ag_leaves(1, st, k)
            yield
            if k == 0:
                add_chunks(st, [0])
            else:
                offs = [CHAIN[k - 1]]
                for off in between:
                    if before(off) == ([0] + list(CHAIN))[k - 1]:
                        for d in sides(st):
                            ag_arrived(1, d, st, off)
                        offs.append(off)
                add_chunks(st, [s * off for off in offs for s in (1, -1) if s * off > -far])
            if k == 1:
                rs_sent(1, st)
            if k == n - 1:
                ag_sent(1, st, 1, CHAIN[n - 2])
            if k == n:
                hg_send[st] = acc_sib[:, span].astype(BF16)
                hg_copy(st).start()
            yield

    loads[0].wait()
    loads[1].wait()
    hid_rows[0] = hid[0].T
    pair[0].wait_recv()
    hid_rows[1] = hid[1].T
    pw_arrived(0, 1, -1)
    fill(0)
    head_slot = len(CHAIN) * 2
    last_slot = len(CHAIN) * 4
    running = [stream(st) for st in range(STREAMS)]
    beside = None
    for slot in range(last_slot + 1):
        for _ in range(3):
            for steps in running:
                next(steps)
        if slot == 0:
            prepare()
        if slot == head_slot:
            beside = plane()
        if beside is not None and next(beside, True):
            beside = None
    for steps in running:
        for _ in steps:
            pass
    if beside is not None:
        for _ in beside:
            pass

    total = pgf[0, pl.ds(rows, 16), :].astype(F32)
    for c in range(1, nz):
        total += pgf[c, pl.ds(rows, 16), :].astype(F32)
    loss_pair[core] = total
    ref = loss_pair.at[core]
    last = 6 + STREAMS
    loss_copy = copy_to(ref, ref, pair_send.at[last], pair_recv.at[last], task=sib)
    loss_copy.start()
    for st in range(STREAMS):
        ag_sent(1, st, CHAIN[-2] + 1, far)
    loss_copy.wait()
    total = loss_pair[0] + loss_pair[1]
    loss_out[0, 0] = jnp.sum(total) * loss_scale
    for st in range(STREAMS):
        span = pl.ds(st * rb, rb)
        hg_copy(st).wait()
        hg_out[:, span] = (acc_own[:, span] + hg_recv[st].astype(F32)).astype(BF16)


def shards(
    hidden, piece_weight, task_embed, task_bias, event_bin, censored, patient_id, patient_rows
):
    patients = patient_rows.shape[0]
    rows, depth = hidden.shape
    tasks, width = task_embed.shape
    pieces = task_bias.shape[1]
    n_task = lax.axis_size("task")
    nx, ny = lax.axis_size("row"), lax.axis_size("section")
    nz = n_task // 2
    half = pieces * width // 2
    bx = tasks // nx
    by = bx // ny
    vmem = pl.BlockSpec(memory_space=pltpu.VMEM)
    in_hbm = pl.BlockSpec(memory_space=pltpu.HBM)
    dma = pltpu.SemaphoreType.DMA
    hg, tg, loss = pl.pallas_call(
        functools.partial(kernel, 1.0 / (patients * tasks * n_task), 1.0 / patients),
        out_shape=(
            pltpu.VMEM((depth, rows), BF16),
            pltpu.VMEM((tasks, width), BF16),
            jax.ShapeDtypeStruct((1, 1), F32),
        ),
        in_specs=[in_hbm] * 8,
        out_specs=(vmem, vmem, pl.BlockSpec(memory_space=pltpu.SMEM)),
        scratch_shapes=[
            pltpu.VMEM((1, rows), jnp.int32),
            pltpu.VMEM((1, patients), jnp.int32),
            pltpu.VMEM((2, depth, rows), BF16),
            pltpu.VMEM((2, rows, depth), BF16),
            pltpu.VMEM((2, depth, half), BF16),
            pltpu.VMEM((2, tasks, width), BF16),
            pltpu.VMEM((2, pieces, tasks), F32),
            pltpu.VMEM((2, rows, tasks), jnp.int32),
            pltpu.VMEM((2, rows, tasks), jnp.int32),
            pltpu.VMEM((rows, tasks), F32),
            pltpu.VMEM((nz, rows, LANES), F32),
            pltpu.VMEM((2, 2, nz // 2, rows, LANES), BF16),
            pltpu.VMEM((2, 2, nz // 2, rows, LANES), BF16),
            pltpu.VMEM((nz, rows, LANES), BF16),
            pltpu.VMEM((nz, rows + 16, LANES), BF16),
            pltpu.VMEM((2, pieces // 2, rows, tasks), BF16),
            pltpu.VMEM((8, tasks), F32),
            pltpu.VMEM((nx, 8, LANES), F32),
            pltpu.VMEM((ny, 8, LANES), F32),
            pltpu.VMEM((2, 16, LANES), F32),
            pltpu.VMEM((2, tasks, width), F32),
            pltpu.VMEM((tasks, width), BF16),
            pltpu.VMEM((tasks, width), BF16),
            pltpu.VMEM((tasks, width), BF16),
            pltpu.VMEM((nx - 1, bx, width), BF16),
            pltpu.VMEM((bx, width), BF16),
            pltpu.VMEM((ny - 1, by, width), BF16),
            pltpu.VMEM((tasks, width), BF16),
            pltpu.VMEM((depth, rows), F32),
            pltpu.VMEM((depth, rows), F32),
            pltpu.VMEM((STREAMS, depth, rows // STREAMS), BF16),
            pltpu.VMEM((STREAMS, depth, rows // STREAMS), BF16),
            dma((4, 2, STREAMS, nz // 2)),
            dma((4, 2, STREAMS, nz // 2)),
            dma((8,)),
            dma((7 + STREAMS,)),
            dma((7 + STREAMS,)),
            dma((nz // 2,)),
            dma((nz // 2,)),
            dma((3, nx - 1)),
            dma((3, nx - 1)),
            dma((3, ny - 1)),
            dma((3, ny - 1)),
        ],
        compiler_params=pltpu.CompilerParams(
            collective_id=0, has_side_effects=True, vmem_limit_bytes=60 * 1024 * 1024
        ),
        cost_estimate=pl.CostEstimate(
            flops=2400000000, bytes_accessed=4000000, transcendentals=600000
        ),
    )(
        hidden.T,
        piece_weight,
        task_embed,
        task_bias.T,
        event_bin,
        censored,
        patient_id.reshape(1, rows),
        patient_rows.reshape(1, patients),
    )
    return hg.T, tg.astype(F32), loss.reshape(())


def solution(mesh):
    return jax.shard_map(
        shards,
        mesh=mesh,
        in_specs=(
            P(("section", "row"), "task"),
            P("task", None),
            P("task", None),
            P("task", None),
            P(("section", "row"), "task"),
            P(("section", "row"), "task"),
            P(("section", "row")),
            P(),
        ),
        out_specs=(P(("section", "row"), "task"), P("task", None), P()),
        check_vma=False,
    )
```

```python
import functools

import jax
import jax.numpy as jnp
from jax import lax
from jax.experimental import pallas as pl
from jax.experimental.pallas import tpu as pltpu
from jax.sharding import PartitionSpec as P

MESH = pl.DeviceIdType.MESH
F32 = jnp.float32
BF16 = jnp.bfloat16
LANES = 128
STREAMS = 2
CHAIN = (2, 4, 6, 8)
NT = (((1,), (1,)), ((), ()))
TN = (((0,), (0,)), ((), ()))


def kernel(
    loss_scale,
    grad_scale,
    hid_hbm,
    pw_hbm,
    te_hbm,
    bias_hbm,
    bins_hbm,
    cens_hbm,
    pid_hbm,
    prow_hbm,
    hg_out,
    tg_out,
    loss_out,
    pid_ref,
    prow_ref,
    hid,
    hid_rows,
    pw,
    te,
    te_t,
    bias,
    bins,
    cens,
    wrow,
    part,
    rs_out,
    rs_in,
    zbuf,
    pgf,
    gbuf,
    loss_acc,
    loss_x,
    loss_y,
    loss_pair,
    tg_acc,
    tg_send,
    tg_recv,
    tx_send,
    tx_recv,
    ty_send,
    ty_recv,
    tg_fin,
    acc_own,
    acc_sib,
    hg_send,
    hg_recv,
    send_sem,
    recv_sem,
    local_sem,
    pair_send,
    pair_recv,
    pw_send,
    pw_recv,
    px_send,
    px_recv,
    py_send,
    py_recv,
):
    rows = hid.shape[2]
    half_cols = pw.shape[2]
    tasks = te.shape[1]
    nz = part.shape[0]
    far = nz // 2
    pieces = half_cols // te.shape[2]
    per_piece = nz // pieces
    rb = rows // STREAMS
    nx = lax.axis_size("row")
    ny = lax.axis_size("section")
    task = lax.axis_index("task")
    x = lax.axis_index("row")
    y = lax.axis_index("section")
    z = task // 2
    core = task % 2
    sib = z * 2 + 1 - core

    def wrap(v):
        return (v + 2 * nz) % nz

    def z_dev(off):
        return wrap(z + off) * 2 + core

    def copy_to(src, dst, ss, rs, **where):
        return pltpu.make_async_remote_copy(
            src_ref=src,
            dst_ref=dst,
            send_sem=ss,
            recv_sem=rs,
            device_id=where,
            device_id_type=MESH,
        )

    mine = pl.ds(pl.multiple_of(core * half_cols, half_cols), half_cols)
    loads = [
        (hid_hbm, hid.at[0]),
        (pw_hbm.at[:, mine], pw.at[0]),
        (te_hbm, te.at[0]),
        (bias_hbm, bias.at[0]),
        (bins_hbm, bins.at[0]),
        (cens_hbm, cens.at[0]),
        (pid_hbm, pid_ref),
        (prow_hbm, prow_ref),
    ]
    loads = [pltpu.make_async_copy(a, b, local_sem.at[i]) for i, (a, b) in enumerate(loads)]
    for load in loads[:2]:
        load.start()

    barrier = pltpu.get_barrier_semaphore()
    strides = sorted({b - a for a, b in zip((0,) + CHAIN, CHAIN)} | {1})
    peers = [dict(task=sib)] + [dict(task=z_dev(s * n)) for n in strides for s in (1, -1)]
    peers += [dict(row=(x + j) % nx) for j in range(1, nx)]
    peers += [dict(section=(y + j) % ny) for j in range(1, ny)]
    for peer in peers:
        pl.semaphore_signal(barrier, inc=1, device_id=peer, device_id_type=MESH)
    pl.semaphore_wait(barrier, len(peers))

    pair = [
        (hid_hbm, hid.at[1]),
        (te_hbm, te.at[1]),
        (bias_hbm, bias.at[1]),
        (bins_hbm, bins.at[1]),
        (cens_hbm, cens.at[1]),
    ]
    pair = [
        copy_to(a, b, pair_send.at[i], pair_recv.at[i], task=sib) for i, (a, b) in enumerate(pair)
    ]

    part_cols = half_cols // far

    def pw_copy(n):
        q = (wrap(z + far) // 2 + n + far) % far
        there = pl.ds(
            pl.multiple_of((1 - core) * half_cols + q * part_cols, part_cols), part_cols
        )
        here = pl.ds(pl.multiple_of(q * part_cols, part_cols), part_cols)
        return copy_to(
            pw_hbm.at[:, there], pw.at[1, :, here], pw_send.at[q], pw_recv.at[q], task=sib
        )

    pw_order = [0] + [s * n for n in range(1, far // 2) for s in (1, -1)] + [far // 2]
    pair[0].start()
    for n in pw_order[:5]:
        pw_copy(n).start()
    for load in loads[2:]:
        load.start()

    def long_way(st):
        return 0 if st < STREAMS // 2 else 1

    def stops(d, st):
        return [c for c in CHAIN if c < far or d == long_way(st)]

    def before(off):
        return max([0] + [c for c in CHAIN if c < off])

    def behind(stop, d, st):
        last = far if d == long_way(st) else far - 1
        found = [off for off in range(1, last + 1) if before(off) == stop]
        return sorted(found, key=lambda off: off not in CHAIN)

    def sides(st):
        return (long_way(st), 1 - long_way(st))

    def rs_copy(ph, d, st, off):
        span = pl.ds(st * rb, rb)
        return copy_to(
            rs_out.at[ph, d, off - 1, span, :],
            rs_in.at[ph, d, off - 1, span, :],
            send_sem.at[2 * ph, d, st, off - 1],
            recv_sem.at[2 * ph, d, st, off - 1],
            task=z_dev((1 - 2 * d) * (off - before(off))),
        )

    def cols(c):
        return pl.ds(pl.multiple_of(c * LANES, LANES), LANES)

    def fill(k):
        stop = ([0] + list(CHAIN))[-1 - k]
        for off in [stop] + list(range(before(stop) + 1, stop)):
            chunks = [wrap(z + off)] if off in (0, far) else [wrap(z - off), wrap(z + off)]
            total = None
            for h in range(2):
                w = jnp.concatenate([pw[h, :, cols(c)] for c in chunks], axis=1)
                dots = jnp.dot(hid_rows[h], w, preferred_element_type=F32)
                total = dots if total is None else total + dots
            for i, c in enumerate(chunks):
                part[c] = total[:, i * LANES : (i + 1) * LANES]

    def rs_send(ph, d, st, off):
        span = pl.ds(st * rb, rb)
        total = part[wrap(z + (1 - 2 * d) * off), span, :]
        if off in stops(d, st):
            for other in behind(off, d, st):
                rs_copy(ph, d, st, other).wait_recv()
                total += rs_in[ph, d, other - 1, span, :].astype(F32)
        rs_out[ph, d, off - 1, span, :] = total.astype(BF16)
        rs_copy(ph, d, st, off).start()

    def rs_total(ph, st):
        span = pl.ds(st * rb, rb)
        total = part[z, span, :]
        for d in sides(st):
            for other in behind(0, d, st):
                rs_copy(ph, d, st, other).wait_recv()
                total += rs_in[ph, d, other - 1, span, :].astype(F32)
        return total

    def rs_chain(ph, st, k):
        stop = ([0] + list(CHAIN))[-1 - k]
        for d in sides(st):
            if k == 0:
                rs_send(ph, d, st, far if d == long_way(st) else far - 1)
            elif stop != far - 1 or d == long_way(st):
                rs_send(ph, d, st, stop)
        if k == 0:
            rs_leaves(ph, st, 0)

    def rs_leaves(ph, st, k):
        stop = ([0] + list(CHAIN))[-1 - k]
        for off in range(stop - 1, before(stop), -1):
            for d in sides(st):
                if off != far - 1 or d == long_way(st):
                    rs_send(ph, d, st, off)

    def rs_sent(ph, st):
        for d in range(2):
            for off in range(1, far + 1 if d == long_way(st) else far):
                rs_copy(ph, d, st, off).wait_send()

    def ag_copy(ph, d, st, off):
        buf = zbuf if ph == 0 else pgf
        extra = 16 if ph == 1 and st == STREAMS - 1 else 0
        sgn = 1 - 2 * d
        ref = buf.at[wrap(z - sgn * before(off)), pl.ds(st * rb, rb + extra), :]
        return copy_to(
            ref,
            ref,
            send_sem.at[2 * ph + 1, d, st, off - 1],
            recv_sem.at[2 * ph + 1, d, st, off - 1],
            task=z_dev(sgn * (off - before(off))),
        )

    def ag_arrived(ph, d, st, off):
        buf = zbuf if ph == 0 else pgf
        extra = 16 if ph == 1 and st == STREAMS - 1 else 0
        sgn = 1 - 2 * d
        if off < far or d == long_way(st):
            ref = buf.at[wrap(z - sgn * off), pl.ds(st * rb, rb + extra), :]
            copy_to(
                ref,
                ref,
                send_sem.at[2 * ph + 1, d, st, off - 1],
                recv_sem.at[2 * ph + 1, d, st, off - 1],
                task=z_dev(sgn * (off - before(off))),
            ).wait_recv()

    def ag_chain(ph, st, k):
        stop = ([0] + list(CHAIN))[k]
        for d in sides(st):
            if k > 0:
                ag_arrived(ph, d, st, stop)
            for off in behind(stop, d, st)[:1]:
                ag_copy(ph, d, st, off).start()

    def ag_leaves(ph, st, k):
        stop = ([0] + list(CHAIN))[k]
        for d in sides(st):
            for off in behind(stop, d, st)[1:]:
                ag_copy(ph, d, st, off).start()

    def ag_sent(ph, st, first, last):
        for d in range(2):
            for off in range(first, last + 1):
                if off < far or d == long_way(st):
                    ag_copy(ph, d, st, off).wait_send()

    between = [off for off in range(1, far) if off not in CHAIN]

    def prepare():
        loads[6].wait()
        loads[7].wait()
        ids = jnp.broadcast_to(pid_ref[...].astype(F32), (prow_ref.shape[1], rows)).T
        lane = lax.broadcasted_iota(jnp.int32, ids.shape, 1).astype(F32)
        record = jnp.where(ids == lane, prow_ref[...].astype(F32), 0.0)
        weight = 1.0 / jnp.sum(record, axis=1, keepdims=True)
        wrow[...] = jnp.broadcast_to(weight, wrow.shape)
        loss_acc[...] = jnp.zeros_like(loss_acc)
        tg_acc[...] = jnp.zeros_like(tg_acc)
        acc_own[...] = jnp.zeros_like(acc_own)
        acc_sib[...] = jnp.zeros_like(acc_sib)

    late = (wrap(z + far + 1) // per_piece) % pieces

    def head(st, first, last):
        span = pl.ds(st * rb, rb)
        order = [(late + 1 + i) % pieces for i in range(first, last)]
        zs = jnp.concatenate(
            [
                jnp.concatenate(
                    [zbuf[p * per_piece + k, span, :] for k in range(per_piece)], axis=1
                )
                for p in order
            ],
            axis=0,
        )
        total = None
        for h in range(2):
            dots = jnp.dot(zs, te_t[h], preferred_element_type=F32)
            edge = bins[h, span, :]
            alive = (1 - cens[h, span, :]).astype(F32)
            weight = wrow[span, :]
            grads = []
            nll = None
            for i, p in enumerate(order):
                piece = core * pieces + p
                logits = dots[i * rb : (i + 1) * rb] + bias[h, pl.ds(piece, 1), :]
                hazard = jnp.exp(logits)
                at = edge == piece
                hazard = jnp.where(edge > piece, hazard, jnp.where(at, 0.5 * hazard, 0.0))
                event = jnp.where(at, alive, 0.0)
                term = hazard - event * logits
                nll = term if nll is None else nll + term
                grad = (weight * (hazard - event)).astype(BF16)
                gbuf[h, p, span, :] = grad
                grads.append(grad)
            nll = (weight * nll).reshape(rb // 8, 8, tasks).sum(axis=0)
            loss_acc[...] += nll
            grads = jnp.concatenate(grads, axis=0)
            dots = jnp.dot(grads, te[h], preferred_element_type=F32)
            total = dots if total is None else total + dots
        for i, p in enumerate(order):
            for k in range(per_piece):
                part[p * per_piece + k, span, :] = total[
                    i * rb : (i + 1) * rb, k * LANES : (k + 1) * LANES
                ]

    def x_copy(j, src, dst, k):
        return copy_to(
            src, dst, px_send.at[k, j - 1], px_recv.at[k, j - 1], row=(x + j) % nx
        )

    def y_copy(j, src, dst, k):
        return copy_to(
            src, dst, py_send.at[k, j - 1], py_recv.at[k, j - 1], section=(y + j) % ny
        )

    def loss_x_copy(j):
        return x_copy(j, loss_x.at[x], loss_x.at[x], 0)

    def loss_y_copy(j):
        return y_copy(j, loss_y.at[y], loss_y.at[y], 0)

    bx = tasks // nx
    by = bx // ny

    def tgx_copy(j):
        peer = (x + j) % nx
        src = tx_send.at[pl.ds(pl.multiple_of(peer * bx, bx), bx), :]
        return x_copy(j, src, tx_recv.at[j - 1], 1)

    def tgy_copy(j):
        peer = (y + j) % ny
        src = ty_send.at[pl.ds(pl.multiple_of(peer * by, by), by), :]
        return y_copy(j, src, ty_recv.at[j - 1], 1)

    def agy_copy(j):
        ref = tg_fin.at[pl.ds(pl.multiple_of(x * bx + y * by, by), by), :]
        return y_copy(j, ref, ref, 2)

    def agx_copy(j):
        ref = tg_fin.at[pl.ds(pl.multiple_of(x * bx, bx), bx), :]
        return x_copy(j, ref, ref, 2)

    tg_copy = copy_to(tg_send, tg_recv, pair_send.at[5], pair_recv.at[5], task=sib)

    def tg_piece(p):
        zp = jnp.concatenate([zbuf[p * per_piece + k] for k in range(per_piece)], axis=1)
        for h in range(2):
            tg_acc[h] += lax.dot_general(gbuf[h, p], zp, TN, preferred_element_type=F32)

    def loss_terms():
        own = sum(loss_y[i] for i in range(1, ny)) + loss_y[0]
        own = jnp.sum(jnp.sum(own, axis=0, keepdims=True), axis=1, keepdims=True)
        own = jnp.broadcast_to(own, (16, LANES))
        place = lax.broadcasted_iota(jnp.int32, own.shape, 1)
        place += LANES * lax.broadcasted_iota(jnp.int32, own.shape, 0)
        high = own.astype(BF16).astype(F32)
        rest = own - high
        middle = rest.astype(BF16).astype(F32)
        low = rest - middle
        terms = jnp.where(
            place == 0, high, jnp.where(place == 1, middle, jnp.where(place == 2, low, 0.0))
        )
        pgf[z, pl.ds(rows, 16), :] = terms.astype(BF16)

    def plane():
        loss_x[x] = loss_acc[:, :LANES] + loss_acc[:, LANES:]
        for j in range(1, nx):
            loss_x_copy(j).start()
        for p in range(pieces // 2):
            tg_piece(p)
        yield
        for p in range(pieces // 2, pieces):
            tg_piece(p)
        tg_send[...] = tg_acc[1].astype(BF16)
        tg_copy.start()
        for j in range(1, nx):
            loss_x_copy(j).wait()
        loss_y[y] = sum(loss_x[i] for i in range(1, nx)) + loss_x[0]
        for j in range(1, ny):
            loss_y_copy(j).start()
        yield
        tg_copy.wait()
        tg_acc[0] += tg_recv[...].astype(F32)
        tx_send[...] = tg_acc[0].astype(BF16)
        for j in range(1, nx):
            tgx_copy(j).start()
        for j in range(1, ny):
            loss_y_copy(j).wait()
        loss_terms()
        yield
        total = tg_acc[0, pl.ds(pl.multiple_of(x * bx, bx), bx), :]
        for j in range(1, nx):
            tgx_copy(j).wait()
            total += tx_recv[j - 1].astype(F32)
        tg_acc[0, pl.ds(0, bx), :] = total
        ty_send[...] = total.astype(BF16)
        for j in range(1, ny):
            tgy_copy(j).start()
        yield
        total = tg_acc[0, pl.ds(pl.multiple_of(y * by, by), by), :]
        for j in range(1, ny):
            tgy_copy(j).wait()
            total += ty_recv[j - 1].astype(F32)
        place = pl.ds(pl.multiple_of(x * bx + y * by, by), by)
        tg_fin[place, :] = (total * grad_scale).astype(BF16)
        for j in range(1, ny):
            agy_copy(j).start()
        yield
        for j in range(1, ny):
            agy_copy(j).wait_send()
            from_y = (y + ny - j) % ny
            ref = tg_fin.at[pl.ds(pl.multiple_of(x * bx + from_y * by, by), by), :]
            y_copy(j, ref, ref, 2).wait_recv()
        for j in range(1, nx):
            agx_copy(j).start()
        yield
        for j in range(1, nx):
            agx_copy(j).wait_send()
            from_x = (x + nx - j) % nx
            ref = tg_fin.at[pl.ds(pl.multiple_of(from_x * bx, bx), bx), :]
            x_copy(j, ref, ref, 2).wait_recv()
        tg_out[...] = tg_fin[...]

    def add_chunks(st, offs):
        span = pl.ds(st * rb, rb)
        chunks = [wrap(z + off) for off in offs]
        value = jnp.concatenate([pgf[c, span, :] for c in chunks], axis=1)
        for h, acc in ((0, acc_own), (1, acc_sib)):
            w = jnp.concatenate([pw[h, :, cols(c)] for c in chunks], axis=1)
            acc[:, span] += lax.dot_general(w, value, NT, preferred_element_type=F32)

    def hg_copy(st):
        return copy_to(
            hg_send.at[st], hg_recv.at[st], pair_send.at[6 + st], pair_recv.at[6 + st], task=sib
        )

    def pw_arrived(*order):
        for m in order:
            pw_copy(m).wait_recv()

    def stream(st):
        span = pl.ds(st * rb, rb)
        n = len(CHAIN)
        for k in range(n):
            rs_chain(0, st, k)
            yield
            if st == 0 and k == 0:
                for m in pw_order[5:]:
                    pw_copy(m).start()
                pw_arrived(2, -2)
                fill(1)
            if k < n - 1:
                rs_leaves(0, st, k + 1)
            yield
            if st == 0 and k < n - 1:
                pw_arrived(*{0: (3, -3), 1: (4,)}.get(k, ()))
                fill(k + 2)
            if st == 0 and k > 0:
                for copy in {1: pair[1:3], 2: pair[3:4], 3: pair[4:5]}[k]:
                    copy.start()
            yield
        zbuf[z, span, :] = rs_total(0, st).astype(BF16)
        for k in range(n):
            ag_chain(0, st, k)
            yield
            ag_leaves(0, st, k)
            yield
            if k == 1:
                rs_sent(0, st)
            if st == 0 and k == 0:
                loads[2].wait()
                pair[1].wait_recv()
                for h in range(2):
                    te_t[h] = te[h].T
            if st == 0 and k == 2:
                for copy in pair:
                    copy.wait_send()
                for m in pw_order:
                    pw_copy(m).wait_send()
            if k == n - 1:
                if st == 0:
                    for i in range(2, 5):
                        loads[1 + i].wait()
                        pair[i].wait_recv()
                for off in between[:-1]:
                    for d in sides(st):
                        ag_arrived(0, d, st, off)
                head(st, 0, pieces // 2)
            yield
        ag_chain(0, st, n)
        for d in sides(st):
            ag_arrived(0, d, st, far - 1)
        head(st, pieces // 2, pieces)
        for k in range(n):
            rs_chain(1, st, k)
            yield
            if k < n - 1:
                rs_leaves(1, st, k + 1)
            yield
            if k == 1:
                ag_sent(0, st, 1, far)
            yield
        pgf[z, span, :] = rs_total(1, st).astype(BF16)
        for k in range(n + 1):
            ag_chain(1, st, k)
            yield
            ag_leaves(1, st, k)
            yield
            if k == 0:
                add_chunks(st, [0])
            else:
                offs = [CHAIN[k - 1]]
                for off in between:
                    if before(off) == ([0] + list(CHAIN))[k - 1]:
                        for d in sides(st):
                            ag_arrived(1, d, st, off)
                        offs.append(off)
                add_chunks(st, [s * off for off in offs for s in (1, -1) if s * off > -far])
            if k == 1:
                rs_sent(1, st)
            if k == n - 1:
                ag_sent(1, st, 1, CHAIN[n - 2])
            if k == n:
                hg_send[st] = acc_sib[:, span].astype(BF16)
                hg_copy(st).start()
            yield

    loads[0].wait()
    loads[1].wait()
    hid_rows[0] = hid[0].T
    pair[0].wait_recv()
    hid_rows[1] = hid[1].T
    pw_arrived(0, 1, -1)
    fill(0)
    head_slot = len(CHAIN) * 2
    last_slot = len(CHAIN) * 4
    running = [stream(st) for st in range(STREAMS)]
    beside = None
    for slot in range(last_slot + 1):
        for _ in range(3):
            for steps in running:
                next(steps)
        if slot == 0:
            prepare()
        if slot == head_slot:
            beside = plane()
        if beside is not None and next(beside, True):
            beside = None
    for steps in running:
        for _ in steps:
            pass
    if beside is not None:
        for _ in beside:
            pass

    total = pgf[0, pl.ds(rows, 16), :].astype(F32)
    for c in range(1, nz):
        total += pgf[c, pl.ds(rows, 16), :].astype(F32)
    loss_pair[core] = total
    ref = loss_pair.at[core]
    last = 6 + STREAMS
    loss_copy = copy_to(ref, ref, pair_send.at[last], pair_recv.at[last], task=sib)
    loss_copy.start()
    for st in range(STREAMS):
        ag_sent(1, st, CHAIN[-2] + 1, far)
    loss_copy.wait()
    total = loss_pair[0] + loss_pair[1]
    loss_out[0, 0] = jnp.sum(total) * loss_scale
    for st in range(STREAMS):
        span = pl.ds(st * rb, rb)
        hg_copy(st).wait()
        hg_out[:, span] = (acc_own[:, span] + hg_recv[st].astype(F32)).astype(BF16)


def shards(
    hidden, piece_weight, task_embed, task_bias, event_bin, censored, patient_id, patient_rows
):
    patients = patient_rows.shape[0]
    rows, depth = hidden.shape
    tasks, width = task_embed.shape
    pieces = task_bias.shape[1]
    n_task = lax.axis_size("task")
    nx, ny = lax.axis_size("row"), lax.axis_size("section")
    nz = n_task // 2
    half = pieces * width // 2
    bx = tasks // nx
    by = bx // ny
    vmem = pl.BlockSpec(memory_space=pltpu.VMEM)
    in_hbm = pl.BlockSpec(memory_space=pltpu.HBM)
    dma = pltpu.SemaphoreType.DMA
    hg, tg, loss = pl.pallas_call(
        functools.partial(kernel, 1.0 / (patients * tasks * n_task), 1.0 / patients),
        out_shape=(
            pltpu.VMEM((depth, rows), BF16),
            pltpu.VMEM((tasks, width), BF16),
            jax.ShapeDtypeStruct((1, 1), F32),
        ),
        in_specs=[in_hbm] * 8,
        out_specs=(vmem, vmem, pl.BlockSpec(memory_space=pltpu.SMEM)),
        scratch_shapes=[
            pltpu.VMEM((1, rows), jnp.int32),
            pltpu.VMEM((1, patients), jnp.int32),
            pltpu.VMEM((2, depth, rows), BF16),
            pltpu.VMEM((2, rows, depth), BF16),
            pltpu.VMEM((2, depth, half), BF16),
            pltpu.VMEM((2, tasks, width), BF16),
            pltpu.VMEM((2, width, tasks), BF16),
            pltpu.VMEM((2, pieces, tasks), F32),
            pltpu.VMEM((2, rows, tasks), jnp.int32),
            pltpu.VMEM((2, rows, tasks), jnp.int32),
            pltpu.VMEM((rows, tasks), F32),
            pltpu.VMEM((nz, rows, LANES), F32),
            pltpu.VMEM((2, 2, nz // 2, rows, LANES), BF16),
            pltpu.VMEM((2, 2, nz // 2, rows, LANES), BF16),
            pltpu.VMEM((nz, rows, LANES), BF16),
            pltpu.VMEM((nz, rows + 16, LANES), BF16),
            pltpu.VMEM((2, pieces // 2, rows, tasks), BF16),
            pltpu.VMEM((8, tasks), F32),
            pltpu.VMEM((nx, 8, LANES), F32),
            pltpu.VMEM((ny, 8, LANES), F32),
            pltpu.VMEM((2, 16, LANES), F32),
            pltpu.VMEM((2, tasks, width), F32),
            pltpu.VMEM((tasks, width), BF16),
            pltpu.VMEM((tasks, width), BF16),
            pltpu.VMEM((tasks, width), BF16),
            pltpu.VMEM((nx - 1, bx, width), BF16),
            pltpu.VMEM((bx, width), BF16),
            pltpu.VMEM((ny - 1, by, width), BF16),
            pltpu.VMEM((tasks, width), BF16),
            pltpu.VMEM((depth, rows), F32),
            pltpu.VMEM((depth, rows), F32),
            pltpu.VMEM((STREAMS, depth, rows // STREAMS), BF16),
            pltpu.VMEM((STREAMS, depth, rows // STREAMS), BF16),
            dma((4, 2, STREAMS, nz // 2)),
            dma((4, 2, STREAMS, nz // 2)),
            dma((8,)),
            dma((7 + STREAMS,)),
            dma((7 + STREAMS,)),
            dma((nz // 2,)),
            dma((nz // 2,)),
            dma((3, nx - 1)),
            dma((3, nx - 1)),
            dma((3, ny - 1)),
            dma((3, ny - 1)),
        ],
        compiler_params=pltpu.CompilerParams(
            collective_id=0, has_side_effects=True, vmem_limit_bytes=60 * 1024 * 1024
        ),
        cost_estimate=pl.CostEstimate(
            flops=2400000000, bytes_accessed=4000000, transcendentals=600000
        ),
    )(
        hidden.T,
        piece_weight,
        task_embed,
        task_bias.T,
        event_bin,
        censored,
        patient_id.reshape(1, rows),
        patient_rows.reshape(1, patients),
    )
    return hg.T, tg.astype(F32), loss.reshape(())


def solution(mesh):
    return jax.shard_map(
        shards,
        mesh=mesh,
        in_specs=(
            P(("section", "row"), "task"),
            P("task", None),
            P("task", None),
            P("task", None),
            P(("section", "row"), "task"),
            P(("section", "row"), "task"),
            P(("section", "row")),
            P(),
        ),
        out_specs=(P(("section", "row"), "task"), P("task", None), P()),
        check_vma=False,
    )
```
